32 devices in a mesh: dp: 16 (over z, x, core), seq: 2 (over y).
Axes of the slice: x: 2, y: 2, z: 4, core: 2. Of those that a mesh axis runs over, the one named last changes fastest.
Arguments:
- frames: bfloat16 [16, 512, 1024], P('dp', 'seq'), may hold values from -6 to 6
- cotangent: bfloat16 [16, 512, 1024], P('dp', 'seq'), may hold values from -6 to 6
- clip_lengths: int32 [16, 2], P('dp'), may hold values from 1 to 400, 512 in all within a row
- params: float32 [16783360], P(('dp', 'seq')), may hold values from -1.5 to 1.5, as said below
- first_moment: float32 [16783360], P(('dp', 'seq')), may hold values from -6 to 6
- second_moment: float32 [16783360], P(('dp', 'seq')), may hold values from 0.1 to 10
Outputs:
- output: bfloat16 [16, 512, 1024], P('dp', 'seq')
- frames_grad: bfloat16 [16, 512, 1024], P('dp', 'seq')
- params_grad: float32 [16783360], P(('dp', 'seq'))
- new_params: float32 [16783360], P(('dp', 'seq'))
- new_first: float32 [16783360], P(('dp', 'seq'))
- new_second: float32 [16783360], P(('dp', 'seq'))
The draws below stay inside these ranges and needn't reach their ends.
Inputs may be any that keep to these rules, and one draw needn't show every extreme that they name: `clip_lengths`: row b lists in order the lengths of the clips packed into sequence b; its last entry counts the padding frames at the end. Each row sums to 512 and no entry exceeds 400. `params`: flat parameters laid out as in the reference program: four matrices, then two norm gains near 1, two norm biases and two layer scales.
All inputs are finite; a program needn't handle non-finite values.
Results may differ from the reference program's by a relative error of at most 0.012.
The reference program's roundings to bfloat16 on the way count: a program that leaves them out, or rounds other values in their place, can miss the bound.
Values may be sent and summed in bfloat16 or wider, within the bound.
No kernel may reach another device: no remote copies, remote signals or barrier semaphores. Data moves between devices by JAX's collectives and lax.ppermute only.
A program may use at most 256 MiB of HBM per device.

```python
import math
import jax
import jax.numpy as jnp
import numpy as np
from jax import lax

D = 1024
HEADS = 16
HEAD_DIM = 64
FF = 4096
WINDOW = 128
MOST_CLIP = 400
FRAMES = 256
LENGTH = 512
SEQS = 16
CLIPS = 2
PARAMS = 16783360


def draw_params(key, part):
    key = jax.random.fold_in(key, 17)
    end_qkv = D * 3 * D
    end_out = end_qkv + D * D
    end_mlp = end_out + D * 2 * FF
    end_down = end_mlp + FF * D
    total_size = end_down + 6 * D
    normal_part = jax.random.truncated_normal(jax.random.fold_in(key, 1), -4.0, 4.0, (total_size,), jnp.float32)
    even_part = jax.random.uniform(jax.random.fold_in(key, 2), (total_size,), jnp.float32, -1.0, 1.0)
    position = jnp.arange(total_size, dtype=jnp.int32)
    row_number = jnp.clip((position - end_down) // D, 0, 5)
    weight_scale = jnp.where(position < end_qkv, D ** (-0.5), jnp.where(position < end_out, (D // 16) ** (-0.5), jnp.where(position < end_mlp, D ** (-0.5), FF ** (-0.5))))
    center_table = jnp.array([1.0, 0.0, 1.0, 0.0, 1.0, 1.0], jnp.float32)
    spread_table = jnp.array([0.4, 0.5, 0.4, 0.5, 0.5, 0.5], jnp.float32)
    vector_part = center_table[row_number] + spread_table[row_number] * even_part
    return jnp.where(position < end_down, normal_part * weight_scale, vector_part).astype(jnp.float32)


def raised(values, rng, source, target, shards_of, factor):
    def block_of(dim):
        return (jnp.arange(values.shape[dim]) // (values.shape[dim] // shards_of)).reshape((-1,) + (1,) * (values.ndim - 1 - dim))

    near = jax.random.permutation(rng, shards_of)[block_of(target)]
    other_side = (block_of(target) + shards_of // 2) % shards_of
    return jnp.where((block_of(source) == near) | (block_of(source) == other_side), factor * values, values)


def block_levels(rng, dims, cuts, smallest, top_value):
    factor_of = 1.0
    for dim, shards_of in cuts:
        heights = jax.random.uniform(jax.random.fold_in(jax.random.fold_in(rng, 6), dim), (shards_of,), jnp.float32, smallest / len(cuts), top_value / len(cuts))
        factor_of = factor_of * jnp.repeat(jnp.exp(heights), dims[dim] // shards_of).reshape((-1,) + (1,) * (len(dims) - 1 - dim))
    return factor_of


def length_profile(count, total, bound, slope):
    loads = [(1 << 20) // math.isqrt(rank ** slope) + 1 for rank in range(2, count + 1)]
    rest, holding = total - bound - (count - 1), [1] * (count - 1)
    while rest > 0:
        free = [i for i in range(count - 1) if holding[i] < bound]
        pool, remaining = sum([loads[i] for i in free]), rest
        for i in free:
            more = min(bound - holding[i], max(1, remaining * loads[i] // pool), rest)
            holding[i] = holding[i] + more
            rest = rest - more
    return np.array([bound] + holding)


def ragged(stream_key, count, total, most, skew):
    if count == 2:
        one = jax.random.randint(stream_key, (), max(1, total - most), min(most, total - 1) + 1)
        return jnp.stack([one, total - one])
    tallies = jnp.asarray(length_profile(count, total, most, skew), jnp.int32)
    twos = (count - 1) // 2
    giver, taker = tallies[1:1 + 2 * twos:2], tallies[2:2 + 2 * twos:2]
    slack = jnp.minimum(giver - 1, most - taker)
    moved = jax.random.randint(jax.random.fold_in(stream_key, 1), (twos,), 0, 1 << 20) % (slack + 1)
    tallies = tallies.at[1:1 + 2 * twos:2].set(giver - moved).at[2:2 + 2 * twos:2].set(taker + moved)
    return tallies[jax.random.permutation(jax.random.fold_in(stream_key, 2), count)]


def centred(rng, shape, scale, bound, shards=(), held_as=jnp.bfloat16):
    entries = scale * jax.random.normal(rng, shape, jnp.float32)
    if shards:
        entries = entries * block_levels(rng, shape, shards, -0.22, 0.18)
    return jnp.clip(entries, -bound, bound).astype(held_as)


def heavy_noise(stream_key, dims, width, most, split, heavy, held_as=jnp.bfloat16):
    drawn = width * jax.random.normal(stream_key, dims, jnp.float32)
    if split:
        drawn = drawn * block_levels(stream_key, dims, split, -0.22, 0.18)
    return jnp.clip(raised(drawn, jax.random.fold_in(stream_key, 3), *heavy), -most, most).astype(held_as)


def setup_inputs(seed: int = 0) -> dict:
    key_list = jax.random.split(jax.random.key(seed), 7)
    return {
        "frames": centred(key_list[0], (SEQS, LENGTH, D), 1.0, 6.0, ((0, 16), (1, 2))),
        "cotangent": heavy_noise(key_list[1], (SEQS, LENGTH, D), 1.0, 6.0, ((0, 16), (1, 2)), (0, 2, 16, 2.0)),
        "clip_lengths": jax.vmap(lambda own: ragged(own, CLIPS, LENGTH, MOST_CLIP, 0))(jax.random.split(key_list[2], SEQS)).reshape((SEQS, CLIPS)).astype(jnp.int32),
        "params": draw_params(jax.random.fold_in(key_list[6], 71), 0),
        "first_moment": centred(key_list[4], (PARAMS,), 1.0, 6.0, ((0, 32),), jnp.float32),
        "second_moment": jnp.clip(jnp.exp(math.log(10.0) - 4.6051702 * jax.random.uniform(key_list[5], (PARAMS,), jnp.float32) ** block_levels(key_list[5], (PARAMS,), ((0, 32),), -0.2, 0.2)), 0.1, 10.0),
    }


@jax.custom_vjp
def low(v):
    return lax.optimization_barrier(v.astype(jnp.bfloat16)).astype(jnp.float32)

@jax.custom_vjp
def low_back(v):
    return v

def low_keep(v):
    return (low(v), None)

def low_pass(kept, grad):
    return (grad,)

def back_keep(v):
    return (v, None)

def back_low(kept, grad):
    return (low(grad),)
low.defvjp(low_keep, low_pass)
low_back.defvjp(back_keep, back_low)
eps_norm = 1e-05
beta_one = 0.9
beta_two = 0.99
learn_rate = 0.01
decay_rate = 0.1
eps_adam = 1e-08
adam_step = 100.0
neg_large = -1e+30
rope_base = 10000.0

def unpack(flat_params):
    end_qkv = D * 3 * D
    end_out = end_qkv + D * D
    end_mlp = end_out + D * 2 * FF
    end_down = end_mlp + FF * D
    w_qkv = flat_params[:end_qkv].reshape(D, 3 * D)
    w_out = flat_params[end_qkv:end_out].reshape(D, D)
    w_gate_up = flat_params[end_out:end_mlp].reshape(D, 2 * FF)
    w_down = flat_params[end_mlp:end_down].reshape(FF, D)
    vectors = flat_params[end_down:].reshape(6, D)
    return (w_qkv, w_out, w_gate_up, w_down, vectors)

def clip_info(lengths, glob):
    clip_ends = jnp.cumsum(lengths, dtype=jnp.int32)
    clip_starts = clip_ends - lengths
    segment = lax.optimization_barrier(jnp.sum((glob[:, None] >= clip_ends[None, :]).astype(jnp.int32), axis=1, dtype=jnp.int32))
    onehot = segment[:, None] == jnp.arange(lengths.shape[0], dtype=jnp.int32)[None, :]
    clip_begin = lax.optimization_barrier(jnp.sum(jnp.where(onehot, clip_starts[None, :], 0), axis=1, dtype=jnp.int32))
    return (segment, (glob - clip_begin).astype(jnp.float32))

def rotate(values, position):
    half_dim = values.shape[-1] // 2
    inverse = jnp.exp(jnp.arange(half_dim, dtype=jnp.float32) * (-2.0 * math.log(rope_base) / HEAD_DIM))
    rot_angle = position[:, None, None] * inverse
    cosine = jnp.cos(rot_angle)
    rot_sine = jnp.sin(rot_angle)
    low_half = values[..., :half_dim]
    high_half = values[..., half_dim:]
    return jnp.concatenate([low_half * cosine - high_half * rot_sine, high_half * cosine + low_half * rot_sine], axis=-1)

def layer_norm(row_vals, norm_gain, norm_bias):
    centered = row_vals - lax.optimization_barrier(jnp.mean(row_vals, axis=-1, keepdims=True))
    inv_scale = lax.rsqrt(lax.optimization_barrier(jnp.mean(centered * centered, axis=-1, keepdims=True)) + eps_norm)
    return centered * inv_scale * norm_gain + norm_bias

def matmul(left, right):
    return jnp.dot(left, right, precision=lax.Precision.HIGHEST, preferred_element_type=jnp.float32)

def run_layer(x_rows, flat_params, lengths):
    w_qkv, w_out, w_gate_up, w_down, vectors = unpack(low(flat_params))
    seq_len = x_rows.shape[0]
    key_count = FRAMES + 2 * WINDOW
    glob = jnp.arange(seq_len, dtype=jnp.int32)
    segment, position = clip_info(lengths, glob)
    glob_pad = jnp.arange(seq_len + 2 * WINDOW, dtype=jnp.int32) - WINDOW
    segment_pad, unused = clip_info(lengths, glob_pad)
    inside_pad = (glob_pad >= 0) & (glob_pad < seq_len)
    keep_rows = (segment != CLIPS - 1).astype(jnp.float32)
    near_band = jnp.abs(jnp.arange(FRAMES)[:, None] + WINDOW - jnp.arange(key_count)[None, :]) < WINDOW
    norm_one = layer_norm(x_rows, vectors[0], vectors[1])
    qkv = low_back(matmul(low(norm_one), w_qkv)).reshape(seq_len, 3, HEADS, HEAD_DIM)
    query_all = low(rotate(qkv[:, 0], position))
    key_all = low(rotate(qkv[:, 1], position))
    value_all = low(qkv[:, 2])
    key_pad = jnp.pad(key_all, ((WINDOW, WINDOW), (0, 0), (0, 0)))
    value_pad = jnp.pad(value_all, ((WINDOW, WINDOW), (0, 0), (0, 0)))
    score_scale = HEAD_DIM ** (-0.5)

    def score_block(block_index):
        row_start = (block_index * FRAMES).astype(jnp.int32)
        query_rows = lax.dynamic_slice_in_dim(query_all, row_start, FRAMES, 0)
        key_rows = lax.dynamic_slice_in_dim(key_pad, row_start, key_count, 0)
        value_rows = lax.dynamic_slice_in_dim(value_pad, row_start, key_count, 0)
        seg_rows = lax.dynamic_slice_in_dim(segment, row_start, FRAMES, 0)
        seg_keys = lax.dynamic_slice_in_dim(segment_pad, row_start, key_count, 0)
        inside = lax.dynamic_slice_in_dim(inside_pad, row_start, key_count, 0)
        window_mask = (seg_rows[:, None] == seg_keys[None, :]) & inside[None, :] & near_band
        raw_scores = jnp.einsum('qhd,khd->hqk', query_rows, key_rows, precision=lax.Precision.HIGHEST) * score_scale
        masked = jnp.where(window_mask[None], low_back(raw_scores), neg_large)
        prob_rows = low(jax.nn.softmax(masked, axis=-1))
        return jnp.einsum('hqk,khd->qhd', prob_rows, value_rows, precision=lax.Precision.HIGHEST)
    blocks = jnp.arange(seq_len // FRAMES, dtype=jnp.int32)
    attn = lax.map(jax.checkpoint(score_block), blocks).reshape(seq_len, HEADS, HEAD_DIM)
    attn_low = low(low_back(attn * keep_rows[:, None, None])).reshape(seq_len, D)
    branch_attn = low_back(matmul(attn_low, w_out))
    mid_rows = x_rows + vectors[4] * branch_attn
    norm_two = layer_norm(mid_rows, vectors[2], vectors[3])
    gate_up = low_back(matmul(low(norm_two), w_gate_up))
    hidden = low(jax.nn.silu(gate_up[:, :FF]) * gate_up[:, FF:])
    branch_mlp = low_back(matmul(hidden, w_down))
    return mid_rows + vectors[5] * branch_mlp

def adam_update(flat_params, grads, first_moment, second_moment):
    new_first = beta_one * first_moment + (1.0 - beta_one) * grads
    new_second = beta_two * second_moment + (1.0 - beta_two) * grads * grads
    corrected_first = new_first / (1.0 - beta_one ** adam_step)
    corrected_second = new_second / (1.0 - beta_two ** adam_step)
    step_size = corrected_first / (jnp.sqrt(corrected_second) + eps_adam) + decay_rate * flat_params
    return (flat_params - learn_rate * step_size, new_first, new_second)

def reference(frames, cotangent, clip_lengths, params, first_moment, second_moment):

    def seq_step(grad_total, seq_items):
        frame_seq, cot_seq, lengths = seq_items

        def layer_of(x_rows, flat_params):
            return run_layer(x_rows, flat_params, lengths)
        out_rows, back_fn = jax.vjp(layer_of, frame_seq.astype(jnp.float32), params)
        d_rows, d_params = back_fn(cot_seq.astype(jnp.float32))
        return (grad_total + d_params, (out_rows.astype(jnp.bfloat16), d_rows.astype(jnp.bfloat16)))
    params_grad, (output, frames_grad) = lax.scan(seq_step, jnp.zeros_like(params), (frames, cotangent, clip_lengths))
    new_params, new_first, new_second = adam_update(params, params_grad, first_moment, second_moment)
    return (output, frames_grad, params_grad, new_params, new_first, new_second)
```

```python
import math

import jax
import jax.numpy as jnp
import numpy as np
from jax import lax
from jax.experimental import pallas as pl
from jax.experimental.pallas import tpu as pltpu
from jax.sharding import Mesh
from jax.sharding import PartitionSpec as P

D = 1024
HEADS = 16
HEAD_DIM = 64
FF = 4096
WINDOW = 128


eps_norm = 1e-05
beta_one = 0.9
beta_two = 0.99
learn_rate = 0.01
decay_rate = 0.1
eps_adam = 1e-08
adam_step = 100.0
neg_large = -1e30
rope_base = 10000.0


def padded(shard, sides, width):
    for axis, dim in sides:
        size, length = (lax.axis_size(axis), shard.shape[dim])
        up = [(i, (i + 1) % size) for i in range(size - 1)]
        down = [(j, i) for i, j in up]
        last = lax.slice_in_dim(shard, length - width, length, axis=dim)
        first = lax.slice_in_dim(shard, 0, width, axis=dim)
        before = lax.ppermute(last, axis, up)
        after = lax.ppermute(first, axis, down)
        shard = jnp.concatenate([before, shard, after], axis=dim)
    return shard


def unpack(flat_params):
    end_qkv = D * 3 * D
    end_out = end_qkv + D * D
    end_mlp = end_out + D * 2 * FF
    end_down = end_mlp + FF * D
    w_qkv = flat_params[:end_qkv].reshape(D, 3 * D)
    w_out = flat_params[end_qkv:end_out].reshape(D, D)
    w_gate_up = flat_params[end_out:end_mlp].reshape(D, 2 * FF)
    w_down = flat_params[end_mlp:end_down].reshape(FF, D)
    vectors = flat_params[end_down:].reshape(6, D).astype(jnp.float32)
    return (w_qkv, w_out, w_gate_up, w_down, vectors)


def clip_info(lengths, glob):
    clip_ends = jnp.cumsum(lengths, axis=1, dtype=jnp.int32)
    clip_starts = clip_ends - lengths
    after_end = (glob[None, :, None] >= clip_ends[:, None, :]).astype(jnp.int32)
    segment = jnp.sum(after_end, axis=2, dtype=jnp.int32)
    onehot = segment[:, :, None] == jnp.arange(lengths.shape[1], dtype=jnp.int32)[None, None, :]
    clip_begin = jnp.sum(jnp.where(onehot, clip_starts[:, None, :], 0), axis=2, dtype=jnp.int32)
    return (segment, (glob[None, :] - clip_begin).astype(jnp.float32))


def rotate(values, position, sign):
    half_dim = values.shape[-1] // 2
    inverse = jnp.exp(
        jnp.arange(half_dim, dtype=jnp.float32) * (-2.0 * math.log(rope_base) / HEAD_DIM)
    )
    rot_angle = position[:, :, None, None] * inverse
    cosine = jnp.cos(rot_angle)
    rot_sine = sign * jnp.sin(rot_angle)
    low_half = values[..., :half_dim]
    high_half = values[..., half_dim:]
    return jnp.concatenate(
        [low_half * cosine - high_half * rot_sine, high_half * cosine + low_half * rot_sine],
        axis=-1,
    )


def norm_forward(row_vals, norm_gain, norm_bias):
    centered = row_vals - jnp.mean(row_vals, axis=-1, keepdims=True)
    inv_scale = lax.rsqrt(jnp.mean(centered * centered, axis=-1, keepdims=True) + eps_norm)
    normed = centered * inv_scale
    return (normed * norm_gain + norm_bias, normed, inv_scale)


def norm_backward(out_grad, normed, inv_scale, norm_gain):
    d_gain = jnp.sum(out_grad * normed, axis=0)
    d_bias = jnp.sum(out_grad, axis=0)
    inner_grad = out_grad * norm_gain
    d_rows = inv_scale * (
        inner_grad
        - jnp.mean(inner_grad, axis=-1, keepdims=True)
        - normed * jnp.mean(inner_grad * normed, axis=-1, keepdims=True)
    )
    return (d_rows, d_gain, d_bias)


def scores_of(query_rows, key_rows, window_mask):
    raw_scores = jnp.einsum(
        "qhd,khd->hqk", query_rows, key_rows, preferred_element_type=jnp.float32
    ) * HEAD_DIM ** (-0.5)
    return jnp.where(window_mask[None], raw_scores, neg_large)


def attend(query_rows, key_rows, value_rows, window_mask):
    masked = scores_of(query_rows, key_rows, window_mask)
    row_max = jnp.max(masked, axis=-1, keepdims=True)
    row_total = jnp.log(jnp.sum(jnp.exp(masked - row_max), axis=-1, keepdims=True)) + row_max
    prob_low = jnp.exp(masked - row_total).astype(jnp.bfloat16)
    attn_rows = jnp.einsum("hqk,khd->qhd", prob_low, value_rows, preferred_element_type=jnp.float32)
    return (attn_rows, row_total[..., 0])


def attend_back(query_rows, key_rows, value_rows, window_mask, row_total, d_attn):
    masked = scores_of(query_rows, key_rows, window_mask)
    prob_rows = jnp.exp(masked - row_total[..., None])
    prob_low = prob_rows.astype(jnp.bfloat16)
    d_values = jnp.einsum("hqk,qhd->khd", prob_low, d_attn, preferred_element_type=jnp.float32)
    d_probs = jnp.einsum("qhd,khd->hqk", d_attn, value_rows, preferred_element_type=jnp.float32)
    inner_sum = jnp.sum(prob_rows * d_probs, axis=-1, keepdims=True)
    d_scores = (prob_rows * (d_probs - inner_sum)).astype(jnp.bfloat16)
    d_query = jnp.einsum(
        "hqk,khd->qhd", d_scores, key_rows, preferred_element_type=jnp.float32
    ) * HEAD_DIM ** (-0.5)
    d_keys = jnp.einsum(
        "hqk,qhd->khd", d_scores, query_rows, preferred_element_type=jnp.float32
    ) * HEAD_DIM ** (-0.5)
    return (d_query, d_keys, d_values)


def adam_update(flat_params, grads, first_moment, second_moment):
    new_first = beta_one * first_moment + (1.0 - beta_one) * grads
    new_second = beta_two * second_moment + (1.0 - beta_two) * grads * grads
    corrected_first = new_first / (1.0 - beta_one**adam_step)
    corrected_second = new_second / (1.0 - beta_two**adam_step)
    step_size = corrected_first / (jnp.sqrt(corrected_second) + eps_adam) + decay_rate * flat_params
    return (flat_params - learn_rate * step_size, new_first, new_second)


def body(frames, cotangent, clip_lengths, params, first_moment, second_moment):
    seq_count, frame_span, model_width = frames.shape
    row_count = seq_count * frame_span
    window_reach = WINDOW
    key_count = frame_span + 2 * window_reach
    head_count = HEADS
    head_size = model_width // head_count
    group_size = 4
    seq_len = lax.axis_size("seq") * frame_span
    seq_start = lax.axis_index("seq") * frame_span
    glob_rows = seq_start + jnp.arange(frame_span, dtype=jnp.int32)
    glob_keys = seq_start - window_reach + jnp.arange(key_count, dtype=jnp.int32)
    seg_rows, pos_rows = clip_info(clip_lengths, glob_rows)
    seg_keys, unused = clip_info(clip_lengths, glob_keys)
    inside = (glob_keys >= 0) & (glob_keys < seq_len)
    near_band = (
        jnp.abs(jnp.arange(frame_span)[:, None] + window_reach - jnp.arange(key_count)[None, :])
        < window_reach
    )
    window_mask = (
        (seg_rows[:, :, None] == seg_keys[:, None, :]) & inside[None, None, :] & near_band[None]
    )
    keep_rows = seg_rows != clip_lengths.shape[1] - 1
    shards = params.astype(jnp.bfloat16)
    gathered = lax.all_gather(shards, ("dp", "seq"), axis=0, tiled=True)
    w_qkv, w_out, w_gate_up, w_down, vectors = unpack(gathered)
    x_rows = frames.reshape(row_count, model_width).astype(jnp.float32)
    norm_one, normed_one, scale_one = norm_forward(x_rows, vectors[0], vectors[1])
    a_low = norm_one.astype(jnp.bfloat16)
    qkv = jnp.dot(a_low, w_qkv, preferred_element_type=jnp.float32).reshape(
        seq_count, frame_span, 3, head_count, head_size
    )
    query_low = rotate(qkv[:, :, 0], pos_rows, 1.0).astype(jnp.bfloat16)
    key_low = rotate(qkv[:, :, 1], pos_rows, 1.0).astype(jnp.bfloat16)
    value_low = qkv[:, :, 2].astype(jnp.bfloat16)
    key_value = jnp.concatenate([key_low, value_low], axis=2).reshape(
        seq_count, frame_span, 2 * model_width
    )
    wide_rows = padded(key_value, (("seq", 1),), window_reach)
    wide_rows = wide_rows.reshape(seq_count, key_count, 2, head_count, head_size)
    key_wide = wide_rows[:, :, 0]
    value_wide = wide_rows[:, :, 1]
    seq_index = 0
    out_parts = []
    total_parts = []
    for head_start in range(0, head_count, group_size):
        head_end = head_start + group_size
        attn_rows, row_total = attend(
            query_low[seq_index, :, head_start:head_end],
            key_wide[seq_index, :, head_start:head_end],
            value_wide[seq_index, :, head_start:head_end],
            window_mask[seq_index],
        )
        out_parts.append(attn_rows)
        total_parts.append(row_total)
    attn_list = [jnp.concatenate(out_parts, axis=1)]
    total_list = [total_parts]
    attn_all = jnp.where(keep_rows[:, :, None, None], jnp.stack(attn_list), 0.0)
    attn_low = attn_all.reshape(row_count, model_width).astype(jnp.bfloat16)
    branch_attn = jnp.dot(attn_low, w_out, preferred_element_type=jnp.float32)
    mid_rows = x_rows + vectors[4] * branch_attn
    norm_two, normed_two, scale_two = norm_forward(mid_rows, vectors[2], vectors[3])
    c_low = norm_two.astype(jnp.bfloat16)
    gate_up = jnp.dot(c_low, w_gate_up, preferred_element_type=jnp.float32)
    gate = gate_up[:, :FF]
    up_rows = gate_up[:, FF:]
    gate_sig = jax.nn.sigmoid(gate)
    hidden = (gate * gate_sig * up_rows).astype(jnp.bfloat16)
    branch_mlp = jnp.dot(hidden, w_down, preferred_element_type=jnp.float32)
    output = (
        (mid_rows + vectors[5] * branch_mlp)
        .astype(jnp.bfloat16)
        .reshape(seq_count, frame_span, model_width)
    )
    gathered = lax.all_gather(shards, ("dp", "seq"), axis=0, tiled=True)
    w_qkv, w_out, w_gate_up, w_down, vectors = unpack(gathered)
    d_rows = cotangent.reshape(row_count, model_width).astype(jnp.float32)
    g_scale_mlp = jnp.sum(d_rows * branch_mlp, axis=0)
    d_mlp = (d_rows * vectors[5]).astype(jnp.bfloat16)
    g_down = jnp.dot(hidden.T, d_mlp, preferred_element_type=jnp.float32)
    d_hidden = jnp.dot(d_mlp, w_down.T, preferred_element_type=jnp.float32)
    d_gate = d_hidden * up_rows * gate_sig * (1.0 + gate * (1.0 - gate_sig))
    d_up = d_hidden * gate * gate_sig
    d_gate_up = jnp.concatenate([d_gate, d_up], axis=1).astype(jnp.bfloat16)
    g_gate_up = jnp.dot(c_low.T, d_gate_up, preferred_element_type=jnp.float32)
    d_two = jnp.dot(d_gate_up, w_gate_up.T, preferred_element_type=jnp.float32)
    d_norm_two, g_gain_two, g_bias_two = norm_backward(d_two, normed_two, scale_two, vectors[2])
    d_mid = d_rows + d_norm_two
    g_scale_attn = jnp.sum(d_mid * branch_attn, axis=0)
    d_branch = (d_mid * vectors[4]).astype(jnp.bfloat16)
    g_out = jnp.dot(attn_low.T, d_branch, preferred_element_type=jnp.float32)
    d_attn_low = jnp.dot(d_branch, w_out.T, preferred_element_type=jnp.float32).astype(jnp.bfloat16)
    d_attn = jnp.where(
        keep_rows[:, :, None, None],
        d_attn_low.reshape(seq_count, frame_span, head_count, head_size),
        jnp.zeros((), jnp.bfloat16),
    )
    seq_index = 0
    query_parts = []
    key_parts = []
    value_parts = []
    for number, head_start in enumerate(range(0, head_count, group_size)):
        head_end = head_start + group_size
        d_query, d_keys, d_values = attend_back(
            query_low[seq_index, :, head_start:head_end],
            key_wide[seq_index, :, head_start:head_end],
            value_wide[seq_index, :, head_start:head_end],
            window_mask[seq_index],
            total_list[seq_index][number],
            d_attn[seq_index, :, head_start:head_end],
        )
        query_parts.append(d_query)
        key_parts.append(d_keys)
        value_parts.append(d_values)
    query_grads = [jnp.concatenate(query_parts, axis=1)]
    key_grads = [jnp.concatenate(key_parts, axis=1)]
    value_grads = [jnp.concatenate(value_parts, axis=1)]
    d_query_all = jnp.stack(query_grads)
    d_pair = jnp.concatenate([jnp.stack(key_grads), jnp.stack(value_grads)], axis=2).reshape(
        seq_count, key_count, 2 * model_width
    )
    rim_rows = jnp.concatenate(
        [d_pair[:, :window_reach], d_pair[:, window_reach + frame_span :]], axis=1
    )
    taken_rows = padded(rim_rows.astype(jnp.bfloat16), (("seq", 1),), window_reach).astype(
        rim_rows.dtype
    )
    own_rows = d_pair[:, window_reach : window_reach + frame_span]
    own_rows = own_rows + jnp.pad(
        taken_rows[:, :window_reach], ((0, 0), (0, frame_span - window_reach), (0, 0))
    )
    own_rows = own_rows + jnp.pad(
        taken_rows[:, 3 * window_reach :], ((0, 0), (frame_span - window_reach, 0), (0, 0))
    )
    own_rows = own_rows.reshape(seq_count, frame_span, 2, head_count, head_size)
    d_qkv = jnp.stack(
        [
            rotate(d_query_all, pos_rows, -1.0),
            rotate(own_rows[:, :, 0], pos_rows, -1.0),
            own_rows[:, :, 1],
        ],
        axis=2,
    )
    d_qkv = d_qkv.reshape(row_count, 3 * model_width).astype(jnp.bfloat16)
    g_qkv = jnp.dot(a_low.T, d_qkv, preferred_element_type=jnp.float32)
    d_one = jnp.dot(d_qkv, w_qkv.T, preferred_element_type=jnp.float32)
    d_norm_one, g_gain_one, g_bias_one = norm_backward(d_one, normed_one, scale_one, vectors[0])
    frames_grad = (
        (d_mid + d_norm_one).astype(jnp.bfloat16).reshape(seq_count, frame_span, model_width)
    )
    small_grads = jnp.stack(
        [g_gain_one, g_bias_one, g_gain_two, g_bias_two, g_scale_attn, g_scale_mlp]
    )
    whole_grad = jnp.concatenate(
        [
            g_qkv.reshape(-1),
            g_out.reshape(-1),
            g_gate_up.reshape(-1),
            g_down.reshape(-1),
            small_grads.reshape(-1),
        ]
    )
    params_grad = lax.psum_scatter(whole_grad, ("dp", "seq"), scatter_dimension=0, tiled=True)
    new_params, new_first, new_second = adam_update(
        params, params_grad, first_moment, second_moment
    )
    return (output, frames_grad, params_grad, new_params, new_first, new_second)


EVERY = ("z", "x", "c", "y")
GROUP = ("z", "x")
RING = ((0, 0), (1, 0), (2, 0), (3, 0), (3, 1), (2, 1), (1, 1), (0, 1))
PLACES = tuple(2 * z + x for z, x in RING)
AHEAD = tuple((PLACES[i], PLACES[(i + 1) % 8]) for i in range(8))
BACK = tuple((b, a) for a, b in AHEAD)
SWAP = ((0, 1), (1, 0))
LINES = 4096
TAIL = 64
SLAB = 16
ROWS = 128 + SLAB
OWN = 256
SCALE = HEAD_DIM ** (-0.5)
VMEM = pltpu.CompilerParams(vmem_limit_bytes=48 * 1024 * 1024)


def kind_of(shard):
    if shard < 6:
        return 0
    return 2 if 8 <= shard < 24 else 1


def piece_lines(kind, dest):
    place, member = divmod(dest, 4)
    if kind == 0:
        return [(512 * place + member, 8), (512 * place + 4 + member, 8)]
    if kind == 1:
        return [(1024 * member + place, 8), (1024 * member + 512 + place, 8)]
    return [(dest, 64), (32 + dest, 64)]


def tail_lines(kind, dest):
    place, member = divmod(dest, 4)
    if kind == 0:
        return [(0, 6, member, 8), (8, 6, 4 + member, 8)] if place == 0 else []
    if kind == 1:
        return [(0, 6, place, 8)] if member == 0 else []
    return [(0, 1, dest, 1)] + ([(8, 1, 32 + dest, 1)] if dest < 16 else [])


def is_kind(shard, kind):
    if kind == 0:
        return shard < 6
    gate_up = (shard >= 8) & (shard < 24)
    if kind == 2:
        return gate_up
    return (shard >= 6) & jnp.logical_not(gate_up) & (shard < 32)


def spread_kernel(me_ref, flat_ref, out_ref, lines_ref):
    me = me_ref[0]
    odd = lax.rem(me, 2) == 1
    start = 48 - (3 * me + 1) // 2
    lane = lax.broadcasted_iota(jnp.int32, (64, 128), 1)

    def shift(step, carry):
        here = flat_ref[pl.ds(start + step * 64, 64), :]
        after = flat_ref[pl.ds(start + step * 64 + 1, 64), :]
        mixed = jnp.where(lane < 64, pltpu.roll(here, 64, 1), pltpu.roll(after, 64, 1))
        lines_ref[pl.ds(pl.multiple_of(step * 64, 64), 64), :] = jnp.where(odd, mixed, here)
        return carry

    lax.fori_loop(0, (LINES + TAIL) // 64, shift, 0, unroll=5)
    for kind in range(3):

        @pl.when(is_kind(me, kind))
        def _(kind=kind):
            for dest in range(32):
                for half, (first, stride) in enumerate(piece_lines(kind, dest)):
                    rows = lines_ref[pl.ds(first, 64, stride), :]
                    out_ref[dest, 64 * half : 64 * half + 64, :] = rows.astype(jnp.bfloat16)

    def slab_of(parts):
        slab = [jnp.zeros((8, 128), jnp.float32)] * 2
        row = lax.broadcasted_iota(jnp.int32, (8, 128), 0)
        for at, count, first, stride in parts:
            if count == 1:
                value = jnp.broadcast_to(lines_ref[LINES + first : LINES + first + 1, :], (8, 128))
            else:
                value = lines_ref[pl.ds(LINES + first, 8, stride), :]
            slab[at // 8] = jnp.where(row < count, value, 0.0)
        return jnp.concatenate(slab, axis=0).astype(jnp.bfloat16)

    for kind in range(3):

        @pl.when(is_kind(me + 1, kind))
        def _(kind=kind):
            for dest in range(32):
                out_ref[dest, 128:ROWS, :] = slab_of(tail_lines(kind, dest))

    @pl.when(me == 31)
    def _():
        for dest in range(32):
            out_ref[dest, 128:ROWS, :] = slab_of([(0, 6, 6 * (dest // 4), 1)])


def spread(params, me):
    flat = jnp.pad(params, (48 * 128, 4224 * 128 - 48 * 128 - params.shape[0])).reshape(4224, 128)
    return pl.pallas_call(
        spread_kernel,
        out_shape=jax.ShapeDtypeStruct((32, ROWS, 128), jnp.bfloat16),
        in_specs=[
            pl.BlockSpec(memory_space=pltpu.SMEM),
            pl.BlockSpec(memory_space=pltpu.VMEM),
        ],
        out_specs=pl.BlockSpec(memory_space=pltpu.VMEM),
        scratch_shapes=[pltpu.VMEM((LINES + TAIL, 128), jnp.float32)],
        compiler_params=VMEM,
        name="spread",
    )(me, flat)


def collect_kernel(me_ref, piece_ref, out_ref, lines_ref):
    me = me_ref[0]
    odd = lax.rem(me, 2) == 1
    lines_ref[LINES:, :] = jnp.zeros((TAIL, 128), jnp.float32)
    for kind in range(3):

        @pl.when(is_kind(me, kind))
        def _(kind=kind):
            for dest in range(32):
                for half, (first, stride) in enumerate(piece_lines(kind, dest)):
                    rows = piece_ref[dest, 64 * half : 64 * half + 64, :].astype(jnp.float32)
                    lines_ref[pl.ds(first, 64, stride), :] = rows

    for kind in range(3):

        @pl.when(is_kind(me + 1, kind))
        def _(kind=kind):
            for dest in range(32):
                slab = piece_ref[dest, 128:ROWS, :].astype(jnp.float32)
                for at, count, first, stride in tail_lines(kind, dest):
                    for k in range(count):
                        line = LINES + first + k * stride
                        lines_ref[line : line + 1, :] = slab[at + k : at + k + 1, :]

    @pl.when(me == 31)
    def _():
        for place in range(8):
            total = piece_ref[4 * place, 128:ROWS, :].astype(jnp.float32)
            for member in range(1, 4):
                total = total + piece_ref[4 * place + member, 128:ROWS, :].astype(jnp.float32)
            for k in range(6):
                line = LINES + 6 * place + k
                lines_ref[line : line + 1, :] = total[k : k + 1, :]

    start = (3 * me) // 2
    lane = lax.broadcasted_iota(jnp.int32, (24, 128), 1)

    def shift(step, carry):
        here = lines_ref[pl.ds(start + step * 24, 24), :]
        after = lines_ref[pl.ds(start + step * 24 + 1, 24), :]
        mixed = jnp.where(lane < 64, pltpu.roll(here, 64, 1), pltpu.roll(after, 64, 1))
        out_ref[pl.ds(pl.multiple_of(step * 24, 8), 24), :] = jnp.where(odd, mixed, here)
        return carry

    lax.fori_loop(0, 4104 // 24, shift, 0, unroll=9)


def collect(pieces, me, count):
    lines = pl.pallas_call(
        collect_kernel,
        out_shape=jax.ShapeDtypeStruct((4104, 128), jnp.float32),
        in_specs=[
            pl.BlockSpec(memory_space=pltpu.SMEM),
            pl.BlockSpec(memory_space=pltpu.VMEM),
        ],
        out_specs=pl.BlockSpec(memory_space=pltpu.VMEM),
        scratch_shapes=[pltpu.VMEM((LINES + TAIL, 128), jnp.float32)],
        compiler_params=VMEM,
        name="collect",
    )(me, pieces)
    return lines.reshape(-1)[:count]


def swap_halves(rows):
    lane = lax.broadcasted_iota(jnp.int32, rows.shape, 1)
    return jnp.where(
        lax.rem(lane, 64) < 32, pltpu.roll(rows, 96, 1), pltpu.roll(rows, 32, 1)
    )


def turn(rows, cosine, signed_sine):
    parts = []
    for at in range(0, rows.shape[1], 128):
        part = rows[:, at : at + 128]
        parts.append(part * cosine + swap_halves(part) * signed_sine)
    return jnp.concatenate(parts, axis=1)


def mask_of(seg_col_ref, seg_row_ref, block):
    row = lax.broadcasted_iota(jnp.int32, (256, 384), 0) + 256 * block
    key = lax.broadcasted_iota(jnp.int32, (256, 384), 1) + 128 * block
    near = jnp.abs(row - key) < WINDOW
    same = seg_col_ref[0, 256 * block : 256 * block + 256, :] == seg_row_ref[0, :, 128 * block : 128 * block + 384]
    return near & same


def nt(left, right):
    return lax.dot_general(left, right, (((1,), (1,)), ((), ())), preferred_element_type=jnp.float32)


def tn(left, right):
    return lax.dot_general(left, right, (((0,), (0,)), ((), ())), preferred_element_type=jnp.float32)


def nn(left, right):
    return jnp.dot(left, right, preferred_element_type=jnp.float32)


def attend_kernel(qkv_ref, cos_ref, sin_ref, seg_col_ref, seg_row_ref, low_ref, attn_ref, lse_ref):
    cosine, sine = cos_ref[0], sin_ref[0]
    low_ref[0, :, :OWN] = turn(qkv_ref[0, :, :OWN], cosine, sine).astype(jnp.bfloat16)
    low_ref[0, :, OWN : 2 * OWN] = turn(qkv_ref[0, :, OWN : 2 * OWN], cosine, sine).astype(jnp.bfloat16)
    low_ref[0, :, 2 * OWN :] = qkv_ref[0, :, 2 * OWN :].astype(jnp.bfloat16)
    for block in range(2):
        rows = slice(256 * block, 256 * block + 256)
        keys = slice(128 * block, 128 * block + 384)
        mask = mask_of(seg_col_ref, seg_row_ref, block)
        keep = seg_col_ref[0, rows, :] != 1
        heads, sums = [], []
        for head in range(4):
            at = 64 * head
            query = low_ref[0, rows, at : at + 64]
            key = low_ref[0, keys, OWN + at : OWN + at + 64]
            value = low_ref[0, keys, 2 * OWN + at : 2 * OWN + at + 64]
            masked = jnp.where(mask, nt(query, key) * SCALE, neg_large)
            top = jnp.max(masked, axis=1, keepdims=True)
            weight = jnp.exp(masked - top)
            total = jnp.sum(weight, axis=1, keepdims=True)
            probs = (weight * (1.0 / total)).astype(jnp.bfloat16)
            heads.append(jnp.where(keep, nn(probs, value), 0.0))
            sums.append(top + jnp.log(total))
        attn_ref[0, rows, :] = jnp.concatenate(heads, axis=1).astype(jnp.bfloat16)
        lse_ref[0, rows, :] = jnp.concatenate(sums, axis=1)


def attend_rows(qkv, cosine, sine, seg):
    per = lambda *dims: pl.BlockSpec((1,) + dims, lambda s: (s,) + (0,) * len(dims))
    return pl.pallas_call(
        attend_kernel,
        grid=(2,),
        out_shape=(
            jax.ShapeDtypeStruct((2, 512, 3 * OWN), jnp.bfloat16),
            jax.ShapeDtypeStruct((2, 512, OWN), jnp.bfloat16),
            jax.ShapeDtypeStruct((2, 512, 4), jnp.float32),
        ),
        in_specs=[per(512, 3 * OWN), per(512, 128), per(512, 128), per(512, 1), per(1, 512)],
        out_specs=(per(512, 3 * OWN), per(512, OWN), per(512, 4)),
        compiler_params=VMEM,
        name="attend",
    )(qkv, cosine, sine, seg[:, :, None], seg[:, None, :])


def attend_back_kernel(low_ref, lse_ref, d_attn_ref, cos_ref, sin_ref, seg_col_ref, seg_row_ref, out_ref, key_ref, value_ref):
    cosine, sine = cos_ref[0], -sin_ref[0]
    key_ref[...] = jnp.zeros_like(key_ref)
    value_ref[...] = jnp.zeros_like(value_ref)
    for block in range(2):
        rows = slice(256 * block, 256 * block + 256)
        keys = slice(128 * block, 128 * block + 384)
        mask = mask_of(seg_col_ref, seg_row_ref, block)
        keep = seg_col_ref[0, rows, :] != 1
        d_queries, d_keys, d_values = [], [], []
        for head in range(4):
            at = 64 * head
            query = low_ref[0, rows, at : at + 64]
            key = low_ref[0, keys, OWN + at : OWN + at + 64]
            value = low_ref[0, keys, 2 * OWN + at : 2 * OWN + at + 64]
            d_attn = d_attn_ref[0, rows, at : at + 64]
            d_attn = jnp.where(keep, d_attn, jnp.zeros_like(d_attn))
            masked = jnp.where(mask, nt(query, key) * SCALE, neg_large)
            probs = jnp.exp(masked - lse_ref[0, rows, head : head + 1])
            d_values.append(tn(probs.astype(jnp.bfloat16), d_attn))
            d_probs = nt(d_attn, value)
            inner = jnp.sum(probs * d_probs, axis=1, keepdims=True)
            d_scores = (probs * (d_probs - inner)).astype(jnp.bfloat16)
            d_queries.append(nn(d_scores, key) * SCALE)
            d_keys.append(tn(d_scores, query) * SCALE)
        d_query = turn(jnp.concatenate(d_queries, axis=1), cosine[rows], sine[rows])
        out_ref[0, rows, :OWN] = d_query.astype(jnp.bfloat16)
        key_ref[keys, :] += jnp.concatenate(d_keys, axis=1)
        value_ref[keys, :] += jnp.concatenate(d_values, axis=1)
    out_ref[0, :, OWN : 2 * OWN] = turn(key_ref[...], cosine, sine).astype(jnp.bfloat16)
    out_ref[0, :, 2 * OWN :] = value_ref[...].astype(jnp.bfloat16)


def attend_rows_back(low, lse, d_attn, cosine, sine, seg):
    per = lambda *dims: pl.BlockSpec((1,) + dims, lambda s: (s,) + (0,) * len(dims))
    return pl.pallas_call(
        attend_back_kernel,
        grid=(2,),
        out_shape=jax.ShapeDtypeStruct((2, 512, 3 * OWN), jnp.bfloat16),
        in_specs=[
            per(512, 3 * OWN), per(512, 4), per(512, OWN), per(512, 128), per(512, 128), per(512, 1), per(1, 512),
        ],
        out_specs=per(512, 3 * OWN),
        scratch_shapes=[pltpu.VMEM((512, OWN), jnp.float32), pltpu.VMEM((512, OWN), jnp.float32)],
        compiler_params=VMEM,
        name="attend_back",
    )(low, lse, d_attn, cosine, sine, seg[:, :, None], seg[:, None, :])


def ring_gather(block, ids):
    rows = block.shape[0]
    half = rows // 2
    total = jnp.zeros((8, rows, 128), block.dtype)

    def put(total, part, step, row=0):
        return lax.dynamic_update_slice(total, part[None], (ids[step % 8], row, 0))

    total = put(total, block, 0)
    ahead = back = block
    for step in range(1, 4):
        ahead = lax.ppermute(ahead, GROUP, AHEAD)
        back = lax.ppermute(back, GROUP, BACK)
        total = put(put(total, ahead, 8 - step), back, step)
    ahead = lax.ppermute(ahead[:half], GROUP, AHEAD)
    back = lax.ppermute(back[half:], GROUP, BACK)
    return put(put(total, ahead, 4), back, 4, half)


def ring_scatter(blocks, ids):
    half = blocks.shape[1] // 2

    def get(step, lo=0, hi=2 * half):
        return lax.dynamic_slice(blocks, (ids[step % 8], lo, 0), (1, hi - lo, 128))[0]

    def add(moved, own):
        return (moved.astype(jnp.float32) + own.astype(jnp.float32)).astype(jnp.bfloat16)

    ahead = lax.ppermute(get(4, 0, half), GROUP, AHEAD)
    back = lax.ppermute(get(4, half, 2 * half), GROUP, BACK)
    ahead = jnp.concatenate([add(ahead, get(3, 0, half)), get(3, half, 2 * half)])
    back = jnp.concatenate([get(5, 0, half), add(back, get(5, half, 2 * half))])
    for step in range(2, 0, -1):
        ahead = add(lax.ppermute(ahead, GROUP, AHEAD), get(step))
        back = add(lax.ppermute(back, GROUP, BACK), get(8 - step))
    ahead = lax.ppermute(ahead, GROUP, AHEAD)
    back = lax.ppermute(back, GROUP, BACK)
    total = get(0).astype(jnp.float32) + ahead.astype(jnp.float32) + back.astype(jnp.float32)
    return total.astype(jnp.bfloat16)


def group_rows(rows, on_first):
    other = lax.ppermute(rows, "y", SWAP)
    first = jnp.where(on_first, rows, other)
    second = jnp.where(on_first, other, rows)
    here = jnp.concatenate([first, second], axis=0)
    return jnp.stack([here, lax.ppermute(here, "c", SWAP)])


def sum_rows(partial, on_first):
    near = lax.ppermute(partial[1].astype(jnp.bfloat16), "c", SWAP)
    here = partial[0] + near.astype(jnp.float32)
    sent = jnp.where(on_first, here[256:], here[:256]).astype(jnp.bfloat16)
    kept = jnp.where(on_first, here[:256], here[256:])
    return kept + lax.ppermute(sent, "y", SWAP).astype(jnp.float32)


def normed_of(rows):
    centered = rows - jnp.mean(rows, axis=-1, keepdims=True)
    inv_scale = lax.rsqrt(jnp.mean(centered * centered, axis=-1, keepdims=True) + eps_norm)
    return centered * inv_scale, inv_scale


def norm_rows_back(out_grad, normed, inv_scale, gain):
    inner = out_grad * gain
    return inv_scale * (
        inner
        - jnp.mean(inner, axis=-1, keepdims=True)
        - normed * jnp.mean(inner * normed, axis=-1, keepdims=True)
    )


def fast_body(frames, cotangent, clip_lengths, params, first_moment, second_moment):
    z, x, c, y = (lax.axis_index(axis) for axis in EVERY)
    me = (((z * 2 + x) * 2 + c) * 2 + y).astype(jnp.int32)
    on_first = y == 0
    place = jnp.asarray([PLACES.index(i) for i in range(8)], jnp.int32)[z * 2 + x]
    ids = lax.dynamic_slice(jnp.asarray(PLACES + PLACES, jnp.int32), (place,), (8,))
    ids = [ids[i] for i in range(8)]

    def own_rows(whole):
        return jnp.where(on_first, whole[0, :256], whole[0, 256:])

    pieces = spread(params, me[None])
    pieces = lax.all_to_all(pieces, EVERY, split_axis=0, concat_axis=0, tiled=True)
    main = pieces[:, :128]
    before = jnp.pad(pieces[:-1, 128:], ((1, 0), (0, 0), (0, 0)))
    main = jnp.concatenate(
        [main[:, :8] + before[:, :8], main[:, 8:64], main[:, 64:72] + before[:, 8:], main[:, 72:]], axis=1
    )
    first_ring = jnp.concatenate([main[:8].reshape(1024, 128), pieces[31, 128:]])
    first_ring = ring_gather(first_ring, ids)
    gate_up_ring = ring_gather(main[8:24].reshape(2048, 128), ids)
    down_ring = ring_gather(main[24:].reshape(1024, 128), ids)

    vectors = first_ring[:, 1024:1030].reshape(6, D).astype(jnp.float32)
    order = np.zeros((384, 384), np.float32)
    for row in range(384):
        order[(row % 3) * 128 + row // 3, row] = 1.0
    order = jnp.asarray(order, jnp.bfloat16)
    w_qkv = first_ring[:, :768].reshape(8, 6, 2, 64, 128).transpose(1, 0, 3, 2, 4).reshape(8, 384, OWN)
    w_qkv = jnp.einsum("pv,gvn->gpn", order, w_qkv, preferred_element_type=jnp.float32).astype(jnp.bfloat16)
    w_qkv = w_qkv.reshape(8, 3, 128, OWN).transpose(0, 2, 1, 3).reshape(D, 3 * OWN)
    w_out_own = first_ring[:, 768:1024].transpose(1, 0, 2).reshape(OWN, D)
    w_out_pair = jnp.concatenate([w_out_own, lax.ppermute(w_out_own, "y", SWAP)])
    w_out = jnp.concatenate([w_out_pair, lax.ppermute(w_out_pair, "c", SWAP)])
    w_gate_up = gate_up_ring.reshape(8, 16, 2, 64, 128).transpose(1, 3, 2, 0, 4).reshape(D, 2048)
    w_down = down_ring.transpose(1, 0, 2).reshape(1024, D)

    frames_all = group_rows(frames[0], on_first)
    cot_all = group_rows(cotangent[0], on_first)
    lengths = jnp.concatenate([clip_lengths, lax.ppermute(clip_lengths, "c", SWAP)])
    seg, pos = clip_info(lengths, jnp.arange(512, dtype=jnp.int32))
    inverse = jnp.exp(
        jnp.asarray(np.arange(128) % 32, jnp.float32) * (-2.0 * math.log(rope_base) / HEAD_DIM)
    )
    angle = pos[:, :, None] * inverse
    cosine = jnp.cos(angle)
    sine = jnp.sin(angle) * jnp.asarray(np.where(np.arange(128) % 64 < 32, -1.0, 1.0), jnp.float32)

    x_all = frames_all.reshape(1024, D).astype(jnp.float32)
    normed_one, scale_one = normed_of(x_all)
    a_low = (normed_one * vectors[0] + vectors[1]).astype(jnp.bfloat16)
    qkv = nn(a_low, w_qkv).reshape(2, 512, 3 * OWN)
    low, attn_own, lse = attend_rows(qkv, cosine, sine, seg)
    attn_pair = jnp.stack([attn_own, lax.ppermute(attn_own, "y", SWAP)])
    attn_far = lax.ppermute(attn_pair, "c", SWAP)
    attn_far = jnp.concatenate([attn_far[:, 1:], attn_far[:, :1]], axis=1)
    attn_all = jnp.concatenate([attn_pair, attn_far]).transpose(1, 2, 0, 3).reshape(1024, D)
    branch_attn = nn(attn_all, w_out)
    mid = x_all + vectors[4] * branch_attn
    normed_two, scale_two = normed_of(mid)
    c_low = (normed_two * vectors[2] + vectors[3]).astype(jnp.bfloat16)
    gate_up = nn(c_low, w_gate_up)
    gate, up = gate_up[:, :1024], gate_up[:, 1024:]
    gate_sig = jax.nn.sigmoid(gate)
    hidden = (gate * gate_sig * up).astype(jnp.bfloat16)
    branch_mlp = nn(hidden, w_down)
    cot_rows = cot_all.reshape(1024, D).astype(jnp.float32)
    g_scale_mlp = jnp.sum(cot_rows * branch_mlp, axis=0)
    mid_own = own_rows(mid.reshape(2, 512, D))
    branch_own = sum_rows(branch_mlp.reshape(2, 512, D), on_first)
    output = (mid_own + vectors[5] * branch_own).astype(jnp.bfloat16)

    d_mlp = (cot_rows * vectors[5]).astype(jnp.bfloat16)
    g_down = tn(hidden, d_mlp).astype(jnp.bfloat16)
    g_down = ring_scatter(g_down.reshape(1024, 8, 128).transpose(1, 0, 2), ids)
    d_hidden = nt(d_mlp, w_down)
    d_gate = d_hidden * up * gate_sig * (1.0 + gate * (1.0 - gate_sig))
    d_up = d_hidden * gate * gate_sig
    d_gate_up = jnp.concatenate([d_gate, d_up], axis=1).astype(jnp.bfloat16)
    g_gate_up = tn(c_low, d_gate_up).astype(jnp.bfloat16)
    g_gate_up = g_gate_up.reshape(16, 64, 2, 8, 128).transpose(3, 0, 2, 1, 4).reshape(8, 2048, 128)
    g_gate_up = ring_scatter(g_gate_up, ids)
    d_c = nt(d_gate_up, w_gate_up)
    g_gain_two = jnp.sum(d_c * normed_two, axis=0)
    g_bias_two = jnp.sum(d_c, axis=0)
    d_c_own = sum_rows(d_c.reshape(2, 512, D), on_first)
    normed_own = own_rows(normed_two.reshape(2, 512, D))
    scale_own = own_rows(scale_two.reshape(2, 512, 1))
    cot_own = cotangent[0].astype(jnp.float32)
    d_mid = cot_own + norm_rows_back(d_c_own, normed_own, scale_own, vectors[2])
    g_scale_attn = jnp.sum(d_mid * own_rows(branch_attn.reshape(2, 512, D)), axis=0)
    d_branch = group_rows((d_mid * vectors[4]).astype(jnp.bfloat16), on_first).reshape(1024, D)
    g_out = tn(attn_own.reshape(1024, OWN), d_branch).astype(jnp.bfloat16)
    d_attn = nt(d_branch, w_out_own).astype(jnp.bfloat16).reshape(2, 512, OWN)
    d_qkv = attend_rows_back(low, lse, d_attn, cosine, sine, seg).reshape(1024, 3 * OWN)
    g_qkv = tn(a_low, d_qkv).astype(jnp.bfloat16)
    d_a = nt(d_qkv, w_qkv)
    g_gain_one = jnp.sum(d_a * normed_one, axis=0)
    g_bias_one = jnp.sum(d_a, axis=0)
    small = jnp.stack([g_gain_one, g_bias_one, g_gain_two, g_bias_two, g_scale_attn, g_scale_mlp])
    small = jnp.pad(small.astype(jnp.bfloat16).reshape(8, 6, 128), ((0, 0), (0, SLAB - 6), (0, 0)))
    g_qkv = g_qkv.reshape(8, 128, 3, OWN).transpose(0, 2, 1, 3).reshape(8, 384, OWN)
    g_qkv = jnp.einsum("pv,gpn->gvn", order, g_qkv, preferred_element_type=jnp.float32).astype(jnp.bfloat16)
    g_qkv = g_qkv.reshape(6, 8, 64, 2, 128).transpose(1, 0, 3, 2, 4).reshape(8, 768, 128)
    g_out = g_out.reshape(OWN, 8, 128).transpose(1, 0, 2)
    g_first = ring_scatter(jnp.concatenate([g_qkv, g_out, small], axis=1), ids)
    d_a_own = sum_rows(d_a.reshape(2, 512, D), on_first)
    d_one = norm_rows_back(
        d_a_own, own_rows(normed_one.reshape(2, 512, D)), own_rows(scale_one.reshape(2, 512, 1)), vectors[0]
    )
    frames_grad = (d_mid + d_one).astype(jnp.bfloat16)

    main = jnp.concatenate([g_first[:1024], g_gate_up, g_down]).reshape(32, 128, 128)
    slab = jnp.concatenate([main[1:, :8], main[1:, 64:72]], axis=1)
    slab = jnp.concatenate([slab, g_first[None, 1024:]])
    pieces = jnp.concatenate([main, slab], axis=1)
    pieces = lax.all_to_all(pieces, EVERY, split_axis=0, concat_axis=0, tiled=True)
    params_grad = collect(pieces, me[None], params.shape[0])
    new_params, new_first, new_second = adam_update(params, params_grad, first_moment, second_moment)
    return (output[None], frames_grad[None], params_grad, new_params, new_first, new_second)


def solution(mesh):
    def run(frames, cotangent, clip_lengths, params, first_moment, second_moment):
        fits = (
            mesh.shape["dp"] == 16
            and mesh.shape["seq"] == 2
            and frames.shape == (16, 512, D)
            and clip_lengths.shape == (16, 2)
        )
        if fits:
            over = Mesh(mesh.devices.reshape(4, 2, 2, 2), EVERY)
            rows, clips, flat = P(("z", "x", "c"), "y", None), P(("z", "x", "c"), None), P(EVERY)
        else:
            over = mesh
            rows, clips, flat = P("dp", "seq", None), P("dp", None), P(("dp", "seq"))
        step = jax.shard_map(
            fast_body if fits else body,
            mesh=over,
            in_specs=(rows, rows, clips, flat, flat, flat),
            out_specs=(rows, rows, flat, flat, flat, flat),
            check_vma=False,
        )
        return step(frames, cotangent, clip_lengths, params, first_moment, second_moment)

    return run
```

```python
import math

import jax
import jax.numpy as jnp
import numpy as np
from jax import lax
from jax.experimental import pallas as pl
from jax.experimental.pallas import tpu as pltpu
from jax.sharding import Mesh
from jax.sharding import PartitionSpec as P

D = 1024
HEADS = 16
HEAD_DIM = 64
FF = 4096
WINDOW = 128


eps_norm = 1e-05
beta_one = 0.9
beta_two = 0.99
learn_rate = 0.01
decay_rate = 0.1
eps_adam = 1e-08
adam_step = 100.0
neg_large = -1e30
rope_base = 10000.0


def padded(shard, sides, width):
    for axis, dim in sides:
        size, length = (lax.axis_size(axis), shard.shape[dim])
        up = [(i, (i + 1) % size) for i in range(size - 1)]
        down = [(j, i) for i, j in up]
        last = lax.slice_in_dim(shard, length - width, length, axis=dim)
        first = lax.slice_in_dim(shard, 0, width, axis=dim)
        before = lax.ppermute(last, axis, up)
        after = lax.ppermute(first, axis, down)
        shard = jnp.concatenate([before, shard, after], axis=dim)
    return shard


def unpack(flat_params):
    end_qkv = D * 3 * D
    end_out = end_qkv + D * D
    end_mlp = end_out + D * 2 * FF
    end_down = end_mlp + FF * D
    w_qkv = flat_params[:end_qkv].reshape(D, 3 * D)
    w_out = flat_params[end_qkv:end_out].reshape(D, D)
    w_gate_up = flat_params[end_out:end_mlp].reshape(D, 2 * FF)
    w_down = flat_params[end_mlp:end_down].reshape(FF, D)
    vectors = flat_params[end_down:].reshape(6, D).astype(jnp.float32)
    return (w_qkv, w_out, w_gate_up, w_down, vectors)


def clip_info(lengths, glob):
    clip_ends = jnp.cumsum(lengths, axis=1, dtype=jnp.int32)
    clip_starts = clip_ends - lengths
    after_end = (glob[None, :, None] >= clip_ends[:, None, :]).astype(jnp.int32)
    segment = jnp.sum(after_end, axis=2, dtype=jnp.int32)
    onehot = segment[:, :, None] == jnp.arange(lengths.shape[1], dtype=jnp.int32)[None, None, :]
    clip_begin = jnp.sum(jnp.where(onehot, clip_starts[:, None, :], 0), axis=2, dtype=jnp.int32)
    return (segment, (glob[None, :] - clip_begin).astype(jnp.float32))


def rotate(values, position, sign):
    half_dim = values.shape[-1] // 2
    inverse = jnp.exp(
        jnp.arange(half_dim, dtype=jnp.float32) * (-2.0 * math.log(rope_base) / HEAD_DIM)
    )
    rot_angle = position[:, :, None, None] * inverse
    cosine = jnp.cos(rot_angle)
    rot_sine = sign * jnp.sin(rot_angle)
    low_half = values[..., :half_dim]
    high_half = values[..., half_dim:]
    return jnp.concatenate(
        [low_half * cosine - high_half * rot_sine, high_half * cosine + low_half * rot_sine],
        axis=-1,
    )


def norm_forward(row_vals, norm_gain, norm_bias):
    centered = row_vals - jnp.mean(row_vals, axis=-1, keepdims=True)
    inv_scale = lax.rsqrt(jnp.mean(centered * centered, axis=-1, keepdims=True) + eps_norm)
    normed = centered * inv_scale
    return (normed * norm_gain + norm_bias, normed, inv_scale)


def norm_backward(out_grad, normed, inv_scale, norm_gain):
    d_gain = jnp.sum(out_grad * normed, axis=0)
    d_bias = jnp.sum(out_grad, axis=0)
    inner_grad = out_grad * norm_gain
    d_rows = inv_scale * (
        inner_grad
        - jnp.mean(inner_grad, axis=-1, keepdims=True)
        - normed * jnp.mean(inner_grad * normed, axis=-1, keepdims=True)
    )
    return (d_rows, d_gain, d_bias)


def scores_of(query_rows, key_rows, window_mask):
    raw_scores = jnp.einsum(
        "qhd,khd->hqk", query_rows, key_rows, preferred_element_type=jnp.float32
    ) * HEAD_DIM ** (-0.5)
    return jnp.where(window_mask[None], raw_scores, neg_large)


def attend(query_rows, key_rows, value_rows, window_mask):
    masked = scores_of(query_rows, key_rows, window_mask)
    row_max = jnp.max(masked, axis=-1, keepdims=True)
    row_total = jnp.log(jnp.sum(jnp.exp(masked - row_max), axis=-1, keepdims=True)) + row_max
    prob_low = jnp.exp(masked - row_total).astype(jnp.bfloat16)
    attn_rows = jnp.einsum("hqk,khd->qhd", prob_low, value_rows, preferred_element_type=jnp.float32)
    return (attn_rows, row_total[..., 0])


def attend_back(query_rows, key_rows, value_rows, window_mask, row_total, d_attn):
    masked = scores_of(query_rows, key_rows, window_mask)
    prob_rows = jnp.exp(masked - row_total[..., None])
    prob_low = prob_rows.astype(jnp.bfloat16)
    d_values = jnp.einsum("hqk,qhd->khd", prob_low, d_attn, preferred_element_type=jnp.float32)
    d_probs = jnp.einsum("qhd,khd->hqk", d_attn, value_rows, preferred_element_type=jnp.float32)
    inner_sum = jnp.sum(prob_rows * d_probs, axis=-1, keepdims=True)
    d_scores = (prob_rows * (d_probs - inner_sum)).astype(jnp.bfloat16)
    d_query = jnp.einsum(
        "hqk,khd->qhd", d_scores, key_rows, preferred_element_type=jnp.float32
    ) * HEAD_DIM ** (-0.5)
    d_keys = jnp.einsum(
        "hqk,qhd->khd", d_scores, query_rows, preferred_element_type=jnp.float32
    ) * HEAD_DIM ** (-0.5)
    return (d_query, d_keys, d_values)


def adam_update(flat_params, grads, first_moment, second_moment):
    new_first = beta_one * first_moment + (1.0 - beta_one) * grads
    new_second = beta_two * second_moment + (1.0 - beta_two) * grads * grads
    corrected_first = new_first / (1.0 - beta_one**adam_step)
    corrected_second = new_second / (1.0 - beta_two**adam_step)
    step_size = corrected_first / (jnp.sqrt(corrected_second) + eps_adam) + decay_rate * flat_params
    return (flat_params - learn_rate * step_size, new_first, new_second)


def body(frames, cotangent, clip_lengths, params, first_moment, second_moment):
    seq_count, frame_span, model_width = frames.shape
    row_count = seq_count * frame_span
    window_reach = WINDOW
    key_count = frame_span + 2 * window_reach
    head_count = HEADS
    head_size = model_width // head_count
    group_size = 4
    seq_len = lax.axis_size("seq") * frame_span
    seq_start = lax.axis_index("seq") * frame_span
    glob_rows = seq_start + jnp.arange(frame_span, dtype=jnp.int32)
    glob_keys = seq_start - window_reach + jnp.arange(key_count, dtype=jnp.int32)
    seg_rows, pos_rows = clip_info(clip_lengths, glob_rows)
    seg_keys, unused = clip_info(clip_lengths, glob_keys)
    inside = (glob_keys >= 0) & (glob_keys < seq_len)
    near_band = (
        jnp.abs(jnp.arange(frame_span)[:, None] + window_reach - jnp.arange(key_count)[None, :])
        < window_reach
    )
    window_mask = (
        (seg_rows[:, :, None] == seg_keys[:, None, :]) & inside[None, None, :] & near_band[None]
    )
    keep_rows = seg_rows != clip_lengths.shape[1] - 1
    shards = params.astype(jnp.bfloat16)
    gathered = lax.all_gather(shards, ("dp", "seq"), axis=0, tiled=True)
    w_qkv, w_out, w_gate_up, w_down, vectors = unpack(gathered)
    x_rows = frames.reshape(row_count, model_width).astype(jnp.float32)
    norm_one, normed_one, scale_one = norm_forward(x_rows, vectors[0], vectors[1])
    a_low = norm_one.astype(jnp.bfloat16)
    qkv = jnp.dot(a_low, w_qkv, preferred_element_type=jnp.float32).reshape(
        seq_count, frame_span, 3, head_count, head_size
    )
    query_low = rotate(qkv[:, :, 0], pos_rows, 1.0).astype(jnp.bfloat16)
    key_low = rotate(qkv[:, :, 1], pos_rows, 1.0).astype(jnp.bfloat16)
    value_low = qkv[:, :, 2].astype(jnp.bfloat16)
    key_value = jnp.concatenate([key_low, value_low], axis=2).reshape(
        seq_count, frame_span, 2 * model_width
    )
    wide_rows = padded(key_value, (("seq", 1),), window_reach)
    wide_rows = wide_rows.reshape(seq_count, key_count, 2, head_count, head_size)
    key_wide = wide_rows[:, :, 0]
    value_wide = wide_rows[:, :, 1]
    seq_index = 0
    out_parts = []
    total_parts = []
    for head_start in range(0, head_count, group_size):
        head_end = head_start + group_size
        attn_rows, row_total = attend(
            query_low[seq_index, :, head_start:head_end],
            key_wide[seq_index, :, head_start:head_end],
            value_wide[seq_index, :, head_start:head_end],
            window_mask[seq_index],
        )
        out_parts.append(attn_rows)
        total_parts.append(row_total)
    attn_list = [jnp.concatenate(out_parts, axis=1)]
    total_list = [total_parts]
    attn_all = jnp.where(keep_rows[:, :, None, None], jnp.stack(attn_list), 0.0)
    attn_low = attn_all.reshape(row_count, model_width).astype(jnp.bfloat16)
    branch_attn = jnp.dot(attn_low, w_out, preferred_element_type=jnp.float32)
    mid_rows = x_rows + vectors[4] * branch_attn
    norm_two, normed_two, scale_two = norm_forward(mid_rows, vectors[2], vectors[3])
    c_low = norm_two.astype(jnp.bfloat16)
    gate_up = jnp.dot(c_low, w_gate_up, preferred_element_type=jnp.float32)
    gate = gate_up[:, :FF]
    up_rows = gate_up[:, FF:]
    gate_sig = jax.nn.sigmoid(gate)
    hidden = (gate * gate_sig * up_rows).astype(jnp.bfloat16)
    branch_mlp = jnp.dot(hidden, w_down, preferred_element_type=jnp.float32)
    output = (
        (mid_rows + vectors[5] * branch_mlp)
        .astype(jnp.bfloat16)
        .reshape(seq_count, frame_span, model_width)
    )
    gathered = lax.all_gather(shards, ("dp", "seq"), axis=0, tiled=True)
    w_qkv, w_out, w_gate_up, w_down, vectors = unpack(gathered)
    d_rows = cotangent.reshape(row_count, model_width).astype(jnp.float32)
    g_scale_mlp = jnp.sum(d_rows * branch_mlp, axis=0)
    d_mlp = (d_rows * vectors[5]).astype(jnp.bfloat16)
    g_down = jnp.dot(hidden.T, d_mlp, preferred_element_type=jnp.float32)
    d_hidden = jnp.dot(d_mlp, w_down.T, preferred_element_type=jnp.float32)
    d_gate = d_hidden * up_rows * gate_sig * (1.0 + gate * (1.0 - gate_sig))
    d_up = d_hidden * gate * gate_sig
    d_gate_up = jnp.concatenate([d_gate, d_up], axis=1).astype(jnp.bfloat16)
    g_gate_up = jnp.dot(c_low.T, d_gate_up, preferred_element_type=jnp.float32)
    d_two = jnp.dot(d_gate_up, w_gate_up.T, preferred_element_type=jnp.float32)
    d_norm_two, g_gain_two, g_bias_two = norm_backward(d_two, normed_two, scale_two, vectors[2])
    d_mid = d_rows + d_norm_two
    g_scale_attn = jnp.sum(d_mid * branch_attn, axis=0)
    d_branch = (d_mid * vectors[4]).astype(jnp.bfloat16)
    g_out = jnp.dot(attn_low.T, d_branch, preferred_element_type=jnp.float32)
    d_attn_low = jnp.dot(d_branch, w_out.T, preferred_element_type=jnp.float32).astype(jnp.bfloat16)
    d_attn = jnp.where(
        keep_rows[:, :, None, None],
        d_attn_low.reshape(seq_count, frame_span, head_count, head_size),
        jnp.zeros((), jnp.bfloat16),
    )
    seq_index = 0
    query_parts = []
    key_parts = []
    value_parts = []
    for number, head_start in enumerate(range(0, head_count, group_size)):
        head_end = head_start + group_size
        d_query, d_keys, d_values = attend_back(
            query_low[seq_index, :, head_start:head_end],
            key_wide[seq_index, :, head_start:head_end],
            value_wide[seq_index, :, head_start:head_end],
            window_mask[seq_index],
            total_list[seq_index][number],
            d_attn[seq_index, :, head_start:head_end],
        )
        query_parts.append(d_query)
        key_parts.append(d_keys)
        value_parts.append(d_values)
    query_grads = [jnp.concatenate(query_parts, axis=1)]
    key_grads = [jnp.concatenate(key_parts, axis=1)]
    value_grads = [jnp.concatenate(value_parts, axis=1)]
    d_query_all = jnp.stack(query_grads)
    d_pair = jnp.concatenate([jnp.stack(key_grads), jnp.stack(value_grads)], axis=2).reshape(
        seq_count, key_count, 2 * model_width
    )
    rim_rows = jnp.concatenate(
        [d_pair[:, :window_reach], d_pair[:, window_reach + frame_span :]], axis=1
    )
    taken_rows = padded(rim_rows.astype(jnp.bfloat16), (("seq", 1),), window_reach).astype(
        rim_rows.dtype
    )
    own_rows = d_pair[:, window_reach : window_reach + frame_span]
    own_rows = own_rows + jnp.pad(
        taken_rows[:, :window_reach], ((0, 0), (0, frame_span - window_reach), (0, 0))
    )
    own_rows = own_rows + jnp.pad(
        taken_rows[:, 3 * window_reach :], ((0, 0), (frame_span - window_reach, 0), (0, 0))
    )
    own_rows = own_rows.reshape(seq_count, frame_span, 2, head_count, head_size)
    d_qkv = jnp.stack(
        [
            rotate(d_query_all, pos_rows, -1.0),
            rotate(own_rows[:, :, 0], pos_rows, -1.0),
            own_rows[:, :, 1],
        ],
        axis=2,
    )
    d_qkv = d_qkv.reshape(row_count, 3 * model_width).astype(jnp.bfloat16)
    g_qkv = jnp.dot(a_low.T, d_qkv, preferred_element_type=jnp.float32)
    d_one = jnp.dot(d_qkv, w_qkv.T, preferred_element_type=jnp.float32)
    d_norm_one, g_gain_one, g_bias_one = norm_backward(d_one, normed_one, scale_one, vectors[0])
    frames_grad = (
        (d_mid + d_norm_one).astype(jnp.bfloat16).reshape(seq_count, frame_span, model_width)
    )
    small_grads = jnp.stack(
        [g_gain_one, g_bias_one, g_gain_two, g_bias_two, g_scale_attn, g_scale_mlp]
    )
    whole_grad = jnp.concatenate(
        [
            g_qkv.reshape(-1),
            g_out.reshape(-1),
            g_gate_up.reshape(-1),
            g_down.reshape(-1),
            small_grads.reshape(-1),
        ]
    )
    params_grad = lax.psum_scatter(whole_grad, ("dp", "seq"), scatter_dimension=0, tiled=True)
    new_params, new_first, new_second = adam_update(
        params, params_grad, first_moment, second_moment
    )
    return (output, frames_grad, params_grad, new_params, new_first, new_second)


EVERY = ("z", "x", "c", "y")
GROUP = ("z", "x")
RING = ((0, 0), (1, 0), (2, 0), (3, 0), (3, 1), (2, 1), (1, 1), (0, 1))
PLACES = tuple(2 * z + x for z, x in RING)
AHEAD = tuple((PLACES[i], PLACES[(i + 1) % 8]) for i in range(8))
BACK = tuple((b, a) for a, b in AHEAD)
SWAP = ((0, 1), (1, 0))
LINES = 4096
TAIL = 64
SLAB = 16
ROWS = 128 + SLAB
OWN = 256
SCALE = HEAD_DIM ** (-0.5)
VMEM = pltpu.CompilerParams(vmem_limit_bytes=48 * 1024 * 1024)


def ring_place(me, step):
    z, x = lax.div(me, 8), lax.rem(lax.div(me, 4), 2)
    at = lax.rem(jnp.where(x == 0, z, 7 - z) + step, 8)
    return jnp.where(at < 4, 2 * at, 15 - 2 * at)


def kind_of(shard):
    if shard < 6:
        return 0
    return 2 if 8 <= shard < 24 else 1


def piece_lines(kind, dest):
    place, member = divmod(dest, 4)
    if kind == 0:
        return [(512 * place + member, 8), (512 * place + 4 + member, 8)]
    if kind == 1:
        return [(1024 * member + place, 8), (1024 * member + 512 + place, 8)]
    return [(dest, 64), (32 + dest, 64)]


def tail_lines(kind, dest):
    place, member = divmod(dest, 4)
    if kind == 0:
        return [(0, 6, member, 8), (8, 6, 4 + member, 8)] if place == 0 else []
    if kind == 1:
        return [(0, 6, place, 8)] if member == 0 else []
    return [(0, 1, dest, 1)] + ([(8, 1, 32 + dest, 1)] if dest < 16 else [])


def is_kind(shard, kind):
    if kind == 0:
        return shard < 6
    gate_up = (shard >= 8) & (shard < 24)
    if kind == 2:
        return gate_up
    return (shard >= 6) & jnp.logical_not(gate_up) & (shard < 32)


def spread_kernel(me_ref, flat_ref, out_ref, lines_ref):
    me = me_ref[0]
    odd = lax.rem(me, 2) == 1
    start = 48 - (3 * me + 1) // 2
    lane = lax.broadcasted_iota(jnp.int32, (64, 128), 1)

    def shift(step, carry):
        here = flat_ref[pl.ds(start + step * 64, 64), :]
        after = flat_ref[pl.ds(start + step * 64 + 1, 64), :]
        mixed = jnp.where(lane < 64, pltpu.roll(here, 64, 1), pltpu.roll(after, 64, 1))
        lines_ref[pl.ds(pl.multiple_of(step * 64, 64), 64), :] = jnp.where(odd, mixed, here)
        return carry

    lax.fori_loop(0, (LINES + TAIL) // 64, shift, 0, unroll=5)
    for kind in range(3):

        @pl.when(is_kind(me, kind))
        def _(kind=kind):
            for dest in range(32):
                for half, (first, stride) in enumerate(piece_lines(kind, dest)):
                    rows = lines_ref[pl.ds(first, 64, stride), :]
                    out_ref[dest, 64 * half : 64 * half + 64, :] = rows.astype(jnp.bfloat16)

    def slab_of(parts):
        slab = [jnp.zeros((8, 128), jnp.float32)] * 2
        row = lax.broadcasted_iota(jnp.int32, (8, 128), 0)
        for at, count, first, stride in parts:
            if count == 1:
                value = jnp.broadcast_to(lines_ref[LINES + first : LINES + first + 1, :], (8, 128))
            else:
                value = lines_ref[pl.ds(LINES + first, 8, stride), :]
            slab[at // 8] = jnp.where(row < count, value, 0.0)
        return jnp.concatenate(slab, axis=0).astype(jnp.bfloat16)

    for kind in range(3):

        @pl.when(is_kind(me + 1, kind))
        def _(kind=kind):
            for dest in range(32):
                out_ref[dest, 128:ROWS, :] = slab_of(tail_lines(kind, dest))

    @pl.when(me == 31)
    def _():
        for dest in range(32):
            out_ref[dest, 128:ROWS, :] = slab_of([(0, 6, 6 * (dest // 4), 1)])


def spread(params, me):
    flat = jnp.pad(params, (48 * 128, 4224 * 128 - 48 * 128 - params.shape[0])).reshape(4224, 128)
    return pl.pallas_call(
        spread_kernel,
        out_shape=jax.ShapeDtypeStruct((32, ROWS, 128), jnp.bfloat16),
        in_specs=[
            pl.BlockSpec(memory_space=pltpu.SMEM),
            pl.BlockSpec(memory_space=pltpu.VMEM),
        ],
        out_specs=pl.BlockSpec(memory_space=pltpu.VMEM),
        scratch_shapes=[pltpu.VMEM((LINES + TAIL, 128), jnp.float32)],
        compiler_params=VMEM,
        name="spread",
    )(me, flat)


def collect_kernel(me_ref, piece_ref, out_ref, lines_ref):
    me = me_ref[0]
    odd = lax.rem(me, 2) == 1
    lines_ref[LINES:, :] = jnp.zeros((TAIL, 128), jnp.float32)
    for kind in range(3):

        @pl.when(is_kind(me, kind))
        def _(kind=kind):
            for dest in range(32):
                for half, (first, stride) in enumerate(piece_lines(kind, dest)):
                    rows = piece_ref[dest, 64 * half : 64 * half + 64, :].astype(jnp.float32)
                    lines_ref[pl.ds(first, 64, stride), :] = rows

    for kind in range(3):

        @pl.when(is_kind(me + 1, kind))
        def _(kind=kind):
            for dest in range(32):
                slab = piece_ref[dest, 128:ROWS, :].astype(jnp.float32)
                for at, count, first, stride in tail_lines(kind, dest):
                    for k in range(count):
                        line = LINES + first + k * stride
                        lines_ref[line : line + 1, :] = slab[at + k : at + k + 1, :]

    @pl.when(me == 31)
    def _():
        for place in range(8):
            total = piece_ref[4 * place, 128:ROWS, :].astype(jnp.float32)
            for member in range(1, 4):
                total = total + piece_ref[4 * place + member, 128:ROWS, :].astype(jnp.float32)
            for k in range(6):
                line = LINES + 6 * place + k
                lines_ref[line : line + 1, :] = total[k : k + 1, :]

    start = (3 * me) // 2
    lane = lax.broadcasted_iota(jnp.int32, (24, 128), 1)

    def shift(step, carry):
        here = lines_ref[pl.ds(start + step * 24, 24), :]
        after = lines_ref[pl.ds(start + step * 24 + 1, 24), :]
        mixed = jnp.where(lane < 64, pltpu.roll(here, 64, 1), pltpu.roll(after, 64, 1))
        out_ref[pl.ds(pl.multiple_of(step * 24, 8), 24), :] = jnp.where(odd, mixed, here)
        return carry

    lax.fori_loop(0, 4104 // 24, shift, 0, unroll=9)


def collect(pieces, me, count):
    lines = pl.pallas_call(
        collect_kernel,
        out_shape=jax.ShapeDtypeStruct((4104, 128), jnp.float32),
        in_specs=[
            pl.BlockSpec(memory_space=pltpu.SMEM),
            pl.BlockSpec(memory_space=pltpu.VMEM),
        ],
        out_specs=pl.BlockSpec(memory_space=pltpu.VMEM),
        scratch_shapes=[pltpu.VMEM((LINES + TAIL, 128), jnp.float32)],
        compiler_params=VMEM,
        name="collect",
    )(me, pieces)
    return lines.reshape(-1)[:count]


def swap_halves(rows):
    lane = lax.broadcasted_iota(jnp.int32, rows.shape, 1)
    return jnp.where(
        lax.rem(lane, 64) < 32, pltpu.roll(rows, 96, 1), pltpu.roll(rows, 32, 1)
    )


def turn(rows, cosine, signed_sine):
    parts = []
    for at in range(0, rows.shape[1], 128):
        part = rows[:, at : at + 128]
        parts.append(part * cosine + swap_halves(part) * signed_sine)
    return jnp.concatenate(parts, axis=1)


def clip_of(length_ref, frame):
    first = length_ref[0, 0]
    return (frame >= first).astype(jnp.int32) + (frame >= first + length_ref[0, 1]).astype(jnp.int32)


def mask_of(length_ref, block):
    row = lax.broadcasted_iota(jnp.int32, (256, 384), 0) + 256 * block
    key = lax.broadcasted_iota(jnp.int32, (256, 384), 1) + 128 * block
    own = clip_of(length_ref, lax.broadcasted_iota(jnp.int32, (256, 1), 0) + 256 * block)
    others = clip_of(length_ref, lax.broadcasted_iota(jnp.int32, (1, 384), 1) + 128 * block)
    return (jnp.abs(row - key) < WINDOW) & (own == others), own != 1


def nt(left, right):
    return lax.dot_general(left, right, (((1,), (1,)), ((), ())), preferred_element_type=jnp.float32)


def tn(left, right):
    return lax.dot_general(left, right, (((0,), (0,)), ((), ())), preferred_element_type=jnp.float32)


def nn(left, right):
    return jnp.dot(left, right, preferred_element_type=jnp.float32)


def cost(flops, moved):
    return pl.CostEstimate(flops=flops, bytes_accessed=moved, transcendentals=0)


def fix_kernel(piece_ref, first_ref, second_ref, third_ref):
    for source in range(32):
        out, at = (first_ref, source) if source < 8 else (second_ref, source - 8) if source < 24 else (third_ref, source - 24)
        out[128 * at : 128 * at + 128, :] = piece_ref[source, :128, :]
        if source:
            slab = piece_ref[source - 1, 128:ROWS, :].astype(jnp.float32)
            for half in range(2):
                rows = piece_ref[source, 64 * half : 64 * half + 16, :].astype(jnp.float32)
                extra = jnp.concatenate([slab[8 * half : 8 * half + 8], jnp.zeros((8, 128), jnp.float32)])
                out[128 * at + 64 * half : 128 * at + 64 * half + 16, :] = (rows + extra).astype(jnp.bfloat16)
    first_ref[1024:, :] = piece_ref[31, 128:ROWS, :]


def fix(pieces):
    return pl.pallas_call(
        fix_kernel,
        out_shape=tuple(jax.ShapeDtypeStruct((n, 128), jnp.bfloat16) for n in (1024 + SLAB, 2048, 1024)),
        compiler_params=VMEM,
        cost_estimate=cost(0, 1 << 22),
        name="fix",
    )(pieces)


def in_order(refs, seq, half, second):
    mine, other = refs[2 * seq], refs[2 * seq + 1]
    return jnp.where(lax.rem(second, 2) == half, mine[...], other[...])


def ring_parts(me_ref, refs):
    me = me_ref[0]
    parts = [(ring_place(me, 0), refs[0], None)]
    for step in range(1, 4):
        parts += [(ring_place(me, 8 - step), refs[2 * step - 1], None), (ring_place(me, step), refs[2 * step], None)]
    half = refs[7].shape[0]
    last = ring_place(me, 4)
    return parts + [(last, refs[7], (0, half)), (last, refs[8], (half, refs[0].shape[0]))]


def join_first_kernel(me_ref, *refs):
    blocks, (qkv_ref, out_ref, vec_ref, lines_ref) = refs[:9], refs[9:]
    for place, block, rows in ring_parts(me_ref, blocks):
        lo, hi = rows or (0, 1024 + SLAB)
        for at, end, ref in ((0, 768, qkv_ref), (768, 1024, out_ref), (1024, 1024 + SLAB, lines_ref)):
            first, last = max(at, lo), min(end, hi)
            if first < last:
                ref[place, first - at : last - at, :] = block[first - lo : last - lo, :]
    slabs = [lines_ref[place].astype(jnp.float32) for place in range(8)]
    for v in range(6):
        for k in range(8):
            line = 8 * v + k
            vec_ref[v : v + 1, 128 * k : 128 * k + 128] = slabs[line // 6][line % 6 : line % 6 + 1]


def join_gate_up_kernel(me_ref, *refs):
    blocks, out_ref = refs[:9], refs[9]
    for place, block, rows in ring_parts(me_ref, blocks):
        lo, hi = rows or (0, 2048)
        for half in range(2):
            at = pl.multiple_of(256 * half + 128 * lax.rem(place, 2), 128)
            for source in range(lo // 128, hi // 128):
                first = 128 * source + 64 * half - lo
                out_ref[lax.div(place, 2), 64 * source : 64 * source + 64, pl.ds(at, 128)] = block[
                    first : first + 64, :
                ]


def join_down_kernel(me_ref, *refs):
    blocks, out_ref = refs[:9], refs[9]
    for place, block, rows in ring_parts(me_ref, blocks):
        lo, hi = rows or (0, 1024)
        out_ref[lo:hi, pl.ds(pl.multiple_of(128 * place, 128), 128)] = block[...]


def join(kernel, me, blocks, out_shape, name, scratch=()):
    return pl.pallas_call(
        kernel,
        out_shape=out_shape,
        in_specs=[SCALAR] + [WHOLE] * 9,
        scratch_shapes=scratch,
        compiler_params=VMEM,
        cost_estimate=cost(0, 4 << 20),
        name=name,
    )(me, *blocks)


def prep_kernel(y_ref, own_ref, pair_ref, far_ref, last_ref, x_ref, mean_ref, inv_ref):
    for block in range(4):
        rows = slice(256 * block, 256 * block + 256)
        x_low = in_order((own_ref, pair_ref, far_ref, last_ref), block // 2, block % 2, y_ref[0])
        x_ref[rows, :] = x_low
        x_rows = x_low.astype(jnp.float32)
        mean = jnp.mean(x_rows, axis=1, keepdims=True)
        centered = x_rows - mean
        mean_ref[rows, :] = mean
        inv_ref[rows, :] = lax.rsqrt(jnp.mean(centered * centered, axis=1, keepdims=True) + eps_norm)


SCALAR = pl.BlockSpec(memory_space=pltpu.SMEM)
WHOLE = pl.BlockSpec(memory_space=pltpu.VMEM)


def prep(second, rows):
    return pl.pallas_call(
        prep_kernel,
        out_shape=(
            jax.ShapeDtypeStruct((1024, D), jnp.bfloat16),
            jax.ShapeDtypeStruct((1024, 1), jnp.float32),
            jax.ShapeDtypeStruct((1024, 1), jnp.float32),
        ),
        in_specs=[SCALAR] + [WHOLE] * 4,
        compiler_params=VMEM,
        cost_estimate=cost(1 << 24, 5 << 20),
        name="prep",
    )(second, *rows)


def front_kernel(
    x_ref, mean_ref, inv_ref, ring_ref, vec_ref, order_ref, cos_ref, sin_ref, length_ref, far_length_ref,
    a_ref, w_ref, low_ref, attn_ref, lse_ref,
):
    gain, bias = vec_ref[0:1, :], vec_ref[1:2, :]
    for block in range(8):
        parts = []
        for chunk in range(6 * block, 6 * block + 6):
            at = 128 * (chunk // 8)
            parts.append(
                jnp.concatenate(
                    [ring_ref[chunk % 8, at : at + 64, :], ring_ref[chunk % 8, at + 64 : at + 128, :]], axis=1
                )
            )
        rows = nn(order_ref[...], jnp.concatenate(parts, axis=0)).astype(jnp.bfloat16)
        for third in range(3):
            w_ref[128 * block : 128 * block + 128, OWN * third : OWN * third + OWN] = rows[
                128 * third : 128 * third + 128
            ]
    for block in range(4):
        rows = slice(256 * block, 256 * block + 256)
        seq, at = block // 2, 256 * (block % 2)
        normed = (x_ref[rows, :].astype(jnp.float32) - mean_ref[rows, :]) * inv_ref[rows, :]
        a_low = (normed * gain + bias).astype(jnp.bfloat16)
        a_ref[rows, :] = a_low
        qkv = nn(a_low, w_ref[...])
        cosine, sine = cos_ref[seq, at : at + 256, :], sin_ref[seq, at : at + 256, :]
        low_ref[rows, : 2 * OWN] = turn(qkv[:, : 2 * OWN], cosine, sine).astype(jnp.bfloat16)
        low_ref[rows, 2 * OWN :] = qkv[:, 2 * OWN :].astype(jnp.bfloat16)
    for seq in range(2):
        for block in range(2):
            at = 512 * seq + 256 * block
            rows = slice(at, at + 256)
            keys = slice(512 * seq + 128 * block, 512 * seq + 128 * block + 384)
            mask, keep = mask_of((length_ref, far_length_ref)[seq], block)
            heads, sums = [], []
            for head in range(4):
                lane = 64 * head
                query = low_ref[rows, lane : lane + 64]
                key = low_ref[keys, OWN + lane : OWN + lane + 64]
                value = low_ref[keys, 2 * OWN + lane : 2 * OWN + lane + 64]
                masked = jnp.where(mask, nt(query, key) * SCALE, neg_large)
                top = jnp.max(masked, axis=1, keepdims=True)
                weight = jnp.exp(masked - top)
                total = jnp.sum(weight, axis=1, keepdims=True)
                probs = (weight * (1.0 / total)).astype(jnp.bfloat16)
                heads.append(jnp.where(keep, nn(probs, value), 0.0))
                sums.append(top + jnp.log(total))
            attn_ref[rows, :] = jnp.concatenate(heads, axis=1).astype(jnp.bfloat16)
            lse_ref[rows, :] = jnp.concatenate(sums, axis=1)


def front(x_all, mean, inv, ring, vectors, order, cosine, sine, lengths):
    return pl.pallas_call(
        front_kernel,
        out_shape=(
            jax.ShapeDtypeStruct((1024, D), jnp.bfloat16),
            jax.ShapeDtypeStruct((D, 3 * OWN), jnp.bfloat16),
            jax.ShapeDtypeStruct((1024, 3 * OWN), jnp.bfloat16),
            jax.ShapeDtypeStruct((1024, OWN), jnp.bfloat16),
            jax.ShapeDtypeStruct((1024, 4), jnp.float32),
        ),
        in_specs=[WHOLE] * 8 + [SCALAR] * 2,
        compiler_params=VMEM,
        cost_estimate=cost(12 << 30, 8 << 20),
        name="front",
    )(x_all, mean, inv, ring, vectors, order, cosine, sine, *lengths)


def mix_kernel(
    x_ref, own_ref, pair_ref, far_ref, last_ref, w_own_ref, w_pair_ref, w_far_ref, w_last_ref, vec_ref,
    c_ref, branch_ref, w_ref,
):
    step = pl.program_id(0)

    @pl.when(step == 0)
    def _():
        for place in range(8):
            lanes = slice(128 * place, 128 * place + 128)
            w_ref[:256, lanes] = w_own_ref[place]
            w_ref[256:512, lanes] = w_pair_ref[place]
            w_ref[512:768, lanes] = w_far_ref[place]
            w_ref[768:, lanes] = w_last_ref[place]

    attn = jnp.concatenate([own_ref[...], pair_ref[...], far_ref[...], last_ref[...]], axis=1)
    branch = nn(attn, w_ref[...])
    normed, _ = normed_of(x_ref[...].astype(jnp.float32) + vec_ref[4:5, :] * branch)
    c_ref[...] = (normed * vec_ref[2:3, :] + vec_ref[3:4, :]).astype(jnp.bfloat16)

    @pl.when(step < 2)
    def _():
        branch_ref[...] = branch


def mix(x_all, attn, w_out, vectors):
    far = pl.BlockSpec((256, OWN), lambda i: (lax.rem(i + 2, 4), 0))
    w_part = pl.BlockSpec((8, 256, 128), lambda i: (0, 0, 0))
    rows = lambda width: pl.BlockSpec((256, width), lambda i: (i, 0))
    return pl.pallas_call(
        mix_kernel,
        grid=(4,),
        out_shape=(
            jax.ShapeDtypeStruct((1024, D), jnp.bfloat16),
            jax.ShapeDtypeStruct((512, D), jnp.float32),
        ),
        in_specs=[
            rows(D),
            rows(OWN),
            rows(OWN),
            far,
            far,
            w_part,
            w_part,
            w_part,
            w_part,
            pl.BlockSpec((6, D), lambda i: (0, 0)),
        ],
        out_specs=(rows(D), pl.BlockSpec((256, D), lambda i: (jnp.minimum(i, 1), 0))),
        scratch_shapes=[pltpu.VMEM((D, D), jnp.bfloat16)],
        compiler_params=VMEM,
        cost_estimate=cost(3 << 30, 10 << 20),
        name="mix",
    )(x_all, *attn, *w_out, vectors)


def gate_kernel(c_ref, w_ref, gate_up_ref, hidden_ref):
    for block in range(4):
        rows = slice(256 * block, 256 * block + 256)
        both = nn(c_ref[rows, :], w_ref[0])
        gate_up_ref[0, rows, :] = both
        gate, up = both[:, :256], both[:, 256:]
        hidden_ref[rows, :] = (gate * jax.nn.sigmoid(gate) * up).astype(jnp.bfloat16)


def gate_step(c_low, w_gate_up):
    chunk = pl.BlockSpec((1, 1024, 512), lambda i: (i, 0, 0))
    return pl.pallas_call(
        gate_kernel,
        grid=(4,),
        out_shape=(
            jax.ShapeDtypeStruct((4, 1024, 512), jnp.float32),
            jax.ShapeDtypeStruct((1024, 1024), jnp.bfloat16),
        ),
        in_specs=[pl.BlockSpec((1024, D), lambda i: (0, 0)), chunk],
        out_specs=(chunk, pl.BlockSpec((1024, 256), lambda i: (0, i))),
        compiler_params=VMEM,
        cost_estimate=cost(5 << 30, 16 << 20),
        name="gate",
    )(c_low, w_gate_up)


def down_grad_kernel(y_ref, hidden_ref, own_ref, pair_ref, far_ref, last_ref, vec_ref, g_ref, d_mlp_ref):
    @pl.when(pl.program_id(0) == 0)
    def _():
        for block in range(4):
            rows = in_order((own_ref, pair_ref, far_ref, last_ref), block // 2, block % 2, y_ref[0])
            d_mlp_ref[256 * block : 256 * block + 256, :] = (rows.astype(jnp.float32) * vec_ref[5:6, :]).astype(
                jnp.bfloat16
            )

    g_down = tn(hidden_ref[...], d_mlp_ref[...]).astype(jnp.bfloat16)
    for pair in range(2):
        for place in range(8):
            g_ref[place, pair] = g_down[128 * pair : 128 * pair + 128, 128 * place : 128 * place + 128]


def down_grad(second, hidden, cot, vectors):
    part = pl.BlockSpec((256, D), lambda i: (0, 0))
    return pl.pallas_call(
        down_grad_kernel,
        grid=(4,),
        out_shape=(
            jax.ShapeDtypeStruct((8, 8, 128, 128), jnp.bfloat16),
            jax.ShapeDtypeStruct((1024, D), jnp.bfloat16),
        ),
        in_specs=[
            SCALAR,
            pl.BlockSpec((1024, 256), lambda i: (0, i)),
            part,
            part,
            part,
            part,
            pl.BlockSpec((6, D), lambda i: (0, 0)),
        ],
        out_specs=(
            pl.BlockSpec((8, 2, 128, 128), lambda i: (0, i, 0, 0)),
            pl.BlockSpec((1024, D), lambda i: (0, 0)),
        ),
        compiler_params=VMEM,
        cost_estimate=cost(3 << 30, 8 << 20),
        name="down_grad",
    )(second, hidden, *cot, vectors)


def put_rows(second, whole_ref, refs):
    for block in range(4):
        seq, half = divmod(block, 2)
        rows = whole_ref[256 * block : 256 * block + 256, :].astype(jnp.bfloat16 if seq else jnp.float32)

        @pl.when(lax.rem(second, 2) == half)
        def _(rows=rows, seq=seq):
            refs[2 * seq + 1][...] = rows

        @pl.when(lax.rem(second, 2) != half)
        def _(rows=rows, seq=seq):
            refs[2 * seq][...] = rows


PARTS = tuple(jax.ShapeDtypeStruct((256, D), t) for t in (jnp.float32, jnp.float32, jnp.bfloat16, jnp.bfloat16))


def hidden_back_kernel(gate_up_ref, d_mlp_ref, w_ref, d_both_ref):
    for block in range(4):
        rows = slice(256 * block, 256 * block + 256)
        d_hidden = nt(d_mlp_ref[rows, :], w_ref[...])
        gate, up = gate_up_ref[0, rows, :256], gate_up_ref[0, rows, 256:]
        sig = jax.nn.sigmoid(gate)
        d_both_ref[0, rows, :256] = (d_hidden * up * sig * (1.0 + gate * (1.0 - sig))).astype(jnp.bfloat16)
        d_both_ref[0, rows, 256:] = (d_hidden * gate * sig).astype(jnp.bfloat16)


def hidden_back(gate_up, d_mlp, w_down):
    chunk = pl.BlockSpec((1, 1024, 512), lambda i: (i, 0, 0))
    return pl.pallas_call(
        hidden_back_kernel,
        grid=(4,),
        out_shape=jax.ShapeDtypeStruct((4, 1024, 512), jnp.bfloat16),
        in_specs=[
            chunk,
            pl.BlockSpec((1024, D), lambda i: (0, 0)),
            pl.BlockSpec((256, D), lambda i: (i, 0)),
        ],
        out_specs=chunk,
        compiler_params=VMEM,
        cost_estimate=cost(4 << 30, 18 << 20),
        name="hidden_back",
    )(gate_up, d_mlp, w_down)


def norm_back_kernel(y_ref, d_both_ref, w_ref, near_sent_ref, near_ref, far_sent_ref, far_ref, d_c_ref):
    for block in range(4):
        rows = slice(256 * block, 256 * block + 256)
        d_c = nt(d_both_ref[0, rows, :], w_ref[0])
        for chunk in range(1, 4):
            d_c += nt(d_both_ref[chunk, rows, :], w_ref[chunk])
        d_c_ref[rows, :] = d_c
    put_rows(y_ref[0], d_c_ref, (near_sent_ref, near_ref, far_sent_ref, far_ref))


def norm_back(second, d_both, w_gate_up):
    return pl.pallas_call(
        norm_back_kernel,
        out_shape=PARTS,
        in_specs=[SCALAR, WHOLE, WHOLE],
        scratch_shapes=[pltpu.VMEM((1024, D), jnp.float32)],
        compiler_params=VMEM,
        cost_estimate=cost(5 << 30, 12 << 20),
        name="norm_back",
    )(second, d_both, w_gate_up)


def gate_grad_kernel(c_ref, d_both_ref, g_ref):
    for block in range(4):
        grad = tn(c_ref[:, 256 * block : 256 * block + 256], d_both_ref[0]).astype(jnp.bfloat16)
        for part in range(4):
            source = 4 * block + part
            for pair in range(2):
                for half in range(2):
                    at = 256 * half + 128 * pair
                    g_ref[pair, 128 * source + 64 * half : 128 * source + 64 * half + 64, :] = grad[
                        64 * part : 64 * part + 64, at : at + 128
                    ]


def gate_grad(c_low, d_both):
    return pl.pallas_call(
        gate_grad_kernel,
        grid=(4,),
        out_shape=jax.ShapeDtypeStruct((8, 2048, 128), jnp.bfloat16),
        in_specs=[pl.BlockSpec((1024, D), lambda i: (0, 0)), pl.BlockSpec((1, 1024, 512), lambda i: (i, 0, 0))],
        out_specs=pl.BlockSpec((2, 2048, 128), lambda i: (i, 0, 0)),
        compiler_params=VMEM,
        cost_estimate=cost(5 << 30, 10 << 20),
        name="gate_grad",
    )(c_low, d_both)


def out_kernel(
    y_ref, hidden_ref, w_ref, own_ref, pair_ref, last_ref, end_ref,
    near_sent_ref, near_ref, far_sent_ref, far_ref, g_scale_ref,
    branch_ref,
):
    total = jnp.zeros((1, D), jnp.float32)
    for block in range(4):
        rows = slice(256 * block, 256 * block + 256)
        branch = nn(hidden_ref[rows, :], w_ref[...])
        branch_ref[rows, :] = branch
        cot = in_order((own_ref, pair_ref, last_ref, end_ref), block // 2, block % 2, y_ref[0])
        total += jnp.sum(cot.astype(jnp.float32) * branch, axis=0, keepdims=True)
    g_scale_ref[...] = total
    put_rows(y_ref[0], branch_ref, (near_sent_ref, near_ref, far_sent_ref, far_ref))


def out_step(second, hidden, down, cot):
    return pl.pallas_call(
        out_kernel,
        out_shape=PARTS + (jax.ShapeDtypeStruct((1, D), jnp.float32),),
        in_specs=[SCALAR] + [WHOLE] * 6,
        scratch_shapes=[pltpu.VMEM((1024, D), jnp.float32)],
        compiler_params=VMEM,
        cost_estimate=cost(3 << 30, 10 << 20),
        name="out",
    )(second, hidden, down, *cot)


def attend_back_kernel(
    y_ref, own_ref, pair_ref, far_ref, last_ref, ring_ref, attn_ref, low_ref, lse_ref, cos_ref, sin_ref,
    length_ref, far_length_ref,
    d_qkv_ref, g_ref,
    d_branch_ref, w_out_ref, key_ref, value_ref,
):
    for place in range(8):
        w_out_ref[:, 128 * place : 128 * place + 128] = ring_ref[place]
    for block in range(4):
        d_branch_ref[256 * block : 256 * block + 256, :] = in_order(
            (own_ref, pair_ref, far_ref, last_ref), block // 2, block % 2, y_ref[0]
        )
    g_out = tn(attn_ref[...], d_branch_ref[...]).astype(jnp.bfloat16)
    for place in range(8):
        g_ref[place] = g_out[:, 128 * place : 128 * place + 128]
    for seq in range(2):
        key_ref[...] = jnp.zeros_like(key_ref)
        value_ref[...] = jnp.zeros_like(value_ref)
        cosine, sine = cos_ref[seq], -sin_ref[seq]
        for block in range(2):
            at = 512 * seq + 256 * block
            rows = slice(at, at + 256)
            span = slice(128 * block, 128 * block + 384)
            keys = slice(512 * seq + 128 * block, 512 * seq + 128 * block + 384)
            mask, keep = mask_of((length_ref, far_length_ref)[seq], block)
            d_attn_all = nt(d_branch_ref[rows, :], w_out_ref[...]).astype(jnp.bfloat16)
            d_attn_all = jnp.where(keep, d_attn_all, jnp.zeros_like(d_attn_all))
            d_queries, d_keys, d_values = [], [], []
            for head in range(4):
                lane = 64 * head
                query = low_ref[rows, lane : lane + 64]
                key = low_ref[keys, OWN + lane : OWN + lane + 64]
                value = low_ref[keys, 2 * OWN + lane : 2 * OWN + lane + 64]
                d_attn = d_attn_all[:, lane : lane + 64]
                masked = jnp.where(mask, nt(query, key) * SCALE, neg_large)
                probs = jnp.exp(masked - lse_ref[rows, head : head + 1])
                d_values.append(tn(probs.astype(jnp.bfloat16), d_attn))
                d_probs = nt(d_attn, value)
                inner = jnp.sum(probs * d_probs, axis=1, keepdims=True)
                d_scores = (probs * (d_probs - inner)).astype(jnp.bfloat16)
                d_queries.append(nn(d_scores, key) * SCALE)
                d_keys.append(tn(d_scores, query) * SCALE)
            part = slice(256 * block, 256 * block + 256)
            d_query = turn(jnp.concatenate(d_queries, axis=1), cosine[part], sine[part])
            d_qkv_ref[rows, :OWN] = d_query.astype(jnp.bfloat16)
            key_ref[span, :] += jnp.concatenate(d_keys, axis=1)
            value_ref[span, :] += jnp.concatenate(d_values, axis=1)
        whole = slice(512 * seq, 512 * seq + 512)
        d_qkv_ref[whole, OWN : 2 * OWN] = turn(key_ref[...], cosine, sine).astype(jnp.bfloat16)
        d_qkv_ref[whole, 2 * OWN :] = value_ref[...].astype(jnp.bfloat16)


def attention_back(second, d_branch, ring, attn, low, lse, cosine, sine, lengths):
    whole = lambda *dims: pl.BlockSpec(dims, lambda i: (0,) * len(dims))
    return pl.pallas_call(
        attend_back_kernel,
        grid=(1,),
        out_shape=(
            jax.ShapeDtypeStruct((1024, 3 * OWN), jnp.bfloat16),
            jax.ShapeDtypeStruct((8, OWN, 128), jnp.bfloat16),
        ),
        in_specs=[
            SCALAR,
            whole(256, D),
            whole(256, D),
            whole(256, D),
            whole(256, D),
            whole(8, OWN, 128),
            whole(1024, OWN),
            whole(1024, 3 * OWN),
            whole(1024, 4),
            whole(2, 512, 128),
            whole(2, 512, 128),
            SCALAR,
            SCALAR,
        ],
        out_specs=(whole(1024, 3 * OWN), whole(8, OWN, 128)),
        scratch_shapes=[
            pltpu.VMEM((1024, D), jnp.bfloat16),
            pltpu.VMEM((OWN, D), jnp.bfloat16),
            pltpu.VMEM((512, OWN), jnp.float32),
            pltpu.VMEM((512, OWN), jnp.float32),
        ],
        compiler_params=VMEM,
        cost_estimate=cost(12 << 30, 10 << 20),
        name="attend_back",
    )(second, *d_branch, ring, attn, low, lse, cosine, sine, *lengths)


def grad_kernel(
    y_ref, a_ref, w_ref, order_ref, d_qkv_ref, g_out_ref, x_ref, mean_ref, inv_ref, small_ref,
    g_ref, near_sent_ref, near_ref, far_sent_ref, far_ref,
    d_a_ref,
):
    g_gain, g_bias = jnp.zeros((1, D), jnp.float32), jnp.zeros((1, D), jnp.float32)
    for block in range(4):
        rows = slice(256 * block, 256 * block + 256)
        d_a = nt(d_qkv_ref[rows, :], w_ref[...])
        normed = (x_ref[rows, :].astype(jnp.float32) - mean_ref[rows, :]) * inv_ref[rows, :]
        g_gain += jnp.sum(d_a * normed, axis=0, keepdims=True)
        g_bias += jnp.sum(d_a, axis=0, keepdims=True)
        d_a_ref[rows, :] = d_a
    put_rows(y_ref[0], d_a_ref, (near_sent_ref, near_ref, far_sent_ref, far_ref))
    for block in range(8):
        grad = tn(a_ref[:, 128 * block : 128 * block + 128], d_qkv_ref[...]).astype(jnp.bfloat16)
        grad = jnp.concatenate([grad[:, OWN * third : OWN * third + OWN] for third in range(3)], axis=0)
        grad = tn(order_ref[...], grad).astype(jnp.bfloat16)
        for part in range(6):
            chunk = 6 * block + part
            at = 128 * (chunk // 8)
            g_ref[chunk % 8, at : at + 64, :] = grad[64 * part : 64 * part + 64, :128]
            g_ref[chunk % 8, at + 64 : at + 128, :] = grad[64 * part : 64 * part + 64, 128:]
    vectors = [g_gain, g_bias] + [small_ref[k : k + 1, :] for k in range(4)]
    lines = [v[:, 128 * k : 128 * k + 128] for v in vectors for k in range(8)]
    for place in range(8):
        g_ref[place, 768:1024, :] = g_out_ref[place]
        rows = lines[6 * place : 6 * place + 6] + [jnp.zeros((SLAB - 6, 128), jnp.float32)]
        g_ref[place, 1024:, :] = jnp.concatenate(rows, axis=0).astype(jnp.bfloat16)


def grad_step(second, a_low, w_qkv, order, d_qkv, g_out, x_all, mean, inv, small):
    return pl.pallas_call(
        grad_kernel,
        out_shape=(jax.ShapeDtypeStruct((8, 1024 + SLAB, 128), jnp.bfloat16),) + PARTS,
        in_specs=[SCALAR] + [WHOLE] * 9,
        scratch_shapes=[pltpu.VMEM((1024, D), jnp.float32)],
        compiler_params=VMEM,
        cost_estimate=cost(8 << 30, 12 << 20),
        name="grad",
    )(second, a_low, w_qkv, order, d_qkv, g_out, x_all, mean, inv, small)


def after(value, *others):
    return lax.optimization_barrier((value,) + others)[0]


def ring_gather(block, waits):
    half = (block.shape[0] // 2 + 15) // 16 * 16
    ahead = back = block
    blocks = [block]
    for step in range(1, 5):
        if step in waits:
            ahead, back = after(ahead, waits[step]), after(back, waits[step])
        if step == 4:
            ahead, back = ahead[:half], back[half:]
        ahead = lax.ppermute(ahead, GROUP, AHEAD)
        back = lax.ppermute(back, GROUP, BACK)
        blocks += [ahead, back]
    return blocks


def ring_scatter(blocks, me, waits):
    rows = blocks.shape[1]
    half = (rows // 2 + 15) // 16 * 16
    sent, came = [], []

    def get(step, lo=0, hi=rows):
        return lax.dynamic_slice(blocks, (ring_place(me, step % 8), 0 * me + lo, 0 * me), (1, hi - lo, 128))[0]

    def add(moved, own):
        return (moved.astype(jnp.float32) + own.astype(jnp.float32)).astype(jnp.bfloat16)

    ahead, back = get(4, 0, half), get(4, half)
    for step in range(1, 5):
        if step in waits:
            ahead, back = after(ahead, *waits[step]), after(back, *waits[step])
        sent.append((ahead, back))
        ahead = lax.ppermute(ahead, GROUP, AHEAD)
        back = lax.ppermute(back, GROUP, BACK)
        came.append((ahead, back))
        if step == 1:
            ahead = jnp.concatenate([add(ahead, get(3, 0, half)), get(3, half)])
            back = jnp.concatenate([get(5, 0, half), add(back, get(5, half))])
        elif step < 4:
            ahead, back = add(ahead, get(4 - step)), add(back, get(4 + step))
    total = get(0).astype(jnp.float32) + ahead.astype(jnp.float32) + back.astype(jnp.float32)
    return total.astype(jnp.bfloat16), sent, came


def to_group(rows, wait=None):
    pair = lax.ppermute(rows, "y", SWAP)
    if wait is not None:
        rows, pair = after(rows, wait), after(pair, wait)
    return rows, pair, lax.ppermute(rows, "c", SWAP), lax.ppermute(pair, "c", SWAP)


def half_sum(near_sent, near, far_sent, far):
    sent = near_sent + lax.ppermute(far_sent, "c", SWAP).astype(jnp.float32)
    return sent.astype(jnp.bfloat16), near, far


def full_sum(sent, near, far):
    here = near + lax.ppermute(far, "c", SWAP).astype(jnp.float32)
    return here + lax.ppermute(sent, "y", SWAP).astype(jnp.float32)


def normed_of(rows):
    centered = rows - jnp.mean(rows, axis=-1, keepdims=True)
    inv_scale = lax.rsqrt(jnp.mean(centered * centered, axis=-1, keepdims=True) + eps_norm)
    return centered * inv_scale, inv_scale


def norm_rows_back(out_grad, normed, inv_scale, gain):
    inner = out_grad * gain
    return inv_scale * (
        inner
        - jnp.mean(inner, axis=-1, keepdims=True)
        - normed * jnp.mean(inner * normed, axis=-1, keepdims=True)
    )


def fast_body(frames, cotangent, clip_lengths, params, first_moment, second_moment):
    z, x, c, y = (lax.axis_index(axis) for axis in EVERY)
    device = (((z * 2 + x) * 2 + c) * 2 + y).astype(jnp.int32)
    me = device[None]
    lengths = (clip_lengths, lax.ppermute(clip_lengths, "c", SWAP))
    order = np.zeros((384, 384), np.float32)
    for row in range(384):
        order[(row % 3) * 128 + row // 3, row] = 1.0
    order = jnp.asarray(order, jnp.bfloat16)

    pieces = spread(params, me)
    pieces = lax.all_to_all(pieces, EVERY, split_axis=0, concat_axis=0, tiled=True)
    first_piece, second_piece, third_piece = fix(pieces)
    first_blocks = ring_gather(first_piece, {})
    ring_qkv, w_own, vectors = join(
        join_first_kernel,
        me,
        first_blocks,
        (
            jax.ShapeDtypeStruct((8, 768, 128), jnp.bfloat16),
            jax.ShapeDtypeStruct((8, OWN, 128), jnp.bfloat16),
            jax.ShapeDtypeStruct((6, D), jnp.float32),
        ),
        "join_first",
        [pltpu.VMEM((8, SLAB, 128), jnp.bfloat16)],
    )
    w_parts = to_group(w_own)

    both = after(jnp.concatenate(lengths), first_piece)
    frame = jnp.arange(512, dtype=jnp.int32)
    starts, ends = both[:, :1], both[:, :1] + both[:, 1:]
    position = jnp.where((frame >= starts) & (frame < ends), frame - starts, frame).astype(jnp.float32)
    inverse = jnp.exp(
        jnp.asarray(np.arange(128) % 32, jnp.float32) * (-2.0 * math.log(rope_base) / HEAD_DIM)
    )
    angle = position[:, :, None] * inverse
    cosine = jnp.cos(angle)
    sine = jnp.sin(angle) * jnp.asarray(np.where(np.arange(128) % 64 < 32, -1.0, 1.0), jnp.float32)
    frames_parts = to_group(after(frames[0], first_piece))
    x_all, mean_one, inv_one = prep(me, frames_parts)
    second_blocks = ring_gather(second_piece, {1: first_blocks[1], 2: first_blocks[5]})
    a_low, w_qkv, low, attn_own, lse = front(x_all, mean_one, inv_one, ring_qkv, vectors, order, cosine, sine, lengths)
    cot_parts = to_group(after(cotangent[0], frames_parts[1]), attn_own)
    attn_parts = to_group(after(attn_own, second_blocks[3]))
    attn_parts = attn_parts[:3] + (after(attn_parts[3], second_blocks[5]),)
    c_low, branch_seq = mix(x_all, attn_parts, w_parts, vectors)
    third_waits = {1: first_blocks[7], 3: c_low}
    third_blocks = ring_gather(third_piece, third_waits)
    second_blocks = second_blocks[:7] + [after(b, c_low) for b in second_blocks[7:]]
    w_gate_up = join(
        join_gate_up_kernel, me, second_blocks, jax.ShapeDtypeStruct((4, 1024, 512), jnp.bfloat16), "join_gate_up"
    )
    gate_up, hidden = gate_step(c_low, after(w_gate_up, third_blocks[3]))
    g_down, d_mlp = down_grad(me, after(hidden, third_blocks[5]), cot_parts, vectors)
    w_down = join(join_down_kernel, me, third_blocks, jax.ShapeDtypeStruct((1024, D), jnp.bfloat16), "join_down")
    down_waits = {1: (third_blocks[7],)}
    g_down, down_sent, down_came = ring_scatter(g_down.reshape(8, 1024, 128), device, down_waits)
    d_both = hidden_back(gate_up, d_mlp, after(w_down, *down_sent[0]))
    d_c_sent, *d_c_kept = half_sum(*norm_back(me, after(d_both, *down_sent[1]), w_gate_up))
    g_gate_up = gate_grad(c_low, after(d_both, d_c_sent))
    g_gate_up, gate_sent, gate_came = ring_scatter(g_gate_up, device, {1: down_sent[3]})

    x_own = frames[0].astype(jnp.float32)
    cot_own = cotangent[0].astype(jnp.float32)
    branch_own = jnp.where(y == 0, branch_seq[:256], branch_seq[256:])
    mid_own = x_own + vectors[4] * branch_own
    normed_two, scale_two = normed_of(mid_own)
    d_c_own = full_sum(d_c_sent, *d_c_kept)
    d_mid = cot_own + norm_rows_back(d_c_own, normed_two, scale_two, vectors[2])
    d_branch_own = (d_mid * vectors[4]).astype(jnp.bfloat16)
    d_branch = to_group(d_branch_own)
    *out_parts, g_scale_mlp = out_step(me, after(hidden, d_branch_own), w_down, cot_parts)
    out_sent, *out_kept = half_sum(*out_parts)
    g_gain_two = jnp.sum(d_c_own * normed_two, axis=0)
    g_bias_two = jnp.sum(d_c_own, axis=0)
    g_scale_attn = jnp.sum(d_mid * branch_own, axis=0)
    small = jnp.concatenate([jnp.stack([g_gain_two, g_bias_two, g_scale_attn]), g_scale_mlp], axis=0)

    d_branch = (after(d_branch[0], *gate_sent[1]),) + d_branch[1:]
    d_qkv, g_out = attention_back(me, d_branch, w_own, attn_own, low, lse, cosine, sine, lengths)
    output = (mid_own + vectors[5] * full_sum(after(out_sent, d_branch[1]), *out_kept)).astype(jnp.bfloat16)
    d_qkv = after(d_qkv, *gate_sent[2])
    g_first, *d_a_parts = grad_step(me, a_low, w_qkv, order, d_qkv, g_out, x_all, mean_one, inv_one, small)
    d_a_sent, *d_a_kept = half_sum(*d_a_parts)
    g_first, _, _ = ring_scatter(g_first, device, {2: (d_a_sent,)})
    normed_one, scale_one = normed_of(x_own)
    d_one = norm_rows_back(full_sum(d_a_sent, *d_a_kept), normed_one, scale_one, vectors[0])
    frames_grad = (d_mid + d_one).astype(jnp.bfloat16)

    g_first = after(g_first, output, frames_grad)
    main = jnp.concatenate([g_first[:1024], g_gate_up, g_down]).reshape(32, 128, 128)
    slab = jnp.concatenate([main[1:, :8], main[1:, 64:72]], axis=1)
    slab = jnp.concatenate([slab, g_first[None, 1024:]])
    pieces = jnp.concatenate([main, slab], axis=1)
    pieces = lax.all_to_all(pieces, EVERY, split_axis=0, concat_axis=0, tiled=True)
    params_grad = collect(pieces, me, params.shape[0])
    new_params, new_first, new_second = adam_update(params, params_grad, first_moment, second_moment)
    return (output[None], frames_grad[None], params_grad, new_params, new_first, new_second)


def solution(mesh):
    def run(frames, cotangent, clip_lengths, params, first_moment, second_moment):
        fits = (
            mesh.shape["dp"] == 16
            and mesh.shape["seq"] == 2
            and frames.shape == (16, 512, D)
            and clip_lengths.shape == (16, 2)
        )
        if fits:
            over = Mesh(mesh.devices.reshape(4, 2, 2, 2), EVERY)
            rows, clips, flat = P(("z", "x", "c"), "y", None), P(("z", "x", "c"), None), P(EVERY)
        else:
            over = mesh
            rows, clips, flat = P("dp", "seq", None), P("dp", None), P(("dp", "seq"))
        step = jax.shard_map(
            fast_body if fits else body,
            mesh=over,
            in_specs=(rows, rows, clips, flat, flat, flat),
            out_specs=(rows, rows, flat, flat, flat, flat),
            check_vma=False,
        )
        return step(frames, cotangent, clip_lengths, params, first_moment, second_moment)

    return run
```

```python
import functools
import math

import jax
import jax.numpy as jnp
import numpy as np
from jax import lax
from jax.experimental import pallas as pl
from jax.experimental.pallas import tpu as pltpu
from jax.sharding import Mesh
from jax.sharding import PartitionSpec as P

D = 1024
HEADS = 16
HEAD_DIM = 64
FF = 4096
WINDOW = 128


eps_norm = 1e-05
beta_one = 0.9
beta_two = 0.99
learn_rate = 0.01
decay_rate = 0.1
eps_adam = 1e-08
adam_step = 100.0
neg_large = -1e30
rope_base = 10000.0


def padded(shard, sides, width):
    for axis, dim in sides:
        size, length = (lax.axis_size(axis), shard.shape[dim])
        up = [(i, (i + 1) % size) for i in range(size - 1)]
        down = [(j, i) for i, j in up]
        last = lax.slice_in_dim(shard, length - width, length, axis=dim)
        first = lax.slice_in_dim(shard, 0, width, axis=dim)
        before = lax.ppermute(last, axis, up)
        after = lax.ppermute(first, axis, down)
        shard = jnp.concatenate([before, shard, after], axis=dim)
    return shard


def unpack(flat_params):
    end_qkv = D * 3 * D
    end_out = end_qkv + D * D
    end_mlp = end_out + D * 2 * FF
    end_down = end_mlp + FF * D
    w_qkv = flat_params[:end_qkv].reshape(D, 3 * D)
    w_out = flat_params[end_qkv:end_out].reshape(D, D)
    w_gate_up = flat_params[end_out:end_mlp].reshape(D, 2 * FF)
    w_down = flat_params[end_mlp:end_down].reshape(FF, D)
    vectors = flat_params[end_down:].reshape(6, D).astype(jnp.float32)
    return (w_qkv, w_out, w_gate_up, w_down, vectors)


def clip_info(lengths, glob):
    clip_ends = jnp.cumsum(lengths, axis=1, dtype=jnp.int32)
    clip_starts = clip_ends - lengths
    after_end = (glob[None, :, None] >= clip_ends[:, None, :]).astype(jnp.int32)
    segment = jnp.sum(after_end, axis=2, dtype=jnp.int32)
    onehot = segment[:, :, None] == jnp.arange(lengths.shape[1], dtype=jnp.int32)[None, None, :]
    clip_begin = jnp.sum(jnp.where(onehot, clip_starts[:, None, :], 0), axis=2, dtype=jnp.int32)
    return (segment, (glob[None, :] - clip_begin).astype(jnp.float32))


def rotate(values, position, sign):
    half_dim = values.shape[-1] // 2
    inverse = jnp.exp(
        jnp.arange(half_dim, dtype=jnp.float32) * (-2.0 * math.log(rope_base) / HEAD_DIM)
    )
    rot_angle = position[:, :, None, None] * inverse
    cosine = jnp.cos(rot_angle)
    rot_sine = sign * jnp.sin(rot_angle)
    low_half = values[..., :half_dim]
    high_half = values[..., half_dim:]
    return jnp.concatenate(
        [low_half * cosine - high_half * rot_sine, high_half * cosine + low_half * rot_sine],
        axis=-1,
    )


def norm_forward(row_vals, norm_gain, norm_bias):
    centered = row_vals - jnp.mean(row_vals, axis=-1, keepdims=True)
    inv_scale = lax.rsqrt(jnp.mean(centered * centered, axis=-1, keepdims=True) + eps_norm)
    normed = centered * inv_scale
    return (normed * norm_gain + norm_bias, normed, inv_scale)


def norm_backward(out_grad, normed, inv_scale, norm_gain):
    d_gain = jnp.sum(out_grad * normed, axis=0)
    d_bias = jnp.sum(out_grad, axis=0)
    inner_grad = out_grad * norm_gain
    d_rows = inv_scale * (
        inner_grad
        - jnp.mean(inner_grad, axis=-1, keepdims=True)
        - normed * jnp.mean(inner_grad * normed, axis=-1, keepdims=True)
    )
    return (d_rows, d_gain, d_bias)


def scores_of(query_rows, key_rows, window_mask):
    raw_scores = jnp.einsum(
        "qhd,khd->hqk", query_rows, key_rows, preferred_element_type=jnp.float32
    ) * HEAD_DIM ** (-0.5)
    return jnp.where(window_mask[None], raw_scores, neg_large)


def attend(query_rows, key_rows, value_rows, window_mask):
    masked = scores_of(query_rows, key_rows, window_mask)
    row_max = jnp.max(masked, axis=-1, keepdims=True)
    row_total = jnp.log(jnp.sum(jnp.exp(masked - row_max), axis=-1, keepdims=True)) + row_max
    prob_low = jnp.exp(masked - row_total).astype(jnp.bfloat16)
    attn_rows = jnp.einsum("hqk,khd->qhd", prob_low, value_rows, preferred_element_type=jnp.float32)
    return (attn_rows, row_total[..., 0])


def attend_back(query_rows, key_rows, value_rows, window_mask, row_total, d_attn):
    masked = scores_of(query_rows, key_rows, window_mask)
    prob_rows = jnp.exp(masked - row_total[..., None])
    prob_low = prob_rows.astype(jnp.bfloat16)
    d_values = jnp.einsum("hqk,qhd->khd", prob_low, d_attn, preferred_element_type=jnp.float32)
    d_probs = jnp.einsum("qhd,khd->hqk", d_attn, value_rows, preferred_element_type=jnp.float32)
    inner_sum = jnp.sum(prob_rows * d_probs, axis=-1, keepdims=True)
    d_scores = (prob_rows * (d_probs - inner_sum)).astype(jnp.bfloat16)
    d_query = jnp.einsum(
        "hqk,khd->qhd", d_scores, key_rows, preferred_element_type=jnp.float32
    ) * HEAD_DIM ** (-0.5)
    d_keys = jnp.einsum(
        "hqk,qhd->khd", d_scores, query_rows, preferred_element_type=jnp.float32
    ) * HEAD_DIM ** (-0.5)
    return (d_query, d_keys, d_values)


def adam_update(flat_params, grads, first_moment, second_moment):
    new_first = beta_one * first_moment + (1.0 - beta_one) * grads
    new_second = beta_two * second_moment + (1.0 - beta_two) * grads * grads
    corrected_first = new_first / (1.0 - beta_one**adam_step)
    corrected_second = new_second / (1.0 - beta_two**adam_step)
    step_size = corrected_first / (jnp.sqrt(corrected_second) + eps_adam) + decay_rate * flat_params
    return (flat_params - learn_rate * step_size, new_first, new_second)


def body(frames, cotangent, clip_lengths, params, first_moment, second_moment):
    seq_count, frame_span, model_width = frames.shape
    row_count = seq_count * frame_span
    window_reach = WINDOW
    key_count = frame_span + 2 * window_reach
    head_count = HEADS
    head_size = model_width // head_count
    group_size = 4
    seq_len = lax.axis_size("seq") * frame_span
    seq_start = lax.axis_index("seq") * frame_span
    glob_rows = seq_start + jnp.arange(frame_span, dtype=jnp.int32)
    glob_keys = seq_start - window_reach + jnp.arange(key_count, dtype=jnp.int32)
    seg_rows, pos_rows = clip_info(clip_lengths, glob_rows)
    seg_keys, unused = clip_info(clip_lengths, glob_keys)
    inside = (glob_keys >= 0) & (glob_keys < seq_len)
    near_band = (
        jnp.abs(jnp.arange(frame_span)[:, None] + window_reach - jnp.arange(key_count)[None, :])
        < window_reach
    )
    window_mask = (
        (seg_rows[:, :, None] == seg_keys[:, None, :]) & inside[None, None, :] & near_band[None]
    )
    keep_rows = seg_rows != clip_lengths.shape[1] - 1
    shards = params.astype(jnp.bfloat16)
    gathered = lax.all_gather(shards, ("dp", "seq"), axis=0, tiled=True)
    w_qkv, w_out, w_gate_up, w_down, vectors = unpack(gathered)
    x_rows = frames.reshape(row_count, model_width).astype(jnp.float32)
    norm_one, normed_one, scale_one = norm_forward(x_rows, vectors[0], vectors[1])
    a_low = norm_one.astype(jnp.bfloat16)
    qkv = jnp.dot(a_low, w_qkv, preferred_element_type=jnp.float32).reshape(
        seq_count, frame_span, 3, head_count, head_size
    )
    query_low = rotate(qkv[:, :, 0], pos_rows, 1.0).astype(jnp.bfloat16)
    key_low = rotate(qkv[:, :, 1], pos_rows, 1.0).astype(jnp.bfloat16)
    value_low = qkv[:, :, 2].astype(jnp.bfloat16)
    key_value = jnp.concatenate([key_low, value_low], axis=2).reshape(
        seq_count, frame_span, 2 * model_width
    )
    wide_rows = padded(key_value, (("seq", 1),), window_reach)
    wide_rows = wide_rows.reshape(seq_count, key_count, 2, head_count, head_size)
    key_wide = wide_rows[:, :, 0]
    value_wide = wide_rows[:, :, 1]
    seq_index = 0
    out_parts = []
    total_parts = []
    for head_start in range(0, head_count, group_size):
        head_end = head_start + group_size
        attn_rows, row_total = attend(
            query_low[seq_index, :, head_start:head_end],
            key_wide[seq_index, :, head_start:head_end],
            value_wide[seq_index, :, head_start:head_end],
            window_mask[seq_index],
        )
        out_parts.append(attn_rows)
        total_parts.append(row_total)
    attn_list = [jnp.concatenate(out_parts, axis=1)]
    total_list = [total_parts]
    attn_all = jnp.where(keep_rows[:, :, None, None], jnp.stack(attn_list), 0.0)
    attn_low = attn_all.reshape(row_count, model_width).astype(jnp.bfloat16)
    branch_attn = jnp.dot(attn_low, w_out, preferred_element_type=jnp.float32)
    mid_rows = x_rows + vectors[4] * branch_attn
    norm_two, normed_two, scale_two = norm_forward(mid_rows, vectors[2], vectors[3])
    c_low = norm_two.astype(jnp.bfloat16)
    gate_up = jnp.dot(c_low, w_gate_up, preferred_element_type=jnp.float32)
    gate = gate_up[:, :FF]
    up_rows = gate_up[:, FF:]
    gate_sig = jax.nn.sigmoid(gate)
    hidden = (gate * gate_sig * up_rows).astype(jnp.bfloat16)
    branch_mlp = jnp.dot(hidden, w_down, preferred_element_type=jnp.float32)
    output = (
        (mid_rows + vectors[5] * branch_mlp)
        .astype(jnp.bfloat16)
        .reshape(seq_count, frame_span, model_width)
    )
    gathered = lax.all_gather(shards, ("dp", "seq"), axis=0, tiled=True)
    w_qkv, w_out, w_gate_up, w_down, vectors = unpack(gathered)
    d_rows = cotangent.reshape(row_count, model_width).astype(jnp.float32)
    g_scale_mlp = jnp.sum(d_rows * branch_mlp, axis=0)
    d_mlp = (d_rows * vectors[5]).astype(jnp.bfloat16)
    g_down = jnp.dot(hidden.T, d_mlp, preferred_element_type=jnp.float32)
    d_hidden = jnp.dot(d_mlp, w_down.T, preferred_element_type=jnp.float32)
    d_gate = d_hidden * up_rows * gate_sig * (1.0 + gate * (1.0 - gate_sig))
    d_up = d_hidden * gate * gate_sig
    d_gate_up = jnp.concatenate([d_gate, d_up], axis=1).astype(jnp.bfloat16)
    g_gate_up = jnp.dot(c_low.T, d_gate_up, preferred_element_type=jnp.float32)
    d_two = jnp.dot(d_gate_up, w_gate_up.T, preferred_element_type=jnp.float32)
    d_norm_two, g_gain_two, g_bias_two = norm_backward(d_two, normed_two, scale_two, vectors[2])
    d_mid = d_rows + d_norm_two
    g_scale_attn = jnp.sum(d_mid * branch_attn, axis=0)
    d_branch = (d_mid * vectors[4]).astype(jnp.bfloat16)
    g_out = jnp.dot(attn_low.T, d_branch, preferred_element_type=jnp.float32)
    d_attn_low = jnp.dot(d_branch, w_out.T, preferred_element_type=jnp.float32).astype(jnp.bfloat16)
    d_attn = jnp.where(
        keep_rows[:, :, None, None],
        d_attn_low.reshape(seq_count, frame_span, head_count, head_size),
        jnp.zeros((), jnp.bfloat16),
    )
    seq_index = 0
    query_parts = []
    key_parts = []
    value_parts = []
    for number, head_start in enumerate(range(0, head_count, group_size)):
        head_end = head_start + group_size
        d_query, d_keys, d_values = attend_back(
            query_low[seq_index, :, head_start:head_end],
            key_wide[seq_index, :, head_start:head_end],
            value_wide[seq_index, :, head_start:head_end],
            window_mask[seq_index],
            total_list[seq_index][number],
            d_attn[seq_index, :, head_start:head_end],
        )
        query_parts.append(d_query)
        key_parts.append(d_keys)
        value_parts.append(d_values)
    query_grads = [jnp.concatenate(query_parts, axis=1)]
    key_grads = [jnp.concatenate(key_parts, axis=1)]
    value_grads = [jnp.concatenate(value_parts, axis=1)]
    d_query_all = jnp.stack(query_grads)
    d_pair = jnp.concatenate([jnp.stack(key_grads), jnp.stack(value_grads)], axis=2).reshape(
        seq_count, key_count, 2 * model_width
    )
    rim_rows = jnp.concatenate(
        [d_pair[:, :window_reach], d_pair[:, window_reach + frame_span :]], axis=1
    )
    taken_rows = padded(rim_rows.astype(jnp.bfloat16), (("seq", 1),), window_reach).astype(
        rim_rows.dtype
    )
    own_rows = d_pair[:, window_reach : window_reach + frame_span]
    own_rows = own_rows + jnp.pad(
        taken_rows[:, :window_reach], ((0, 0), (0, frame_span - window_reach), (0, 0))
    )
    own_rows = own_rows + jnp.pad(
        taken_rows[:, 3 * window_reach :], ((0, 0), (frame_span - window_reach, 0), (0, 0))
    )
    own_rows = own_rows.reshape(seq_count, frame_span, 2, head_count, head_size)
    d_qkv = jnp.stack(
        [
            rotate(d_query_all, pos_rows, -1.0),
            rotate(own_rows[:, :, 0], pos_rows, -1.0),
            own_rows[:, :, 1],
        ],
        axis=2,
    )
    d_qkv = d_qkv.reshape(row_count, 3 * model_width).astype(jnp.bfloat16)
    g_qkv = jnp.dot(a_low.T, d_qkv, preferred_element_type=jnp.float32)
    d_one = jnp.dot(d_qkv, w_qkv.T, preferred_element_type=jnp.float32)
    d_norm_one, g_gain_one, g_bias_one = norm_backward(d_one, normed_one, scale_one, vectors[0])
    frames_grad = (
        (d_mid + d_norm_one).astype(jnp.bfloat16).reshape(seq_count, frame_span, model_width)
    )
    small_grads = jnp.stack(
        [g_gain_one, g_bias_one, g_gain_two, g_bias_two, g_scale_attn, g_scale_mlp]
    )
    whole_grad = jnp.concatenate(
        [
            g_qkv.reshape(-1),
            g_out.reshape(-1),
            g_gate_up.reshape(-1),
            g_down.reshape(-1),
            small_grads.reshape(-1),
        ]
    )
    params_grad = lax.psum_scatter(whole_grad, ("dp", "seq"), scatter_dimension=0, tiled=True)
    new_params, new_first, new_second = adam_update(
        params, params_grad, first_moment, second_moment
    )
    return (output, frames_grad, params_grad, new_params, new_first, new_second)


EVERY = ("z", "x", "c", "y")
GROUP = ("z", "x")
RING = ((0, 0), (1, 0), (2, 0), (3, 0), (3, 1), (2, 1), (1, 1), (0, 1))
PLACES = tuple(2 * z + x for z, x in RING)
AHEAD = tuple((PLACES[i], PLACES[(i + 1) % 8]) for i in range(8))
BACK = tuple((b, a) for a, b in AHEAD)
SWAP = ((0, 1), (1, 0))
LINES = 4096
TAIL = 64
SLAB = 16
ROWS = 128 + SLAB
OWN = 256
SCALE = HEAD_DIM ** (-0.5)
SCALAR = pl.BlockSpec(memory_space=pltpu.SMEM)
WHOLE = pl.BlockSpec(memory_space=pltpu.VMEM)
HBM = pl.BlockSpec(memory_space=pltpu.HBM)
ANY = pl.BlockSpec(memory_space=pl.ANY)


def vmem(mebibytes):
    return pltpu.CompilerParams(vmem_limit_bytes=mebibytes << 20)


def ring_place(me, step):
    z, x = lax.div(me, 8), lax.rem(lax.div(me, 4), 2)
    at = lax.rem(jnp.where(x == 0, z, 7 - z) + step, 8)
    return jnp.where(at < 4, 2 * at, 15 - 2 * at)


def kind_of(shard):
    if shard < 6:
        return 0
    return 2 if 8 <= shard < 24 else 1


def piece_lines(kind, dest):
    place, member = divmod(dest, 4)
    if kind == 0:
        return [(512 * place + member, 8), (512 * place + 4 + member, 8)]
    if kind == 1:
        return [(1024 * member + place, 8), (1024 * member + 512 + place, 8)]
    return [(dest, 64), (32 + dest, 64)]


def tail_lines(kind, dest):
    place, member = divmod(dest, 4)
    if kind == 0:
        return [(0, 6, member, 8), (8, 6, 4 + member, 8)] if place == 0 else []
    if kind == 1:
        return [(0, 6, place, 8)] if member == 0 else []
    return [(0, 1, dest, 1)] + ([(8, 1, 32 + dest, 1)] if dest < 16 else [])


def is_kind(shard, kind):
    if kind == 0:
        return shard < 6
    gate_up = (shard >= 8) & (shard < 24)
    if kind == 2:
        return gate_up
    return (shard >= 6) & jnp.logical_not(gate_up) & (shard < 32)


def spread_kernel(me_ref, flat_ref, out_ref, lines_ref):
    me = me_ref[0]
    odd = lax.rem(me, 2) == 1
    start = 48 - (3 * me + 1) // 2
    lane = lax.broadcasted_iota(jnp.int32, (64, 128), 1)

    def shift(step, carry):
        here = flat_ref[pl.ds(start + step * 64, 64), :]
        after = flat_ref[pl.ds(start + step * 64 + 1, 64), :]
        mixed = jnp.where(lane < 64, pltpu.roll(here, 64, 1), pltpu.roll(after, 64, 1))
        lines_ref[pl.ds(pl.multiple_of(step * 64, 64), 64), :] = jnp.where(odd, mixed, here)
        return carry

    lax.fori_loop(0, (LINES + TAIL) // 64, shift, 0, unroll=5)
    for kind in range(3):

        @pl.when(is_kind(me, kind))
        def _(kind=kind):
            for dest in range(32):
                for half, (first, stride) in enumerate(piece_lines(kind, dest)):
                    rows = lines_ref[pl.ds(first, 64, stride), :]
                    out_ref[dest, 64 * half : 64 * half + 64, :] = rows.astype(jnp.bfloat16)

    def slab_of(parts):
        slab = [jnp.zeros((8, 128), jnp.float32)] * 2
        row = lax.broadcasted_iota(jnp.int32, (8, 128), 0)
        for at, count, first, stride in parts:
            if count == 1:
                value = jnp.broadcast_to(lines_ref[LINES + first : LINES + first + 1, :], (8, 128))
            else:
                value = lines_ref[pl.ds(LINES + first, 8, stride), :]
            slab[at // 8] = jnp.where(row < count, value, 0.0)
        return jnp.concatenate(slab, axis=0).astype(jnp.bfloat16)

    for kind in range(3):

        @pl.when(is_kind(me + 1, kind))
        def _(kind=kind):
            for dest in range(32):
                out_ref[dest, 128:ROWS, :] = slab_of(tail_lines(kind, dest))

    @pl.when(me == 31)
    def _():
        for dest in range(32):
            out_ref[dest, 128:ROWS, :] = slab_of([(0, 6, 6 * (dest // 4), 1)])


def spread(params, me):
    flat = jnp.pad(params, (48 * 128, 4224 * 128 - 48 * 128 - params.shape[0])).reshape(4224, 128)
    return pl.pallas_call(
        spread_kernel,
        out_shape=jax.ShapeDtypeStruct((32, ROWS, 128), jnp.bfloat16),
        in_specs=[
            pl.BlockSpec(memory_space=pltpu.SMEM),
            pl.BlockSpec(memory_space=pltpu.VMEM),
        ],
        out_specs=pl.BlockSpec(memory_space=pltpu.VMEM),
        scratch_shapes=[pltpu.VMEM((LINES + TAIL, 128), jnp.float32)],
        compiler_params=vmem(12),
        name="spread",
    )(me, flat)


def collect_kernel(me_ref, piece_ref, out_ref, lines_ref):
    me = me_ref[0]
    odd = lax.rem(me, 2) == 1
    lines_ref[LINES:, :] = jnp.zeros((TAIL, 128), jnp.float32)
    for kind in range(3):

        @pl.when(is_kind(me, kind))
        def _(kind=kind):
            for dest in range(32):
                for half, (first, stride) in enumerate(piece_lines(kind, dest)):
                    rows = piece_ref[dest, 64 * half : 64 * half + 64, :].astype(jnp.float32)
                    lines_ref[pl.ds(first, 64, stride), :] = rows

    for kind in range(3):

        @pl.when(is_kind(me + 1, kind))
        def _(kind=kind):
            for dest in range(32):
                slab = piece_ref[dest, 128:ROWS, :].astype(jnp.float32)
                for at, count, first, stride in tail_lines(kind, dest):
                    for k in range(count):
                        line = LINES + first + k * stride
                        lines_ref[line : line + 1, :] = slab[at + k : at + k + 1, :]

    @pl.when(me == 31)
    def _():
        for place in range(8):
            total = piece_ref[4 * place, 128:ROWS, :].astype(jnp.float32)
            for member in range(1, 4):
                total = total + piece_ref[4 * place + member, 128:ROWS, :].astype(jnp.float32)
            for k in range(6):
                line = LINES + 6 * place + k
                lines_ref[line : line + 1, :] = total[k : k + 1, :]

    start = (3 * me) // 2
    lane = lax.broadcasted_iota(jnp.int32, (24, 128), 1)

    def shift(step, carry):
        here = lines_ref[pl.ds(start + step * 24, 24), :]
        after = lines_ref[pl.ds(start + step * 24 + 1, 24), :]
        mixed = jnp.where(lane < 64, pltpu.roll(here, 64, 1), pltpu.roll(after, 64, 1))
        out_ref[pl.ds(pl.multiple_of(step * 24, 8), 24), :] = jnp.where(odd, mixed, here)
        return carry

    lax.fori_loop(0, 4104 // 24, shift, 0, unroll=9)


def collect(pieces, me, count):
    lines = pl.pallas_call(
        collect_kernel,
        out_shape=jax.ShapeDtypeStruct((4104, 128), jnp.float32),
        in_specs=[
            pl.BlockSpec(memory_space=pltpu.SMEM),
            pl.BlockSpec(memory_space=pltpu.VMEM),
        ],
        out_specs=pl.BlockSpec(memory_space=pltpu.VMEM),
        scratch_shapes=[pltpu.VMEM((LINES + TAIL, 128), jnp.float32)],
        compiler_params=vmem(12),
        name="collect",
    )(me, pieces)
    return lines.reshape(-1)[:count]


def swap_halves(rows):
    lane = lax.broadcasted_iota(jnp.int32, rows.shape, 1)
    return jnp.where(
        lax.rem(lane, 64) < 32, pltpu.roll(rows, 96, 1), pltpu.roll(rows, 32, 1)
    )


def turn(rows, cosine, signed_sine):
    parts = []
    for at in range(0, rows.shape[1], 128):
        part = rows[:, at : at + 128]
        parts.append(part * cosine + swap_halves(part) * signed_sine)
    return jnp.concatenate(parts, axis=1)


def clip_of(length_ref, frame):
    first = length_ref[0, 0]
    return (frame >= first).astype(jnp.int32) + (frame >= first + length_ref[0, 1]).astype(jnp.int32)


def mask_of(length_ref, block):
    row = lax.broadcasted_iota(jnp.int32, (256, 384), 0) + 256 * block
    key = lax.broadcasted_iota(jnp.int32, (256, 384), 1) + 128 * block
    own = clip_of(length_ref, lax.broadcasted_iota(jnp.int32, (256, 1), 0) + 256 * block)
    others = clip_of(length_ref, lax.broadcasted_iota(jnp.int32, (1, 384), 1) + 128 * block)
    return (jnp.abs(row - key) < WINDOW) & (own == others), own != 1


def nt(left, right):
    return lax.dot_general(left, right, (((1,), (1,)), ((), ())), preferred_element_type=jnp.float32)


def tn(left, right):
    return lax.dot_general(left, right, (((0,), (0,)), ((), ())), preferred_element_type=jnp.float32)


def nn(left, right):
    return jnp.dot(left, right, preferred_element_type=jnp.float32)


def cost(flops, moved):
    return pl.CostEstimate(flops=flops, bytes_accessed=moved, transcendentals=0)


def fix_kernel(piece_ref, first_ref, second_ref, third_ref):
    for source in range(32):
        out, at = (first_ref, source) if source < 8 else (second_ref, source - 8) if source < 24 else (third_ref, source - 24)
        out[128 * at : 128 * at + 128, :] = piece_ref[source, :128, :]
        if source:
            slab = piece_ref[source - 1, 128:ROWS, :].astype(jnp.float32)
            for half in range(2):
                rows = piece_ref[source, 64 * half : 64 * half + 16, :].astype(jnp.float32)
                extra = jnp.concatenate([slab[8 * half : 8 * half + 8], jnp.zeros((8, 128), jnp.float32)])
                out[128 * at + 64 * half : 128 * at + 64 * half + 16, :] = (rows + extra).astype(jnp.bfloat16)
    first_ref[1024:, :] = piece_ref[31, 128:ROWS, :]


def fix(pieces):
    return pl.pallas_call(
        fix_kernel,
        out_shape=tuple(jax.ShapeDtypeStruct((n, 128), jnp.bfloat16) for n in (1024 + SLAB, 2048, 1024)),
        in_specs=[WHOLE],
        out_specs=(WHOLE,) * 3,
        compiler_params=vmem(12),
        cost_estimate=cost(0, 1 << 22),
        name="fix",
    )(pieces)


def in_order(refs, seq, half, second):
    mine, other = refs[2 * seq], refs[2 * seq + 1]
    return jnp.where(lax.rem(second, 2) == half, mine[...], other[...])


def ring_parts(me_ref, refs):
    me = me_ref[0]
    parts = [(ring_place(me, 0), refs[0], None)]
    for step in range(1, 4):
        parts += [(ring_place(me, 8 - step), refs[2 * step - 1], None), (ring_place(me, step), refs[2 * step], None)]
    half = refs[7].shape[0]
    last = ring_place(me, 4)
    return parts + [(last, refs[7], (0, half)), (last, refs[8], (half, half + refs[8].shape[0]))]


def copy_all(pairs, done):
    copies = [pltpu.make_async_copy(source, target, done.at[k]) for k, (source, target) in enumerate(pairs)]
    for copy in copies:
        copy.start()
    for copy in copies:
        copy.wait()


def join_first_kernel(me_ref, *refs):
    blocks, (qkv_ref, out_ref, vec_ref, lines_ref, _) = refs[:9], refs[9:]
    for place, block, rows in ring_parts(me_ref, blocks):
        lo, hi = rows or (0, 1024 + SLAB)
        for at, end, ref in ((0, 768, qkv_ref), (768, 1024, out_ref), (1024, 1024 + SLAB, lines_ref)):
            first, last = max(at, lo), min(end, hi)
            if first < last:
                ref[place, first - at : last - at, :] = block[first - lo : last - lo, :]
    slabs = [lines_ref[place].astype(jnp.float32) for place in range(8)]
    for v in range(6):
        for k in range(8):
            line = 8 * v + k
            vec_ref[v : v + 1, 128 * k : 128 * k + 128] = slabs[line // 6][line % 6 : line % 6 + 1]


def join_gate_up_kernel(me_ref, *refs):
    blocks, (out_ref, done) = refs[:9], refs[9:]
    pairs = []
    for place, block, rows in ring_parts(me_ref, blocks):
        lo, hi = rows or (0, 16)
        for half in range(2):
            at = pl.multiple_of(256 * half + 128 * lax.rem(place, 2), 128)
            pairs.append((block.at[:, half], out_ref.at[lax.div(place, 2), lo:hi, :, pl.ds(at, 128)]))
    copy_all(pairs, done)


def join_down_kernel(me_ref, *refs):
    blocks, (out_ref, done) = refs[:9], refs[9:]
    pairs = []
    for place, block, rows in ring_parts(me_ref, blocks):
        lo, hi = rows or (0, 1024)
        pairs.append((block, out_ref.at[lo:hi, pl.ds(pl.multiple_of(128 * place, 128), 128)]))
    copy_all(pairs, done)


def join_out_kernel(*refs):
    w_ref = refs[4]
    for k in range(4):
        for place in range(8):
            w_ref[256 * k : 256 * k + 256, 128 * place : 128 * place + 128] = refs[k][place]


def join_out(parts):
    return pl.pallas_call(
        join_out_kernel,
        out_shape=jax.ShapeDtypeStruct((D, D), jnp.bfloat16),
        in_specs=[WHOLE] * 4,
        out_specs=WHOLE,
        compiler_params=vmem(12),
        cost_estimate=cost(0, 4 << 20),
        name="join_out",
    )(*parts)


def join(kernel, me, blocks, out_shape, name, scratch=(), space=WHOLE):
    if space is HBM:
        blocks = [pltpu.with_memory_space_constraint(block, pltpu.HBM) for block in blocks]
    return pl.pallas_call(
        kernel,
        out_shape=out_shape,
        in_specs=[SCALAR] + [space] * 9,
        out_specs=jax.tree.map(lambda _: WHOLE, out_shape),
        scratch_shapes=list(scratch) + [pltpu.SemaphoreType.DMA((32,))],
        compiler_params=vmem(12),
        cost_estimate=cost(0, 4 << 20),
        name=name,
    )(me, *blocks)


def prep_kernel(y_ref, own_ref, pair_ref, far_ref, last_ref, x_ref, mean_ref, inv_ref):
    for block in range(4):
        rows = slice(256 * block, 256 * block + 256)
        x_low = in_order((own_ref, pair_ref, far_ref, last_ref), block // 2, block % 2, y_ref[0])
        x_ref[rows, :] = x_low
        x_rows = x_low.astype(jnp.float32)
        mean = jnp.mean(x_rows, axis=1, keepdims=True)
        centered = x_rows - mean
        mean_ref[rows, :] = mean
        inv_ref[rows, :] = lax.rsqrt(jnp.mean(centered * centered, axis=1, keepdims=True) + eps_norm)


def prep(second, rows):
    return pl.pallas_call(
        prep_kernel,
        out_shape=(
            jax.ShapeDtypeStruct((1024, D), jnp.bfloat16),
            jax.ShapeDtypeStruct((1024, 1), jnp.float32),
            jax.ShapeDtypeStruct((1024, 1), jnp.float32),
        ),
        in_specs=[SCALAR] + [WHOLE] * 4,
        out_specs=(WHOLE,) * 3,
        compiler_params=vmem(12),
        cost_estimate=cost(1 << 24, 5 << 20),
        name="prep",
    )(second, *rows)


def front_kernel(
    x_ref, mean_ref, inv_ref, ring_ref, vec_ref, order_ref, cos_ref, sin_ref, length_ref, far_length_ref,
    a_out, w_out, low_out, attn_ref, lse_out,
    a_ref, w_ref, low_ref, lse_ref, done,
):
    copies = [
        pltpu.make_async_copy(ref, out, done.at[k])
        for k, (ref, out) in enumerate(((w_ref, w_out), (a_ref, a_out), (low_ref, low_out), (lse_ref, lse_out)))
    ]
    gain, bias = vec_ref[0:1, :], vec_ref[1:2, :]
    for block in range(8):
        parts = []
        for chunk in range(6 * block, 6 * block + 6):
            at = 128 * (chunk // 8)
            parts.append(
                jnp.concatenate(
                    [ring_ref[chunk % 8, at : at + 64, :], ring_ref[chunk % 8, at + 64 : at + 128, :]], axis=1
                )
            )
        rows = nn(order_ref[...], jnp.concatenate(parts, axis=0)).astype(jnp.bfloat16)
        for third in range(3):
            w_ref[128 * block : 128 * block + 128, OWN * third : OWN * third + OWN] = rows[
                128 * third : 128 * third + 128
            ]
    copies[0].start()
    for block in range(4):
        rows = slice(256 * block, 256 * block + 256)
        seq, at = block // 2, 256 * (block % 2)
        normed = (x_ref[rows, :].astype(jnp.float32) - mean_ref[rows, :]) * inv_ref[rows, :]
        a_low = (normed * gain + bias).astype(jnp.bfloat16)
        a_ref[rows, :] = a_low
        qkv = nn(a_low, w_ref[...])
        cosine, sine = cos_ref[seq, at : at + 256, :], sin_ref[seq, at : at + 256, :]
        low_ref[rows, : 2 * OWN] = turn(qkv[:, : 2 * OWN], cosine, sine).astype(jnp.bfloat16)
        low_ref[rows, 2 * OWN :] = qkv[:, 2 * OWN :].astype(jnp.bfloat16)
    copies[1].start()
    copies[2].start()
    for seq in range(2):
        for block in range(2):
            at = 512 * seq + 256 * block
            rows = slice(at, at + 256)
            keys = slice(512 * seq + 128 * block, 512 * seq + 128 * block + 384)
            mask, keep = mask_of((length_ref, far_length_ref)[seq], block)
            heads, sums = [], []
            for head in range(4):
                lane = 64 * head
                query = low_ref[rows, lane : lane + 64]
                key = low_ref[keys, OWN + lane : OWN + lane + 64]
                value = low_ref[keys, 2 * OWN + lane : 2 * OWN + lane + 64]
                masked = jnp.where(mask, nt(query, key) * SCALE, neg_large)
                top = jnp.max(masked, axis=1, keepdims=True)
                weight = jnp.exp(masked - top)
                total = jnp.sum(weight, axis=1, keepdims=True)
                probs = (weight * (1.0 / total)).astype(jnp.bfloat16)
                heads.append(jnp.where(keep, nn(probs, value), 0.0))
                sums.append(top + jnp.log(total))
            attn_ref[rows, :] = jnp.concatenate(heads, axis=1).astype(jnp.bfloat16)
            lse_ref[rows, :] = jnp.concatenate(sums, axis=1)
    copies[3].start()
    for copy in copies:
        copy.wait()


def front(x_all, mean, inv, ring, vectors, order, cosine, sine, lengths):
    return pl.pallas_call(
        front_kernel,
        out_shape=(
            pltpu.HBM((1024, D), jnp.bfloat16),
            pltpu.HBM((D, 3 * OWN), jnp.bfloat16),
            pltpu.HBM((1024, 3 * OWN), jnp.bfloat16),
            jax.ShapeDtypeStruct((1024, OWN), jnp.bfloat16),
            pltpu.HBM((1024, 4), jnp.float32),
        ),
        in_specs=[WHOLE] * 8 + [SCALAR] * 2,
        out_specs=(HBM, HBM, HBM, WHOLE, HBM),
        scratch_shapes=[
            pltpu.VMEM((1024, D), jnp.bfloat16),
            pltpu.VMEM((D, 3 * OWN), jnp.bfloat16),
            pltpu.VMEM((1024, 3 * OWN), jnp.bfloat16),
            pltpu.VMEM((1024, 4), jnp.float32),
            pltpu.SemaphoreType.DMA((4,)),
        ],
        compiler_params=vmem(14),
        cost_estimate=cost(12 << 30, 8 << 20),
        name="front",
    )(x_all, mean, inv, ring, vectors, order, cosine, sine, *lengths)


def mix_kernel(x_ref, own_ref, pair_ref, far_ref, last_ref, w_ref, vec_ref, c_ref, branch_ref):
    for block in range(4):
        rows = slice(256 * block, 256 * block + 256)
        other = (block + 2) % 4
        far = slice(256 * other, 256 * other + 256)
        attn = jnp.concatenate([own_ref[rows, :], pair_ref[rows, :], far_ref[far, :], last_ref[far, :]], axis=1)
        branch = nn(attn, w_ref[...])
        normed, _ = normed_of(x_ref[rows, :].astype(jnp.float32) + vec_ref[4:5, :] * branch)
        c_ref[rows, :] = (normed * vec_ref[2:3, :] + vec_ref[3:4, :]).astype(jnp.bfloat16)
        if block < 2:
            branch_ref[rows, :] = branch


def mix(x_all, attn, w_out, vectors):
    return pl.pallas_call(
        mix_kernel,
        out_shape=(
            pltpu.VMEM((1024, D), jnp.bfloat16),
            jax.ShapeDtypeStruct((512, D), jnp.float32),
        ),
        in_specs=[WHOLE] * 7,
        out_specs=(WHOLE, WHOLE),
        compiler_params=vmem(12),
        cost_estimate=cost(3 << 30, 10 << 20),
        name="mix",
    )(x_all, *attn, w_out, vectors)


def gate_kernel(c_ref, w_ref, gate_up_ref, hidden_ref):
    for block in range(4):
        rows = slice(256 * block, 256 * block + 256)
        for chunk in range(4):
            both = nn(c_ref[rows, :], w_ref[chunk])
            gate_up_ref[chunk, rows, :] = both
            gate, up = both[:, :256], both[:, 256:]
            hidden_ref[rows, 256 * chunk : 256 * chunk + 256] = (gate * jax.nn.sigmoid(gate) * up).astype(
                jnp.bfloat16
            )


def gate_step(c_low, w_gate_up):
    return pl.pallas_call(
        gate_kernel,
        out_shape=(
            jax.ShapeDtypeStruct((4, 1024, 512), jnp.float32),
            jax.ShapeDtypeStruct((1024, 1024), jnp.bfloat16),
        ),
        in_specs=[WHOLE] * 2,
        out_specs=(WHOLE, WHOLE),
        compiler_params=vmem(12),
        cost_estimate=cost(5 << 30, 16 << 20),
        name="gate",
    )(c_low, w_gate_up)


def down_grad_kernel(me_ref, hidden_ref, own_ref, pair_ref, far_ref, last_ref, vec_ref, g_ref, d_mlp_ref):
    for block in range(4):
        rows = in_order((own_ref, pair_ref, far_ref, last_ref), block // 2, block % 2, me_ref[0])
        d_mlp_ref[256 * block : 256 * block + 256, :] = (rows.astype(jnp.float32) * vec_ref[5:6, :]).astype(
            jnp.bfloat16
        )
    for source in range(0, 8, 2):
        g_down = tn(hidden_ref[:, 128 * source : 128 * source + 256], d_mlp_ref[...]).astype(jnp.bfloat16)
        for pair in range(2):
            for place in range(8):
                at = 128 * (source + pair)
                g_ref[place, at : at + 128, :] = g_down[128 * pair : 128 * pair + 128, 128 * place : 128 * place + 128]


def down_grad(me, hidden, cot, vectors):
    return pl.pallas_call(
        down_grad_kernel,
        out_shape=(
            jax.ShapeDtypeStruct((8, 1024, 128), jnp.bfloat16),
            jax.ShapeDtypeStruct((1024, D), jnp.bfloat16),
        ),
        in_specs=[SCALAR] + [WHOLE] * 6,
        out_specs=(WHOLE, WHOLE),
        compiler_params=vmem(12),
        cost_estimate=cost(3 << 30, 8 << 20),
        name="down_grad",
    )(me, hidden, *cot, vectors)


def put_rows(second, whole_ref, refs):
    for block in range(4):
        seq, half = divmod(block, 2)
        rows = whole_ref[256 * block : 256 * block + 256, :].astype(jnp.bfloat16 if seq else jnp.float32)

        @pl.when(lax.rem(second, 2) == half)
        def _(rows=rows, seq=seq):
            refs[2 * seq + 1][...] = rows

        @pl.when(lax.rem(second, 2) != half)
        def _(rows=rows, seq=seq):
            refs[2 * seq][...] = rows


PARTS = tuple(jax.ShapeDtypeStruct((256, D), t) for t in (jnp.float32, jnp.float32, jnp.bfloat16, jnp.bfloat16))


def hidden_back_kernel(gate_up_ref, d_mlp_ref, w_ref, d_both_ref):
    for block in range(4):
        rows = slice(256 * block, 256 * block + 256)
        for chunk in range(4):
            d_hidden = nt(d_mlp_ref[rows, :], w_ref[256 * chunk : 256 * chunk + 256, :])
            gate, up = gate_up_ref[chunk, rows, :256], gate_up_ref[chunk, rows, 256:]
            sig = jax.nn.sigmoid(gate)
            d_both_ref[chunk, rows, :256] = (d_hidden * up * sig * (1.0 + gate * (1.0 - sig))).astype(jnp.bfloat16)
            d_both_ref[chunk, rows, 256:] = (d_hidden * gate * sig).astype(jnp.bfloat16)


def hidden_back(gate_up, d_mlp, w_down):
    return pl.pallas_call(
        hidden_back_kernel,
        out_shape=jax.ShapeDtypeStruct((4, 1024, 512), jnp.bfloat16),
        in_specs=[WHOLE] * 3,
        out_specs=WHOLE,
        compiler_params=vmem(12),
        cost_estimate=cost(4 << 30, 18 << 20),
        name="hidden_back",
    )(gate_up, d_mlp, w_down)


def norm_back_kernel(y_ref, d_both_ref, w_ref, near_sent_ref, near_ref, far_sent_ref, far_ref, d_c_ref):
    for block in range(4):
        rows = slice(256 * block, 256 * block + 256)
        d_c = nt(d_both_ref[0, rows, :], w_ref[0])
        for chunk in range(1, 4):
            d_c += nt(d_both_ref[chunk, rows, :], w_ref[chunk])
        d_c_ref[rows, :] = d_c
    put_rows(y_ref[0], d_c_ref, (near_sent_ref, near_ref, far_sent_ref, far_ref))


def norm_back(second, d_both, w_gate_up):
    return pl.pallas_call(
        norm_back_kernel,
        out_shape=PARTS,
        in_specs=[SCALAR, WHOLE, WHOLE],
        scratch_shapes=[pltpu.VMEM((1024, D), jnp.float32)],
        out_specs=(WHOLE,) * 4,
        compiler_params=vmem(12),
        cost_estimate=cost(5 << 30, 12 << 20),
        name="norm_back",
    )(second, d_both, w_gate_up)


def gate_grad_kernel(c_ref, d_both_ref, g_ref):
    for chunk in range(4):
        for block in range(4):
            grad = tn(c_ref[:, 256 * block : 256 * block + 256], d_both_ref[chunk]).astype(jnp.bfloat16)
            for part in range(4):
                source = 4 * block + part
                for pair in range(2):
                    for half in range(2):
                        at = 256 * half + 128 * pair
                        first = 128 * source + 64 * half
                        g_ref[2 * chunk + pair, first : first + 64, :] = grad[64 * part : 64 * part + 64, at : at + 128]


def gate_grad(c_low, d_both):
    return pl.pallas_call(
        gate_grad_kernel,
        out_shape=jax.ShapeDtypeStruct((8, 2048, 128), jnp.bfloat16),
        in_specs=[WHOLE] * 2,
        out_specs=WHOLE,
        compiler_params=vmem(12),
        cost_estimate=cost(5 << 30, 10 << 20),
        name="gate_grad",
    )(c_low, d_both)


def out_kernel(
    y_ref, hidden_ref, w_ref, own_ref, pair_ref, last_ref, end_ref,
    near_sent_ref, near_ref, far_sent_ref, far_ref, g_scale_ref,
    branch_ref,
):
    total = jnp.zeros((1, D), jnp.float32)
    for block in range(4):
        rows = slice(256 * block, 256 * block + 256)
        branch = nn(hidden_ref[rows, :], w_ref[...])
        branch_ref[rows, :] = branch
        cot = in_order((own_ref, pair_ref, last_ref, end_ref), block // 2, block % 2, y_ref[0])
        total += jnp.sum(cot.astype(jnp.float32) * branch, axis=0, keepdims=True)
    g_scale_ref[...] = total
    put_rows(y_ref[0], branch_ref, (near_sent_ref, near_ref, far_sent_ref, far_ref))


def out_step(second, hidden, down, cot):
    return pl.pallas_call(
        out_kernel,
        out_shape=PARTS + (jax.ShapeDtypeStruct((1, D), jnp.float32),),
        in_specs=[SCALAR] + [WHOLE] * 6,
        scratch_shapes=[pltpu.VMEM((1024, D), jnp.float32)],
        out_specs=(WHOLE,) * 5,
        compiler_params=vmem(12),
        cost_estimate=cost(3 << 30, 10 << 20),
        name="out",
    )(second, hidden, down, *cot)


def attend_back_kernel(
    y_ref, own_ref, pair_ref, far_ref, last_ref, ring_ref, attn_ref, low_ref, lse_ref, cos_ref, sin_ref,
    length_ref, far_length_ref,
    d_qkv_ref, g_ref,
    d_branch_ref, w_out_ref, key_ref, value_ref,
):
    for place in range(8):
        w_out_ref[:, 128 * place : 128 * place + 128] = ring_ref[place]
    for block in range(4):
        d_branch_ref[256 * block : 256 * block + 256, :] = in_order(
            (own_ref, pair_ref, far_ref, last_ref), block // 2, block % 2, y_ref[0]
        )
    g_out = tn(attn_ref[...], d_branch_ref[...]).astype(jnp.bfloat16)
    for place in range(8):
        g_ref[place] = g_out[:, 128 * place : 128 * place + 128]
    for seq in range(2):
        key_ref[...] = jnp.zeros_like(key_ref)
        value_ref[...] = jnp.zeros_like(value_ref)
        cosine, sine = cos_ref[seq], -sin_ref[seq]
        for block in range(2):
            at = 512 * seq + 256 * block
            rows = slice(at, at + 256)
            span = slice(128 * block, 128 * block + 384)
            keys = slice(512 * seq + 128 * block, 512 * seq + 128 * block + 384)
            mask, keep = mask_of((length_ref, far_length_ref)[seq], block)
            d_attn_all = nt(d_branch_ref[rows, :], w_out_ref[...]).astype(jnp.bfloat16)
            d_attn_all = jnp.where(keep, d_attn_all, jnp.zeros_like(d_attn_all))
            d_queries, d_keys, d_values = [], [], []
            for head in range(4):
                lane = 64 * head
                query = low_ref[rows, lane : lane + 64]
                key = low_ref[keys, OWN + lane : OWN + lane + 64]
                value = low_ref[keys, 2 * OWN + lane : 2 * OWN + lane + 64]
                d_attn = d_attn_all[:, lane : lane + 64]
                masked = jnp.where(mask, nt(query, key) * SCALE, neg_large)
                probs = jnp.exp(masked - lse_ref[rows, head : head + 1])
                d_values.append(tn(probs.astype(jnp.bfloat16), d_attn))
                d_probs = nt(d_attn, value)
                inner = jnp.sum(probs * d_probs, axis=1, keepdims=True)
                d_scores = (probs * (d_probs - inner)).astype(jnp.bfloat16)
                d_queries.append(nn(d_scores, key) * SCALE)
                d_keys.append(tn(d_scores, query) * SCALE)
            part = slice(256 * block, 256 * block + 256)
            d_query = turn(jnp.concatenate(d_queries, axis=1), cosine[part], sine[part])
            d_qkv_ref[rows, :OWN] = d_query.astype(jnp.bfloat16)
            key_ref[span, :] += jnp.concatenate(d_keys, axis=1)
            value_ref[span, :] += jnp.concatenate(d_values, axis=1)
        whole = slice(512 * seq, 512 * seq + 512)
        d_qkv_ref[whole, OWN : 2 * OWN] = turn(key_ref[...], cosine, sine).astype(jnp.bfloat16)
        d_qkv_ref[whole, 2 * OWN :] = value_ref[...].astype(jnp.bfloat16)


def attention_back(me, d_branch, ring, attn, low, lse, cosine, sine, lengths):
    return pl.pallas_call(
        attend_back_kernel,
        out_shape=(
            jax.ShapeDtypeStruct((1024, 3 * OWN), jnp.bfloat16),
            jax.ShapeDtypeStruct((8, OWN, 128), jnp.bfloat16),
        ),
        in_specs=[SCALAR] + [WHOLE] * 10 + [SCALAR] * 2,
        out_specs=(WHOLE, WHOLE),
        scratch_shapes=[
            pltpu.VMEM((1024, D), jnp.bfloat16),
            pltpu.VMEM((OWN, D), jnp.bfloat16),
            pltpu.VMEM((512, OWN), jnp.float32),
            pltpu.VMEM((512, OWN), jnp.float32),
        ],
        compiler_params=vmem(12),
        cost_estimate=cost(12 << 30, 10 << 20),
        name="attend_back",
    )(me, *d_branch, ring, attn, low, lse, cosine, sine, *lengths)


def grad_kernel(
    y_ref, a_ref, w_ref, order_ref, d_qkv_ref, g_out_ref, x_ref, mean_ref, inv_ref, small_ref,
    g_ref, near_sent_ref, near_ref, far_sent_ref, far_ref,
    d_a_ref,
):
    g_gain, g_bias = jnp.zeros((1, D), jnp.float32), jnp.zeros((1, D), jnp.float32)
    for block in range(4):
        rows = slice(256 * block, 256 * block + 256)
        d_a = nt(d_qkv_ref[rows, :], w_ref[...])
        normed = (x_ref[rows, :].astype(jnp.float32) - mean_ref[rows, :]) * inv_ref[rows, :]
        g_gain += jnp.sum(d_a * normed, axis=0, keepdims=True)
        g_bias += jnp.sum(d_a, axis=0, keepdims=True)
        d_a_ref[rows, :] = d_a
    put_rows(y_ref[0], d_a_ref, (near_sent_ref, near_ref, far_sent_ref, far_ref))
    for block in range(8):
        grad = tn(a_ref[:, 128 * block : 128 * block + 128], d_qkv_ref[...]).astype(jnp.bfloat16)
        grad = jnp.concatenate([grad[:, OWN * third : OWN * third + OWN] for third in range(3)], axis=0)
        grad = tn(order_ref[...], grad).astype(jnp.bfloat16)
        for part in range(6):
            chunk = 6 * block + part
            at = 128 * (chunk // 8)
            g_ref[chunk % 8, at : at + 64, :] = grad[64 * part : 64 * part + 64, :128]
            g_ref[chunk % 8, at + 64 : at + 128, :] = grad[64 * part : 64 * part + 64, 128:]
    vectors = [g_gain, g_bias] + [small_ref[k : k + 1, :] for k in range(4)]
    lines = [v[:, 128 * k : 128 * k + 128] for v in vectors for k in range(8)]
    for place in range(8):
        g_ref[place, 768:1024, :] = g_out_ref[place]
        rows = lines[6 * place : 6 * place + 6] + [jnp.zeros((SLAB - 6, 128), jnp.float32)]
        g_ref[place, 1024:, :] = jnp.concatenate(rows, axis=0).astype(jnp.bfloat16)


def grad_step(second, a_low, w_qkv, order, d_qkv, g_out, x_all, mean, inv, small):
    return pl.pallas_call(
        grad_kernel,
        out_shape=(jax.ShapeDtypeStruct((8, 1024 + SLAB, 128), jnp.bfloat16),) + PARTS,
        in_specs=[SCALAR] + [WHOLE] * 9,
        scratch_shapes=[pltpu.VMEM((1024, D), jnp.float32)],
        out_specs=(WHOLE,) * 5,
        compiler_params=vmem(12),
        cost_estimate=cost(8 << 30, 12 << 20),
        name="grad",
    )(second, a_low, w_qkv, order, d_qkv, g_out, x_all, mean, inv, small)


def after(values, *others):
    if isinstance(values, tuple):
        return lax.optimization_barrier(values + others)[: len(values)]
    return lax.optimization_barrier((values,) + others)[0]


def both_ways(ahead, back):
    return lax.optimization_barrier((lax.ppermute(ahead, GROUP, AHEAD), lax.ppermute(back, GROUP, BACK)))


class Gather:
    def __init__(self, block):
        self.blocks = [block]
        self.next = (block, block)
        self.half = (block.shape[0] // 2 + 15) // 16 * 16
        self.count = 0

    def step(self, *waits):
        self.count += 1
        ahead, back = after(self.next, *waits) if waits else self.next
        if self.count == 4:
            ahead, back = ahead[: self.half], back[self.half :]
        self.next = both_ways(ahead, back)
        self.blocks += self.next
        return self.next


class Scatter:
    def __init__(self, blocks, me):
        self.blocks, self.me = blocks, me
        self.rows = blocks.shape[1]
        self.half = (self.rows // 2 + 15) // 16 * 16
        self.count = 0
        self.next = (self.get(4, 0, self.half), self.get(4, self.half))

    def get(self, step, lo=0, hi=None):
        hi = self.rows if hi is None else hi
        at = (ring_place(self.me, step % 8), 0 * self.me + lo, 0 * self.me)
        return lax.dynamic_slice(self.blocks, at, (1, hi - lo, 128))[0]

    def step(self, *waits):
        self.count += 1
        ahead, back = came = both_ways(*(after(self.next, *waits) if waits else self.next))

        def add(moved, own):
            return (moved.astype(jnp.float32) + own.astype(jnp.float32)).astype(jnp.bfloat16)

        if self.count == 1:
            half = self.half
            ahead = jnp.concatenate([add(ahead, self.get(3, 0, half)), self.get(3, half)])
            back = jnp.concatenate([self.get(5, 0, half), add(back, self.get(5, half))])
        elif self.count < 4:
            ahead, back = add(ahead, self.get(4 - self.count)), add(back, self.get(4 + self.count))
        else:
            total = self.get(0).astype(jnp.float32) + ahead.astype(jnp.float32) + back.astype(jnp.float32)
            self.total = total.astype(jnp.bfloat16)
        self.next = (ahead, back)
        return came


def to_pair(rows, *waits):
    rows = after(rows, *waits) if waits else rows
    return rows, lax.ppermute(rows, "y", SWAP)


def to_group(pair, *waits):
    pair = after(tuple(pair), *waits) if waits else pair
    return tuple(pair) + tuple(lax.ppermute(rows, "c", SWAP) for rows in pair)


def half_sum(near_sent, near, far_sent, far):
    sent = near_sent + lax.ppermute(far_sent, "c", SWAP).astype(jnp.float32)
    kept = near + lax.ppermute(far, "c", SWAP).astype(jnp.float32)
    return lax.optimization_barrier((sent.astype(jnp.bfloat16), kept))


def full_sum(sent, kept):
    return kept + lax.ppermute(sent, "y", SWAP).astype(jnp.float32)


def normed_of(rows):
    centered = rows - jnp.mean(rows, axis=-1, keepdims=True)
    inv_scale = lax.rsqrt(jnp.mean(centered * centered, axis=-1, keepdims=True) + eps_norm)
    return centered * inv_scale, inv_scale


def norm_rows_back(out_grad, normed, inv_scale, gain):
    inner = out_grad * gain
    return inv_scale * (
        inner
        - jnp.mean(inner, axis=-1, keepdims=True)
        - normed * jnp.mean(inner * normed, axis=-1, keepdims=True)
    )


def fast_body(frames, cotangent, clip_lengths, params, first_moment, second_moment):
    z, x, c, y = (lax.axis_index(axis) for axis in EVERY)
    device = (((z * 2 + x) * 2 + c) * 2 + y).astype(jnp.int32)
    me = device[None]
    lengths = (clip_lengths, lax.ppermute(clip_lengths, "c", SWAP))
    order = np.zeros((384, 384), np.float32)
    for row in range(384):
        order[(row % 3) * 128 + row // 3, row] = 1.0
    order = jnp.asarray(order, jnp.bfloat16)

    pieces = spread(params, me)
    pieces = lax.all_to_all(pieces, EVERY, split_axis=0, concat_axis=0, tiled=True)
    first_piece, second_piece, third_piece = fix(pieces)
    first, second, third = Gather(first_piece), Gather(second_piece), Gather(third_piece)
    frames_pair = to_pair(frames[0], first_piece)
    came = first.step()
    cot_pair = to_pair(cotangent[0], frames_pair[1])
    lengths = after(lengths, first_piece)
    both = jnp.concatenate(lengths)
    frame = jnp.arange(512, dtype=jnp.int32)
    starts, ends = both[:, :1], both[:, :1] + both[:, 1:]
    position = jnp.where((frame >= starts) & (frame < ends), frame - starts, frame).astype(jnp.float32)
    inverse = jnp.exp(
        jnp.asarray(np.arange(128) % 32, jnp.float32) * (-2.0 * math.log(rope_base) / HEAD_DIM)
    )
    angle = position[:, :, None] * inverse
    cosine = jnp.cos(angle)
    sine = jnp.sin(angle) * jnp.asarray(np.where(np.arange(128) % 64 < 32, -1.0, 1.0), jnp.float32)
    second.step(*first.step(cosine, sine))
    frames_parts = to_group(after(frames_pair, *came))
    first.step(frames_pair[1])
    x_all, mean_one, inv_one = prep(me, frames_parts)
    first.step(x_all)
    ring_qkv, w_own, vectors = join(
        join_first_kernel,
        me,
        first.blocks,
        (
            jax.ShapeDtypeStruct((8, 768, 128), jnp.bfloat16),
            jax.ShapeDtypeStruct((8, OWN, 128), jnp.bfloat16),
            jax.ShapeDtypeStruct((6, D), jnp.float32),
        ),
        "join_first",
        [pltpu.VMEM((8, SLAB, 128), jnp.bfloat16)],
    )

    w_pair = to_pair(w_own)
    x_all, ring_qkv = after((x_all, ring_qkv), *second.next, cot_pair[1])
    a_low, w_qkv, low, attn_own, lse = front(x_all, mean_one, inv_one, ring_qkv, vectors, order, cosine, sine, lengths)
    came = second.step(ring_qkv)
    attn_pair = to_pair(attn_own, *came, w_pair[1])
    w_out = join_out(to_group(w_pair, attn_own))
    came = second.step(attn_own)
    attn_parts = to_group(attn_pair, w_out)
    attn_parts = attn_parts[:2] + after(attn_parts[2:], *came)
    c_low, branch_seq = mix(x_all, attn_parts, w_out, vectors)
    came = third.step(*attn_parts[2:])
    came = second.step(*attn_parts[2:]) + came
    second.blocks[7:] = after(came[:2], c_low)
    w_gate_up = join(
        join_gate_up_kernel,
        me,
        [block.reshape(-1, 2, 64, 128) for block in second.blocks],
        jax.ShapeDtypeStruct((4, 16, 64, 512), jnp.bfloat16),
        "join_gate_up",
        space=HBM,
    ).reshape(4, 1024, 512)
    cot_parts = to_group(cot_pair, c_low)
    gate_up, hidden = gate_step(after(c_low, *came[2:]), w_gate_up)
    came = third.step(c_low)
    g_down, d_mlp = down_grad(me, after(hidden, *came), cot_parts, vectors)
    third.step(hidden)
    third.step(g_down)
    w_down = join(join_down_kernel, me, third.blocks, jax.ShapeDtypeStruct((1024, D), jnp.bfloat16), "join_down", space=HBM)

    down = Scatter(g_down, device)
    d_both = hidden_back(gate_up, d_mlp, w_down)
    came = down.step(*third.next)
    d_both = after(d_both, *came)
    d_c_parts = norm_back(me, d_both, w_gate_up)
    came = down.step(d_both)
    d_c_sent, d_c_kept = half_sum(*after(tuple(d_c_parts), *came))
    g_gate_up = gate_grad(c_low, after(d_both, d_c_sent, d_c_kept))
    came = down.step(d_c_sent)
    gate_grads = Scatter(after(g_gate_up, *came), device)
    down.step()
    gate_grads.step()

    x_own = frames[0].astype(jnp.float32)
    cot_own = cotangent[0].astype(jnp.float32)
    branch_own = jnp.where(y == 0, branch_seq[:256], branch_seq[256:])
    mid_own = x_own + vectors[4] * branch_own
    normed_two, scale_two = normed_of(mid_own)
    d_c_own = full_sum(d_c_sent, d_c_kept)
    d_mid = cot_own + norm_rows_back(d_c_own, normed_two, scale_two, vectors[2])
    d_branch_own = (d_mid * vectors[4]).astype(jnp.bfloat16)
    d_branch_pair = to_pair(d_branch_own)
    hidden = after(hidden, d_branch_own, *down.next, *gate_grads.next)
    *out_parts, g_scale_mlp = out_step(me, hidden, w_down, cot_parts)
    came = gate_grads.step(d_branch_own)
    d_branch = to_group(d_branch_pair, *came, g_scale_mlp)
    out_sent, out_kept = half_sum(*out_parts)
    g_gain_two = jnp.sum(d_c_own * normed_two, axis=0)
    g_bias_two = jnp.sum(d_c_own, axis=0)
    g_scale_attn = jnp.sum(d_mid * branch_own, axis=0)
    small = jnp.concatenate([jnp.stack([g_gain_two, g_bias_two, g_scale_attn]), g_scale_mlp], axis=0)

    d_branch = after(d_branch, small)
    d_qkv, g_out = attention_back(me, d_branch, w_own, attn_own, low, lse, cosine, sine, lengths)
    came = gate_grads.step(*d_branch)
    out_sent = after(out_sent, *d_branch)
    output = (mid_own + vectors[5] * full_sum(out_sent, out_kept)).astype(jnp.bfloat16)
    d_qkv = after(d_qkv, *came)
    g_first, *d_a_parts = grad_step(me, a_low, w_qkv, order, d_qkv, g_out, x_all, mean_one, inv_one, small)
    came = gate_grads.step(d_qkv)
    first_grads = Scatter(after(g_first, *came), device)
    first_grads.step(output)
    d_a_sent, d_a_kept = half_sum(*d_a_parts)
    first_grads.step(d_a_sent)
    first_grads.step()
    normed_one, scale_one = normed_of(x_own)
    d_one = norm_rows_back(full_sum(d_a_sent, d_a_kept), normed_one, scale_one, vectors[0])
    frames_grad = (d_mid + d_one).astype(jnp.bfloat16)
    first_grads.step(frames_grad)
    g_first, g_gate_up, g_down = first_grads.total, gate_grads.total, down.total

    main = jnp.concatenate([g_first[:1024], g_gate_up, g_down]).reshape(32, 128, 128)
    slab = jnp.concatenate([main[1:, :8], main[1:, 64:72]], axis=1)
    slab = jnp.concatenate([slab, g_first[None, 1024:]])
    pieces = jnp.concatenate([main, slab], axis=1)
    pieces = lax.all_to_all(pieces, EVERY, split_axis=0, concat_axis=0, tiled=True)
    params_grad = collect(pieces, me, params.shape[0])
    new_params, new_first, new_second = adam_update(params, params_grad, first_moment, second_moment)
    return (output[None], frames_grad[None], params_grad, new_params, new_first, new_second)


def solution(mesh):
    def run(frames, cotangent, clip_lengths, params, first_moment, second_moment):
        fits = (
            mesh.shape["dp"] == 16
            and mesh.shape["seq"] == 2
            and frames.shape == (16, 512, D)
            and clip_lengths.shape == (16, 2)
        )
        if fits:
            over = Mesh(mesh.devices.reshape(4, 2, 2, 2), EVERY)
            rows, clips, flat = P(("z", "x", "c"), "y", None), P(("z", "x", "c"), None), P(EVERY)
        else:
            over = mesh
            rows, clips, flat = P("dp", "seq", None), P("dp", None), P(("dp", "seq"))
        step = jax.shard_map(
            fast_body if fits else body,
            mesh=over,
            in_specs=(rows, rows, clips, flat, flat, flat),
            out_specs=(rows, rows, flat, flat, flat, flat),
            check_vma=False,
        )
        return step(frames, cotangent, clip_lengths, params, first_moment, second_moment)

    return run
```

```python
import functools
import math

import jax
import jax.numpy as jnp
import numpy as np
from jax import lax
from jax.experimental import pallas as pl
from jax.experimental.pallas import tpu as pltpu
from jax.sharding import Mesh
from jax.sharding import PartitionSpec as P

D = 1024
HEADS = 16
HEAD_DIM = 64
FF = 4096
WINDOW = 128


eps_norm = 1e-05
beta_one = 0.9
beta_two = 0.99
learn_rate = 0.01
decay_rate = 0.1
eps_adam = 1e-08
adam_step = 100.0
neg_large = -1e30
rope_base = 10000.0


def padded(shard, sides, width):
    for axis, dim in sides:
        size, length = (lax.axis_size(axis), shard.shape[dim])
        up = [(i, (i + 1) % size) for i in range(size - 1)]
        down = [(j, i) for i, j in up]
        last = lax.slice_in_dim(shard, length - width, length, axis=dim)
        first = lax.slice_in_dim(shard, 0, width, axis=dim)
        before = lax.ppermute(last, axis, up)
        after = lax.ppermute(first, axis, down)
        shard = jnp.concatenate([before, shard, after], axis=dim)
    return shard


def unpack(flat_params):
    end_qkv = D * 3 * D
    end_out = end_qkv + D * D
    end_mlp = end_out + D * 2 * FF
    end_down = end_mlp + FF * D
    w_qkv = flat_params[:end_qkv].reshape(D, 3 * D)
    w_out = flat_params[end_qkv:end_out].reshape(D, D)
    w_gate_up = flat_params[end_out:end_mlp].reshape(D, 2 * FF)
    w_down = flat_params[end_mlp:end_down].reshape(FF, D)
    vectors = flat_params[end_down:].reshape(6, D).astype(jnp.float32)
    return (w_qkv, w_out, w_gate_up, w_down, vectors)


def clip_info(lengths, glob):
    clip_ends = jnp.cumsum(lengths, axis=1, dtype=jnp.int32)
    clip_starts = clip_ends - lengths
    after_end = (glob[None, :, None] >= clip_ends[:, None, :]).astype(jnp.int32)
    segment = jnp.sum(after_end, axis=2, dtype=jnp.int32)
    onehot = segment[:, :, None] == jnp.arange(lengths.shape[1], dtype=jnp.int32)[None, None, :]
    clip_begin = jnp.sum(jnp.where(onehot, clip_starts[:, None, :], 0), axis=2, dtype=jnp.int32)
    return (segment, (glob[None, :] - clip_begin).astype(jnp.float32))


def rotate(values, position, sign):
    half_dim = values.shape[-1] // 2
    inverse = jnp.exp(
        jnp.arange(half_dim, dtype=jnp.float32) * (-2.0 * math.log(rope_base) / HEAD_DIM)
    )
    rot_angle = position[:, :, None, None] * inverse
    cosine = jnp.cos(rot_angle)
    rot_sine = sign * jnp.sin(rot_angle)
    low_half = values[..., :half_dim]
    high_half = values[..., half_dim:]
    return jnp.concatenate(
        [low_half * cosine - high_half * rot_sine, high_half * cosine + low_half * rot_sine],
        axis=-1,
    )


def norm_forward(row_vals, norm_gain, norm_bias):
    centered = row_vals - jnp.mean(row_vals, axis=-1, keepdims=True)
    inv_scale = lax.rsqrt(jnp.mean(centered * centered, axis=-1, keepdims=True) + eps_norm)
    normed = centered * inv_scale
    return (normed * norm_gain + norm_bias, normed, inv_scale)


def norm_backward(out_grad, normed, inv_scale, norm_gain):
    d_gain = jnp.sum(out_grad * normed, axis=0)
    d_bias = jnp.sum(out_grad, axis=0)
    inner_grad = out_grad * norm_gain
    d_rows = inv_scale * (
        inner_grad
        - jnp.mean(inner_grad, axis=-1, keepdims=True)
        - normed * jnp.mean(inner_grad * normed, axis=-1, keepdims=True)
    )
    return (d_rows, d_gain, d_bias)


def scores_of(query_rows, key_rows, window_mask):
    raw_scores = jnp.einsum(
        "qhd,khd->hqk", query_rows, key_rows, preferred_element_type=jnp.float32
    ) * HEAD_DIM ** (-0.5)
    return jnp.where(window_mask[None], raw_scores, neg_large)


def attend(query_rows, key_rows, value_rows, window_mask):
    masked = scores_of(query_rows, key_rows, window_mask)
    row_max = jnp.max(masked, axis=-1, keepdims=True)
    row_total = jnp.log(jnp.sum(jnp.exp(masked - row_max), axis=-1, keepdims=True)) + row_max
    prob_low = jnp.exp(masked - row_total).astype(jnp.bfloat16)
    attn_rows = jnp.einsum("hqk,khd->qhd", prob_low, value_rows, preferred_element_type=jnp.float32)
    return (attn_rows, row_total[..., 0])


def attend_back(query_rows, key_rows, value_rows, window_mask, row_total, d_attn):
    masked = scores_of(query_rows, key_rows, window_mask)
    prob_rows = jnp.exp(masked - row_total[..., None])
    prob_low = prob_rows.astype(jnp.bfloat16)
    d_values = jnp.einsum("hqk,qhd->khd", prob_low, d_attn, preferred_element_type=jnp.float32)
    d_probs = jnp.einsum("qhd,khd->hqk", d_attn, value_rows, preferred_element_type=jnp.float32)
    inner_sum = jnp.sum(prob_rows * d_probs, axis=-1, keepdims=True)
    d_scores = (prob_rows * (d_probs - inner_sum)).astype(jnp.bfloat16)
    d_query = jnp.einsum(
        "hqk,khd->qhd", d_scores, key_rows, preferred_element_type=jnp.float32
    ) * HEAD_DIM ** (-0.5)
    d_keys = jnp.einsum(
        "hqk,qhd->khd", d_scores, query_rows, preferred_element_type=jnp.float32
    ) * HEAD_DIM ** (-0.5)
    return (d_query, d_keys, d_values)


def adam_update(flat_params, grads, first_moment, second_moment):
    new_first = beta_one * first_moment + (1.0 - beta_one) * grads
    new_second = beta_two * second_moment + (1.0 - beta_two) * grads * grads
    corrected_first = new_first / (1.0 - beta_one**adam_step)
    corrected_second = new_second / (1.0 - beta_two**adam_step)
    step_size = corrected_first / (jnp.sqrt(corrected_second) + eps_adam) + decay_rate * flat_params
    return (flat_params - learn_rate * step_size, new_first, new_second)


def body(frames, cotangent, clip_lengths, params, first_moment, second_moment):
    seq_count, frame_span, model_width = frames.shape
    row_count = seq_count * frame_span
    window_reach = WINDOW
    key_count = frame_span + 2 * window_reach
    head_count = HEADS
    head_size = model_width // head_count
    group_size = 4
    seq_len = lax.axis_size("seq") * frame_span
    seq_start = lax.axis_index("seq") * frame_span
    glob_rows = seq_start + jnp.arange(frame_span, dtype=jnp.int32)
    glob_keys = seq_start - window_reach + jnp.arange(key_count, dtype=jnp.int32)
    seg_rows, pos_rows = clip_info(clip_lengths, glob_rows)
    seg_keys, unused = clip_info(clip_lengths, glob_keys)
    inside = (glob_keys >= 0) & (glob_keys < seq_len)
    near_band = (
        jnp.abs(jnp.arange(frame_span)[:, None] + window_reach - jnp.arange(key_count)[None, :])
        < window_reach
    )
    window_mask = (
        (seg_rows[:, :, None] == seg_keys[:, None, :]) & inside[None, None, :] & near_band[None]
    )
    keep_rows = seg_rows != clip_lengths.shape[1] - 1
    shards = params.astype(jnp.bfloat16)
    gathered = lax.all_gather(shards, ("dp", "seq"), axis=0, tiled=True)
    w_qkv, w_out, w_gate_up, w_down, vectors = unpack(gathered)
    x_rows = frames.reshape(row_count, model_width).astype(jnp.float32)
    norm_one, normed_one, scale_one = norm_forward(x_rows, vectors[0], vectors[1])
    a_low = norm_one.astype(jnp.bfloat16)
    qkv = jnp.dot(a_low, w_qkv, preferred_element_type=jnp.float32).reshape(
        seq_count, frame_span, 3, head_count, head_size
    )
    query_low = rotate(qkv[:, :, 0], pos_rows, 1.0).astype(jnp.bfloat16)
    key_low = rotate(qkv[:, :, 1], pos_rows, 1.0).astype(jnp.bfloat16)
    value_low = qkv[:, :, 2].astype(jnp.bfloat16)
    key_value = jnp.concatenate([key_low, value_low], axis=2).reshape(
        seq_count, frame_span, 2 * model_width
    )
    wide_rows = padded(key_value, (("seq", 1),), window_reach)
    wide_rows = wide_rows.reshape(seq_count, key_count, 2, head_count, head_size)
    key_wide = wide_rows[:, :, 0]
    value_wide = wide_rows[:, :, 1]
    seq_index = 0
    out_parts = []
    total_parts = []
    for head_start in range(0, head_count, group_size):
        head_end = head_start + group_size
        attn_rows, row_total = attend(
            query_low[seq_index, :, head_start:head_end],
            key_wide[seq_index, :, head_start:head_end],
            value_wide[seq_index, :, head_start:head_end],
            window_mask[seq_index],
        )
        out_parts.append(attn_rows)
        total_parts.append(row_total)
    attn_list = [jnp.concatenate(out_parts, axis=1)]
    total_list = [total_parts]
    attn_all = jnp.where(keep_rows[:, :, None, None], jnp.stack(attn_list), 0.0)
    attn_low = attn_all.reshape(row_count, model_width).astype(jnp.bfloat16)
    branch_attn = jnp.dot(attn_low, w_out, preferred_element_type=jnp.float32)
    mid_rows = x_rows + vectors[4] * branch_attn
    norm_two, normed_two, scale_two = norm_forward(mid_rows, vectors[2], vectors[3])
    c_low = norm_two.astype(jnp.bfloat16)
    gate_up = jnp.dot(c_low, w_gate_up, preferred_element_type=jnp.float32)
    gate = gate_up[:, :FF]
    up_rows = gate_up[:, FF:]
    gate_sig = jax.nn.sigmoid(gate)
    hidden = (gate * gate_sig * up_rows).astype(jnp.bfloat16)
    branch_mlp = jnp.dot(hidden, w_down, preferred_element_type=jnp.float32)
    output = (
        (mid_rows + vectors[5] * branch_mlp)
        .astype(jnp.bfloat16)
        .reshape(seq_count, frame_span, model_width)
    )
    gathered = lax.all_gather(shards, ("dp", "seq"), axis=0, tiled=True)
    w_qkv, w_out, w_gate_up, w_down, vectors = unpack(gathered)
    d_rows = cotangent.reshape(row_count, model_width).astype(jnp.float32)
    g_scale_mlp = jnp.sum(d_rows * branch_mlp, axis=0)
    d_mlp = (d_rows * vectors[5]).astype(jnp.bfloat16)
    g_down = jnp.dot(hidden.T, d_mlp, preferred_element_type=jnp.float32)
    d_hidden = jnp.dot(d_mlp, w_down.T, preferred_element_type=jnp.float32)
    d_gate = d_hidden * up_rows * gate_sig * (1.0 + gate * (1.0 - gate_sig))
    d_up = d_hidden * gate * gate_sig
    d_gate_up = jnp.concatenate([d_gate, d_up], axis=1).astype(jnp.bfloat16)
    g_gate_up = jnp.dot(c_low.T, d_gate_up, preferred_element_type=jnp.float32)
    d_two = jnp.dot(d_gate_up, w_gate_up.T, preferred_element_type=jnp.float32)
    d_norm_two, g_gain_two, g_bias_two = norm_backward(d_two, normed_two, scale_two, vectors[2])
    d_mid = d_rows + d_norm_two
    g_scale_attn = jnp.sum(d_mid * branch_attn, axis=0)
    d_branch = (d_mid * vectors[4]).astype(jnp.bfloat16)
    g_out = jnp.dot(attn_low.T, d_branch, preferred_element_type=jnp.float32)
    d_attn_low = jnp.dot(d_branch, w_out.T, preferred_element_type=jnp.float32).astype(jnp.bfloat16)
    d_attn = jnp.where(
        keep_rows[:, :, None, None],
        d_attn_low.reshape(seq_count, frame_span, head_count, head_size),
        jnp.zeros((), jnp.bfloat16),
    )
    seq_index = 0
    query_parts = []
    key_parts = []
    value_parts = []
    for number, head_start in enumerate(range(0, head_count, group_size)):
        head_end = head_start + group_size
        d_query, d_keys, d_values = attend_back(
            query_low[seq_index, :, head_start:head_end],
            key_wide[seq_index, :, head_start:head_end],
            value_wide[seq_index, :, head_start:head_end],
            window_mask[seq_index],
            total_list[seq_index][number],
            d_attn[seq_index, :, head_start:head_end],
        )
        query_parts.append(d_query)
        key_parts.append(d_keys)
        value_parts.append(d_values)
    query_grads = [jnp.concatenate(query_parts, axis=1)]
    key_grads = [jnp.concatenate(key_parts, axis=1)]
    value_grads = [jnp.concatenate(value_parts, axis=1)]
    d_query_all = jnp.stack(query_grads)
    d_pair = jnp.concatenate([jnp.stack(key_grads), jnp.stack(value_grads)], axis=2).reshape(
        seq_count, key_count, 2 * model_width
    )
    rim_rows = jnp.concatenate(
        [d_pair[:, :window_reach], d_pair[:, window_reach + frame_span :]], axis=1
    )
    taken_rows = padded(rim_rows.astype(jnp.bfloat16), (("seq", 1),), window_reach).astype(
        rim_rows.dtype
    )
    own_rows = d_pair[:, window_reach : window_reach + frame_span]
    own_rows = own_rows + jnp.pad(
        taken_rows[:, :window_reach], ((0, 0), (0, frame_span - window_reach), (0, 0))
    )
    own_rows = own_rows + jnp.pad(
        taken_rows[:, 3 * window_reach :], ((0, 0), (frame_span - window_reach, 0), (0, 0))
    )
    own_rows = own_rows.reshape(seq_count, frame_span, 2, head_count, head_size)
    d_qkv = jnp.stack(
        [
            rotate(d_query_all, pos_rows, -1.0),
            rotate(own_rows[:, :, 0], pos_rows, -1.0),
            own_rows[:, :, 1],
        ],
        axis=2,
    )
    d_qkv = d_qkv.reshape(row_count, 3 * model_width).astype(jnp.bfloat16)
    g_qkv = jnp.dot(a_low.T, d_qkv, preferred_element_type=jnp.float32)
    d_one = jnp.dot(d_qkv, w_qkv.T, preferred_element_type=jnp.float32)
    d_norm_one, g_gain_one, g_bias_one = norm_backward(d_one, normed_one, scale_one, vectors[0])
    frames_grad = (
        (d_mid + d_norm_one).astype(jnp.bfloat16).reshape(seq_count, frame_span, model_width)
    )
    small_grads = jnp.stack(
        [g_gain_one, g_bias_one, g_gain_two, g_bias_two, g_scale_attn, g_scale_mlp]
    )
    whole_grad = jnp.concatenate(
        [
            g_qkv.reshape(-1),
            g_out.reshape(-1),
            g_gate_up.reshape(-1),
            g_down.reshape(-1),
            small_grads.reshape(-1),
        ]
    )
    params_grad = lax.psum_scatter(whole_grad, ("dp", "seq"), scatter_dimension=0, tiled=True)
    new_params, new_first, new_second = adam_update(
        params, params_grad, first_moment, second_moment
    )
    return (output, frames_grad, params_grad, new_params, new_first, new_second)


EVERY = ("z", "x", "c", "y")
GROUP = ("z", "x")
RING = ((0, 0), (1, 0), (2, 0), (3, 0), (3, 1), (2, 1), (1, 1), (0, 1))
PLACES = tuple(2 * z + x for z, x in RING)
AHEAD = tuple((PLACES[i], PLACES[(i + 1) % 8]) for i in range(8))
BACK = tuple((b, a) for a, b in AHEAD)
SWAP = ((0, 1), (1, 0))
LINES = 4096
TAIL = 64
SLAB = 16
ROWS = 128 + SLAB
OWN = 256
SCALE = HEAD_DIM ** (-0.5)
SCALAR = pl.BlockSpec(memory_space=pltpu.SMEM)
WHOLE = pl.BlockSpec(memory_space=pltpu.VMEM)
HBM = pl.BlockSpec(memory_space=pltpu.HBM)
ANY = pl.BlockSpec(memory_space=pl.ANY)


def vmem(mebibytes):
    return pltpu.CompilerParams(vmem_limit_bytes=mebibytes << 20)


def ring_place(me, step):
    z, x = lax.div(me, 8), lax.rem(lax.div(me, 4), 2)
    at = lax.rem(jnp.where(x == 0, z, 7 - z) + step, 8)
    return jnp.where(at < 4, 2 * at, 15 - 2 * at)


def kind_of(shard):
    if shard < 6:
        return 0
    return 2 if 8 <= shard < 24 else 1


def piece_lines(kind, dest):
    place, member = divmod(dest, 4)
    if kind == 0:
        return [(512 * place + member, 8), (512 * place + 4 + member, 8)]
    if kind == 1:
        return [(1024 * member + place, 8), (1024 * member + 512 + place, 8)]
    return [(dest, 64), (32 + dest, 64)]


def tail_lines(kind, dest):
    place, member = divmod(dest, 4)
    if kind == 0:
        return [(0, 6, member, 8), (8, 6, 4 + member, 8)] if place == 0 else []
    if kind == 1:
        return [(0, 6, place, 8)] if member == 0 else []
    return [(0, 1, dest, 1)] + ([(8, 1, 32 + dest, 1)] if dest < 16 else [])


def is_kind(shard, kind):
    if kind == 0:
        return shard < 6
    gate_up = (shard >= 8) & (shard < 24)
    if kind == 2:
        return gate_up
    return (shard >= 6) & jnp.logical_not(gate_up) & (shard < 32)


def spread_kernel(me_ref, flat_ref, out_ref, lines_ref):
    me = me_ref[0]
    odd = lax.rem(me, 2) == 1
    start = 48 - (3 * me + 1) // 2
    lane = lax.broadcasted_iota(jnp.int32, (64, 128), 1)

    def shift(step, carry):
        here = flat_ref[pl.ds(start + step * 64, 64), :]
        after = flat_ref[pl.ds(start + step * 64 + 1, 64), :]
        mixed = jnp.where(lane < 64, pltpu.roll(here, 64, 1), pltpu.roll(after, 64, 1))
        lines_ref[pl.ds(pl.multiple_of(step * 64, 64), 64), :] = jnp.where(odd, mixed, here)
        return carry

    lax.fori_loop(0, (LINES + TAIL) // 64, shift, 0, unroll=5)
    for kind in range(3):

        @pl.when(is_kind(me, kind))
        def _(kind=kind):
            for dest in range(32):
                for half, (first, stride) in enumerate(piece_lines(kind, dest)):
                    rows = lines_ref[pl.ds(first, 64, stride), :]
                    out_ref[dest, 64 * half : 64 * half + 64, :] = rows.astype(jnp.bfloat16)

    def slab_of(parts):
        slab = [jnp.zeros((8, 128), jnp.float32)] * 2
        row = lax.broadcasted_iota(jnp.int32, (8, 128), 0)
        for at, count, first, stride in parts:
            if count == 1:
                value = jnp.broadcast_to(lines_ref[LINES + first : LINES + first + 1, :], (8, 128))
            else:
                value = lines_ref[pl.ds(LINES + first, 8, stride), :]
            slab[at // 8] = jnp.where(row < count, value, 0.0)
        return jnp.concatenate(slab, axis=0).astype(jnp.bfloat16)

    for kind in range(3):

        @pl.when(is_kind(me + 1, kind))
        def _(kind=kind):
            for dest in range(32):
                out_ref[dest, 128:ROWS, :] = slab_of(tail_lines(kind, dest))

    @pl.when(me == 31)
    def _():
        for dest in range(32):
            out_ref[dest, 128:ROWS, :] = slab_of([(0, 6, 6 * (dest // 4), 1)])


def spread(params, me):
    flat = jnp.pad(params, (48 * 128, 4224 * 128 - 48 * 128 - params.shape[0])).reshape(4224, 128)
    return pl.pallas_call(
        spread_kernel,
        out_shape=jax.ShapeDtypeStruct((32, ROWS, 128), jnp.bfloat16),
        in_specs=[
            pl.BlockSpec(memory_space=pltpu.SMEM),
            pl.BlockSpec(memory_space=pltpu.VMEM),
        ],
        out_specs=pl.BlockSpec(memory_space=pltpu.VMEM),
        scratch_shapes=[pltpu.VMEM((LINES + TAIL, 128), jnp.float32)],
        compiler_params=vmem(12),
        name="spread",
    )(me, flat)


def collect_kernel(me_ref, piece_ref, out_ref, lines_ref):
    me = me_ref[0]
    odd = lax.rem(me, 2) == 1
    lines_ref[LINES:, :] = jnp.zeros((TAIL, 128), jnp.float32)
    for kind in range(3):

        @pl.when(is_kind(me, kind))
        def _(kind=kind):
            for dest in range(32):
                for half, (first, stride) in enumerate(piece_lines(kind, dest)):
                    rows = piece_ref[dest, 64 * half : 64 * half + 64, :].astype(jnp.float32)
                    lines_ref[pl.ds(first, 64, stride), :] = rows

    for kind in range(3):

        @pl.when(is_kind(me + 1, kind))
        def _(kind=kind):
            for dest in range(32):
                slab = piece_ref[dest, 128:ROWS, :].astype(jnp.float32)
                for at, count, first, stride in tail_lines(kind, dest):
                    for k in range(count):
                        line = LINES + first + k * stride
                        lines_ref[line : line + 1, :] = slab[at + k : at + k + 1, :]

    @pl.when(me == 31)
    def _():
        for place in range(8):
            total = piece_ref[4 * place, 128:ROWS, :].astype(jnp.float32)
            for member in range(1, 4):
                total = total + piece_ref[4 * place + member, 128:ROWS, :].astype(jnp.float32)
            for k in range(6):
                line = LINES + 6 * place + k
                lines_ref[line : line + 1, :] = total[k : k + 1, :]

    start = (3 * me) // 2
    lane = lax.broadcasted_iota(jnp.int32, (24, 128), 1)

    def shift(step, carry):
        here = lines_ref[pl.ds(start + step * 24, 24), :]
        after = lines_ref[pl.ds(start + step * 24 + 1, 24), :]
        mixed = jnp.where(lane < 64, pltpu.roll(here, 64, 1), pltpu.roll(after, 64, 1))
        out_ref[pl.ds(pl.multiple_of(step * 24, 8), 24), :] = jnp.where(odd, mixed, here)
        return carry

    lax.fori_loop(0, 4104 // 24, shift, 0, unroll=9)


def collect(pieces, me, count):
    lines = pl.pallas_call(
        collect_kernel,
        out_shape=jax.ShapeDtypeStruct((4104, 128), jnp.float32),
        in_specs=[
            pl.BlockSpec(memory_space=pltpu.SMEM),
            pl.BlockSpec(memory_space=pltpu.VMEM),
        ],
        out_specs=pl.BlockSpec(memory_space=pltpu.VMEM),
        scratch_shapes=[pltpu.VMEM((LINES + TAIL, 128), jnp.float32)],
        compiler_params=vmem(12),
        name="collect",
    )(me, pieces)
    return lines.reshape(-1)[:count]


def swap_halves(rows):
    lane = lax.broadcasted_iota(jnp.int32, rows.shape, 1)
    return jnp.where(
        lax.rem(lane, 64) < 32, pltpu.roll(rows, 96, 1), pltpu.roll(rows, 32, 1)
    )


def turn(rows, cosine, signed_sine):
    parts = []
    for at in range(0, rows.shape[1], 128):
        part = rows[:, at : at + 128]
        parts.append(part * cosine + swap_halves(part) * signed_sine)
    return jnp.concatenate(parts, axis=1)


def clip_of(length_ref, frame):
    first = length_ref[0, 0]
    return (frame >= first).astype(jnp.int32) + (frame >= first + length_ref[0, 1]).astype(jnp.int32)


def mask_of(length_ref, block):
    row = lax.broadcasted_iota(jnp.int32, (256, 384), 0) + 256 * block
    key = lax.broadcasted_iota(jnp.int32, (256, 384), 1) + 128 * block
    own = clip_of(length_ref, lax.broadcasted_iota(jnp.int32, (256, 1), 0) + 256 * block)
    others = clip_of(length_ref, lax.broadcasted_iota(jnp.int32, (1, 384), 1) + 128 * block)
    return (jnp.abs(row - key) < WINDOW) & (own == others), own != 1


def nt(left, right):
    return lax.dot_general(left, right, (((1,), (1,)), ((), ())), preferred_element_type=jnp.float32)


def tn(left, right):
    return lax.dot_general(left, right, (((0,), (0,)), ((), ())), preferred_element_type=jnp.float32)


def nn(left, right):
    return jnp.dot(left, right, preferred_element_type=jnp.float32)


def cost(flops, moved):
    return pl.CostEstimate(flops=flops, bytes_accessed=moved, transcendentals=0)


def fix_kernel(piece_ref, first_ref, second_ref, third_ref):
    for source in range(32):
        out, at = (first_ref, source) if source < 8 else (second_ref, source - 8) if source < 24 else (third_ref, source - 24)
        out[128 * at : 128 * at + 128, :] = piece_ref[source, :128, :]
        if source:
            slab = piece_ref[source - 1, 128:ROWS, :].astype(jnp.float32)
            for half in range(2):
                rows = piece_ref[source, 64 * half : 64 * half + 16, :].astype(jnp.float32)
                extra = jnp.concatenate([slab[8 * half : 8 * half + 8], jnp.zeros((8, 128), jnp.float32)])
                out[128 * at + 64 * half : 128 * at + 64 * half + 16, :] = (rows + extra).astype(jnp.bfloat16)
    first_ref[1024:, :] = piece_ref[31, 128:ROWS, :]


def fix(pieces):
    return pl.pallas_call(
        fix_kernel,
        out_shape=tuple(jax.ShapeDtypeStruct((n, 128), jnp.bfloat16) for n in (1024 + SLAB, 2048, 1024)),
        in_specs=[WHOLE],
        out_specs=(WHOLE,) * 3,
        compiler_params=vmem(12),
        cost_estimate=cost(0, 1 << 22),
        name="fix",
    )(pieces)


def in_order(refs, seq, half, second):
    mine, other = refs[2 * seq], refs[2 * seq + 1]
    return jnp.where(lax.rem(second, 2) == half, mine[...], other[...])


def ring_parts(me_ref, refs):
    me = me_ref[0]
    parts = [(ring_place(me, 0), refs[0], None)]
    for step in range(1, 4):
        parts += [(ring_place(me, 8 - step), refs[2 * step - 1], None), (ring_place(me, step), refs[2 * step], None)]
    half = refs[7].shape[0]
    last = ring_place(me, 4)
    return parts + [(last, refs[7], (0, half)), (last, refs[8], (half, half + refs[8].shape[0]))]


def copy_all(pairs, done):
    copies = [pltpu.make_async_copy(source, target, done.at[k]) for k, (source, target) in enumerate(pairs)]
    for copy in copies:
        copy.start()
    for copy in copies:
        copy.wait()


def join_first_kernel(me_ref, *refs):
    blocks, (qkv_ref, out_ref, vec_ref, lines_ref, _) = refs[:9], refs[9:]
    for place, block, rows in ring_parts(me_ref, blocks):
        lo, hi = rows or (0, 1024 + SLAB)
        for at, end, ref in ((0, 768, qkv_ref), (768, 1024, out_ref), (1024, 1024 + SLAB, lines_ref)):
            first, last = max(at, lo), min(end, hi)
            if first < last:
                ref[place, first - at : last - at, :] = block[first - lo : last - lo, :]
    slabs = [lines_ref[place].astype(jnp.float32) for place in range(8)]
    for v in range(6):
        for k in range(8):
            line = 8 * v + k
            vec_ref[v : v + 1, 128 * k : 128 * k + 128] = slabs[line // 6][line % 6 : line % 6 + 1]


def join_gate_up_kernel(me_ref, *refs):
    blocks, (out_ref, done) = refs[:9], refs[9:]
    pairs = []
    for place, block, rows in ring_parts(me_ref, blocks):
        lo, hi = rows or (0, 16)
        for half in range(2):
            at = pl.multiple_of(256 * half + 128 * lax.rem(place, 2), 128)
            pairs.append((block.at[:, half], out_ref.at[lax.div(place, 2), lo:hi, :, pl.ds(at, 128)]))
    copy_all(pairs, done)


def join_down_kernel(me_ref, *refs):
    blocks, (out_ref, done) = refs[:9], refs[9:]
    pairs = []
    for place, block, rows in ring_parts(me_ref, blocks):
        lo, hi = rows or (0, 1024)
        pairs.append((block, out_ref.at[lo:hi, pl.ds(pl.multiple_of(128 * place, 128), 128)]))
    copy_all(pairs, done)


def join_out_kernel(*refs):
    w_ref = refs[4]
    for k in range(4):
        for place in range(8):
            w_ref[256 * k : 256 * k + 256, 128 * place : 128 * place + 128] = refs[k][place]


def join_out(parts):
    return pl.pallas_call(
        join_out_kernel,
        out_shape=jax.ShapeDtypeStruct((D, D), jnp.bfloat16),
        in_specs=[WHOLE] * 4,
        out_specs=WHOLE,
        compiler_params=vmem(12),
        cost_estimate=cost(0, 4 << 20),
        name="join_out",
    )(*parts)


def join(kernel, me, blocks, out_shape, name, scratch=(), space=WHOLE):
    if space is HBM:
        blocks = [pltpu.with_memory_space_constraint(block, pltpu.HBM) for block in blocks]
    return pl.pallas_call(
        kernel,
        out_shape=out_shape,
        in_specs=[SCALAR] + [space] * 9,
        out_specs=jax.tree.map(lambda _: WHOLE, out_shape),
        scratch_shapes=list(scratch) + [pltpu.SemaphoreType.DMA((32,))],
        compiler_params=vmem(12),
        cost_estimate=cost(0, 4 << 20),
        name=name,
    )(me, *blocks)


def prep_kernel(y_ref, own_ref, pair_ref, far_ref, last_ref, x_ref, mean_ref, inv_ref):
    for block in range(4):
        rows = slice(256 * block, 256 * block + 256)
        x_low = in_order((own_ref, pair_ref, far_ref, last_ref), block // 2, block % 2, y_ref[0])
        x_ref[rows, :] = x_low
        x_rows = x_low.astype(jnp.float32)
        mean = jnp.mean(x_rows, axis=1, keepdims=True)
        centered = x_rows - mean
        mean_ref[rows, :] = mean
        inv_ref[rows, :] = lax.rsqrt(jnp.mean(centered * centered, axis=1, keepdims=True) + eps_norm)


def prep(second, rows):
    return pl.pallas_call(
        prep_kernel,
        out_shape=(
            jax.ShapeDtypeStruct((1024, D), jnp.bfloat16),
            jax.ShapeDtypeStruct((1024, 1), jnp.float32),
            jax.ShapeDtypeStruct((1024, 1), jnp.float32),
        ),
        in_specs=[SCALAR] + [WHOLE] * 4,
        out_specs=(WHOLE,) * 3,
        compiler_params=vmem(12),
        cost_estimate=cost(1 << 24, 5 << 20),
        name="prep",
    )(second, *rows)


def front_kernel(
    x_ref, mean_ref, inv_ref, ring_ref, vec_ref, order_ref, cos_ref, sin_ref, length_ref, far_length_ref,
    a_out, w_out, low_out, attn_ref, lse_out,
    a_ref, w_ref, low_ref, lse_ref, done,
):
    copies = [
        pltpu.make_async_copy(ref, out, done.at[k])
        for k, (ref, out) in enumerate(((w_ref, w_out), (a_ref, a_out), (low_ref, low_out), (lse_ref, lse_out)))
    ]
    gain, bias = vec_ref[0:1, :], vec_ref[1:2, :]
    for block in range(8):
        parts = []
        for chunk in range(6 * block, 6 * block + 6):
            at = 128 * (chunk // 8)
            parts.append(
                jnp.concatenate(
                    [ring_ref[chunk % 8, at : at + 64, :], ring_ref[chunk % 8, at + 64 : at + 128, :]], axis=1
                )
            )
        rows = nn(order_ref[...], jnp.concatenate(parts, axis=0)).astype(jnp.bfloat16)
        for third in range(3):
            w_ref[128 * block : 128 * block + 128, OWN * third : OWN * third + OWN] = rows[
                128 * third : 128 * third + 128
            ]
    copies[0].start()
    for block in range(4):
        rows = slice(256 * block, 256 * block + 256)
        seq, at = block // 2, 256 * (block % 2)
        normed = (x_ref[rows, :].astype(jnp.float32) - mean_ref[rows, :]) * inv_ref[rows, :]
        a_low = (normed * gain + bias).astype(jnp.bfloat16)
        a_ref[rows, :] = a_low
        qkv = nn(a_low, w_ref[...])
        cosine, sine = cos_ref[seq, at : at + 256, :], sin_ref[seq, at : at + 256, :]
        low_ref[rows, : 2 * OWN] = turn(qkv[:, : 2 * OWN], cosine, sine).astype(jnp.bfloat16)
        low_ref[rows, 2 * OWN :] = qkv[:, 2 * OWN :].astype(jnp.bfloat16)
    copies[1].start()
    copies[2].start()
    for seq in range(2):
        for block in range(2):
            at = 512 * seq + 256 * block
            rows = slice(at, at + 256)
            keys = slice(512 * seq + 128 * block, 512 * seq + 128 * block + 384)
            mask, keep = mask_of((length_ref, far_length_ref)[seq], block)
            heads, sums = [], []
            for head in range(4):
                lane = 64 * head
                query = low_ref[rows, lane : lane + 64]
                key = low_ref[keys, OWN + lane : OWN + lane + 64]
                value = low_ref[keys, 2 * OWN + lane : 2 * OWN + lane + 64]
                masked = jnp.where(mask, nt(query, key) * SCALE, neg_large)
                top = jnp.max(masked, axis=1, keepdims=True)
                weight = jnp.exp(masked - top)
                total = jnp.sum(weight, axis=1, keepdims=True)
                probs = (weight * (1.0 / total)).astype(jnp.bfloat16)
                heads.append(jnp.where(keep, nn(probs, value), 0.0))
                sums.append(top + jnp.log(total))
            attn_ref[rows, :] = jnp.concatenate(heads, axis=1).astype(jnp.bfloat16)
            lse_ref[rows, :] = jnp.concatenate(sums, axis=1)
    copies[3].start()
    for copy in copies:
        copy.wait()


def front(x_all, mean, inv, ring, vectors, order, cosine, sine, lengths):
    return pl.pallas_call(
        front_kernel,
        out_shape=(
            pltpu.HBM((1024, D), jnp.bfloat16),
            pltpu.HBM((D, 3 * OWN), jnp.bfloat16),
            pltpu.HBM((1024, 3 * OWN), jnp.bfloat16),
            jax.ShapeDtypeStruct((1024, OWN), jnp.bfloat16),
            pltpu.HBM((1024, 4), jnp.float32),
        ),
        in_specs=[WHOLE] * 8 + [SCALAR] * 2,
        out_specs=(HBM, HBM, HBM, WHOLE, HBM),
        scratch_shapes=[
            pltpu.VMEM((1024, D), jnp.bfloat16),
            pltpu.VMEM((D, 3 * OWN), jnp.bfloat16),
            pltpu.VMEM((1024, 3 * OWN), jnp.bfloat16),
            pltpu.VMEM((1024, 4), jnp.float32),
            pltpu.SemaphoreType.DMA((4,)),
        ],
        compiler_params=vmem(14),
        cost_estimate=cost(12 << 30, 8 << 20),
        name="front",
    )(x_all, mean, inv, ring, vectors, order, cosine, sine, *lengths)


def mix_kernel(x_ref, own_ref, pair_ref, far_ref, last_ref, w_ref, vec_ref, c_ref, branch_ref):
    for block in range(4):
        rows = slice(256 * block, 256 * block + 256)
        other = (block + 2) % 4
        far = slice(256 * other, 256 * other + 256)
        attn = jnp.concatenate([own_ref[rows, :], pair_ref[rows, :], far_ref[far, :], last_ref[far, :]], axis=1)
        branch = nn(attn, w_ref[...])
        normed, _ = normed_of(x_ref[rows, :].astype(jnp.float32) + vec_ref[4:5, :] * branch)
        c_ref[rows, :] = (normed * vec_ref[2:3, :] + vec_ref[3:4, :]).astype(jnp.bfloat16)
        if block < 2:
            branch_ref[rows, :] = branch


def mix(x_all, attn, w_out, vectors):
    return pl.pallas_call(
        mix_kernel,
        out_shape=(
            pltpu.VMEM((1024, D), jnp.bfloat16),
            jax.ShapeDtypeStruct((512, D), jnp.float32),
        ),
        in_specs=[WHOLE] * 7,
        out_specs=(WHOLE, WHOLE),
        compiler_params=vmem(12),
        cost_estimate=cost(3 << 30, 10 << 20),
        name="mix",
    )(x_all, *attn, w_out, vectors)


def gate_kernel(c_ref, w_ref, gate_up_ref, hidden_ref):
    for block in range(4):
        rows = slice(256 * block, 256 * block + 256)
        for chunk in range(4):
            both = nn(c_ref[rows, :], w_ref[chunk])
            gate_up_ref[chunk, rows, :] = both
            gate, up = both[:, :256], both[:, 256:]
            hidden_ref[rows, 256 * chunk : 256 * chunk + 256] = (gate * jax.nn.sigmoid(gate) * up).astype(
                jnp.bfloat16
            )


def gate_step(c_low, w_gate_up):
    return pl.pallas_call(
        gate_kernel,
        out_shape=(
            jax.ShapeDtypeStruct((4, 1024, 512), jnp.float32),
            jax.ShapeDtypeStruct((1024, 1024), jnp.bfloat16),
        ),
        in_specs=[WHOLE] * 2,
        out_specs=(WHOLE, WHOLE),
        compiler_params=vmem(12),
        cost_estimate=cost(5 << 30, 16 << 20),
        name="gate",
    )(c_low, w_gate_up)


def down_grad_kernel(me_ref, hidden_ref, own_ref, pair_ref, far_ref, last_ref, vec_ref, g_ref, d_mlp_ref):
    for block in range(4):
        rows = in_order((own_ref, pair_ref, far_ref, last_ref), block // 2, block % 2, me_ref[0])
        d_mlp_ref[256 * block : 256 * block + 256, :] = (rows.astype(jnp.float32) * vec_ref[5:6, :]).astype(
            jnp.bfloat16
        )
    for source in range(0, 8, 2):
        g_down = tn(hidden_ref[:, 128 * source : 128 * source + 256], d_mlp_ref[...]).astype(jnp.bfloat16)
        for pair in range(2):
            for place in range(8):
                at = 128 * (source + pair)
                g_ref[place, at : at + 128, :] = g_down[128 * pair : 128 * pair + 128, 128 * place : 128 * place + 128]


def down_grad(me, hidden, cot, vectors):
    return pl.pallas_call(
        down_grad_kernel,
        out_shape=(
            jax.ShapeDtypeStruct((8, 1024, 128), jnp.bfloat16),
            jax.ShapeDtypeStruct((1024, D), jnp.bfloat16),
        ),
        in_specs=[SCALAR] + [WHOLE] * 6,
        out_specs=(WHOLE, WHOLE),
        compiler_params=vmem(12),
        cost_estimate=cost(3 << 30, 8 << 20),
        name="down_grad",
    )(me, hidden, *cot, vectors)


def put_rows(me, whole_ref, refs, done=None):
    y = lax.rem(me, 2)
    copies = []
    for k, (ref, half) in enumerate(zip(refs, (1 - y, y, 1 - y, y))):
        rows = pl.ds(pl.multiple_of(512 * (k // 2) + 256 * half, 256), 256)
        if done is not None and k < 2:
            copies.append(pltpu.make_async_copy(whole_ref.at[rows, :], ref, done.at[k]))
            copies[-1].start()
        else:
            ref[...] = whole_ref[rows, :].astype(ref.dtype)
    for copy in copies:
        copy.wait()


PARTS = tuple(jax.ShapeDtypeStruct((256, D), t) for t in (jnp.float32, jnp.float32, jnp.bfloat16, jnp.bfloat16))


def hidden_back_kernel(gate_up_ref, d_mlp_ref, w_ref, d_both_ref):
    for block in range(4):
        rows = slice(256 * block, 256 * block + 256)
        for chunk in range(4):
            d_hidden = nt(d_mlp_ref[rows, :], w_ref[256 * chunk : 256 * chunk + 256, :])
            gate, up = gate_up_ref[chunk, rows, :256], gate_up_ref[chunk, rows, 256:]
            sig = jax.nn.sigmoid(gate)
            d_both_ref[chunk, rows, :256] = (d_hidden * up * sig * (1.0 + gate * (1.0 - sig))).astype(jnp.bfloat16)
            d_both_ref[chunk, rows, 256:] = (d_hidden * gate * sig).astype(jnp.bfloat16)


def hidden_back(gate_up, d_mlp, w_down):
    return pl.pallas_call(
        hidden_back_kernel,
        out_shape=jax.ShapeDtypeStruct((4, 1024, 512), jnp.bfloat16),
        in_specs=[WHOLE] * 3,
        out_specs=WHOLE,
        compiler_params=vmem(12),
        cost_estimate=cost(4 << 30, 18 << 20),
        name="hidden_back",
    )(gate_up, d_mlp, w_down)


def norm_back_kernel(y_ref, d_both_ref, w_ref, near_sent_ref, near_ref, far_sent_ref, far_ref, d_c_ref):
    for block in range(4):
        rows = slice(256 * block, 256 * block + 256)
        d_c = nt(d_both_ref[0, rows, :], w_ref[0])
        for chunk in range(1, 4):
            d_c += nt(d_both_ref[chunk, rows, :], w_ref[chunk])
        d_c_ref[rows, :] = d_c
    put_rows(y_ref[0], d_c_ref, (near_sent_ref, near_ref, far_sent_ref, far_ref))


def norm_back(second, d_both, w_gate_up):
    return pl.pallas_call(
        norm_back_kernel,
        out_shape=PARTS,
        in_specs=[SCALAR, WHOLE, WHOLE],
        scratch_shapes=[pltpu.VMEM((1024, D), jnp.float32)],
        out_specs=(WHOLE,) * 4,
        compiler_params=vmem(12),
        cost_estimate=cost(5 << 30, 12 << 20),
        name="norm_back",
    )(second, d_both, w_gate_up)


def gate_grad_kernel(c_ref, d_both_ref, g_ref):
    for chunk in range(4):
        for block in range(4):
            grad = tn(c_ref[:, 256 * block : 256 * block + 256], d_both_ref[chunk]).astype(jnp.bfloat16)
            for part in range(4):
                source = 4 * block + part
                for pair in range(2):
                    for half in range(2):
                        at = 256 * half + 128 * pair
                        first = 128 * source + 64 * half
                        g_ref[2 * chunk + pair, first : first + 64, :] = grad[64 * part : 64 * part + 64, at : at + 128]


def gate_grad(c_low, d_both):
    return pl.pallas_call(
        gate_grad_kernel,
        out_shape=jax.ShapeDtypeStruct((8, 2048, 128), jnp.bfloat16),
        in_specs=[WHOLE] * 2,
        out_specs=WHOLE,
        compiler_params=vmem(12),
        cost_estimate=cost(5 << 30, 10 << 20),
        name="gate_grad",
    )(c_low, d_both)


def out_kernel(
    y_ref, hidden_ref, w_ref, own_ref, pair_ref, last_ref, end_ref,
    near_sent_ref, near_ref, far_sent_ref, far_ref, g_scale_ref,
    branch_ref, done,
):
    total = jnp.zeros((1, D), jnp.float32)
    for block in range(4):
        rows = slice(256 * block, 256 * block + 256)
        branch = nn(hidden_ref[rows, :], w_ref[...])
        branch_ref[rows, :] = branch
        cot = in_order((own_ref, pair_ref, last_ref, end_ref), block // 2, block % 2, y_ref[0])
        total += jnp.sum(cot.astype(jnp.float32) * branch, axis=0, keepdims=True)
    g_scale_ref[...] = total
    put_rows(y_ref[0], branch_ref, (near_sent_ref, near_ref, far_sent_ref, far_ref), done)


def out_step(second, hidden, down, cot):
    return pl.pallas_call(
        out_kernel,
        out_shape=(pltpu.HBM((256, D), jnp.float32),) * 2 + PARTS[2:] + (jax.ShapeDtypeStruct((1, D), jnp.float32),),
        in_specs=[SCALAR] + [WHOLE] * 6,
        scratch_shapes=[pltpu.VMEM((1024, D), jnp.float32), pltpu.SemaphoreType.DMA((2,))],
        out_specs=(HBM, HBM, WHOLE, WHOLE, WHOLE),
        compiler_params=vmem(12),
        cost_estimate=cost(3 << 30, 10 << 20),
        name="out",
    )(second, hidden, down, *cot)


def attend_back_kernel(
    y_ref, own_ref, pair_ref, far_ref, last_ref, ring_ref, attn_ref, low_ref, lse_ref, cos_ref, sin_ref,
    length_ref, far_length_ref,
    d_qkv_ref, g_ref,
    d_branch_ref, w_out_ref, key_ref, value_ref,
):
    for place in range(8):
        w_out_ref[:, 128 * place : 128 * place + 128] = ring_ref[place]
    for block in range(4):
        d_branch_ref[256 * block : 256 * block + 256, :] = in_order(
            (own_ref, pair_ref, far_ref, last_ref), block // 2, block % 2, y_ref[0]
        )
    g_out = tn(attn_ref[...], d_branch_ref[...]).astype(jnp.bfloat16)
    for place in range(8):
        g_ref[place] = g_out[:, 128 * place : 128 * place + 128]
    for seq in range(2):
        key_ref[...] = jnp.zeros_like(key_ref)
        value_ref[...] = jnp.zeros_like(value_ref)
        cosine, sine = cos_ref[seq], -sin_ref[seq]
        for block in range(2):
            at = 512 * seq + 256 * block
            rows = slice(at, at + 256)
            span = slice(128 * block, 128 * block + 384)
            keys = slice(512 * seq + 128 * block, 512 * seq + 128 * block + 384)
            mask, keep = mask_of((length_ref, far_length_ref)[seq], block)
            d_attn_all = nt(d_branch_ref[rows, :], w_out_ref[...]).astype(jnp.bfloat16)
            d_attn_all = jnp.where(keep, d_attn_all, jnp.zeros_like(d_attn_all))
            d_queries, d_keys, d_values = [], [], []
            for head in range(4):
                lane = 64 * head
                query = low_ref[rows, lane : lane + 64]
                key = low_ref[keys, OWN + lane : OWN + lane + 64]
                value = low_ref[keys, 2 * OWN + lane : 2 * OWN + lane + 64]
                d_attn = d_attn_all[:, lane : lane + 64]
                masked = jnp.where(mask, nt(query, key) * SCALE, neg_large)
                probs = jnp.exp(masked - lse_ref[rows, head : head + 1])
                d_values.append(tn(probs.astype(jnp.bfloat16), d_attn))
                d_probs = nt(d_attn, value)
                inner = jnp.sum(probs * d_probs, axis=1, keepdims=True)
                d_scores = (probs * (d_probs - inner)).astype(jnp.bfloat16)
                d_queries.append(nn(d_scores, key) * SCALE)
                d_keys.append(tn(d_scores, query) * SCALE)
            part = slice(256 * block, 256 * block + 256)
            d_query = turn(jnp.concatenate(d_queries, axis=1), cosine[part], sine[part])
            d_qkv_ref[rows, :OWN] = d_query.astype(jnp.bfloat16)
            key_ref[span, :] += jnp.concatenate(d_keys, axis=1)
            value_ref[span, :] += jnp.concatenate(d_values, axis=1)
        whole = slice(512 * seq, 512 * seq + 512)
        d_qkv_ref[whole, OWN : 2 * OWN] = turn(key_ref[...], cosine, sine).astype(jnp.bfloat16)
        d_qkv_ref[whole, 2 * OWN :] = value_ref[...].astype(jnp.bfloat16)


def attention_back(me, d_branch, ring, attn, low, lse, cosine, sine, lengths):
    return pl.pallas_call(
        attend_back_kernel,
        out_shape=(
            jax.ShapeDtypeStruct((1024, 3 * OWN), jnp.bfloat16),
            jax.ShapeDtypeStruct((8, OWN, 128), jnp.bfloat16),
        ),
        in_specs=[SCALAR] + [WHOLE] * 10 + [SCALAR] * 2,
        out_specs=(WHOLE, WHOLE),
        scratch_shapes=[
            pltpu.VMEM((1024, D), jnp.bfloat16),
            pltpu.VMEM((OWN, D), jnp.bfloat16),
            pltpu.VMEM((512, OWN), jnp.float32),
            pltpu.VMEM((512, OWN), jnp.float32),
        ],
        compiler_params=vmem(12),
        cost_estimate=cost(12 << 30, 10 << 20),
        name="attend_back",
    )(me, *d_branch, ring, attn, low, lse, cosine, sine, *lengths)


def grad_kernel(
    y_ref, a_ref, w_ref, order_ref, d_qkv_ref, g_out_ref, x_ref, mean_ref, inv_ref, small_ref,
    g_ref, near_sent_ref, near_ref, far_sent_ref, far_ref,
    d_a_ref,
):
    g_gain, g_bias = jnp.zeros((1, D), jnp.float32), jnp.zeros((1, D), jnp.float32)
    for block in range(4):
        rows = slice(256 * block, 256 * block + 256)
        d_a = nt(d_qkv_ref[rows, :], w_ref[...])
        normed = (x_ref[rows, :].astype(jnp.float32) - mean_ref[rows, :]) * inv_ref[rows, :]
        g_gain += jnp.sum(d_a * normed, axis=0, keepdims=True)
        g_bias += jnp.sum(d_a, axis=0, keepdims=True)
        d_a_ref[rows, :] = d_a
    put_rows(y_ref[0], d_a_ref, (near_sent_ref, near_ref, far_sent_ref, far_ref))
    for block in range(8):
        grad = tn(a_ref[:, 128 * block : 128 * block + 128], d_qkv_ref[...]).astype(jnp.bfloat16)
        grad = jnp.concatenate([grad[:, OWN * third : OWN * third + OWN] for third in range(3)], axis=0)
        grad = tn(order_ref[...], grad).astype(jnp.bfloat16)
        for part in range(6):
            chunk = 6 * block + part
            at = 128 * (chunk // 8)
            g_ref[chunk % 8, at : at + 64, :] = grad[64 * part : 64 * part + 64, :128]
            g_ref[chunk % 8, at + 64 : at + 128, :] = grad[64 * part : 64 * part + 64, 128:]
    vectors = [g_gain, g_bias] + [small_ref[k : k + 1, :] for k in range(4)]
    lines = [v[:, 128 * k : 128 * k + 128] for v in vectors for k in range(8)]
    for place in range(8):
        g_ref[place, 768:1024, :] = g_out_ref[place]
        rows = lines[6 * place : 6 * place + 6] + [jnp.zeros((SLAB - 6, 128), jnp.float32)]
        g_ref[place, 1024:, :] = jnp.concatenate(rows, axis=0).astype(jnp.bfloat16)


def grad_step(second, a_low, w_qkv, order, d_qkv, g_out, x_all, mean, inv, small):
    return pl.pallas_call(
        grad_kernel,
        out_shape=(jax.ShapeDtypeStruct((8, 1024 + SLAB, 128), jnp.bfloat16),) + PARTS,
        in_specs=[SCALAR] + [WHOLE] * 9,
        scratch_shapes=[pltpu.VMEM((1024, D), jnp.float32)],
        out_specs=(WHOLE,) * 5,
        compiler_params=vmem(12),
        cost_estimate=cost(8 << 30, 12 << 20),
        name="grad",
    )(second, a_low, w_qkv, order, d_qkv, g_out, x_all, mean, inv, small)


def after(values, *others):
    if isinstance(values, tuple):
        return lax.optimization_barrier(values + others)[: len(values)]
    return lax.optimization_barrier((values,) + others)[0]


def both_ways(ahead, back):
    return lax.optimization_barrier((lax.ppermute(ahead, GROUP, AHEAD), lax.ppermute(back, GROUP, BACK)))


class Gather:
    def __init__(self, block):
        self.blocks = [block]
        self.next = (block, block)
        self.half = (block.shape[0] // 2 + 15) // 16 * 16
        self.count = 0

    def step(self, *waits, hold=()):
        self.count += 1
        ahead, back = after(self.next, *waits) if waits else self.next
        if self.count == 4:
            ahead, back = ahead[: self.half], back[self.half :]
        self.next = after(both_ways(ahead, back), *hold)
        self.blocks += self.next
        return self.next


class Scatter:
    def __init__(self, blocks, me):
        self.blocks, self.me = blocks, me
        self.rows = blocks.shape[1]
        self.half = (self.rows // 2 + 15) // 16 * 16
        self.count = 0
        self.next = (self.get(4, 0, self.half), self.get(4, self.half))

    def get(self, step, lo=0, hi=None):
        hi = self.rows if hi is None else hi
        at = (ring_place(self.me, step % 8), 0 * self.me + lo, 0 * self.me)
        return lax.dynamic_slice(self.blocks, at, (1, hi - lo, 128))[0]

    def step(self, *waits, hold=()):
        self.count += 1
        ahead, back = came = after(both_ways(*(after(self.next, *waits) if waits else self.next)), *hold)

        def add(moved, own):
            return (moved.astype(jnp.float32) + own.astype(jnp.float32)).astype(jnp.bfloat16)

        if self.count == 1:
            half = self.half
            ahead = jnp.concatenate([add(ahead, self.get(3, 0, half)), self.get(3, half)])
            back = jnp.concatenate([self.get(5, 0, half), add(back, self.get(5, half))])
        elif self.count < 4:
            ahead, back = add(ahead, self.get(4 - self.count)), add(back, self.get(4 + self.count))
        else:
            total = self.get(0).astype(jnp.float32) + ahead.astype(jnp.float32) + back.astype(jnp.float32)
            self.total = total.astype(jnp.bfloat16)
        self.next = (ahead, back)
        return came


def to_pair(rows, *waits):
    rows = after(rows, *waits) if waits else rows
    return rows, lax.ppermute(rows, "y", SWAP)


def to_group(pair, *waits):
    pair = after(tuple(pair), *waits) if waits else pair
    return tuple(pair) + tuple(lax.ppermute(rows, "c", SWAP) for rows in pair)


def half_sum(near_sent, near, far_sent, far):
    sent = near_sent + lax.ppermute(far_sent, "c", SWAP).astype(jnp.float32)
    kept = near + lax.ppermute(far, "c", SWAP).astype(jnp.float32)
    return lax.optimization_barrier((sent.astype(jnp.bfloat16), kept))


def full_sum(sent, kept):
    return kept + lax.ppermute(sent, "y", SWAP).astype(jnp.float32)


def normed_of(rows):
    centered = rows - jnp.mean(rows, axis=-1, keepdims=True)
    inv_scale = lax.rsqrt(jnp.mean(centered * centered, axis=-1, keepdims=True) + eps_norm)
    return centered * inv_scale, inv_scale


def norm_rows_back(out_grad, normed, inv_scale, gain):
    inner = out_grad * gain
    return inv_scale * (
        inner
        - jnp.mean(inner, axis=-1, keepdims=True)
        - normed * jnp.mean(inner * normed, axis=-1, keepdims=True)
    )


def fast_body(frames, cotangent, clip_lengths, params, first_moment, second_moment):
    z, x, c, y = (lax.axis_index(axis) for axis in EVERY)
    device = (((z * 2 + x) * 2 + c) * 2 + y).astype(jnp.int32)
    me = device[None]
    lengths = (clip_lengths, lax.ppermute(clip_lengths, "c", SWAP))
    order = np.zeros((384, 384), np.float32)
    for row in range(384):
        order[(row % 3) * 128 + row // 3, row] = 1.0
    order = jnp.asarray(order, jnp.bfloat16)

    pieces = spread(params, me)
    pieces = lax.all_to_all(pieces, EVERY, split_axis=0, concat_axis=0, tiled=True)
    first_piece, second_piece, third_piece = fix(pieces)
    first, second, third = Gather(first_piece), Gather(second_piece), Gather(third_piece)
    frames_pair = to_pair(frames[0], first_piece)
    came = first.step()
    cot_pair = to_pair(cotangent[0], frames_pair[1])
    lengths = after(lengths, first_piece)
    both = jnp.concatenate(lengths)
    frame = jnp.arange(512, dtype=jnp.int32)
    starts, ends = both[:, :1], both[:, :1] + both[:, 1:]
    position = jnp.where((frame >= starts) & (frame < ends), frame - starts, frame).astype(jnp.float32)
    inverse = jnp.exp(
        jnp.asarray(np.arange(128) % 32, jnp.float32) * (-2.0 * math.log(rope_base) / HEAD_DIM)
    )
    angle = position[:, :, None] * inverse
    cosine = jnp.cos(angle)
    sine = jnp.sin(angle) * jnp.asarray(np.where(np.arange(128) % 64 < 32, -1.0, 1.0), jnp.float32)
    second.step(*first.step(cosine, sine))
    frames_parts = to_group(after(frames_pair, *came))
    first.step(frames_pair[1])
    x_all, mean_one, inv_one = prep(me, frames_parts)
    first.step(x_all)
    ring_qkv, w_own, vectors = join(
        join_first_kernel,
        me,
        first.blocks,
        (
            jax.ShapeDtypeStruct((8, 768, 128), jnp.bfloat16),
            jax.ShapeDtypeStruct((8, OWN, 128), jnp.bfloat16),
            jax.ShapeDtypeStruct((6, D), jnp.float32),
        ),
        "join_first",
        [pltpu.VMEM((8, SLAB, 128), jnp.bfloat16)],
    )

    w_pair = to_pair(w_own)
    x_all, ring_qkv = after((x_all, ring_qkv), *second.next, cot_pair[1])
    a_low, w_qkv, low, attn_own, lse = front(x_all, mean_one, inv_one, ring_qkv, vectors, order, cosine, sine, lengths)
    came = second.step(ring_qkv)
    attn_pair = to_pair(attn_own, *came, w_pair[1])
    w_out = join_out(to_group(w_pair, attn_own))
    came = second.step(attn_own)
    attn_parts = to_group(attn_pair, w_out)
    attn_parts = attn_parts[:2] + after(attn_parts[2:], *came)
    c_low, branch_seq = mix(x_all, attn_parts, w_out, vectors)
    came = third.step(*attn_parts[2:])
    came = second.step(*attn_parts[2:]) + came
    second.blocks[7:] = after(came[:2], c_low)
    w_gate_up = join(
        join_gate_up_kernel,
        me,
        [block.reshape(-1, 2, 64, 128) for block in second.blocks],
        jax.ShapeDtypeStruct((4, 16, 64, 512), jnp.bfloat16),
        "join_gate_up",
        space=HBM,
    ).reshape(4, 1024, 512)
    cot_parts = to_group(cot_pair, c_low)
    gate_up, hidden = gate_step(after(c_low, *came[2:]), w_gate_up)
    came = third.step(c_low)
    g_down, d_mlp = down_grad(me, after(hidden, *came), cot_parts, vectors)
    third.step(hidden)
    third.step(g_down)
    w_down = join(join_down_kernel, me, third.blocks, jax.ShapeDtypeStruct((1024, D), jnp.bfloat16), "join_down", space=HBM)

    down = Scatter(g_down, device)
    d_both = hidden_back(gate_up, d_mlp, w_down)
    came = down.step(*third.next)
    d_both = after(d_both, *came)
    d_c_parts = norm_back(me, d_both, w_gate_up)
    came = down.step(d_both)
    d_c_sent, d_c_kept = half_sum(*after(tuple(d_c_parts), *came))
    g_gate_up = gate_grad(c_low, after(d_both, d_c_sent, d_c_kept))
    came = down.step(d_c_sent, hold=(g_gate_up,))
    gate_grads = Scatter(after(g_gate_up, *came), device)

    x_own = frames[0].astype(jnp.float32)
    cot_own = cotangent[0].astype(jnp.float32)
    branch_own = jnp.where(y == 0, branch_seq[:256], branch_seq[256:])
    mid_own = x_own + vectors[4] * branch_own
    normed_two, scale_two = normed_of(mid_own)
    d_c_own = full_sum(d_c_sent, d_c_kept)
    d_mid = cot_own + norm_rows_back(d_c_own, normed_two, scale_two, vectors[2])
    d_branch_own = (d_mid * vectors[4]).astype(jnp.bfloat16)
    d_branch_pair = to_pair(d_branch_own)
    came = gate_grads.step(hold=(d_branch_own,))
    hidden = after(hidden, d_branch_own, *came)
    *out_parts, g_scale_mlp = out_step(me, hidden, w_down, cot_parts)
    came = gate_grads.step(d_branch_own, hold=(g_scale_mlp,))
    d_branch = to_group(d_branch_pair, *came, g_scale_mlp)
    out_sent, out_kept = half_sum(*out_parts)
    g_gain_two = jnp.sum(d_c_own * normed_two, axis=0)
    g_bias_two = jnp.sum(d_c_own, axis=0)
    g_scale_attn = jnp.sum(d_mid * branch_own, axis=0)
    small = jnp.concatenate([jnp.stack([g_gain_two, g_bias_two, g_scale_attn]), g_scale_mlp], axis=0)

    d_branch = after(d_branch, small)
    d_qkv, g_out = attention_back(me, d_branch, w_own, attn_own, low, lse, cosine, sine, lengths)
    came = gate_grads.step(*d_branch, hold=(d_qkv,))
    out_sent = after(out_sent, *d_branch)
    output = (mid_own + vectors[5] * full_sum(out_sent, out_kept)).astype(jnp.bfloat16)
    d_qkv = after(d_qkv, *came)
    g_first, *d_a_parts = grad_step(me, a_low, w_qkv, order, d_qkv, g_out, x_all, mean_one, inv_one, small)
    came = gate_grads.step(d_qkv, hold=(g_first,))
    down.step(*came)
    first_grads = Scatter(after(g_first, *came), device)
    first_grads.step(output)
    d_a_sent, d_a_kept = half_sum(*d_a_parts)
    first_grads.step(d_a_sent, *down.next)
    first_grads.step()
    normed_one, scale_one = normed_of(x_own)
    d_one = norm_rows_back(full_sum(d_a_sent, d_a_kept), normed_one, scale_one, vectors[0])
    frames_grad = (d_mid + d_one).astype(jnp.bfloat16)
    first_grads.step(frames_grad)
    g_first, g_gate_up, g_down = first_grads.total, gate_grads.total, down.total

    main = jnp.concatenate([g_first[:1024], g_gate_up, g_down]).reshape(32, 128, 128)
    slab = jnp.concatenate([main[1:, :8], main[1:, 64:72]], axis=1)
    slab = jnp.concatenate([slab, g_first[None, 1024:]])
    pieces = jnp.concatenate([main, slab], axis=1)
    pieces = lax.all_to_all(pieces, EVERY, split_axis=0, concat_axis=0, tiled=True)
    params_grad = collect(pieces, me, params.shape[0])
    new_params, new_first, new_second = adam_update(params, params_grad, first_moment, second_moment)
    return (output[None], frames_grad[None], params_grad, new_params, new_first, new_second)


def solution(mesh):
    def run(frames, cotangent, clip_lengths, params, first_moment, second_moment):
        fits = (
            mesh.shape["dp"] == 16
            and mesh.shape["seq"] == 2
            and frames.shape == (16, 512, D)
            and clip_lengths.shape == (16, 2)
        )
        if fits:
            over = Mesh(mesh.devices.reshape(4, 2, 2, 2), EVERY)
            rows, clips, flat = P(("z", "x", "c"), "y", None), P(("z", "x", "c"), None), P(EVERY)
        else:
            over = mesh
            rows, clips, flat = P("dp", "seq", None), P("dp", None), P(("dp", "seq"))
        step = jax.shard_map(
            fast_body if fits else body,
            mesh=over,
            in_specs=(rows, rows, clips, flat, flat, flat),
            out_specs=(rows, rows, flat, flat, flat, flat),
            check_vma=False,
        )
        return step(frames, cotangent, clip_lengths, params, first_moment, second_moment)

    return run
```

```python
import functools
import math

import jax
import jax.numpy as jnp
import numpy as np
from jax import lax
from jax.experimental import pallas as pl
from jax.experimental.pallas import tpu as pltpu
from jax.sharding import Mesh
from jax.sharding import PartitionSpec as P

D = 1024
HEADS = 16
HEAD_DIM = 64
FF = 4096
WINDOW = 128


eps_norm = 1e-05
beta_one = 0.9
beta_two = 0.99
learn_rate = 0.01
decay_rate = 0.1
eps_adam = 1e-08
adam_step = 100.0
neg_large = -1e30
rope_base = 10000.0


def padded(shard, sides, width):
    for axis, dim in sides:
        size, length = (lax.axis_size(axis), shard.shape[dim])
        up = [(i, (i + 1) % size) for i in range(size - 1)]
        down = [(j, i) for i, j in up]
        last = lax.slice_in_dim(shard, length - width, length, axis=dim)
        first = lax.slice_in_dim(shard, 0, width, axis=dim)
        before = lax.ppermute(last, axis, up)
        after = lax.ppermute(first, axis, down)
        shard = jnp.concatenate([before, shard, after], axis=dim)
    return shard


def unpack(flat_params):
    end_qkv = D * 3 * D
    end_out = end_qkv + D * D
    end_mlp = end_out + D * 2 * FF
    end_down = end_mlp + FF * D
    w_qkv = flat_params[:end_qkv].reshape(D, 3 * D)
    w_out = flat_params[end_qkv:end_out].reshape(D, D)
    w_gate_up = flat_params[end_out:end_mlp].reshape(D, 2 * FF)
    w_down = flat_params[end_mlp:end_down].reshape(FF, D)
    vectors = flat_params[end_down:].reshape(6, D).astype(jnp.float32)
    return (w_qkv, w_out, w_gate_up, w_down, vectors)


def clip_info(lengths, glob):
    clip_ends = jnp.cumsum(lengths, axis=1, dtype=jnp.int32)
    clip_starts = clip_ends - lengths
    after_end = (glob[None, :, None] >= clip_ends[:, None, :]).astype(jnp.int32)
    segment = jnp.sum(after_end, axis=2, dtype=jnp.int32)
    onehot = segment[:, :, None] == jnp.arange(lengths.shape[1], dtype=jnp.int32)[None, None, :]
    clip_begin = jnp.sum(jnp.where(onehot, clip_starts[:, None, :], 0), axis=2, dtype=jnp.int32)
    return (segment, (glob[None, :] - clip_begin).astype(jnp.float32))


def rotate(values, position, sign):
    half_dim = values.shape[-1] // 2
    inverse = jnp.exp(
        jnp.arange(half_dim, dtype=jnp.float32) * (-2.0 * math.log(rope_base) / HEAD_DIM)
    )
    rot_angle = position[:, :, None, None] * inverse
    cosine = jnp.cos(rot_angle)
    rot_sine = sign * jnp.sin(rot_angle)
    low_half = values[..., :half_dim]
    high_half = values[..., half_dim:]
    return jnp.concatenate(
        [low_half * cosine - high_half * rot_sine, high_half * cosine + low_half * rot_sine],
        axis=-1,
    )


def norm_forward(row_vals, norm_gain, norm_bias):
    centered = row_vals - jnp.mean(row_vals, axis=-1, keepdims=True)
    inv_scale = lax.rsqrt(jnp.mean(centered * centered, axis=-1, keepdims=True) + eps_norm)
    normed = centered * inv_scale
    return (normed * norm_gain + norm_bias, normed, inv_scale)


def norm_backward(out_grad, normed, inv_scale, norm_gain):
    d_gain = jnp.sum(out_grad * normed, axis=0)
    d_bias = jnp.sum(out_grad, axis=0)
    inner_grad = out_grad * norm_gain
    d_rows = inv_scale * (
        inner_grad
        - jnp.mean(inner_grad, axis=-1, keepdims=True)
        - normed * jnp.mean(inner_grad * normed, axis=-1, keepdims=True)
    )
    return (d_rows, d_gain, d_bias)


def scores_of(query_rows, key_rows, window_mask):
    raw_scores = jnp.einsum(
        "qhd,khd->hqk", query_rows, key_rows, preferred_element_type=jnp.float32
    ) * HEAD_DIM ** (-0.5)
    return jnp.where(window_mask[None], raw_scores, neg_large)


def attend(query_rows, key_rows, value_rows, window_mask):
    masked = scores_of(query_rows, key_rows, window_mask)
    row_max = jnp.max(masked, axis=-1, keepdims=True)
    row_total = jnp.log(jnp.sum(jnp.exp(masked - row_max), axis=-1, keepdims=True)) + row_max
    prob_low = jnp.exp(masked - row_total).astype(jnp.bfloat16)
    attn_rows = jnp.einsum("hqk,khd->qhd", prob_low, value_rows, preferred_element_type=jnp.float32)
    return (attn_rows, row_total[..., 0])


def attend_back(query_rows, key_rows, value_rows, window_mask, row_total, d_attn):
    masked = scores_of(query_rows, key_rows, window_mask)
    prob_rows = jnp.exp(masked - row_total[..., None])
    prob_low = prob_rows.astype(jnp.bfloat16)
    d_values = jnp.einsum("hqk,qhd->khd", prob_low, d_attn, preferred_element_type=jnp.float32)
    d_probs = jnp.einsum("qhd,khd->hqk", d_attn, value_rows, preferred_element_type=jnp.float32)
    inner_sum = jnp.sum(prob_rows * d_probs, axis=-1, keepdims=True)
    d_scores = (prob_rows * (d_probs - inner_sum)).astype(jnp.bfloat16)
    d_query = jnp.einsum(
        "hqk,khd->qhd", d_scores, key_rows, preferred_element_type=jnp.float32
    ) * HEAD_DIM ** (-0.5)
    d_keys = jnp.einsum(
        "hqk,qhd->khd", d_scores, query_rows, preferred_element_type=jnp.float32
    ) * HEAD_DIM ** (-0.5)
    return (d_query, d_keys, d_values)


def adam_update(flat_params, grads, first_moment, second_moment):
    new_first = beta_one * first_moment + (1.0 - beta_one) * grads
    new_second = beta_two * second_moment + (1.0 - beta_two) * grads * grads
    corrected_first = new_first / (1.0 - beta_one**adam_step)
    corrected_second = new_second / (1.0 - beta_two**adam_step)
    step_size = corrected_first / (jnp.sqrt(corrected_second) + eps_adam) + decay_rate * flat_params
    return (flat_params - learn_rate * step_size, new_first, new_second)


def body(frames, cotangent, clip_lengths, params, first_moment, second_moment):
    seq_count, frame_span, model_width = frames.shape
    row_count = seq_count * frame_span
    window_reach = WINDOW
    key_count = frame_span + 2 * window_reach
    head_count = HEADS
    head_size = model_width // head_count
    group_size = 4
    seq_len = lax.axis_size("seq") * frame_span
    seq_start = lax.axis_index("seq") * frame_span
    glob_rows = seq_start + jnp.arange(frame_span, dtype=jnp.int32)
    glob_keys = seq_start - window_reach + jnp.arange(key_count, dtype=jnp.int32)
    seg_rows, pos_rows = clip_info(clip_lengths, glob_rows)
    seg_keys, unused = clip_info(clip_lengths, glob_keys)
    inside = (glob_keys >= 0) & (glob_keys < seq_len)
    near_band = (
        jnp.abs(jnp.arange(frame_span)[:, None] + window_reach - jnp.arange(key_count)[None, :])
        < window_reach
    )
    window_mask = (
        (seg_rows[:, :, None] == seg_keys[:, None, :]) & inside[None, None, :] & near_band[None]
    )
    keep_rows = seg_rows != clip_lengths.shape[1] - 1
    shards = params.astype(jnp.bfloat16)
    gathered = lax.all_gather(shards, ("dp", "seq"), axis=0, tiled=True)
    w_qkv, w_out, w_gate_up, w_down, vectors = unpack(gathered)
    x_rows = frames.reshape(row_count, model_width).astype(jnp.float32)
    norm_one, normed_one, scale_one = norm_forward(x_rows, vectors[0], vectors[1])
    a_low = norm_one.astype(jnp.bfloat16)
    qkv = jnp.dot(a_low, w_qkv, preferred_element_type=jnp.float32).reshape(
        seq_count, frame_span, 3, head_count, head_size
    )
    query_low = rotate(qkv[:, :, 0], pos_rows, 1.0).astype(jnp.bfloat16)
    key_low = rotate(qkv[:, :, 1], pos_rows, 1.0).astype(jnp.bfloat16)
    value_low = qkv[:, :, 2].astype(jnp.bfloat16)
    key_value = jnp.concatenate([key_low, value_low], axis=2).reshape(
        seq_count, frame_span, 2 * model_width
    )
    wide_rows = padded(key_value, (("seq", 1),), window_reach)
    wide_rows = wide_rows.reshape(seq_count, key_count, 2, head_count, head_size)
    key_wide = wide_rows[:, :, 0]
    value_wide = wide_rows[:, :, 1]
    seq_index = 0
    out_parts = []
    total_parts = []
    for head_start in range(0, head_count, group_size):
        head_end = head_start + group_size
        attn_rows, row_total = attend(
            query_low[seq_index, :, head_start:head_end],
            key_wide[seq_index, :, head_start:head_end],
            value_wide[seq_index, :, head_start:head_end],
            window_mask[seq_index],
        )
        out_parts.append(attn_rows)
        total_parts.append(row_total)
    attn_list = [jnp.concatenate(out_parts, axis=1)]
    total_list = [total_parts]
    attn_all = jnp.where(keep_rows[:, :, None, None], jnp.stack(attn_list), 0.0)
    attn_low = attn_all.reshape(row_count, model_width).astype(jnp.bfloat16)
    branch_attn = jnp.dot(attn_low, w_out, preferred_element_type=jnp.float32)
    mid_rows = x_rows + vectors[4] * branch_attn
    norm_two, normed_two, scale_two = norm_forward(mid_rows, vectors[2], vectors[3])
    c_low = norm_two.astype(jnp.bfloat16)
    gate_up = jnp.dot(c_low, w_gate_up, preferred_element_type=jnp.float32)
    gate = gate_up[:, :FF]
    up_rows = gate_up[:, FF:]
    gate_sig = jax.nn.sigmoid(gate)
    hidden = (gate * gate_sig * up_rows).astype(jnp.bfloat16)
    branch_mlp = jnp.dot(hidden, w_down, preferred_element_type=jnp.float32)
    output = (
        (mid_rows + vectors[5] * branch_mlp)
        .astype(jnp.bfloat16)
        .reshape(seq_count, frame_span, model_width)
    )
    gathered = lax.all_gather(shards, ("dp", "seq"), axis=0, tiled=True)
    w_qkv, w_out, w_gate_up, w_down, vectors = unpack(gathered)
    d_rows = cotangent.reshape(row_count, model_width).astype(jnp.float32)
    g_scale_mlp = jnp.sum(d_rows * branch_mlp, axis=0)
    d_mlp = (d_rows * vectors[5]).astype(jnp.bfloat16)
    g_down = jnp.dot(hidden.T, d_mlp, preferred_element_type=jnp.float32)
    d_hidden = jnp.dot(d_mlp, w_down.T, preferred_element_type=jnp.float32)
    d_gate = d_hidden * up_rows * gate_sig * (1.0 + gate * (1.0 - gate_sig))
    d_up = d_hidden * gate * gate_sig
    d_gate_up = jnp.concatenate([d_gate, d_up], axis=1).astype(jnp.bfloat16)
    g_gate_up = jnp.dot(c_low.T, d_gate_up, preferred_element_type=jnp.float32)
    d_two = jnp.dot(d_gate_up, w_gate_up.T, preferred_element_type=jnp.float32)
    d_norm_two, g_gain_two, g_bias_two = norm_backward(d_two, normed_two, scale_two, vectors[2])
    d_mid = d_rows + d_norm_two
    g_scale_attn = jnp.sum(d_mid * branch_attn, axis=0)
    d_branch = (d_mid * vectors[4]).astype(jnp.bfloat16)
    g_out = jnp.dot(attn_low.T, d_branch, preferred_element_type=jnp.float32)
    d_attn_low = jnp.dot(d_branch, w_out.T, preferred_element_type=jnp.float32).astype(jnp.bfloat16)
    d_attn = jnp.where(
        keep_rows[:, :, None, None],
        d_attn_low.reshape(seq_count, frame_span, head_count, head_size),
        jnp.zeros((), jnp.bfloat16),
    )
    seq_index = 0
    query_parts = []
    key_parts = []
    value_parts = []
    for number, head_start in enumerate(range(0, head_count, group_size)):
        head_end = head_start + group_size
        d_query, d_keys, d_values = attend_back(
            query_low[seq_index, :, head_start:head_end],
            key_wide[seq_index, :, head_start:head_end],
            value_wide[seq_index, :, head_start:head_end],
            window_mask[seq_index],
            total_list[seq_index][number],
            d_attn[seq_index, :, head_start:head_end],
        )
        query_parts.append(d_query)
        key_parts.append(d_keys)
        value_parts.append(d_values)
    query_grads = [jnp.concatenate(query_parts, axis=1)]
    key_grads = [jnp.concatenate(key_parts, axis=1)]
    value_grads = [jnp.concatenate(value_parts, axis=1)]
    d_query_all = jnp.stack(query_grads)
    d_pair = jnp.concatenate([jnp.stack(key_grads), jnp.stack(value_grads)], axis=2).reshape(
        seq_count, key_count, 2 * model_width
    )
    rim_rows = jnp.concatenate(
        [d_pair[:, :window_reach], d_pair[:, window_reach + frame_span :]], axis=1
    )
    taken_rows = padded(rim_rows.astype(jnp.bfloat16), (("seq", 1),), window_reach).astype(
        rim_rows.dtype
    )
    own_rows = d_pair[:, window_reach : window_reach + frame_span]
    own_rows = own_rows + jnp.pad(
        taken_rows[:, :window_reach], ((0, 0), (0, frame_span - window_reach), (0, 0))
    )
    own_rows = own_rows + jnp.pad(
        taken_rows[:, 3 * window_reach :], ((0, 0), (frame_span - window_reach, 0), (0, 0))
    )
    own_rows = own_rows.reshape(seq_count, frame_span, 2, head_count, head_size)
    d_qkv = jnp.stack(
        [
            rotate(d_query_all, pos_rows, -1.0),
            rotate(own_rows[:, :, 0], pos_rows, -1.0),
            own_rows[:, :, 1],
        ],
        axis=2,
    )
    d_qkv = d_qkv.reshape(row_count, 3 * model_width).astype(jnp.bfloat16)
    g_qkv = jnp.dot(a_low.T, d_qkv, preferred_element_type=jnp.float32)
    d_one = jnp.dot(d_qkv, w_qkv.T, preferred_element_type=jnp.float32)
    d_norm_one, g_gain_one, g_bias_one = norm_backward(d_one, normed_one, scale_one, vectors[0])
    frames_grad = (
        (d_mid + d_norm_one).astype(jnp.bfloat16).reshape(seq_count, frame_span, model_width)
    )
    small_grads = jnp.stack(
        [g_gain_one, g_bias_one, g_gain_two, g_bias_two, g_scale_attn, g_scale_mlp]
    )
    whole_grad = jnp.concatenate(
        [
            g_qkv.reshape(-1),
            g_out.reshape(-1),
            g_gate_up.reshape(-1),
            g_down.reshape(-1),
            small_grads.reshape(-1),
        ]
    )
    params_grad = lax.psum_scatter(whole_grad, ("dp", "seq"), scatter_dimension=0, tiled=True)
    new_params, new_first, new_second = adam_update(
        params, params_grad, first_moment, second_moment
    )
    return (output, frames_grad, params_grad, new_params, new_first, new_second)


EVERY = ("z", "x", "c", "y")
GROUP = ("z", "x")
RING = ((0, 0), (1, 0), (2, 0), (3, 0), (3, 1), (2, 1), (1, 1), (0, 1))
PLACES = tuple(2 * z + x for z, x in RING)
AHEAD = tuple((PLACES[i], PLACES[(i + 1) % 8]) for i in range(8))
BACK = tuple((b, a) for a, b in AHEAD)
SWAP = ((0, 1), (1, 0))
LINES = 4096
TAIL = 64
SLAB = 16
ROWS = 128 + SLAB
OWN = 256
SCALE = HEAD_DIM ** (-0.5)
SCALAR = pl.BlockSpec(memory_space=pltpu.SMEM)
WHOLE = pl.BlockSpec(memory_space=pltpu.VMEM)
HBM = pl.BlockSpec(memory_space=pltpu.HBM)
ANY = pl.BlockSpec(memory_space=pl.ANY)


def vmem(mebibytes):
    return pltpu.CompilerParams(vmem_limit_bytes=mebibytes << 20)


def ring_place(me, step):
    z, x = lax.div(me, 8), lax.rem(lax.div(me, 4), 2)
    at = lax.rem(jnp.where(x == 0, z, 7 - z) + step, 8)
    return jnp.where(at < 4, 2 * at, 15 - 2 * at)


def kind_of(shard):
    if shard < 6:
        return 0
    return 2 if 8 <= shard < 24 else 1


def piece_lines(kind, dest):
    place, member = divmod(dest, 4)
    if kind == 0:
        return [(512 * place + member, 8), (512 * place + 4 + member, 8)]
    if kind == 1:
        return [(1024 * member + place, 8), (1024 * member + 512 + place, 8)]
    return [(dest, 64), (32 + dest, 64)]


def tail_lines(kind, dest):
    place, member = divmod(dest, 4)
    if kind == 0:
        return [(0, 6, member, 8), (8, 6, 4 + member, 8)] if place == 0 else []
    if kind == 1:
        return [(0, 6, place, 8)] if member == 0 else []
    return [(0, 1, dest, 1)] + ([(8, 1, 32 + dest, 1)] if dest < 16 else [])


def is_kind(shard, kind):
    if kind == 0:
        return shard < 6
    gate_up = (shard >= 8) & (shard < 24)
    if kind == 2:
        return gate_up
    return (shard >= 6) & jnp.logical_not(gate_up) & (shard < 32)


def spread_kernel(me_ref, flat_ref, out_ref, lines_ref):
    me = me_ref[0]
    odd = lax.rem(me, 2) == 1
    start = 48 - (3 * me + 1) // 2
    lane = lax.broadcasted_iota(jnp.int32, (64, 128), 1)

    def shift(step, carry):
        here = flat_ref[pl.ds(start + step * 64, 64), :]
        after = flat_ref[pl.ds(start + step * 64 + 1, 64), :]
        mixed = jnp.where(lane < 64, pltpu.roll(here, 64, 1), pltpu.roll(after, 64, 1))
        lines_ref[pl.ds(pl.multiple_of(step * 64, 64), 64), :] = jnp.where(odd, mixed, here)
        return carry

    lax.fori_loop(0, (LINES + TAIL) // 64, shift, 0, unroll=5)
    for kind in range(3):

        @pl.when(is_kind(me, kind))
        def _(kind=kind):
            for dest in range(32):
                for half, (first, stride) in enumerate(piece_lines(kind, dest)):
                    rows = lines_ref[pl.ds(first, 64, stride), :]
                    out_ref[dest, 64 * half : 64 * half + 64, :] = rows.astype(jnp.bfloat16)

    def slab_of(parts):
        slab = [jnp.zeros((8, 128), jnp.float32)] * 2
        row = lax.broadcasted_iota(jnp.int32, (8, 128), 0)
        for at, count, first, stride in parts:
            if count == 1:
                value = jnp.broadcast_to(lines_ref[LINES + first : LINES + first + 1, :], (8, 128))
            else:
                value = lines_ref[pl.ds(LINES + first, 8, stride), :]
            slab[at // 8] = jnp.where(row < count, value, 0.0)
        return jnp.concatenate(slab, axis=0).astype(jnp.bfloat16)

    for kind in range(3):

        @pl.when(is_kind(me + 1, kind))
        def _(kind=kind):
            for dest in range(32):
                out_ref[dest, 128:ROWS, :] = slab_of(tail_lines(kind, dest))

    @pl.when(me == 31)
    def _():
        for dest in range(32):
            out_ref[dest, 128:ROWS, :] = slab_of([(0, 6, 6 * (dest // 4), 1)])


def spread(params, me):
    flat = jnp.pad(params, (48 * 128, 4224 * 128 - 48 * 128 - params.shape[0])).reshape(4224, 128)
    return pl.pallas_call(
        spread_kernel,
        out_shape=jax.ShapeDtypeStruct((32, ROWS, 128), jnp.bfloat16),
        in_specs=[
            pl.BlockSpec(memory_space=pltpu.SMEM),
            pl.BlockSpec(memory_space=pltpu.VMEM),
        ],
        out_specs=pl.BlockSpec(memory_space=pltpu.VMEM),
        scratch_shapes=[pltpu.VMEM((LINES + TAIL, 128), jnp.float32)],
        compiler_params=vmem(12),
        name="spread",
    )(me, flat)


def collect_kernel(me_ref, piece_ref, out_ref, lines_ref):
    me = me_ref[0]
    odd = lax.rem(me, 2) == 1
    lines_ref[LINES:, :] = jnp.zeros((TAIL, 128), jnp.float32)
    for kind in range(3):

        @pl.when(is_kind(me, kind))
        def _(kind=kind):
            for dest in range(32):
                for half, (first, stride) in enumerate(piece_lines(kind, dest)):
                    rows = piece_ref[dest, 64 * half : 64 * half + 64, :].astype(jnp.float32)
                    lines_ref[pl.ds(first, 64, stride), :] = rows

    for kind in range(3):

        @pl.when(is_kind(me + 1, kind))
        def _(kind=kind):
            for dest in range(32):
                slab = piece_ref[dest, 128:ROWS, :].astype(jnp.float32)
                for at, count, first, stride in tail_lines(kind, dest):
                    for k in range(count):
                        line = LINES + first + k * stride
                        lines_ref[line : line + 1, :] = slab[at + k : at + k + 1, :]

    @pl.when(me == 31)
    def _():
        for place in range(8):
            total = piece_ref[4 * place, 128:ROWS, :].astype(jnp.float32)
            for member in range(1, 4):
                total = total + piece_ref[4 * place + member, 128:ROWS, :].astype(jnp.float32)
            for k in range(6):
                line = LINES + 6 * place + k
                lines_ref[line : line + 1, :] = total[k : k + 1, :]

    start = (3 * me) // 2
    lane = lax.broadcasted_iota(jnp.int32, (24, 128), 1)

    def shift(step, carry):
        here = lines_ref[pl.ds(start + step * 24, 24), :]
        after = lines_ref[pl.ds(start + step * 24 + 1, 24), :]
        mixed = jnp.where(lane < 64, pltpu.roll(here, 64, 1), pltpu.roll(after, 64, 1))
        out_ref[pl.ds(pl.multiple_of(step * 24, 8), 24), :] = jnp.where(odd, mixed, here)
        return carry

    lax.fori_loop(0, 4104 // 24, shift, 0, unroll=9)


def collect(pieces, me, count):
    lines = pl.pallas_call(
        collect_kernel,
        out_shape=jax.ShapeDtypeStruct((4104, 128), jnp.float32),
        in_specs=[
            pl.BlockSpec(memory_space=pltpu.SMEM),
            pl.BlockSpec(memory_space=pltpu.VMEM),
        ],
        out_specs=pl.BlockSpec(memory_space=pltpu.VMEM),
        scratch_shapes=[pltpu.VMEM((LINES + TAIL, 128), jnp.float32)],
        compiler_params=vmem(12),
        name="collect",
    )(me, pieces)
    return lines.reshape(-1)[:count]


def swap_halves(rows):
    lane = lax.broadcasted_iota(jnp.int32, rows.shape, 1)
    return jnp.where(
        lax.rem(lane, 64) < 32, pltpu.roll(rows, 96, 1), pltpu.roll(rows, 32, 1)
    )


def turn(rows, cosine, signed_sine):
    parts = []
    for at in range(0, rows.shape[1], 128):
        part = rows[:, at : at + 128]
        parts.append(part * cosine + swap_halves(part) * signed_sine)
    return jnp.concatenate(parts, axis=1)


def clip_of(length_ref, frame):
    first = length_ref[0, 0]
    return (frame >= first).astype(jnp.int32) + (frame >= first + length_ref[0, 1]).astype(jnp.int32)


def mask_of(length_ref, block):
    row = lax.broadcasted_iota(jnp.int32, (256, 384), 0) + 256 * block
    key = lax.broadcasted_iota(jnp.int32, (256, 384), 1) + 128 * block
    own = clip_of(length_ref, lax.broadcasted_iota(jnp.int32, (256, 1), 0) + 256 * block)
    others = clip_of(length_ref, lax.broadcasted_iota(jnp.int32, (1, 384), 1) + 128 * block)
    return (jnp.abs(row - key) < WINDOW) & (own == others), own != 1


def nt(left, right):
    return lax.dot_general(left, right, (((1,), (1,)), ((), ())), preferred_element_type=jnp.float32)


def tn(left, right):
    return lax.dot_general(left, right, (((0,), (0,)), ((), ())), preferred_element_type=jnp.float32)


def nn(left, right):
    return jnp.dot(left, right, preferred_element_type=jnp.float32)


def cost(flops, moved):
    return pl.CostEstimate(flops=flops, bytes_accessed=moved, transcendentals=0)


def fix_kernel(piece_ref, first_ref, second_ref, third_ref):
    for source in range(32):
        out, at = (first_ref, source) if source < 8 else (second_ref, source - 8) if source < 24 else (third_ref, source - 24)
        out[128 * at : 128 * at + 128, :] = piece_ref[source, :128, :]
        if source:
            slab = piece_ref[source - 1, 128:ROWS, :].astype(jnp.float32)
            for half in range(2):
                rows = piece_ref[source, 64 * half : 64 * half + 16, :].astype(jnp.float32)
                extra = jnp.concatenate([slab[8 * half : 8 * half + 8], jnp.zeros((8, 128), jnp.float32)])
                out[128 * at + 64 * half : 128 * at + 64 * half + 16, :] = (rows + extra).astype(jnp.bfloat16)
    first_ref[1024:, :] = piece_ref[31, 128:ROWS, :]


def fix(pieces):
    return pl.pallas_call(
        fix_kernel,
        out_shape=tuple(jax.ShapeDtypeStruct((n, 128), jnp.bfloat16) for n in (1024 + SLAB, 2048, 1024)),
        in_specs=[WHOLE],
        out_specs=(WHOLE,) * 3,
        compiler_params=vmem(12),
        cost_estimate=cost(0, 1 << 22),
        name="fix",
    )(pieces)


def in_order(refs, seq, half, second):
    mine, other = refs[2 * seq], refs[2 * seq + 1]
    return jnp.where(lax.rem(second, 2) == half, mine[...], other[...])


def ring_parts(me_ref, refs):
    me = me_ref[0]
    parts = [(ring_place(me, 0), refs[0], None)]
    for step in range(1, 4):
        parts += [(ring_place(me, 8 - step), refs[2 * step - 1], None), (ring_place(me, step), refs[2 * step], None)]
    half = refs[7].shape[0]
    last = ring_place(me, 4)
    return parts + [(last, refs[7], (0, half)), (last, refs[8], (half, half + refs[8].shape[0]))]


def copy_all(pairs, done):
    copies = [pltpu.make_async_copy(source, target, done.at[k]) for k, (source, target) in enumerate(pairs)]
    for copy in copies:
        copy.start()
    for copy in copies:
        copy.wait()


def join_first_kernel(me_ref, *refs):
    blocks, (qkv_ref, out_ref, vec_ref, lines_ref, _) = refs[:9], refs[9:]
    for place, block, rows in ring_parts(me_ref, blocks):
        lo, hi = rows or (0, 1024 + SLAB)
        for at, end, ref in ((0, 768, qkv_ref), (768, 1024, out_ref), (1024, 1024 + SLAB, lines_ref)):
            first, last = max(at, lo), min(end, hi)
            if first < last:
                ref[place, first - at : last - at, :] = block[first - lo : last - lo, :]
    slabs = [lines_ref[place].astype(jnp.float32) for place in range(8)]
    for v in range(6):
        for k in range(8):
            line = 8 * v + k
            vec_ref[v : v + 1, 128 * k : 128 * k + 128] = slabs[line // 6][line % 6 : line % 6 + 1]


def join_gate_up_kernel(which, me_ref, *refs):
    blocks, (out_ref, done) = refs[:9], refs[-2:]
    pairs = []
    for place, block, rows in ring_parts(me_ref, blocks)[which]:
        lo, hi = rows or (0, 16)
        for half in range(2):
            at = pl.multiple_of(256 * half + 128 * lax.rem(place, 2), 128)
            pairs.append((block.at[:, half], out_ref.at[lax.div(place, 2), lo:hi, :, pl.ds(at, 128)]))
    copy_all(pairs, done)


def join_down_kernel(which, me_ref, *refs):
    blocks, (out_ref, done) = refs[:9], refs[-2:]
    pairs = []
    for place, block, rows in ring_parts(me_ref, blocks)[which]:
        lo, hi = rows or (0, 1024)
        pairs.append((block, out_ref.at[lo:hi, pl.ds(pl.multiple_of(128 * place, 128), 128)]))
    copy_all(pairs, done)


def join_out_kernel(*refs):
    w_ref = refs[4]
    for k in range(4):
        for place in range(8):
            w_ref[256 * k : 256 * k + 256, 128 * place : 128 * place + 128] = refs[k][place]


def join_out(parts):
    return pl.pallas_call(
        join_out_kernel,
        out_shape=jax.ShapeDtypeStruct((D, D), jnp.bfloat16),
        in_specs=[WHOLE] * 4,
        out_specs=WHOLE,
        compiler_params=vmem(12),
        cost_estimate=cost(0, 4 << 20),
        name="join_out",
    )(*parts)


def join(kernel, me, blocks, out_shape, name, scratch=(), space=WHOLE):
    if space is HBM:
        blocks = [pltpu.with_memory_space_constraint(block, pltpu.HBM) for block in blocks]
    return pl.pallas_call(
        kernel,
        out_shape=out_shape,
        in_specs=[SCALAR] + [space] * 9,
        out_specs=jax.tree.map(lambda _: WHOLE, out_shape),
        scratch_shapes=list(scratch) + [pltpu.SemaphoreType.DMA((32,))],
        compiler_params=vmem(12),
        cost_estimate=cost(0, 4 << 20),
        name=name,
    )(me, *blocks)


def join_rest_kernel(kernel, me_ref, last_ref, end_ref, _, out_ref, done):
    kernel(slice(7, 9), me_ref, *([last_ref] * 8 + [end_ref]), out_ref, done)


def join_twice(kernel, me, blocks, out_shape, name):
    early = [pltpu.with_memory_space_constraint(block, pltpu.HBM) for block in blocks[:7]]
    whole = pl.pallas_call(
        lambda me_ref, *refs: kernel(slice(0, 7), me_ref, *refs[:7], refs[6], refs[6], *refs[7:]),
        out_shape=out_shape,
        in_specs=[SCALAR] + [HBM] * 7,
        out_specs=WHOLE,
        scratch_shapes=[pltpu.SemaphoreType.DMA((32,))],
        compiler_params=vmem(12),
        cost_estimate=cost(0, 4 << 20),
        name=name,
    )(me, *early)
    last = after(tuple(blocks[7:]), whole)
    return pl.pallas_call(
        functools.partial(join_rest_kernel, kernel),
        out_shape=out_shape,
        in_specs=[SCALAR, ANY, ANY, WHOLE],
        out_specs=WHOLE,
        input_output_aliases={3: 0},
        scratch_shapes=[pltpu.SemaphoreType.DMA((32,))],
        compiler_params=vmem(12),
        cost_estimate=cost(0, 4 << 20),
        name=name + "_rest",
    )(me, *last, whole)


def prep_kernel(y_ref, own_ref, pair_ref, far_ref, last_ref, x_ref, mean_ref, inv_ref):
    for block in range(4):
        rows = slice(256 * block, 256 * block + 256)
        x_low = in_order((own_ref, pair_ref, far_ref, last_ref), block // 2, block % 2, y_ref[0])
        x_ref[rows, :] = x_low
        x_rows = x_low.astype(jnp.float32)
        mean = jnp.mean(x_rows, axis=1, keepdims=True)
        centered = x_rows - mean
        mean_ref[rows, :] = mean
        inv_ref[rows, :] = lax.rsqrt(jnp.mean(centered * centered, axis=1, keepdims=True) + eps_norm)


def prep(second, rows):
    return pl.pallas_call(
        prep_kernel,
        out_shape=(
            jax.ShapeDtypeStruct((1024, D), jnp.bfloat16),
            jax.ShapeDtypeStruct((1024, 1), jnp.float32),
            jax.ShapeDtypeStruct((1024, 1), jnp.float32),
        ),
        in_specs=[SCALAR] + [WHOLE] * 4,
        out_specs=(WHOLE,) * 3,
        compiler_params=vmem(12),
        cost_estimate=cost(1 << 24, 5 << 20),
        name="prep",
    )(second, *rows)


def front_kernel(
    x_ref, mean_ref, inv_ref, ring_ref, vec_ref, order_ref, cos_ref, sin_ref, length_ref, far_length_ref,
    a_out, w_out, low_out, attn_ref, lse_out,
    a_ref, w_ref, low_ref, lse_ref, done,
):
    copies = [
        pltpu.make_async_copy(ref, out, done.at[k])
        for k, (ref, out) in enumerate(((w_ref, w_out), (a_ref, a_out), (low_ref, low_out), (lse_ref, lse_out)))
    ]
    gain, bias = vec_ref[0:1, :], vec_ref[1:2, :]
    for block in range(8):
        parts = []
        for chunk in range(6 * block, 6 * block + 6):
            at = 128 * (chunk // 8)
            parts.append(
                jnp.concatenate(
                    [ring_ref[chunk % 8, at : at + 64, :], ring_ref[chunk % 8, at + 64 : at + 128, :]], axis=1
                )
            )
        rows = nn(order_ref[...], jnp.concatenate(parts, axis=0)).astype(jnp.bfloat16)
        for third in range(3):
            w_ref[128 * block : 128 * block + 128, OWN * third : OWN * third + OWN] = rows[
                128 * third : 128 * third + 128
            ]
    copies[0].start()
    for block in range(4):
        rows = slice(256 * block, 256 * block + 256)
        seq, at = block // 2, 256 * (block % 2)
        normed = (x_ref[rows, :].astype(jnp.float32) - mean_ref[rows, :]) * inv_ref[rows, :]
        a_low = (normed * gain + bias).astype(jnp.bfloat16)
        a_ref[rows, :] = a_low
        qkv = nn(a_low, w_ref[...])
        cosine, sine = cos_ref[seq, at : at + 256, :], sin_ref[seq, at : at + 256, :]
        low_ref[rows, : 2 * OWN] = turn(qkv[:, : 2 * OWN], cosine, sine).astype(jnp.bfloat16)
        low_ref[rows, 2 * OWN :] = qkv[:, 2 * OWN :].astype(jnp.bfloat16)
    copies[1].start()
    copies[2].start()
    for seq in range(2):
        for block in range(2):
            at = 512 * seq + 256 * block
            rows = slice(at, at + 256)
            keys = slice(512 * seq + 128 * block, 512 * seq + 128 * block + 384)
            mask, keep = mask_of((length_ref, far_length_ref)[seq], block)
            heads, sums = [], []
            for head in range(4):
                lane = 64 * head
                query = low_ref[rows, lane : lane + 64]
                key = low_ref[keys, OWN + lane : OWN + lane + 64]
                value = low_ref[keys, 2 * OWN + lane : 2 * OWN + lane + 64]
                masked = jnp.where(mask, nt(query, key) * SCALE, neg_large)
                top = jnp.max(masked, axis=1, keepdims=True)
                weight = jnp.exp(masked - top)
                total = jnp.sum(weight, axis=1, keepdims=True)
                probs = (weight * (1.0 / total)).astype(jnp.bfloat16)
                heads.append(jnp.where(keep, nn(probs, value), 0.0))
                sums.append(top + jnp.log(total))
            attn_ref[rows, :] = jnp.concatenate(heads, axis=1).astype(jnp.bfloat16)
            lse_ref[rows, :] = jnp.concatenate(sums, axis=1)
    copies[3].start()
    for copy in copies:
        copy.wait()


def front(x_all, mean, inv, ring, vectors, order, cosine, sine, lengths):
    return pl.pallas_call(
        front_kernel,
        out_shape=(
            pltpu.HBM((1024, D), jnp.bfloat16),
            pltpu.HBM((D, 3 * OWN), jnp.bfloat16),
            pltpu.HBM((1024, 3 * OWN), jnp.bfloat16),
            jax.ShapeDtypeStruct((1024, OWN), jnp.bfloat16),
            pltpu.HBM((1024, 4), jnp.float32),
        ),
        in_specs=[WHOLE] * 8 + [SCALAR] * 2,
        out_specs=(HBM, HBM, HBM, WHOLE, HBM),
        scratch_shapes=[
            pltpu.VMEM((1024, D), jnp.bfloat16),
            pltpu.VMEM((D, 3 * OWN), jnp.bfloat16),
            pltpu.VMEM((1024, 3 * OWN), jnp.bfloat16),
            pltpu.VMEM((1024, 4), jnp.float32),
            pltpu.SemaphoreType.DMA((4,)),
        ],
        compiler_params=vmem(14),
        cost_estimate=cost(12 << 30, 8 << 20),
        name="front",
    )(x_all, mean, inv, ring, vectors, order, cosine, sine, *lengths)


def mix_kernel(x_ref, own_ref, pair_ref, far_ref, last_ref, w_ref, vec_ref, c_ref, branch_ref):
    for block in range(4):
        rows = slice(256 * block, 256 * block + 256)
        other = (block + 2) % 4
        far = slice(256 * other, 256 * other + 256)
        attn = jnp.concatenate([own_ref[rows, :], pair_ref[rows, :], far_ref[far, :], last_ref[far, :]], axis=1)
        branch = nn(attn, w_ref[...])
        normed, _ = normed_of(x_ref[rows, :].astype(jnp.float32) + vec_ref[4:5, :] * branch)
        c_ref[rows, :] = (normed * vec_ref[2:3, :] + vec_ref[3:4, :]).astype(jnp.bfloat16)
        if block < 2:
            branch_ref[rows, :] = branch


def mix(x_all, attn, w_out, vectors):
    return pl.pallas_call(
        mix_kernel,
        out_shape=(
            pltpu.VMEM((1024, D), jnp.bfloat16),
            jax.ShapeDtypeStruct((512, D), jnp.float32),
        ),
        in_specs=[WHOLE] * 7,
        out_specs=(WHOLE, WHOLE),
        compiler_params=vmem(12),
        cost_estimate=cost(3 << 30, 10 << 20),
        name="mix",
    )(x_all, *attn, w_out, vectors)


def gate_kernel(c_ref, w_ref, gate_up_ref, hidden_ref):
    for block in range(4):
        rows = slice(256 * block, 256 * block + 256)
        for chunk in range(4):
            both = nn(c_ref[rows, :], w_ref[chunk])
            gate_up_ref[chunk, rows, :] = both
            gate, up = both[:, :256], both[:, 256:]
            hidden_ref[rows, 256 * chunk : 256 * chunk + 256] = (gate * jax.nn.sigmoid(gate) * up).astype(
                jnp.bfloat16
            )


def gate_step(c_low, w_gate_up):
    return pl.pallas_call(
        gate_kernel,
        out_shape=(
            jax.ShapeDtypeStruct((4, 1024, 512), jnp.float32),
            jax.ShapeDtypeStruct((1024, 1024), jnp.bfloat16),
        ),
        in_specs=[WHOLE] * 2,
        out_specs=(WHOLE, WHOLE),
        compiler_params=vmem(12),
        cost_estimate=cost(5 << 30, 16 << 20),
        name="gate",
    )(c_low, w_gate_up)


def down_grad_kernel(me_ref, hidden_ref, own_ref, pair_ref, far_ref, last_ref, vec_ref, g_ref, d_mlp_ref):
    for block in range(4):
        rows = in_order((own_ref, pair_ref, far_ref, last_ref), block // 2, block % 2, me_ref[0])
        d_mlp_ref[256 * block : 256 * block + 256, :] = (rows.astype(jnp.float32) * vec_ref[5:6, :]).astype(
            jnp.bfloat16
        )
    for source in range(0, 8, 2):
        g_down = tn(hidden_ref[:, 128 * source : 128 * source + 256], d_mlp_ref[...]).astype(jnp.bfloat16)
        for pair in range(2):
            for place in range(8):
                at = 128 * (source + pair)
                g_ref[place, at : at + 128, :] = g_down[128 * pair : 128 * pair + 128, 128 * place : 128 * place + 128]


def down_grad(me, hidden, cot, vectors):
    return pl.pallas_call(
        down_grad_kernel,
        out_shape=(
            jax.ShapeDtypeStruct((8, 1024, 128), jnp.bfloat16),
            jax.ShapeDtypeStruct((1024, D), jnp.bfloat16),
        ),
        in_specs=[SCALAR] + [WHOLE] * 6,
        out_specs=(WHOLE, WHOLE),
        compiler_params=vmem(12),
        cost_estimate=cost(3 << 30, 8 << 20),
        name="down_grad",
    )(me, hidden, *cot, vectors)


def put_rows(me, whole_ref, refs, done=None):
    y = lax.rem(me, 2)
    copies = []
    for k, (ref, half) in enumerate(zip(refs, (1 - y, y, 1 - y, y))):
        rows = pl.ds(pl.multiple_of(512 * (k // 2) + 256 * half, 256), 256)
        if done is not None and k < 2:
            copies.append(pltpu.make_async_copy(whole_ref.at[rows, :], ref, done.at[k]))
            copies[-1].start()
        else:
            ref[...] = whole_ref[rows, :].astype(ref.dtype)
    for copy in copies:
        copy.wait()


PARTS = tuple(jax.ShapeDtypeStruct((256, D), t) for t in (jnp.float32, jnp.float32, jnp.bfloat16, jnp.bfloat16))


def hidden_back_kernel(gate_up_ref, d_mlp_ref, w_ref, d_both_ref):
    for block in range(4):
        rows = slice(256 * block, 256 * block + 256)
        for chunk in range(4):
            d_hidden = nt(d_mlp_ref[rows, :], w_ref[256 * chunk : 256 * chunk + 256, :])
            gate, up = gate_up_ref[chunk, rows, :256], gate_up_ref[chunk, rows, 256:]
            sig = jax.nn.sigmoid(gate)
            d_both_ref[chunk, rows, :256] = (d_hidden * up * sig * (1.0 + gate * (1.0 - sig))).astype(jnp.bfloat16)
            d_both_ref[chunk, rows, 256:] = (d_hidden * gate * sig).astype(jnp.bfloat16)


def hidden_back(gate_up, d_mlp, w_down):
    return pl.pallas_call(
        hidden_back_kernel,
        out_shape=jax.ShapeDtypeStruct((4, 1024, 512), jnp.bfloat16),
        in_specs=[WHOLE] * 3,
        out_specs=WHOLE,
        compiler_params=vmem(12),
        cost_estimate=cost(4 << 30, 18 << 20),
        name="hidden_back",
    )(gate_up, d_mlp, w_down)


def norm_back_kernel(y_ref, d_both_ref, w_ref, near_sent_ref, near_ref, far_sent_ref, far_ref, d_c_ref):
    for block in range(4):
        rows = slice(256 * block, 256 * block + 256)
        d_c = nt(d_both_ref[0, rows, :], w_ref[0])
        for chunk in range(1, 4):
            d_c += nt(d_both_ref[chunk, rows, :], w_ref[chunk])
        d_c_ref[rows, :] = d_c
    put_rows(y_ref[0], d_c_ref, (near_sent_ref, near_ref, far_sent_ref, far_ref))


def norm_back(second, d_both, w_gate_up):
    return pl.pallas_call(
        norm_back_kernel,
        out_shape=PARTS,
        in_specs=[SCALAR, WHOLE, WHOLE],
        scratch_shapes=[pltpu.VMEM((1024, D), jnp.float32)],
        out_specs=(WHOLE,) * 4,
        compiler_params=vmem(12),
        cost_estimate=cost(5 << 30, 12 << 20),
        name="norm_back",
    )(second, d_both, w_gate_up)


def gate_grad_kernel(c_ref, d_both_ref, g_ref):
    for chunk in range(4):
        for block in range(4):
            grad = tn(c_ref[:, 256 * block : 256 * block + 256], d_both_ref[chunk]).astype(jnp.bfloat16)
            for part in range(4):
                source = 4 * block + part
                for pair in range(2):
                    for half in range(2):
                        at = 256 * half + 128 * pair
                        first = 128 * source + 64 * half
                        g_ref[2 * chunk + pair, first : first + 64, :] = grad[64 * part : 64 * part + 64, at : at + 128]


def gate_grad(c_low, d_both):
    return pl.pallas_call(
        gate_grad_kernel,
        out_shape=jax.ShapeDtypeStruct((8, 2048, 128), jnp.bfloat16),
        in_specs=[WHOLE] * 2,
        out_specs=WHOLE,
        compiler_params=vmem(12),
        cost_estimate=cost(5 << 30, 10 << 20),
        name="gate_grad",
    )(c_low, d_both)


def out_kernel(
    y_ref, hidden_ref, w_ref, own_ref, pair_ref, last_ref, end_ref,
    near_sent_ref, near_ref, far_sent_ref, far_ref, g_scale_ref,
    branch_ref, done,
):
    total = jnp.zeros((1, D), jnp.float32)
    for block in range(4):
        rows = slice(256 * block, 256 * block + 256)
        branch = nn(hidden_ref[rows, :], w_ref[...])
        branch_ref[rows, :] = branch
        cot = in_order((own_ref, pair_ref, last_ref, end_ref), block // 2, block % 2, y_ref[0])
        total += jnp.sum(cot.astype(jnp.float32) * branch, axis=0, keepdims=True)
    g_scale_ref[...] = total
    put_rows(y_ref[0], branch_ref, (near_sent_ref, near_ref, far_sent_ref, far_ref), done)


def out_step(second, hidden, down, cot):
    return pl.pallas_call(
        out_kernel,
        out_shape=(pltpu.HBM((256, D), jnp.float32),) * 2 + PARTS[2:] + (jax.ShapeDtypeStruct((1, D), jnp.float32),),
        in_specs=[SCALAR] + [WHOLE] * 6,
        scratch_shapes=[pltpu.VMEM((1024, D), jnp.float32), pltpu.SemaphoreType.DMA((2,))],
        out_specs=(HBM, HBM, WHOLE, WHOLE, WHOLE),
        compiler_params=vmem(12),
        cost_estimate=cost(3 << 30, 10 << 20),
        name="out",
    )(second, hidden, down, *cot)


def attend_back_kernel(
    y_ref, own_ref, pair_ref, far_ref, last_ref, ring_ref, attn_ref, low_ref, lse_ref, cos_ref, sin_ref,
    length_ref, far_length_ref,
    d_qkv_ref, g_ref,
    d_branch_ref, w_out_ref, key_ref, value_ref,
):
    for place in range(8):
        w_out_ref[:, 128 * place : 128 * place + 128] = ring_ref[place]
    for block in range(4):
        d_branch_ref[256 * block : 256 * block + 256, :] = in_order(
            (own_ref, pair_ref, far_ref, last_ref), block // 2, block % 2, y_ref[0]
        )
    g_out = tn(attn_ref[...], d_branch_ref[...]).astype(jnp.bfloat16)
    for place in range(8):
        g_ref[place] = g_out[:, 128 * place : 128 * place + 128]
    for seq in range(2):
        key_ref[...] = jnp.zeros_like(key_ref)
        value_ref[...] = jnp.zeros_like(value_ref)
        cosine, sine = cos_ref[seq], -sin_ref[seq]
        for block in range(2):
            at = 512 * seq + 256 * block
            rows = slice(at, at + 256)
            span = slice(128 * block, 128 * block + 384)
            keys = slice(512 * seq + 128 * block, 512 * seq + 128 * block + 384)
            mask, keep = mask_of((length_ref, far_length_ref)[seq], block)
            d_attn_all = nt(d_branch_ref[rows, :], w_out_ref[...]).astype(jnp.bfloat16)
            d_attn_all = jnp.where(keep, d_attn_all, jnp.zeros_like(d_attn_all))
            d_queries, d_keys, d_values = [], [], []
            for head in range(4):
                lane = 64 * head
                query = low_ref[rows, lane : lane + 64]
                key = low_ref[keys, OWN + lane : OWN + lane + 64]
                value = low_ref[keys, 2 * OWN + lane : 2 * OWN + lane + 64]
                d_attn = d_attn_all[:, lane : lane + 64]
                masked = jnp.where(mask, nt(query, key) * SCALE, neg_large)
                probs = jnp.exp(masked - lse_ref[rows, head : head + 1])
                d_values.append(tn(probs.astype(jnp.bfloat16), d_attn))
                d_probs = nt(d_attn, value)
                inner = jnp.sum(probs * d_probs, axis=1, keepdims=True)
                d_scores = (probs * (d_probs - inner)).astype(jnp.bfloat16)
                d_queries.append(nn(d_scores, key) * SCALE)
                d_keys.append(tn(d_scores, query) * SCALE)
            part = slice(256 * block, 256 * block + 256)
            d_query = turn(jnp.concatenate(d_queries, axis=1), cosine[part], sine[part])
            d_qkv_ref[rows, :OWN] = d_query.astype(jnp.bfloat16)
            key_ref[span, :] += jnp.concatenate(d_keys, axis=1)
            value_ref[span, :] += jnp.concatenate(d_values, axis=1)
        whole = slice(512 * seq, 512 * seq + 512)
        d_qkv_ref[whole, OWN : 2 * OWN] = turn(key_ref[...], cosine, sine).astype(jnp.bfloat16)
        d_qkv_ref[whole, 2 * OWN :] = value_ref[...].astype(jnp.bfloat16)


def attention_back(me, d_branch, ring, attn, low, lse, cosine, sine, lengths):
    return pl.pallas_call(
        attend_back_kernel,
        out_shape=(
            jax.ShapeDtypeStruct((1024, 3 * OWN), jnp.bfloat16),
            jax.ShapeDtypeStruct((8, OWN, 128), jnp.bfloat16),
        ),
        in_specs=[SCALAR] + [WHOLE] * 10 + [SCALAR] * 2,
        out_specs=(WHOLE, WHOLE),
        scratch_shapes=[
            pltpu.VMEM((1024, D), jnp.bfloat16),
            pltpu.VMEM((OWN, D), jnp.bfloat16),
            pltpu.VMEM((512, OWN), jnp.float32),
            pltpu.VMEM((512, OWN), jnp.float32),
        ],
        compiler_params=vmem(12),
        cost_estimate=cost(12 << 30, 10 << 20),
        name="attend_back",
    )(me, *d_branch, ring, attn, low, lse, cosine, sine, *lengths)


def grad_kernel(
    y_ref, a_ref, w_ref, order_ref, d_qkv_ref, g_out_ref, x_ref, mean_ref, inv_ref, small_ref,
    g_ref, near_sent_ref, near_ref, far_sent_ref, far_ref,
    d_a_ref,
):
    g_gain, g_bias = jnp.zeros((1, D), jnp.float32), jnp.zeros((1, D), jnp.float32)
    for block in range(4):
        rows = slice(256 * block, 256 * block + 256)
        d_a = nt(d_qkv_ref[rows, :], w_ref[...])
        normed = (x_ref[rows, :].astype(jnp.float32) - mean_ref[rows, :]) * inv_ref[rows, :]
        g_gain += jnp.sum(d_a * normed, axis=0, keepdims=True)
        g_bias += jnp.sum(d_a, axis=0, keepdims=True)
        d_a_ref[rows, :] = d_a
    put_rows(y_ref[0], d_a_ref, (near_sent_ref, near_ref, far_sent_ref, far_ref))
    for block in range(8):
        grad = tn(a_ref[:, 128 * block : 128 * block + 128], d_qkv_ref[...]).astype(jnp.bfloat16)
        grad = jnp.concatenate([grad[:, OWN * third : OWN * third + OWN] for third in range(3)], axis=0)
        grad = tn(order_ref[...], grad).astype(jnp.bfloat16)
        for part in range(6):
            chunk = 6 * block + part
            at = 128 * (chunk // 8)
            g_ref[chunk % 8, at : at + 64, :] = grad[64 * part : 64 * part + 64, :128]
            g_ref[chunk % 8, at + 64 : at + 128, :] = grad[64 * part : 64 * part + 64, 128:]
    vectors = [g_gain, g_bias] + [small_ref[k : k + 1, :] for k in range(4)]
    lines = [v[:, 128 * k : 128 * k + 128] for v in vectors for k in range(8)]
    for place in range(8):
        g_ref[place, 768:1024, :] = g_out_ref[place]
        rows = lines[6 * place : 6 * place + 6] + [jnp.zeros((SLAB - 6, 128), jnp.float32)]
        g_ref[place, 1024:, :] = jnp.concatenate(rows, axis=0).astype(jnp.bfloat16)


def grad_step(second, a_low, w_qkv, order, d_qkv, g_out, x_all, mean, inv, small):
    return pl.pallas_call(
        grad_kernel,
        out_shape=(jax.ShapeDtypeStruct((8, 1024 + SLAB, 128), jnp.bfloat16),) + PARTS,
        in_specs=[SCALAR] + [WHOLE] * 9,
        scratch_shapes=[pltpu.VMEM((1024, D), jnp.float32)],
        out_specs=(WHOLE,) * 5,
        compiler_params=vmem(12),
        cost_estimate=cost(8 << 30, 12 << 20),
        name="grad",
    )(second, a_low, w_qkv, order, d_qkv, g_out, x_all, mean, inv, small)


def after(values, *others):
    if isinstance(values, tuple):
        return lax.optimization_barrier(values + others)[: len(values)]
    return lax.optimization_barrier((values,) + others)[0]


def both_ways(ahead, back):
    return lax.optimization_barrier((lax.ppermute(ahead, GROUP, AHEAD), lax.ppermute(back, GROUP, BACK)))


class Gather:
    def __init__(self, block):
        self.blocks = [block]
        self.next = (block, block)
        self.half = (block.shape[0] // 2 + 15) // 16 * 16
        self.count = 0

    def step(self, *waits, hold=()):
        self.count += 1
        ahead, back = after(self.next, *waits) if waits else self.next
        if self.count == 4:
            ahead, back = ahead[: self.half], back[self.half :]
        self.next = after(both_ways(ahead, back), *hold)
        self.blocks += self.next
        return self.next


class Scatter:
    def __init__(self, blocks, me):
        self.blocks, self.me = blocks, me
        self.rows = blocks.shape[1]
        self.half = (self.rows // 2 + 15) // 16 * 16
        self.count = 0
        self.next = (self.get(4, 0, self.half), self.get(4, self.half))

    def get(self, step, lo=0, hi=None):
        hi = self.rows if hi is None else hi
        at = (ring_place(self.me, step % 8), 0 * self.me + lo, 0 * self.me)
        return lax.dynamic_slice(self.blocks, at, (1, hi - lo, 128))[0]

    def step(self, *waits, hold=()):
        self.count += 1
        ahead, back = came = after(both_ways(*(after(self.next, *waits) if waits else self.next)), *hold)

        def add(moved, own):
            return (moved.astype(jnp.float32) + own.astype(jnp.float32)).astype(jnp.bfloat16)

        if self.count == 1:
            half = self.half
            ahead = jnp.concatenate([add(ahead, self.get(3, 0, half)), self.get(3, half)])
            back = jnp.concatenate([self.get(5, 0, half), add(back, self.get(5, half))])
        elif self.count < 4:
            ahead, back = add(ahead, self.get(4 - self.count)), add(back, self.get(4 + self.count))
        else:
            total = self.get(0).astype(jnp.float32) + ahead.astype(jnp.float32) + back.astype(jnp.float32)
            self.total = total.astype(jnp.bfloat16)
        self.next = (ahead, back)
        return came


def to_pair(rows, *waits):
    rows = after(rows, *waits) if waits else rows
    return rows, lax.ppermute(rows, "y", SWAP)


def to_group(pair, *waits):
    pair = after(tuple(pair), *waits) if waits else pair
    return tuple(pair) + tuple(lax.ppermute(rows, "c", SWAP) for rows in pair)


def half_sum(near_sent, near, far_sent, far):
    sent = near_sent + lax.ppermute(far_sent, "c", SWAP).astype(jnp.float32)
    kept = near + lax.ppermute(far, "c", SWAP).astype(jnp.float32)
    return lax.optimization_barrier((sent.astype(jnp.bfloat16), kept))


def full_sum(sent, kept):
    return kept + lax.ppermute(sent, "y", SWAP).astype(jnp.float32)


def normed_of(rows):
    centered = rows - jnp.mean(rows, axis=-1, keepdims=True)
    inv_scale = lax.rsqrt(jnp.mean(centered * centered, axis=-1, keepdims=True) + eps_norm)
    return centered * inv_scale, inv_scale


def norm_rows_back(out_grad, normed, inv_scale, gain):
    inner = out_grad * gain
    return inv_scale * (
        inner
        - jnp.mean(inner, axis=-1, keepdims=True)
        - normed * jnp.mean(inner * normed, axis=-1, keepdims=True)
    )


def fast_body(frames, cotangent, clip_lengths, params, first_moment, second_moment):
    z, x, c, y = (lax.axis_index(axis) for axis in EVERY)
    device = (((z * 2 + x) * 2 + c) * 2 + y).astype(jnp.int32)
    me = device[None]
    lengths = (clip_lengths, lax.ppermute(clip_lengths, "c", SWAP))
    order = np.zeros((384, 384), np.float32)
    for row in range(384):
        order[(row % 3) * 128 + row // 3, row] = 1.0
    order = jnp.asarray(order, jnp.bfloat16)

    pieces = spread(params, me)
    pieces = lax.all_to_all(pieces, EVERY, split_axis=0, concat_axis=0, tiled=True)
    first_piece, second_piece, third_piece = fix(pieces)
    first, second, third = Gather(first_piece), Gather(second_piece), Gather(third_piece)
    frames_pair = to_pair(frames[0], first_piece)
    came = first.step()
    cot_pair = to_pair(cotangent[0], frames_pair[1])
    lengths = after(lengths, first_piece)
    both = jnp.concatenate(lengths)
    frame = jnp.arange(512, dtype=jnp.int32)
    starts, ends = both[:, :1], both[:, :1] + both[:, 1:]
    position = jnp.where((frame >= starts) & (frame < ends), frame - starts, frame).astype(jnp.float32)
    inverse = jnp.exp(
        jnp.asarray(np.arange(128) % 32, jnp.float32) * (-2.0 * math.log(rope_base) / HEAD_DIM)
    )
    angle = position[:, :, None] * inverse
    cosine = jnp.cos(angle)
    sine = jnp.sin(angle) * jnp.asarray(np.where(np.arange(128) % 64 < 32, -1.0, 1.0), jnp.float32)
    came_second = first.step(cosine, sine)
    frames_parts = to_group(after(frames_pair, *came))
    first.step(frames_pair[1])
    x_all, mean_one, inv_one = prep(me, frames_parts)
    first.step(x_all)
    second.step(*came_second)
    ring_qkv, w_own, vectors = join(
        join_first_kernel,
        me,
        first.blocks,
        (
            jax.ShapeDtypeStruct((8, 768, 128), jnp.bfloat16),
            jax.ShapeDtypeStruct((8, OWN, 128), jnp.bfloat16),
            jax.ShapeDtypeStruct((6, D), jnp.float32),
        ),
        "join_first",
        [pltpu.VMEM((8, SLAB, 128), jnp.bfloat16)],
    )

    w_pair = to_pair(w_own)
    x_all, ring_qkv = after((x_all, ring_qkv), *second.next, cot_pair[1])
    came = second.step(ring_qkv)
    a_low, w_qkv, low, attn_own, lse = front(x_all, mean_one, inv_one, ring_qkv, vectors, order, cosine, sine, lengths)
    attn_pair = to_pair(attn_own, *came, w_pair[1])
    w_out = join_out(to_group(w_pair, attn_own))
    came = second.step(attn_own)
    attn_parts = to_group(attn_pair, w_out)
    attn_parts = attn_parts[:2] + after(attn_parts[2:], *came)
    c_low, branch_seq = mix(x_all, attn_parts, w_out, vectors)
    third.step(*attn_parts[2:])
    came = second.step(*attn_parts[2:])
    second.blocks[7:] = after(came, c_low)
    came = third.next
    blocks = [block.reshape(-1, 2, 64, 128) for block in second.blocks]
    shape = jax.ShapeDtypeStruct((4, 16, 64, 512), jnp.bfloat16)
    w_gate_up = join(functools.partial(join_gate_up_kernel, slice(0, 9)), me, blocks, shape, "join_gate_up", space=HBM)
    w_gate_up = w_gate_up.reshape(4, 1024, 512)
    cot_parts = to_group(cot_pair, c_low)
    gate_up, hidden = gate_step(after(c_low, *came), w_gate_up)
    came = third.step(c_low)
    g_down, d_mlp = down_grad(me, after(hidden, *came), cot_parts, vectors)
    third.step(hidden)
    third.step(g_down)
    shape = jax.ShapeDtypeStruct((1024, D), jnp.bfloat16)
    third.blocks[0] = after(third.blocks[0], g_down)
    w_down = join_twice(join_down_kernel, me, third.blocks, shape, "join_down")

    down = Scatter(g_down, device)
    d_both = hidden_back(gate_up, d_mlp, w_down)
    came = down.step(*third.next)
    d_both = after(d_both, *came)
    d_c_parts = norm_back(me, d_both, w_gate_up)
    came = down.step(d_both)
    d_c_sent, d_c_kept = half_sum(*after(tuple(d_c_parts), *came))
    g_gate_up = gate_grad(c_low, after(d_both, d_c_sent, d_c_kept))
    came = down.step(d_c_sent, hold=(g_gate_up,))
    gate_grads = Scatter(g_gate_up, device)

    x_own = frames[0].astype(jnp.float32)
    cot_own = cotangent[0].astype(jnp.float32)
    branch_own = jnp.where(y == 0, branch_seq[:256], branch_seq[256:])
    mid_own = x_own + vectors[4] * branch_own
    normed_two, scale_two = normed_of(mid_own)
    d_c_own = full_sum(d_c_sent, d_c_kept)
    d_mid = cot_own + norm_rows_back(d_c_own, normed_two, scale_two, vectors[2])
    d_branch_own = (d_mid * vectors[4]).astype(jnp.bfloat16)
    d_branch_pair = to_pair(d_branch_own)
    down.step(hold=(d_branch_own,))
    came = gate_grads.step(hold=(d_branch_own,))
    hidden = after(hidden, d_branch_own, *came)
    *out_parts, g_scale_mlp = out_step(me, hidden, w_down, cot_parts)
    came = gate_grads.step(d_branch_own, hold=(g_scale_mlp,))
    d_branch = to_group(d_branch_pair, *came, g_scale_mlp)
    out_sent, out_kept = half_sum(*out_parts)
    g_gain_two = jnp.sum(d_c_own * normed_two, axis=0)
    g_bias_two = jnp.sum(d_c_own, axis=0)
    g_scale_attn = jnp.sum(d_mid * branch_own, axis=0)
    small = jnp.concatenate([jnp.stack([g_gain_two, g_bias_two, g_scale_attn]), g_scale_mlp], axis=0)

    d_branch = after(d_branch, small)
    d_qkv, g_out = attention_back(me, d_branch, w_own, attn_own, low, lse, cosine, sine, lengths)
    came = gate_grads.step(*d_branch, hold=(d_qkv,))
    out_sent = after(out_sent, *d_branch)
    output = (mid_own + vectors[5] * full_sum(out_sent, out_kept)).astype(jnp.bfloat16)
    d_qkv = after(d_qkv, *came)
    g_first, *d_a_parts = grad_step(me, a_low, w_qkv, order, d_qkv, g_out, x_all, mean_one, inv_one, small)
    came = gate_grads.step(d_qkv, hold=(g_first,))
    first_grads = Scatter(after(g_first, *came), device)
    first_grads.step(output)
    d_a_sent, d_a_kept = half_sum(*d_a_parts)
    first_grads.step(d_a_sent)
    first_grads.step()
    normed_one, scale_one = normed_of(x_own)
    d_one = norm_rows_back(full_sum(d_a_sent, d_a_kept), normed_one, scale_one, vectors[0])
    frames_grad = (d_mid + d_one).astype(jnp.bfloat16)
    first_grads.step(frames_grad)
    g_first, g_gate_up, g_down = first_grads.total, gate_grads.total, down.total

    main = jnp.concatenate([g_first[:1024], g_gate_up, g_down]).reshape(32, 128, 128)
    slab = jnp.concatenate([main[1:, :8], main[1:, 64:72]], axis=1)
    slab = jnp.concatenate([slab, g_first[None, 1024:]])
    pieces = jnp.concatenate([main, slab], axis=1)
    pieces = lax.all_to_all(pieces, EVERY, split_axis=0, concat_axis=0, tiled=True)
    params_grad = collect(pieces, me, params.shape[0])
    new_params, new_first, new_second = adam_update(params, params_grad, first_moment, second_moment)
    return (output[None], frames_grad[None], params_grad, new_params, new_first, new_second)


def solution(mesh):
    def run(frames, cotangent, clip_lengths, params, first_moment, second_moment):
        fits = (
            mesh.shape["dp"] == 16
            and mesh.shape["seq"] == 2
            and frames.shape == (16, 512, D)
            and clip_lengths.shape == (16, 2)
        )
        if fits:
            over = Mesh(mesh.devices.reshape(4, 2, 2, 2), EVERY)
            rows, clips, flat = P(("z", "x", "c"), "y", None), P(("z", "x", "c"), None), P(EVERY)
        else:
            over = mesh
            rows, clips, flat = P("dp", "seq", None), P("dp", None), P(("dp", "seq"))
        step = jax.shard_map(
            fast_body if fits else body,
            mesh=over,
            in_specs=(rows, rows, clips, flat, flat, flat),
            out_specs=(rows, rows, flat, flat, flat, flat),
            check_vma=False,
        )
        return step(frames, cotangent, clip_lengths, params, first_moment, second_moment)

    return run
```

```python
import functools
import math

import jax
import jax.numpy as jnp
import numpy as np
from jax import lax
from jax.experimental import pallas as pl
from jax.experimental.pallas import tpu as pltpu
from jax.sharding import Mesh
from jax.sharding import PartitionSpec as P

D = 1024
HEADS = 16
HEAD_DIM = 64
FF = 4096
WINDOW = 128


eps_norm = 1e-05
beta_one = 0.9
beta_two = 0.99
learn_rate = 0.01
decay_rate = 0.1
eps_adam = 1e-08
adam_step = 100.0
neg_large = -1e30
rope_base = 10000.0


def padded(shard, sides, width):
    for axis, dim in sides:
        size, length = (lax.axis_size(axis), shard.shape[dim])
        up = [(i, (i + 1) % size) for i in range(size - 1)]
        down = [(j, i) for i, j in up]
        last = lax.slice_in_dim(shard, length - width, length, axis=dim)
        first = lax.slice_in_dim(shard, 0, width, axis=dim)
        before = lax.ppermute(last, axis, up)
        after = lax.ppermute(first, axis, down)
        shard = jnp.concatenate([before, shard, after], axis=dim)
    return shard


def unpack(flat_params):
    end_qkv = D * 3 * D
    end_out = end_qkv + D * D
    end_mlp = end_out + D * 2 * FF
    end_down = end_mlp + FF * D
    w_qkv = flat_params[:end_qkv].reshape(D, 3 * D)
    w_out = flat_params[end_qkv:end_out].reshape(D, D)
    w_gate_up = flat_params[end_out:end_mlp].reshape(D, 2 * FF)
    w_down = flat_params[end_mlp:end_down].reshape(FF, D)
    vectors = flat_params[end_down:].reshape(6, D).astype(jnp.float32)
    return (w_qkv, w_out, w_gate_up, w_down, vectors)


def clip_info(lengths, glob):
    clip_ends = jnp.cumsum(lengths, axis=1, dtype=jnp.int32)
    clip_starts = clip_ends - lengths
    after_end = (glob[None, :, None] >= clip_ends[:, None, :]).astype(jnp.int32)
    segment = jnp.sum(after_end, axis=2, dtype=jnp.int32)
    onehot = segment[:, :, None] == jnp.arange(lengths.shape[1], dtype=jnp.int32)[None, None, :]
    clip_begin = jnp.sum(jnp.where(onehot, clip_starts[:, None, :], 0), axis=2, dtype=jnp.int32)
    return (segment, (glob[None, :] - clip_begin).astype(jnp.float32))


def rotate(values, position, sign):
    half_dim = values.shape[-1] // 2
    inverse = jnp.exp(
        jnp.arange(half_dim, dtype=jnp.float32) * (-2.0 * math.log(rope_base) / HEAD_DIM)
    )
    rot_angle = position[:, :, None, None] * inverse
    cosine = jnp.cos(rot_angle)
    rot_sine = sign * jnp.sin(rot_angle)
    low_half = values[..., :half_dim]
    high_half = values[..., half_dim:]
    return jnp.concatenate(
        [low_half * cosine - high_half * rot_sine, high_half * cosine + low_half * rot_sine],
        axis=-1,
    )


def norm_forward(row_vals, norm_gain, norm_bias):
    centered = row_vals - jnp.mean(row_vals, axis=-1, keepdims=True)
    inv_scale = lax.rsqrt(jnp.mean(centered * centered, axis=-1, keepdims=True) + eps_norm)
    normed = centered * inv_scale
    return (normed * norm_gain + norm_bias, normed, inv_scale)


def norm_backward(out_grad, normed, inv_scale, norm_gain):
    d_gain = jnp.sum(out_grad * normed, axis=0)
    d_bias = jnp.sum(out_grad, axis=0)
    inner_grad = out_grad * norm_gain
    d_rows = inv_scale * (
        inner_grad
        - jnp.mean(inner_grad, axis=-1, keepdims=True)
        - normed * jnp.mean(inner_grad * normed, axis=-1, keepdims=True)
    )
    return (d_rows, d_gain, d_bias)


def scores_of(query_rows, key_rows, window_mask):
    raw_scores = jnp.einsum(
        "qhd,khd->hqk", query_rows, key_rows, preferred_element_type=jnp.float32
    ) * HEAD_DIM ** (-0.5)
    return jnp.where(window_mask[None], raw_scores, neg_large)


def attend(query_rows, key_rows, value_rows, window_mask):
    masked = scores_of(query_rows, key_rows, window_mask)
    row_max = jnp.max(masked, axis=-1, keepdims=True)
    row_total = jnp.log(jnp.sum(jnp.exp(masked - row_max), axis=-1, keepdims=True)) + row_max
    prob_low = jnp.exp(masked - row_total).astype(jnp.bfloat16)
    attn_rows = jnp.einsum("hqk,khd->qhd", prob_low, value_rows, preferred_element_type=jnp.float32)
    return (attn_rows, row_total[..., 0])


def attend_back(query_rows, key_rows, value_rows, window_mask, row_total, d_attn):
    masked = scores_of(query_rows, key_rows, window_mask)
    prob_rows = jnp.exp(masked - row_total[..., None])
    prob_low = prob_rows.astype(jnp.bfloat16)
    d_values = jnp.einsum("hqk,qhd->khd", prob_low, d_attn, preferred_element_type=jnp.float32)
    d_probs = jnp.einsum("qhd,khd->hqk", d_attn, value_rows, preferred_element_type=jnp.float32)
    inner_sum = jnp.sum(prob_rows * d_probs, axis=-1, keepdims=True)
    d_scores = (prob_rows * (d_probs - inner_sum)).astype(jnp.bfloat16)
    d_query = jnp.einsum(
        "hqk,khd->qhd", d_scores, key_rows, preferred_element_type=jnp.float32
    ) * HEAD_DIM ** (-0.5)
    d_keys = jnp.einsum(
        "hqk,qhd->khd", d_scores, query_rows, preferred_element_type=jnp.float32
    ) * HEAD_DIM ** (-0.5)
    return (d_query, d_keys, d_values)


def adam_update(flat_params, grads, first_moment, second_moment):
    new_first = beta_one * first_moment + (1.0 - beta_one) * grads
    new_second = beta_two * second_moment + (1.0 - beta_two) * grads * grads
    corrected_first = new_first / (1.0 - beta_one**adam_step)
    corrected_second = new_second / (1.0 - beta_two**adam_step)
    step_size = corrected_first / (jnp.sqrt(corrected_second) + eps_adam) + decay_rate * flat_params
    return (flat_params - learn_rate * step_size, new_first, new_second)


def body(frames, cotangent, clip_lengths, params, first_moment, second_moment):
    seq_count, frame_span, model_width = frames.shape
    row_count = seq_count * frame_span
    window_reach = WINDOW
    key_count = frame_span + 2 * window_reach
    head_count = HEADS
    head_size = model_width // head_count
    group_size = 4
    seq_len = lax.axis_size("seq") * frame_span
    seq_start = lax.axis_index("seq") * frame_span
    glob_rows = seq_start + jnp.arange(frame_span, dtype=jnp.int32)
    glob_keys = seq_start - window_reach + jnp.arange(key_count, dtype=jnp.int32)
    seg_rows, pos_rows = clip_info(clip_lengths, glob_rows)
    seg_keys, unused = clip_info(clip_lengths, glob_keys)
    inside = (glob_keys >= 0) & (glob_keys < seq_len)
    near_band = (
        jnp.abs(jnp.arange(frame_span)[:, None] + window_reach - jnp.arange(key_count)[None, :])
        < window_reach
    )
    window_mask = (
        (seg_rows[:, :, None] == seg_keys[:, None, :]) & inside[None, None, :] & near_band[None]
    )
    keep_rows = seg_rows != clip_lengths.shape[1] - 1
    shards = params.astype(jnp.bfloat16)
    gathered = lax.all_gather(shards, ("dp", "seq"), axis=0, tiled=True)
    w_qkv, w_out, w_gate_up, w_down, vectors = unpack(gathered)
    x_rows = frames.reshape(row_count, model_width).astype(jnp.float32)
    norm_one, normed_one, scale_one = norm_forward(x_rows, vectors[0], vectors[1])
    a_low = norm_one.astype(jnp.bfloat16)
    qkv = jnp.dot(a_low, w_qkv, preferred_element_type=jnp.float32).reshape(
        seq_count, frame_span, 3, head_count, head_size
    )
    query_low = rotate(qkv[:, :, 0], pos_rows, 1.0).astype(jnp.bfloat16)
    key_low = rotate(qkv[:, :, 1], pos_rows, 1.0).astype(jnp.bfloat16)
    value_low = qkv[:, :, 2].astype(jnp.bfloat16)
    key_value = jnp.concatenate([key_low, value_low], axis=2).reshape(
        seq_count, frame_span, 2 * model_width
    )
    wide_rows = padded(key_value, (("seq", 1),), window_reach)
    wide_rows = wide_rows.reshape(seq_count, key_count, 2, head_count, head_size)
    key_wide = wide_rows[:, :, 0]
    value_wide = wide_rows[:, :, 1]
    seq_index = 0
    out_parts = []
    total_parts = []
    for head_start in range(0, head_count, group_size):
        head_end = head_start + group_size
        attn_rows, row_total = attend(
            query_low[seq_index, :, head_start:head_end],
            key_wide[seq_index, :, head_start:head_end],
            value_wide[seq_index, :, head_start:head_end],
            window_mask[seq_index],
        )
        out_parts.append(attn_rows)
        total_parts.append(row_total)
    attn_list = [jnp.concatenate(out_parts, axis=1)]
    total_list = [total_parts]
    attn_all = jnp.where(keep_rows[:, :, None, None], jnp.stack(attn_list), 0.0)
    attn_low = attn_all.reshape(row_count, model_width).astype(jnp.bfloat16)
    branch_attn = jnp.dot(attn_low, w_out, preferred_element_type=jnp.float32)
    mid_rows = x_rows + vectors[4] * branch_attn
    norm_two, normed_two, scale_two = norm_forward(mid_rows, vectors[2], vectors[3])
    c_low = norm_two.astype(jnp.bfloat16)
    gate_up = jnp.dot(c_low, w_gate_up, preferred_element_type=jnp.float32)
    gate = gate_up[:, :FF]
    up_rows = gate_up[:, FF:]
    gate_sig = jax.nn.sigmoid(gate)
    hidden = (gate * gate_sig * up_rows).astype(jnp.bfloat16)
    branch_mlp = jnp.dot(hidden, w_down, preferred_element_type=jnp.float32)
    output = (
        (mid_rows + vectors[5] * branch_mlp)
        .astype(jnp.bfloat16)
        .reshape(seq_count, frame_span, model_width)
    )
    gathered = lax.all_gather(shards, ("dp", "seq"), axis=0, tiled=True)
    w_qkv, w_out, w_gate_up, w_down, vectors = unpack(gathered)
    d_rows = cotangent.reshape(row_count, model_width).astype(jnp.float32)
    g_scale_mlp = jnp.sum(d_rows * branch_mlp, axis=0)
    d_mlp = (d_rows * vectors[5]).astype(jnp.bfloat16)
    g_down = jnp.dot(hidden.T, d_mlp, preferred_element_type=jnp.float32)
    d_hidden = jnp.dot(d_mlp, w_down.T, preferred_element_type=jnp.float32)
    d_gate = d_hidden * up_rows * gate_sig * (1.0 + gate * (1.0 - gate_sig))
    d_up = d_hidden * gate * gate_sig
    d_gate_up = jnp.concatenate([d_gate, d_up], axis=1).astype(jnp.bfloat16)
    g_gate_up = jnp.dot(c_low.T, d_gate_up, preferred_element_type=jnp.float32)
    d_two = jnp.dot(d_gate_up, w_gate_up.T, preferred_element_type=jnp.float32)
    d_norm_two, g_gain_two, g_bias_two = norm_backward(d_two, normed_two, scale_two, vectors[2])
    d_mid = d_rows + d_norm_two
    g_scale_attn = jnp.sum(d_mid * branch_attn, axis=0)
    d_branch = (d_mid * vectors[4]).astype(jnp.bfloat16)
    g_out = jnp.dot(attn_low.T, d_branch, preferred_element_type=jnp.float32)
    d_attn_low = jnp.dot(d_branch, w_out.T, preferred_element_type=jnp.float32).astype(jnp.bfloat16)
    d_attn = jnp.where(
        keep_rows[:, :, None, None],
        d_attn_low.reshape(seq_count, frame_span, head_count, head_size),
        jnp.zeros((), jnp.bfloat16),
    )
    seq_index = 0
    query_parts = []
    key_parts = []
    value_parts = []
    for number, head_start in enumerate(range(0, head_count, group_size)):
        head_end = head_start + group_size
        d_query, d_keys, d_values = attend_back(
            query_low[seq_index, :, head_start:head_end],
            key_wide[seq_index, :, head_start:head_end],
            value_wide[seq_index, :, head_start:head_end],
            window_mask[seq_index],
            total_list[seq_index][number],
            d_attn[seq_index, :, head_start:head_end],
        )
        query_parts.append(d_query)
        key_parts.append(d_keys)
        value_parts.append(d_values)
    query_grads = [jnp.concatenate(query_parts, axis=1)]
    key_grads = [jnp.concatenate(key_parts, axis=1)]
    value_grads = [jnp.concatenate(value_parts, axis=1)]
    d_query_all = jnp.stack(query_grads)
    d_pair = jnp.concatenate([jnp.stack(key_grads), jnp.stack(value_grads)], axis=2).reshape(
        seq_count, key_count, 2 * model_width
    )
    rim_rows = jnp.concatenate(
        [d_pair[:, :window_reach], d_pair[:, window_reach + frame_span :]], axis=1
    )
    taken_rows = padded(rim_rows.astype(jnp.bfloat16), (("seq", 1),), window_reach).astype(
        rim_rows.dtype
    )
    own_rows = d_pair[:, window_reach : window_reach + frame_span]
    own_rows = own_rows + jnp.pad(
        taken_rows[:, :window_reach], ((0, 0), (0, frame_span - window_reach), (0, 0))
    )
    own_rows = own_rows + jnp.pad(
        taken_rows[:, 3 * window_reach :], ((0, 0), (frame_span - window_reach, 0), (0, 0))
    )
    own_rows = own_rows.reshape(seq_count, frame_span, 2, head_count, head_size)
    d_qkv = jnp.stack(
        [
            rotate(d_query_all, pos_rows, -1.0),
            rotate(own_rows[:, :, 0], pos_rows, -1.0),
            own_rows[:, :, 1],
        ],
        axis=2,
    )
    d_qkv = d_qkv.reshape(row_count, 3 * model_width).astype(jnp.bfloat16)
    g_qkv = jnp.dot(a_low.T, d_qkv, preferred_element_type=jnp.float32)
    d_one = jnp.dot(d_qkv, w_qkv.T, preferred_element_type=jnp.float32)
    d_norm_one, g_gain_one, g_bias_one = norm_backward(d_one, normed_one, scale_one, vectors[0])
    frames_grad = (
        (d_mid + d_norm_one).astype(jnp.bfloat16).reshape(seq_count, frame_span, model_width)
    )
    small_grads = jnp.stack(
        [g_gain_one, g_bias_one, g_gain_two, g_bias_two, g_scale_attn, g_scale_mlp]
    )
    whole_grad = jnp.concatenate(
        [
            g_qkv.reshape(-1),
            g_out.reshape(-1),
            g_gate_up.reshape(-1),
            g_down.reshape(-1),
            small_grads.reshape(-1),
        ]
    )
    params_grad = lax.psum_scatter(whole_grad, ("dp", "seq"), scatter_dimension=0, tiled=True)
    new_params, new_first, new_second = adam_update(
        params, params_grad, first_moment, second_moment
    )
    return (output, frames_grad, params_grad, new_params, new_first, new_second)


EVERY = ("z", "x", "c", "y")
GROUP = ("z", "x")
RING = ((0, 0), (1, 0), (2, 0), (3, 0), (3, 1), (2, 1), (1, 1), (0, 1))
PLACES = tuple(2 * z + x for z, x in RING)
AHEAD = tuple((PLACES[i], PLACES[(i + 1) % 8]) for i in range(8))
BACK = tuple((b, a) for a, b in AHEAD)
SWAP = ((0, 1), (1, 0))
LINES = 4096
TAIL = 64
PITCH = 72
SLAB = 16
ROWS = 128 + SLAB
OWN = 256
SCALE = HEAD_DIM ** (-0.5)
SCALAR = pl.BlockSpec(memory_space=pltpu.SMEM)
WHOLE = pl.BlockSpec(memory_space=pltpu.VMEM)
HBM = pl.BlockSpec(memory_space=pltpu.HBM)
ANY = pl.BlockSpec(memory_space=pl.ANY)


def vmem(mebibytes):
    return pltpu.CompilerParams(vmem_limit_bytes=mebibytes << 20)


def ring_place(me, step):
    z, x = lax.div(me, 8), lax.rem(lax.div(me, 4), 2)
    at = lax.rem(jnp.where(x == 0, z, 7 - z) + step, 8)
    return jnp.where(at < 4, 2 * at, 15 - 2 * at)


def kind_of(shard):
    if shard < 6:
        return 0
    return 2 if 8 <= shard < 24 else 1


def piece_lines(kind, dest, pitch=64):
    place, member = divmod(dest, 4)
    if kind == 0:
        return [(512 * place + member, 8), (512 * place + 4 + member, 8)]
    if kind == 1:
        return [(1024 * member + place, 8), (1024 * member + 512 + place, 8)]
    return [(dest, pitch), (32 + dest, pitch)]


def tail_lines(kind, dest):
    place, member = divmod(dest, 4)
    if kind == 0:
        return [(0, 6, member, 8), (8, 6, 4 + member, 8)] if place == 0 else []
    if kind == 1:
        return [(0, 6, place, 8)] if member == 0 else []
    return [(0, 1, dest, 1)] + ([(8, 1, 32 + dest, 1)] if dest < 16 else [])


def is_kind(shard, kind):
    if kind == 0:
        return shard < 6
    gate_up = (shard >= 8) & (shard < 24)
    if kind == 2:
        return gate_up
    return (shard >= 6) & jnp.logical_not(gate_up) & (shard < 32)


def spread_kernel(me_ref, flat_ref, out_ref, lines_ref, tail_ref):
    me = me_ref[0]
    odd = lax.rem(me, 2) == 1
    start = 48 - (3 * me + 1) // 2
    lane = lax.broadcasted_iota(jnp.int32, (64, 128), 1)

    def shifted(step):
        here = flat_ref[pl.ds(start + step * 64, 64), :]
        after = flat_ref[pl.ds(start + step * 64 + 1, 64), :]
        mixed = jnp.where(lane < 64, pltpu.roll(here, 64, 1), pltpu.roll(after, 64, 1))
        return jnp.where(odd, mixed, here)

    def fill(pitch):
        def body(step, carry):
            lines_ref[pl.ds(pl.multiple_of(step * pitch, 8), 64), :] = shifted(step)
            return carry

        lax.fori_loop(0, LINES // 64, body, 0, unroll=4)

    tail_ref[...] = shifted(LINES // 64)
    for kind in range(3):

        @pl.when(is_kind(me, kind))
        def _(kind=kind):
            pitch = PITCH if kind == 2 else 64
            fill(pitch)
            for dest in range(32):
                for half, (first, stride) in enumerate(piece_lines(kind, dest, pitch)):
                    rows = lines_ref[pl.ds(first, 64, stride), :]
                    out_ref[dest, 64 * half : 64 * half + 64, :] = rows.astype(jnp.bfloat16)

    def slab_of(parts):
        slab = [jnp.zeros((8, 128), jnp.float32)] * 2
        row = lax.broadcasted_iota(jnp.int32, (8, 128), 0)
        for at, count, first, stride in parts:
            if count == 1:
                value = jnp.broadcast_to(tail_ref[first : first + 1, :], (8, 128))
            else:
                value = tail_ref[pl.ds(first, 8, stride), :]
            slab[at // 8] = jnp.where(row < count, value, 0.0)
        return jnp.concatenate(slab, axis=0).astype(jnp.bfloat16)

    for kind in range(3):

        @pl.when(is_kind(me + 1, kind))
        def _(kind=kind):
            for dest in range(32):
                out_ref[dest, 128:ROWS, :] = slab_of(tail_lines(kind, dest))

    @pl.when(me == 31)
    def _():
        for dest in range(32):
            out_ref[dest, 128:ROWS, :] = slab_of([(0, 6, 6 * (dest // 4), 1)])


def spread(params, me):
    flat = jnp.pad(params, (48 * 128, 4224 * 128 - 48 * 128 - params.shape[0])).reshape(4224, 128)
    return pl.pallas_call(
        spread_kernel,
        out_shape=jax.ShapeDtypeStruct((32, ROWS, 128), jnp.bfloat16),
        in_specs=[
            pl.BlockSpec(memory_space=pltpu.SMEM),
            pl.BlockSpec(memory_space=pltpu.VMEM),
        ],
        out_specs=pl.BlockSpec(memory_space=pltpu.VMEM),
        scratch_shapes=[
            pltpu.VMEM((LINES // 64 * PITCH, 128), jnp.float32),
            pltpu.VMEM((TAIL, 128), jnp.float32),
        ],
        compiler_params=vmem(12),
        name="spread",
    )(me, flat)


def collect_kernel(me_ref, piece_ref, out_ref, lines_ref, rows_ref):
    me = me_ref[0]
    odd = lax.rem(me, 2) == 1
    lines_ref[LINES:, :] = jnp.zeros((TAIL, 128), jnp.float32)
    for kind in range(3):

        @pl.when(is_kind(me, kind))
        def _(kind=kind):
            if kind == 2:
                for dest in range(32):
                    rows_ref[136 * dest : 136 * dest + 128, :] = piece_ref[dest, :128, :].astype(jnp.float32)
                for row in range(128):
                    first = 64 * (row % 64) + 32 * (row // 64)
                    lines_ref[first : first + 32, :] = rows_ref[pl.ds(row, 32, 136), :]
                return
            for dest in range(32):
                for half, (first, stride) in enumerate(piece_lines(kind, dest)):
                    rows = piece_ref[dest, 64 * half : 64 * half + 64, :].astype(jnp.float32)
                    lines_ref[pl.ds(first, 64, stride), :] = rows

    for kind in range(3):

        @pl.when(is_kind(me + 1, kind))
        def _(kind=kind):
            for dest in range(32):
                slab = piece_ref[dest, 128:ROWS, :].astype(jnp.float32)
                for at, count, first, stride in tail_lines(kind, dest):
                    for k in range(count):
                        line = LINES + first + k * stride
                        lines_ref[line : line + 1, :] = slab[at + k : at + k + 1, :]

    @pl.when(me == 31)
    def _():
        for place in range(8):
            total = piece_ref[4 * place, 128:ROWS, :].astype(jnp.float32)
            for member in range(1, 4):
                total = total + piece_ref[4 * place + member, 128:ROWS, :].astype(jnp.float32)
            for k in range(6):
                line = LINES + 6 * place + k
                lines_ref[line : line + 1, :] = total[k : k + 1, :]

    start = (3 * me) // 2
    lane = lax.broadcasted_iota(jnp.int32, (24, 128), 1)

    def shift(step, carry):
        here = lines_ref[pl.ds(start + step * 24, 24), :]
        after = lines_ref[pl.ds(start + step * 24 + 1, 24), :]
        mixed = jnp.where(lane < 64, pltpu.roll(here, 64, 1), pltpu.roll(after, 64, 1))
        out_ref[pl.ds(pl.multiple_of(step * 24, 8), 24), :] = jnp.where(odd, mixed, here)
        return carry

    lax.fori_loop(0, 4104 // 24, shift, 0, unroll=9)


def collect(pieces, me, count):
    lines = pl.pallas_call(
        collect_kernel,
        out_shape=jax.ShapeDtypeStruct((4104, 128), jnp.float32),
        in_specs=[
            pl.BlockSpec(memory_space=pltpu.SMEM),
            pl.BlockSpec(memory_space=pltpu.VMEM),
        ],
        out_specs=pl.BlockSpec(memory_space=pltpu.VMEM),
        scratch_shapes=[
            pltpu.VMEM((LINES + TAIL, 128), jnp.float32),
            pltpu.VMEM((32 * 136, 128), jnp.float32),
        ],
        compiler_params=vmem(12),
        name="collect",
    )(me, pieces)
    return lines.reshape(-1)[:count]


def swap_halves(rows):
    lane = lax.broadcasted_iota(jnp.int32, rows.shape, 1)
    return jnp.where(
        lax.rem(lane, 64) < 32, pltpu.roll(rows, 96, 1), pltpu.roll(rows, 32, 1)
    )


def turn(rows, cosine, signed_sine):
    parts = []
    for at in range(0, rows.shape[1], 128):
        part = rows[:, at : at + 128]
        parts.append(part * cosine + swap_halves(part) * signed_sine)
    return jnp.concatenate(parts, axis=1)


def clip_of(length_ref, frame):
    first = length_ref[0, 0]
    return (frame >= first).astype(jnp.int32) + (frame >= first + length_ref[0, 1]).astype(jnp.int32)


def mask_of(length_ref, block):
    row = lax.broadcasted_iota(jnp.int32, (256, 384), 0) + 256 * block
    key = lax.broadcasted_iota(jnp.int32, (256, 384), 1) + 128 * block
    own = clip_of(length_ref, lax.broadcasted_iota(jnp.int32, (256, 1), 0) + 256 * block)
    others = clip_of(length_ref, lax.broadcasted_iota(jnp.int32, (1, 384), 1) + 128 * block)
    return (jnp.abs(row - key) < WINDOW) & (own == others), own != 1


def nt(left, right):
    return lax.dot_general(left, right, (((1,), (1,)), ((), ())), preferred_element_type=jnp.float32)


def tn(left, right):
    return lax.dot_general(left, right, (((0,), (0,)), ((), ())), preferred_element_type=jnp.float32)


def nn(left, right):
    return jnp.dot(left, right, preferred_element_type=jnp.float32)


def cost(flops, moved):
    return pl.CostEstimate(flops=flops, bytes_accessed=moved, transcendentals=0)


def fix_kernel(piece_ref, first_ref, second_ref, third_ref):
    for source in range(32):
        out, at = (first_ref, source) if source < 8 else (second_ref, source - 8) if source < 24 else (third_ref, source - 24)
        out[128 * at : 128 * at + 128, :] = piece_ref[source, :128, :]
        if source:
            slab = piece_ref[source - 1, 128:ROWS, :].astype(jnp.float32)
            for half in range(2):
                rows = piece_ref[source, 64 * half : 64 * half + 16, :].astype(jnp.float32)
                extra = jnp.concatenate([slab[8 * half : 8 * half + 8], jnp.zeros((8, 128), jnp.float32)])
                out[128 * at + 64 * half : 128 * at + 64 * half + 16, :] = (rows + extra).astype(jnp.bfloat16)
    first_ref[1024:, :] = piece_ref[31, 128:ROWS, :]


def fix(pieces):
    return pl.pallas_call(
        fix_kernel,
        out_shape=tuple(jax.ShapeDtypeStruct((n, 128), jnp.bfloat16) for n in (1024 + SLAB, 2048, 1024)),
        in_specs=[WHOLE],
        out_specs=(WHOLE,) * 3,
        compiler_params=vmem(12),
        cost_estimate=cost(0, 1 << 22),
        name="fix",
    )(pieces)


def in_order(refs, seq, half, second):
    mine, other = refs[2 * seq], refs[2 * seq + 1]
    return jnp.where(lax.rem(second, 2) == half, mine[...], other[...])


def ring_parts(me_ref, refs):
    me = me_ref[0]
    parts = [(ring_place(me, 0), refs[0], None)]
    for step in range(1, 4):
        parts += [(ring_place(me, 8 - step), refs[2 * step - 1], None), (ring_place(me, step), refs[2 * step], None)]
    half = refs[7].shape[0]
    last = ring_place(me, 4)
    return parts + [(last, refs[7], (0, half)), (last, refs[8], (half, half + refs[8].shape[0]))]


def copy_all(pairs, done):
    copies = [pltpu.make_async_copy(source, target, done.at[k]) for k, (source, target) in enumerate(pairs)]
    for copy in copies:
        copy.start()
    for copy in copies:
        copy.wait()


def join_first_kernel(me_ref, *refs):
    blocks, (qkv_ref, out_ref, vec_ref, lines_ref, _) = refs[:9], refs[9:]
    for place, block, rows in ring_parts(me_ref, blocks):
        lo, hi = rows or (0, 1024 + SLAB)
        for at, end, ref in ((0, 768, qkv_ref), (768, 1024, out_ref), (1024, 1024 + SLAB, lines_ref)):
            first, last = max(at, lo), min(end, hi)
            if first < last:
                ref[place, first - at : last - at, :] = block[first - lo : last - lo, :]
    slabs = [lines_ref[place].astype(jnp.float32) for place in range(8)]
    for v in range(6):
        for k in range(8):
            line = 8 * v + k
            vec_ref[v : v + 1, 128 * k : 128 * k + 128] = slabs[line // 6][line % 6 : line % 6 + 1]


def join_gate_up_kernel(which, me_ref, *refs):
    blocks, (out_ref, done) = refs[:9], refs[-2:]
    pairs = []
    for place, block, rows in ring_parts(me_ref, blocks)[which]:
        lo, hi = rows or (0, 16)
        for half in range(2):
            at = pl.multiple_of(256 * half + 128 * lax.rem(place, 2), 128)
            pairs.append((block.at[:, half], out_ref.at[lax.div(place, 2), lo:hi, :, pl.ds(at, 128)]))
    copy_all(pairs, done)


def join_down_kernel(which, me_ref, *refs):
    blocks, (out_ref, done) = refs[:9], refs[-2:]
    pairs = []
    for place, block, rows in ring_parts(me_ref, blocks)[which]:
        lo, hi = rows or (0, 1024)
        pairs.append((block, out_ref.at[lo:hi, pl.ds(pl.multiple_of(128 * place, 128), 128)]))
    copy_all(pairs, done)


def join_out_kernel(*refs):
    w_ref = refs[4]
    for k in range(4):
        for place in range(8):
            w_ref[256 * k : 256 * k + 256, 128 * place : 128 * place + 128] = refs[k][place]


def join_out(parts):
    return pl.pallas_call(
        join_out_kernel,
        out_shape=jax.ShapeDtypeStruct((D, D), jnp.bfloat16),
        in_specs=[WHOLE] * 4,
        out_specs=WHOLE,
        compiler_params=vmem(12),
        cost_estimate=cost(0, 4 << 20),
        name="join_out",
    )(*parts)


def join(kernel, me, blocks, out_shape, name, scratch=(), space=WHOLE):
    if space is HBM:
        blocks = [pltpu.with_memory_space_constraint(block, pltpu.HBM) for block in blocks]
    return pl.pallas_call(
        kernel,
        out_shape=out_shape,
        in_specs=[SCALAR] + [space] * 9,
        out_specs=jax.tree.map(lambda _: WHOLE, out_shape),
        scratch_shapes=list(scratch) + [pltpu.SemaphoreType.DMA((32,))],
        compiler_params=vmem(12),
        cost_estimate=cost(0, 4 << 20),
        name=name,
    )(me, *blocks)


def join_rest_kernel(kernel, me_ref, last_ref, end_ref, _, out_ref, done):
    kernel(slice(7, 9), me_ref, *([last_ref] * 8 + [end_ref]), out_ref, done)


def join_twice(kernel, me, blocks, out_shape, name):
    early = [pltpu.with_memory_space_constraint(block, pltpu.HBM) for block in blocks[:7]]
    whole = pl.pallas_call(
        lambda me_ref, *refs: kernel(slice(0, 7), me_ref, *refs[:7], refs[6], refs[6], *refs[7:]),
        out_shape=out_shape,
        in_specs=[SCALAR] + [HBM] * 7,
        out_specs=WHOLE,
        scratch_shapes=[pltpu.SemaphoreType.DMA((32,))],
        compiler_params=vmem(12),
        cost_estimate=cost(0, 4 << 20),
        name=name,
    )(me, *early)
    last = after(tuple(blocks[7:]), whole)
    return pl.pallas_call(
        functools.partial(join_rest_kernel, kernel),
        out_shape=out_shape,
        in_specs=[SCALAR, ANY, ANY, WHOLE],
        out_specs=WHOLE,
        input_output_aliases={3: 0},
        scratch_shapes=[pltpu.SemaphoreType.DMA((32,))],
        compiler_params=vmem(12),
        cost_estimate=cost(0, 4 << 20),
        name=name + "_rest",
    )(me, *last, whole)


def prep_kernel(y_ref, own_ref, pair_ref, far_ref, last_ref, x_ref, mean_ref, inv_ref):
    for block in range(4):
        rows = slice(256 * block, 256 * block + 256)
        x_low = in_order((own_ref, pair_ref, far_ref, last_ref), block // 2, block % 2, y_ref[0])
        x_ref[rows, :] = x_low
        x_rows = x_low.astype(jnp.float32)
        mean = jnp.mean(x_rows, axis=1, keepdims=True)
        centered = x_rows - mean
        mean_ref[rows, :] = mean
        inv_ref[rows, :] = lax.rsqrt(jnp.mean(centered * centered, axis=1, keepdims=True) + eps_norm)


def prep(second, rows):
    return pl.pallas_call(
        prep_kernel,
        out_shape=(
            jax.ShapeDtypeStruct((1024, D), jnp.bfloat16),
            jax.ShapeDtypeStruct((1024, 1), jnp.float32),
            jax.ShapeDtypeStruct((1024, 1), jnp.float32),
        ),
        in_specs=[SCALAR] + [WHOLE] * 4,
        out_specs=(WHOLE,) * 3,
        compiler_params=vmem(12),
        cost_estimate=cost(1 << 24, 5 << 20),
        name="prep",
    )(second, *rows)


def front_kernel(
    x_ref, mean_ref, inv_ref, ring_ref, vec_ref, order_ref, cos_ref, sin_ref, length_ref, far_length_ref,
    a_out, w_out, low_out, attn_ref, lse_out,
    a_ref, w_ref, low_ref, lse_ref, done,
):
    copies = [
        pltpu.make_async_copy(ref, out, done.at[k])
        for k, (ref, out) in enumerate(((w_ref, w_out), (a_ref, a_out), (low_ref, low_out), (lse_ref, lse_out)))
    ]
    gain, bias = vec_ref[0:1, :], vec_ref[1:2, :]
    for block in range(8):
        parts = []
        for chunk in range(6 * block, 6 * block + 6):
            at = 128 * (chunk // 8)
            parts.append(
                jnp.concatenate(
                    [ring_ref[chunk % 8, at : at + 64, :], ring_ref[chunk % 8, at + 64 : at + 128, :]], axis=1
                )
            )
        rows = nn(order_ref[...], jnp.concatenate(parts, axis=0)).astype(jnp.bfloat16)
        for third in range(3):
            w_ref[128 * block : 128 * block + 128, OWN * third : OWN * third + OWN] = rows[
                128 * third : 128 * third + 128
            ]
    copies[0].start()
    for block in range(4):
        rows = slice(256 * block, 256 * block + 256)
        seq, at = block // 2, 256 * (block % 2)
        normed = (x_ref[rows, :].astype(jnp.float32) - mean_ref[rows, :]) * inv_ref[rows, :]
        a_low = (normed * gain + bias).astype(jnp.bfloat16)
        a_ref[rows, :] = a_low
        qkv = nn(a_low, w_ref[...])
        cosine, sine = cos_ref[seq, at : at + 256, :], sin_ref[seq, at : at + 256, :]
        low_ref[rows, : 2 * OWN] = turn(qkv[:, : 2 * OWN], cosine, sine).astype(jnp.bfloat16)
        low_ref[rows, 2 * OWN :] = qkv[:, 2 * OWN :].astype(jnp.bfloat16)
    copies[1].start()
    copies[2].start()
    for seq in range(2):
        for block in range(2):
            at = 512 * seq + 256 * block
            rows = slice(at, at + 256)
            keys = slice(512 * seq + 128 * block, 512 * seq + 128 * block + 384)
            mask, keep = mask_of((length_ref, far_length_ref)[seq], block)
            heads, sums = [], []
            for head in range(4):
                lane = 64 * head
                query = low_ref[rows, lane : lane + 64]
                key = low_ref[keys, OWN + lane : OWN + lane + 64]
                value = low_ref[keys, 2 * OWN + lane : 2 * OWN + lane + 64]
                masked = jnp.where(mask, nt(query, key) * SCALE, neg_large)
                top = jnp.max(masked, axis=1, keepdims=True)
                weight = jnp.exp(masked - top)
                total = jnp.sum(weight, axis=1, keepdims=True)
                probs = (weight * (1.0 / total)).astype(jnp.bfloat16)
                heads.append(jnp.where(keep, nn(probs, value), 0.0))
                sums.append(top + jnp.log(total))
            attn_ref[rows, :] = jnp.concatenate(heads, axis=1).astype(jnp.bfloat16)
            lse_ref[rows, :] = jnp.concatenate(sums, axis=1)
    copies[3].start()
    for copy in copies:
        copy.wait()


def front(x_all, mean, inv, ring, vectors, order, cosine, sine, lengths):
    return pl.pallas_call(
        front_kernel,
        out_shape=(
            pltpu.HBM((1024, D), jnp.bfloat16),
            pltpu.HBM((D, 3 * OWN), jnp.bfloat16),
            pltpu.HBM((1024, 3 * OWN), jnp.bfloat16),
            jax.ShapeDtypeStruct((1024, OWN), jnp.bfloat16),
            pltpu.HBM((1024, 4), jnp.float32),
        ),
        in_specs=[WHOLE] * 8 + [SCALAR] * 2,
        out_specs=(HBM, HBM, HBM, WHOLE, HBM),
        scratch_shapes=[
            pltpu.VMEM((1024, D), jnp.bfloat16),
            pltpu.VMEM((D, 3 * OWN), jnp.bfloat16),
            pltpu.VMEM((1024, 3 * OWN), jnp.bfloat16),
            pltpu.VMEM((1024, 4), jnp.float32),
            pltpu.SemaphoreType.DMA((4,)),
        ],
        compiler_params=vmem(14),
        cost_estimate=cost(12 << 30, 8 << 20),
        name="front",
    )(x_all, mean, inv, ring, vectors, order, cosine, sine, *lengths)


def mix_kernel(x_ref, own_ref, pair_ref, far_ref, last_ref, w_ref, vec_ref, c_ref, branch_ref):
    for block in range(4):
        rows = slice(256 * block, 256 * block + 256)
        other = (block + 2) % 4
        far = slice(256 * other, 256 * other + 256)
        attn = jnp.concatenate([own_ref[rows, :], pair_ref[rows, :], far_ref[far, :], last_ref[far, :]], axis=1)
        branch = nn(attn, w_ref[...])
        normed, _ = normed_of(x_ref[rows, :].astype(jnp.float32) + vec_ref[4:5, :] * branch)
        c_ref[rows, :] = (normed * vec_ref[2:3, :] + vec_ref[3:4, :]).astype(jnp.bfloat16)
        if block < 2:
            branch_ref[rows, :] = branch


def mix(x_all, attn, w_out, vectors):
    return pl.pallas_call(
        mix_kernel,
        out_shape=(
            pltpu.VMEM((1024, D), jnp.bfloat16),
            jax.ShapeDtypeStruct((512, D), jnp.float32),
        ),
        in_specs=[WHOLE] * 7,
        out_specs=(WHOLE, WHOLE),
        compiler_params=vmem(12),
        cost_estimate=cost(3 << 30, 10 << 20),
        name="mix",
    )(x_all, *attn, w_out, vectors)


def gate_kernel(c_ref, w_ref, gate_up_ref, hidden_ref):
    for block in range(4):
        rows = slice(256 * block, 256 * block + 256)
        for chunk in range(4):
            both = nn(c_ref[rows, :], w_ref[chunk])
            gate_up_ref[chunk, rows, :] = both
            gate, up = both[:, :256], both[:, 256:]
            hidden_ref[rows, 256 * chunk : 256 * chunk + 256] = (gate * jax.nn.sigmoid(gate) * up).astype(
                jnp.bfloat16
            )


def gate_step(c_low, w_gate_up):
    return pl.pallas_call(
        gate_kernel,
        out_shape=(
            jax.ShapeDtypeStruct((4, 1024, 512), jnp.float32),
            jax.ShapeDtypeStruct((1024, 1024), jnp.bfloat16),
        ),
        in_specs=[WHOLE] * 2,
        out_specs=(WHOLE, WHOLE),
        compiler_params=vmem(12),
        cost_estimate=cost(5 << 30, 16 << 20),
        name="gate",
    )(c_low, w_gate_up)


def down_grad_kernel(me_ref, hidden_ref, own_ref, pair_ref, far_ref, last_ref, vec_ref, g_ref, d_mlp_ref):
    for block in range(4):
        rows = in_order((own_ref, pair_ref, far_ref, last_ref), block // 2, block % 2, me_ref[0])
        d_mlp_ref[256 * block : 256 * block + 256, :] = (rows.astype(jnp.float32) * vec_ref[5:6, :]).astype(
            jnp.bfloat16
        )
    for source in range(0, 8, 2):
        g_down = tn(hidden_ref[:, 128 * source : 128 * source + 256], d_mlp_ref[...]).astype(jnp.bfloat16)
        for pair in range(2):
            for place in range(8):
                at = 128 * (source + pair)
                g_ref[place, at : at + 128, :] = g_down[128 * pair : 128 * pair + 128, 128 * place : 128 * place + 128]


def down_grad(me, hidden, cot, vectors):
    return pl.pallas_call(
        down_grad_kernel,
        out_shape=(
            jax.ShapeDtypeStruct((8, 1024, 128), jnp.bfloat16),
            jax.ShapeDtypeStruct((1024, D), jnp.bfloat16),
        ),
        in_specs=[SCALAR] + [WHOLE] * 6,
        out_specs=(WHOLE, WHOLE),
        compiler_params=vmem(12),
        cost_estimate=cost(3 << 30, 8 << 20),
        name="down_grad",
    )(me, hidden, *cot, vectors)


def put_rows(me, whole_ref, refs, done=None):
    y = lax.rem(me, 2)
    copies = []
    for k, (ref, half) in enumerate(zip(refs, (1 - y, y, 1 - y, y))):
        rows = pl.ds(pl.multiple_of(512 * (k // 2) + 256 * half, 256), 256)
        if done is not None and k < 2:
            copies.append(pltpu.make_async_copy(whole_ref.at[rows, :], ref, done.at[k]))
            copies[-1].start()
        else:
            ref[...] = whole_ref[rows, :].astype(ref.dtype)
    for copy in copies:
        copy.wait()


PARTS = tuple(jax.ShapeDtypeStruct((256, D), t) for t in (jnp.float32, jnp.float32, jnp.bfloat16, jnp.bfloat16))


def hidden_back_kernel(gate_up_ref, d_mlp_ref, w_ref, d_both_ref):
    for block in range(4):
        rows = slice(256 * block, 256 * block + 256)
        for chunk in range(4):
            d_hidden = nt(d_mlp_ref[rows, :], w_ref[256 * chunk : 256 * chunk + 256, :])
            gate, up = gate_up_ref[chunk, rows, :256], gate_up_ref[chunk, rows, 256:]
            sig = jax.nn.sigmoid(gate)
            d_both_ref[chunk, rows, :256] = (d_hidden * up * sig * (1.0 + gate * (1.0 - sig))).astype(jnp.bfloat16)
            d_both_ref[chunk, rows, 256:] = (d_hidden * gate * sig).astype(jnp.bfloat16)


def hidden_back(gate_up, d_mlp, w_down):
    return pl.pallas_call(
        hidden_back_kernel,
        out_shape=jax.ShapeDtypeStruct((4, 1024, 512), jnp.bfloat16),
        in_specs=[WHOLE] * 3,
        out_specs=WHOLE,
        compiler_params=vmem(12),
        cost_estimate=cost(4 << 30, 18 << 20),
        name="hidden_back",
    )(gate_up, d_mlp, w_down)


def norm_back_kernel(y_ref, d_both_ref, w_ref, near_sent_ref, near_ref, far_sent_ref, far_ref, d_c_ref):
    for block in range(4):
        rows = slice(256 * block, 256 * block + 256)
        d_c = nt(d_both_ref[0, rows, :], w_ref[0])
        for chunk in range(1, 4):
            d_c += nt(d_both_ref[chunk, rows, :], w_ref[chunk])
        d_c_ref[rows, :] = d_c
    put_rows(y_ref[0], d_c_ref, (near_sent_ref, near_ref, far_sent_ref, far_ref))


def norm_back(second, d_both, w_gate_up):
    return pl.pallas_call(
        norm_back_kernel,
        out_shape=PARTS,
        in_specs=[SCALAR, WHOLE, WHOLE],
        scratch_shapes=[pltpu.VMEM((1024, D), jnp.float32)],
        out_specs=(WHOLE,) * 4,
        compiler_params=vmem(12),
        cost_estimate=cost(5 << 30, 12 << 20),
        name="norm_back",
    )(second, d_both, w_gate_up)


def gate_grad_kernel(c_ref, d_both_ref, g_ref):
    for chunk in range(4):
        for block in range(4):
            grad = tn(c_ref[:, 256 * block : 256 * block + 256], d_both_ref[chunk]).astype(jnp.bfloat16)
            for part in range(4):
                source = 4 * block + part
                for pair in range(2):
                    for half in range(2):
                        at = 256 * half + 128 * pair
                        first = 128 * source + 64 * half
                        g_ref[2 * chunk + pair, first : first + 64, :] = grad[64 * part : 64 * part + 64, at : at + 128]


def gate_grad(c_low, d_both):
    return pl.pallas_call(
        gate_grad_kernel,
        out_shape=jax.ShapeDtypeStruct((8, 2048, 128), jnp.bfloat16),
        in_specs=[WHOLE] * 2,
        out_specs=WHOLE,
        compiler_params=vmem(12),
        cost_estimate=cost(5 << 30, 10 << 20),
        name="gate_grad",
    )(c_low, d_both)


def out_kernel(
    y_ref, hidden_ref, w_ref, own_ref, pair_ref, last_ref, end_ref,
    near_sent_ref, near_ref, far_sent_ref, far_ref, g_scale_ref,
    branch_ref, done,
):
    total = jnp.zeros((1, D), jnp.float32)
    for block in range(4):
        rows = slice(256 * block, 256 * block + 256)
        branch = nn(hidden_ref[rows, :], w_ref[...])
        branch_ref[rows, :] = branch
        cot = in_order((own_ref, pair_ref, last_ref, end_ref), block // 2, block % 2, y_ref[0])
        total += jnp.sum(cot.astype(jnp.float32) * branch, axis=0, keepdims=True)
    g_scale_ref[...] = total
    put_rows(y_ref[0], branch_ref, (near_sent_ref, near_ref, far_sent_ref, far_ref), done)


def out_step(second, hidden, down, cot):
    return pl.pallas_call(
        out_kernel,
        out_shape=(pltpu.HBM((256, D), jnp.float32),) * 2 + PARTS[2:] + (jax.ShapeDtypeStruct((1, D), jnp.float32),),
        in_specs=[SCALAR] + [WHOLE] * 6,
        scratch_shapes=[pltpu.VMEM((1024, D), jnp.float32), pltpu.SemaphoreType.DMA((2,))],
        out_specs=(HBM, HBM, WHOLE, WHOLE, WHOLE),
        compiler_params=vmem(12),
        cost_estimate=cost(3 << 30, 10 << 20),
        name="out",
    )(second, hidden, down, *cot)


def attend_back_kernel(
    y_ref, own_ref, pair_ref, far_ref, last_ref, ring_ref, attn_ref, low_ref, lse_ref, cos_ref, sin_ref,
    length_ref, far_length_ref,
    d_qkv_ref, g_ref,
    d_branch_ref, w_out_ref, key_ref, value_ref,
):
    for place in range(8):
        w_out_ref[:, 128 * place : 128 * place + 128] = ring_ref[place]
    for block in range(4):
        d_branch_ref[256 * block : 256 * block + 256, :] = in_order(
            (own_ref, pair_ref, far_ref, last_ref), block // 2, block % 2, y_ref[0]
        )
    g_out = tn(attn_ref[...], d_branch_ref[...]).astype(jnp.bfloat16)
    for place in range(8):
        g_ref[place] = g_out[:, 128 * place : 128 * place + 128]
    for seq in range(2):
        key_ref[...] = jnp.zeros_like(key_ref)
        value_ref[...] = jnp.zeros_like(value_ref)
        cosine, sine = cos_ref[seq], -sin_ref[seq]
        for block in range(2):
            at = 512 * seq + 256 * block
            rows = slice(at, at + 256)
            span = slice(128 * block, 128 * block + 384)
            keys = slice(512 * seq + 128 * block, 512 * seq + 128 * block + 384)
            mask, keep = mask_of((length_ref, far_length_ref)[seq], block)
            d_attn_all = nt(d_branch_ref[rows, :], w_out_ref[...]).astype(jnp.bfloat16)
            d_attn_all = jnp.where(keep, d_attn_all, jnp.zeros_like(d_attn_all))
            d_queries, d_keys, d_values = [], [], []
            for head in range(4):
                lane = 64 * head
                query = low_ref[rows, lane : lane + 64]
                key = low_ref[keys, OWN + lane : OWN + lane + 64]
                value = low_ref[keys, 2 * OWN + lane : 2 * OWN + lane + 64]
                d_attn = d_attn_all[:, lane : lane + 64]
                masked = jnp.where(mask, nt(query, key) * SCALE, neg_large)
                probs = jnp.exp(masked - lse_ref[rows, head : head + 1])
                d_values.append(tn(probs.astype(jnp.bfloat16), d_attn))
                d_probs = nt(d_attn, value)
                inner = jnp.sum(probs * d_probs, axis=1, keepdims=True)
                d_scores = (probs * (d_probs - inner)).astype(jnp.bfloat16)
                d_queries.append(nn(d_scores, key) * SCALE)
                d_keys.append(tn(d_scores, query) * SCALE)
            part = slice(256 * block, 256 * block + 256)
            d_query = turn(jnp.concatenate(d_queries, axis=1), cosine[part], sine[part])
            d_qkv_ref[rows, :OWN] = d_query.astype(jnp.bfloat16)
            key_ref[span, :] += jnp.concatenate(d_keys, axis=1)
            value_ref[span, :] += jnp.concatenate(d_values, axis=1)
        whole = slice(512 * seq, 512 * seq + 512)
        d_qkv_ref[whole, OWN : 2 * OWN] = turn(key_ref[...], cosine, sine).astype(jnp.bfloat16)
        d_qkv_ref[whole, 2 * OWN :] = value_ref[...].astype(jnp.bfloat16)


def attention_back(me, d_branch, ring, attn, low, lse, cosine, sine, lengths):
    return pl.pallas_call(
        attend_back_kernel,
        out_shape=(
            jax.ShapeDtypeStruct((1024, 3 * OWN), jnp.bfloat16),
            jax.ShapeDtypeStruct((8, OWN, 128), jnp.bfloat16),
        ),
        in_specs=[SCALAR] + [WHOLE] * 10 + [SCALAR] * 2,
        out_specs=(WHOLE, WHOLE),
        scratch_shapes=[
            pltpu.VMEM((1024, D), jnp.bfloat16),
            pltpu.VMEM((OWN, D), jnp.bfloat16),
            pltpu.VMEM((512, OWN), jnp.float32),
            pltpu.VMEM((512, OWN), jnp.float32),
        ],
        compiler_params=vmem(12),
        cost_estimate=cost(12 << 30, 10 << 20),
        name="attend_back",
    )(me, *d_branch, ring, attn, low, lse, cosine, sine, *lengths)


def grad_kernel(
    y_ref, a_ref, w_ref, order_ref, d_qkv_ref, g_out_ref, x_ref, mean_ref, inv_ref, small_ref,
    g_ref, near_sent_ref, near_ref, far_sent_ref, far_ref,
    d_a_ref,
):
    g_gain, g_bias = jnp.zeros((1, D), jnp.float32), jnp.zeros((1, D), jnp.float32)
    for block in range(4):
        rows = slice(256 * block, 256 * block + 256)
        d_a = nt(d_qkv_ref[rows, :], w_ref[...])
        normed = (x_ref[rows, :].astype(jnp.float32) - mean_ref[rows, :]) * inv_ref[rows, :]
        g_gain += jnp.sum(d_a * normed, axis=0, keepdims=True)
        g_bias += jnp.sum(d_a, axis=0, keepdims=True)
        d_a_ref[rows, :] = d_a
    put_rows(y_ref[0], d_a_ref, (near_sent_ref, near_ref, far_sent_ref, far_ref))
    for block in range(8):
        grad = tn(a_ref[:, 128 * block : 128 * block + 128], d_qkv_ref[...]).astype(jnp.bfloat16)
        grad = jnp.concatenate([grad[:, OWN * third : OWN * third + OWN] for third in range(3)], axis=0)
        grad = tn(order_ref[...], grad).astype(jnp.bfloat16)
        for part in range(6):
            chunk = 6 * block + part
            at = 128 * (chunk // 8)
            g_ref[chunk % 8, at : at + 64, :] = grad[64 * part : 64 * part + 64, :128]
            g_ref[chunk % 8, at + 64 : at + 128, :] = grad[64 * part : 64 * part + 64, 128:]
    vectors = [g_gain, g_bias] + [small_ref[k : k + 1, :] for k in range(4)]
    lines = [v[:, 128 * k : 128 * k + 128] for v in vectors for k in range(8)]
    for place in range(8):
        g_ref[place, 768:1024, :] = g_out_ref[place]
        rows = lines[6 * place : 6 * place + 6] + [jnp.zeros((SLAB - 6, 128), jnp.float32)]
        g_ref[place, 1024:, :] = jnp.concatenate(rows, axis=0).astype(jnp.bfloat16)


def grad_step(second, a_low, w_qkv, order, d_qkv, g_out, x_all, mean, inv, small):
    return pl.pallas_call(
        grad_kernel,
        out_shape=(jax.ShapeDtypeStruct((8, 1024 + SLAB, 128), jnp.bfloat16),) + PARTS,
        in_specs=[SCALAR] + [WHOLE] * 9,
        scratch_shapes=[pltpu.VMEM((1024, D), jnp.float32)],
        out_specs=(WHOLE,) * 5,
        compiler_params=vmem(12),
        cost_estimate=cost(8 << 30, 12 << 20),
        name="grad",
    )(second, a_low, w_qkv, order, d_qkv, g_out, x_all, mean, inv, small)


def after(values, *others):
    if isinstance(values, tuple):
        return lax.optimization_barrier(values + others)[: len(values)]
    return lax.optimization_barrier((values,) + others)[0]


def both_ways(ahead, back):
    return lax.optimization_barrier((lax.ppermute(ahead, GROUP, AHEAD), lax.ppermute(back, GROUP, BACK)))


class Gather:
    def __init__(self, block):
        self.blocks = [block]
        self.next = (block, block)
        self.half = (block.shape[0] // 2 + 15) // 16 * 16
        self.count = 0

    def step(self, *waits, hold=()):
        self.count += 1
        ahead, back = after(self.next, *waits) if waits else self.next
        if self.count == 4:
            ahead, back = ahead[: self.half], back[self.half :]
        self.next = after(both_ways(ahead, back), *hold)
        self.blocks += self.next
        return self.next


class Scatter:
    def __init__(self, blocks, me):
        self.blocks, self.me = blocks, me
        self.rows = blocks.shape[1]
        self.half = (self.rows // 2 + 15) // 16 * 16
        self.count = 0
        self.next = (self.get(4, 0, self.half), self.get(4, self.half))

    def get(self, step, lo=0, hi=None):
        hi = self.rows if hi is None else hi
        at = (ring_place(self.me, step % 8), 0 * self.me + lo, 0 * self.me)
        return lax.dynamic_slice(self.blocks, at, (1, hi - lo, 128))[0]

    def step(self, *waits, hold=()):
        self.count += 1
        ahead, back = came = after(both_ways(*(after(self.next, *waits) if waits else self.next)), *hold)

        def add(moved, own):
            return (moved.astype(jnp.float32) + own.astype(jnp.float32)).astype(jnp.bfloat16)

        if self.count == 1:
            half = self.half
            ahead = jnp.concatenate([add(ahead, self.get(3, 0, half)), self.get(3, half)])
            back = jnp.concatenate([self.get(5, 0, half), add(back, self.get(5, half))])
        elif self.count < 4:
            ahead, back = add(ahead, self.get(4 - self.count)), add(back, self.get(4 + self.count))
        else:
            total = self.get(0).astype(jnp.float32) + ahead.astype(jnp.float32) + back.astype(jnp.float32)
            self.total = total.astype(jnp.bfloat16)
        self.next = (ahead, back)
        return came


def to_pair(rows, *waits):
    rows = after(rows, *waits) if waits else rows
    return rows, lax.ppermute(rows, "y", SWAP)


def to_group(pair, *waits):
    pair = after(tuple(pair), *waits) if waits else pair
    return tuple(pair) + tuple(lax.ppermute(rows, "c", SWAP) for rows in pair)


def half_sum(near_sent, near, far_sent, far):
    sent = near_sent + lax.ppermute(far_sent, "c", SWAP).astype(jnp.float32)
    kept = near + lax.ppermute(far, "c", SWAP).astype(jnp.float32)
    return lax.optimization_barrier((sent.astype(jnp.bfloat16), kept))


def full_sum(sent, kept):
    return kept + lax.ppermute(sent, "y", SWAP).astype(jnp.float32)


def normed_of(rows):
    centered = rows - jnp.mean(rows, axis=-1, keepdims=True)
    inv_scale = lax.rsqrt(jnp.mean(centered * centered, axis=-1, keepdims=True) + eps_norm)
    return centered * inv_scale, inv_scale


def norm_rows_back(out_grad, normed, inv_scale, gain):
    inner = out_grad * gain
    return inv_scale * (
        inner
        - jnp.mean(inner, axis=-1, keepdims=True)
        - normed * jnp.mean(inner * normed, axis=-1, keepdims=True)
    )


def fast_body(frames, cotangent, clip_lengths, params, first_moment, second_moment):
    z, x, c, y = (lax.axis_index(axis) for axis in EVERY)
    device = (((z * 2 + x) * 2 + c) * 2 + y).astype(jnp.int32)
    me = device[None]
    lengths = (clip_lengths, lax.ppermute(clip_lengths, "c", SWAP))
    order = np.zeros((384, 384), np.float32)
    for row in range(384):
        order[(row % 3) * 128 + row // 3, row] = 1.0
    order = jnp.asarray(order, jnp.bfloat16)

    pieces = spread(params, me)
    pieces = lax.all_to_all(pieces, EVERY, split_axis=0, concat_axis=0, tiled=True)
    first_piece, second_piece, third_piece = fix(pieces)
    first, second, third = Gather(first_piece), Gather(second_piece), Gather(third_piece)
    frames_pair = to_pair(frames[0], first_piece)
    came = first.step()
    cot_pair = to_pair(cotangent[0], frames_pair[1])
    lengths = after(lengths, first_piece)
    both = jnp.concatenate(lengths)
    frame = jnp.arange(512, dtype=jnp.int32)
    starts, ends = both[:, :1], both[:, :1] + both[:, 1:]
    position = jnp.where((frame >= starts) & (frame < ends), frame - starts, frame).astype(jnp.float32)
    inverse = jnp.exp(
        jnp.asarray(np.arange(128) % 32, jnp.float32) * (-2.0 * math.log(rope_base) / HEAD_DIM)
    )
    angle = position[:, :, None] * inverse
    cosine = jnp.cos(angle)
    sine = jnp.sin(angle) * jnp.asarray(np.where(np.arange(128) % 64 < 32, -1.0, 1.0), jnp.float32)
    came_second = first.step(cosine, sine)
    frames_parts = to_group(after(frames_pair, *came))
    first.step(frames_pair[1])
    x_all, mean_one, inv_one = prep(me, frames_parts)
    first.step(x_all)
    second.step(*came_second)
    ring_qkv, w_own, vectors = join(
        join_first_kernel,
        me,
        first.blocks,
        (
            jax.ShapeDtypeStruct((8, 768, 128), jnp.bfloat16),
            jax.ShapeDtypeStruct((8, OWN, 128), jnp.bfloat16),
            jax.ShapeDtypeStruct((6, D), jnp.float32),
        ),
        "join_first",
        [pltpu.VMEM((8, SLAB, 128), jnp.bfloat16)],
    )

    w_pair = to_pair(w_own)
    x_all, ring_qkv = after((x_all, ring_qkv), *second.next, cot_pair[1])
    came = second.step(ring_qkv)
    a_low, w_qkv, low, attn_own, lse = front(x_all, mean_one, inv_one, ring_qkv, vectors, order, cosine, sine, lengths)
    attn_pair = to_pair(attn_own, *came, w_pair[1])
    w_out = join_out(to_group(w_pair, attn_own))
    came = second.step(attn_own)
    attn_parts = to_group(attn_pair, w_out)
    attn_parts = attn_parts[:2] + after(attn_parts[2:], *came)
    c_low, branch_seq = mix(x_all, attn_parts, w_out, vectors)
    third.step(*attn_parts[2:])
    came = second.step(*attn_parts[2:])
    second.blocks[7:] = after(came, c_low)
    came = third.next
    blocks = [block.reshape(-1, 2, 64, 128) for block in second.blocks]
    shape = jax.ShapeDtypeStruct((4, 16, 64, 512), jnp.bfloat16)
    w_gate_up = join(functools.partial(join_gate_up_kernel, slice(0, 9)), me, blocks, shape, "join_gate_up", space=HBM)
    w_gate_up = w_gate_up.reshape(4, 1024, 512)
    cot_parts = to_group(cot_pair, c_low)
    gate_up, hidden = gate_step(after(c_low, *came), w_gate_up)
    came = third.step(c_low)
    g_down, d_mlp = down_grad(me, after(hidden, *came), cot_parts, vectors)
    third.step(hidden)
    third.step(g_down)
    shape = jax.ShapeDtypeStruct((1024, D), jnp.bfloat16)
    third.blocks[0] = after(third.blocks[0], g_down)
    w_down = join_twice(join_down_kernel, me, third.blocks, shape, "join_down")

    down = Scatter(g_down, device)
    d_both = hidden_back(gate_up, d_mlp, w_down)
    came = down.step(*third.next)
    d_both = after(d_both, *came)
    d_c_parts = norm_back(me, d_both, w_gate_up)
    came = down.step(d_both)
    d_c_sent, d_c_kept = half_sum(*after(tuple(d_c_parts), *came))
    g_gate_up = gate_grad(c_low, after(d_both, d_c_sent, d_c_kept))
    came = down.step(d_c_sent, hold=(g_gate_up,))
    gate_grads = Scatter(g_gate_up, device)

    x_own = frames[0].astype(jnp.float32)
    cot_own = cotangent[0].astype(jnp.float32)
    branch_own = jnp.where(y == 0, branch_seq[:256], branch_seq[256:])
    mid_own = x_own + vectors[4] * branch_own
    normed_two, scale_two = normed_of(mid_own)
    d_c_own = full_sum(d_c_sent, d_c_kept)
    d_mid = cot_own + norm_rows_back(d_c_own, normed_two, scale_two, vectors[2])
    d_branch_own = (d_mid * vectors[4]).astype(jnp.bfloat16)
    d_branch_pair = to_pair(d_branch_own)
    down.step(hold=(d_branch_own,))
    came = gate_grads.step(hold=(d_branch_own,))
    hidden = after(hidden, d_branch_own, *came)
    *out_parts, g_scale_mlp = out_step(me, hidden, w_down, cot_parts)
    came = gate_grads.step(d_branch_own, hold=(g_scale_mlp,))
    d_branch = to_group(d_branch_pair, *came, g_scale_mlp)
    out_sent, out_kept = half_sum(*out_parts)
    g_gain_two = jnp.sum(d_c_own * normed_two, axis=0)
    g_bias_two = jnp.sum(d_c_own, axis=0)
    g_scale_attn = jnp.sum(d_mid * branch_own, axis=0)
    small = jnp.concatenate([jnp.stack([g_gain_two, g_bias_two, g_scale_attn]), g_scale_mlp], axis=0)

    d_branch = after(d_branch, small)
    d_qkv, g_out = attention_back(me, d_branch, w_own, attn_own, low, lse, cosine, sine, lengths)
    came = gate_grads.step(*d_branch, hold=(d_qkv,))
    out_sent = after(out_sent, *d_branch)
    output = (mid_own + vectors[5] * full_sum(out_sent, out_kept)).astype(jnp.bfloat16)
    d_qkv = after(d_qkv, *came)
    g_first, *d_a_parts = grad_step(me, a_low, w_qkv, order, d_qkv, g_out, x_all, mean_one, inv_one, small)
    came = gate_grads.step(d_qkv, hold=(g_first,))
    first_grads = Scatter(after(g_first, *came), device)
    first_grads.step(output)
    d_a_sent, d_a_kept = half_sum(*d_a_parts)
    first_grads.step(d_a_sent)
    first_grads.step()
    normed_one, scale_one = normed_of(x_own)
    d_one = norm_rows_back(full_sum(d_a_sent, d_a_kept), normed_one, scale_one, vectors[0])
    frames_grad = (d_mid + d_one).astype(jnp.bfloat16)
    first_grads.step(frames_grad)
    g_first, g_gate_up, g_down = first_grads.total, gate_grads.total, down.total

    main = jnp.concatenate([g_first[:1024], g_gate_up, g_down]).reshape(32, 128, 128)
    slab = jnp.concatenate([main[1:, :8], main[1:, 64:72]], axis=1)
    slab = jnp.concatenate([slab, g_first[None, 1024:]])
    pieces = jnp.concatenate([main, slab], axis=1)
    pieces = lax.all_to_all(pieces, EVERY, split_axis=0, concat_axis=0, tiled=True)
    params_grad = collect(pieces, me, params.shape[0])
    new_params, new_first, new_second = adam_update(params, params_grad, first_moment, second_moment)
    return (output[None], frames_grad[None], params_grad, new_params, new_first, new_second)


def solution(mesh):
    def run(frames, cotangent, clip_lengths, params, first_moment, second_moment):
        fits = (
            mesh.shape["dp"] == 16
            and mesh.shape["seq"] == 2
            and frames.shape == (16, 512, D)
            and clip_lengths.shape == (16, 2)
        )
        if fits:
            over = Mesh(mesh.devices.reshape(4, 2, 2, 2), EVERY)
            rows, clips, flat = P(("z", "x", "c"), "y", None), P(("z", "x", "c"), None), P(EVERY)
        else:
            over = mesh
            rows, clips, flat = P("dp", "seq", None), P("dp", None), P(("dp", "seq"))
        step = jax.shard_map(
            fast_body if fits else body,
            mesh=over,
            in_specs=(rows, rows, clips, flat, flat, flat),
            out_specs=(rows, rows, flat, flat, flat, flat),
            check_vma=False,
        )
        return step(frames, cotangent, clip_lengths, params, first_moment, second_moment)

    return run
```

```python
import functools
import math

import jax
import jax.numpy as jnp
import numpy as np
from jax import lax
from jax.experimental import pallas as pl
from jax.experimental.pallas import tpu as pltpu
from jax.sharding import Mesh
from jax.sharding import PartitionSpec as P

D = 1024
HEADS = 16
HEAD_DIM = 64
FF = 4096
WINDOW = 128


eps_norm = 1e-05
beta_one = 0.9
beta_two = 0.99
learn_rate = 0.01
decay_rate = 0.1
eps_adam = 1e-08
adam_step = 100.0
neg_large = -1e30
rope_base = 10000.0


def padded(shard, sides, width):
    for axis, dim in sides:
        size, length = (lax.axis_size(axis), shard.shape[dim])
        up = [(i, (i + 1) % size) for i in range(size - 1)]
        down = [(j, i) for i, j in up]
        last = lax.slice_in_dim(shard, length - width, length, axis=dim)
        first = lax.slice_in_dim(shard, 0, width, axis=dim)
        before = lax.ppermute(last, axis, up)
        after = lax.ppermute(first, axis, down)
        shard = jnp.concatenate([before, shard, after], axis=dim)
    return shard


def unpack(flat_params):
    end_qkv = D * 3 * D
    end_out = end_qkv + D * D
    end_mlp = end_out + D * 2 * FF
    end_down = end_mlp + FF * D
    w_qkv = flat_params[:end_qkv].reshape(D, 3 * D)
    w_out = flat_params[end_qkv:end_out].reshape(D, D)
    w_gate_up = flat_params[end_out:end_mlp].reshape(D, 2 * FF)
    w_down = flat_params[end_mlp:end_down].reshape(FF, D)
    vectors = flat_params[end_down:].reshape(6, D).astype(jnp.float32)
    return (w_qkv, w_out, w_gate_up, w_down, vectors)


def clip_info(lengths, glob):
    clip_ends = jnp.cumsum(lengths, axis=1, dtype=jnp.int32)
    clip_starts = clip_ends - lengths
    after_end = (glob[None, :, None] >= clip_ends[:, None, :]).astype(jnp.int32)
    segment = jnp.sum(after_end, axis=2, dtype=jnp.int32)
    onehot = segment[:, :, None] == jnp.arange(lengths.shape[1], dtype=jnp.int32)[None, None, :]
    clip_begin = jnp.sum(jnp.where(onehot, clip_starts[:, None, :], 0), axis=2, dtype=jnp.int32)
    return (segment, (glob[None, :] - clip_begin).astype(jnp.float32))


def rotate(values, position, sign):
    half_dim = values.shape[-1] // 2
    inverse = jnp.exp(
        jnp.arange(half_dim, dtype=jnp.float32) * (-2.0 * math.log(rope_base) / HEAD_DIM)
    )
    rot_angle = position[:, :, None, None] * inverse
    cosine = jnp.cos(rot_angle)
    rot_sine = sign * jnp.sin(rot_angle)
    low_half = values[..., :half_dim]
    high_half = values[..., half_dim:]
    return jnp.concatenate(
        [low_half * cosine - high_half * rot_sine, high_half * cosine + low_half * rot_sine],
        axis=-1,
    )


def norm_forward(row_vals, norm_gain, norm_bias):
    centered = row_vals - jnp.mean(row_vals, axis=-1, keepdims=True)
    inv_scale = lax.rsqrt(jnp.mean(centered * centered, axis=-1, keepdims=True) + eps_norm)
    normed = centered * inv_scale
    return (normed * norm_gain + norm_bias, normed, inv_scale)


def norm_backward(out_grad, normed, inv_scale, norm_gain):
    d_gain = jnp.sum(out_grad * normed, axis=0)
    d_bias = jnp.sum(out_grad, axis=0)
    inner_grad = out_grad * norm_gain
    d_rows = inv_scale * (
        inner_grad
        - jnp.mean(inner_grad, axis=-1, keepdims=True)
        - normed * jnp.mean(inner_grad * normed, axis=-1, keepdims=True)
    )
    return (d_rows, d_gain, d_bias)


def scores_of(query_rows, key_rows, window_mask):
    raw_scores = jnp.einsum(
        "qhd,khd->hqk", query_rows, key_rows, preferred_element_type=jnp.float32
    ) * HEAD_DIM ** (-0.5)
    return jnp.where(window_mask[None], raw_scores, neg_large)


def attend(query_rows, key_rows, value_rows, window_mask):
    masked = scores_of(query_rows, key_rows, window_mask)
    row_max = jnp.max(masked, axis=-1, keepdims=True)
    row_total = jnp.log(jnp.sum(jnp.exp(masked - row_max), axis=-1, keepdims=True)) + row_max
    prob_low = jnp.exp(masked - row_total).astype(jnp.bfloat16)
    attn_rows = jnp.einsum("hqk,khd->qhd", prob_low, value_rows, preferred_element_type=jnp.float32)
    return (attn_rows, row_total[..., 0])


def attend_back(query_rows, key_rows, value_rows, window_mask, row_total, d_attn):
    masked = scores_of(query_rows, key_rows, window_mask)
    prob_rows = jnp.exp(masked - row_total[..., None])
    prob_low = prob_rows.astype(jnp.bfloat16)
    d_values = jnp.einsum("hqk,qhd->khd", prob_low, d_attn, preferred_element_type=jnp.float32)
    d_probs = jnp.einsum("qhd,khd->hqk", d_attn, value_rows, preferred_element_type=jnp.float32)
    inner_sum = jnp.sum(prob_rows * d_probs, axis=-1, keepdims=True)
    d_scores = (prob_rows * (d_probs - inner_sum)).astype(jnp.bfloat16)
    d_query = jnp.einsum(
        "hqk,khd->qhd", d_scores, key_rows, preferred_element_type=jnp.float32
    ) * HEAD_DIM ** (-0.5)
    d_keys = jnp.einsum(
        "hqk,qhd->khd", d_scores, query_rows, preferred_element_type=jnp.float32
    ) * HEAD_DIM ** (-0.5)
    return (d_query, d_keys, d_values)


def adam_update(flat_params, grads, first_moment, second_moment):
    new_first = beta_one * first_moment + (1.0 - beta_one) * grads
    new_second = beta_two * second_moment + (1.0 - beta_two) * grads * grads
    corrected_first = new_first / (1.0 - beta_one**adam_step)
    corrected_second = new_second / (1.0 - beta_two**adam_step)
    step_size = corrected_first / (jnp.sqrt(corrected_second) + eps_adam) + decay_rate * flat_params
    return (flat_params - learn_rate * step_size, new_first, new_second)


def body(frames, cotangent, clip_lengths, params, first_moment, second_moment):
    seq_count, frame_span, model_width = frames.shape
    row_count = seq_count * frame_span
    window_reach = WINDOW
    key_count = frame_span + 2 * window_reach
    head_count = HEADS
    head_size = model_width // head_count
    group_size = 4
    seq_len = lax.axis_size("seq") * frame_span
    seq_start = lax.axis_index("seq") * frame_span
    glob_rows = seq_start + jnp.arange(frame_span, dtype=jnp.int32)
    glob_keys = seq_start - window_reach + jnp.arange(key_count, dtype=jnp.int32)
    seg_rows, pos_rows = clip_info(clip_lengths, glob_rows)
    seg_keys, unused = clip_info(clip_lengths, glob_keys)
    inside = (glob_keys >= 0) & (glob_keys < seq_len)
    near_band = (
        jnp.abs(jnp.arange(frame_span)[:, None] + window_reach - jnp.arange(key_count)[None, :])
        < window_reach
    )
    window_mask = (
        (seg_rows[:, :, None] == seg_keys[:, None, :]) & inside[None, None, :] & near_band[None]
    )
    keep_rows = seg_rows != clip_lengths.shape[1] - 1
    shards = params.astype(jnp.bfloat16)
    gathered = lax.all_gather(shards, ("dp", "seq"), axis=0, tiled=True)
    w_qkv, w_out, w_gate_up, w_down, vectors = unpack(gathered)
    x_rows = frames.reshape(row_count, model_width).astype(jnp.float32)
    norm_one, normed_one, scale_one = norm_forward(x_rows, vectors[0], vectors[1])
    a_low = norm_one.astype(jnp.bfloat16)
    qkv = jnp.dot(a_low, w_qkv, preferred_element_type=jnp.float32).reshape(
        seq_count, frame_span, 3, head_count, head_size
    )
    query_low = rotate(qkv[:, :, 0], pos_rows, 1.0).astype(jnp.bfloat16)
    key_low = rotate(qkv[:, :, 1], pos_rows, 1.0).astype(jnp.bfloat16)
    value_low = qkv[:, :, 2].astype(jnp.bfloat16)
    key_value = jnp.concatenate([key_low, value_low], axis=2).reshape(
        seq_count, frame_span, 2 * model_width
    )
    wide_rows = padded(key_value, (("seq", 1),), window_reach)
    wide_rows = wide_rows.reshape(seq_count, key_count, 2, head_count, head_size)
    key_wide = wide_rows[:, :, 0]
    value_wide = wide_rows[:, :, 1]
    seq_index = 0
    out_parts = []
    total_parts = []
    for head_start in range(0, head_count, group_size):
        head_end = head_start + group_size
        attn_rows, row_total = attend(
            query_low[seq_index, :, head_start:head_end],
            key_wide[seq_index, :, head_start:head_end],
            value_wide[seq_index, :, head_start:head_end],
            window_mask[seq_index],
        )
        out_parts.append(attn_rows)
        total_parts.append(row_total)
    attn_list = [jnp.concatenate(out_parts, axis=1)]
    total_list = [total_parts]
    attn_all = jnp.where(keep_rows[:, :, None, None], jnp.stack(attn_list), 0.0)
    attn_low = attn_all.reshape(row_count, model_width).astype(jnp.bfloat16)
    branch_attn = jnp.dot(attn_low, w_out, preferred_element_type=jnp.float32)
    mid_rows = x_rows + vectors[4] * branch_attn
    norm_two, normed_two, scale_two = norm_forward(mid_rows, vectors[2], vectors[3])
    c_low = norm_two.astype(jnp.bfloat16)
    gate_up = jnp.dot(c_low, w_gate_up, preferred_element_type=jnp.float32)
    gate = gate_up[:, :FF]
    up_rows = gate_up[:, FF:]
    gate_sig = jax.nn.sigmoid(gate)
    hidden = (gate * gate_sig * up_rows).astype(jnp.bfloat16)
    branch_mlp = jnp.dot(hidden, w_down, preferred_element_type=jnp.float32)
    output = (
        (mid_rows + vectors[5] * branch_mlp)
        .astype(jnp.bfloat16)
        .reshape(seq_count, frame_span, model_width)
    )
    gathered = lax.all_gather(shards, ("dp", "seq"), axis=0, tiled=True)
    w_qkv, w_out, w_gate_up, w_down, vectors = unpack(gathered)
    d_rows = cotangent.reshape(row_count, model_width).astype(jnp.float32)
    g_scale_mlp = jnp.sum(d_rows * branch_mlp, axis=0)
    d_mlp = (d_rows * vectors[5]).astype(jnp.bfloat16)
    g_down = jnp.dot(hidden.T, d_mlp, preferred_element_type=jnp.float32)
    d_hidden = jnp.dot(d_mlp, w_down.T, preferred_element_type=jnp.float32)
    d_gate = d_hidden * up_rows * gate_sig * (1.0 + gate * (1.0 - gate_sig))
    d_up = d_hidden * gate * gate_sig
    d_gate_up = jnp.concatenate([d_gate, d_up], axis=1).astype(jnp.bfloat16)
    g_gate_up = jnp.dot(c_low.T, d_gate_up, preferred_element_type=jnp.float32)
    d_two = jnp.dot(d_gate_up, w_gate_up.T, preferred_element_type=jnp.float32)
    d_norm_two, g_gain_two, g_bias_two = norm_backward(d_two, normed_two, scale_two, vectors[2])
    d_mid = d_rows + d_norm_two
    g_scale_attn = jnp.sum(d_mid * branch_attn, axis=0)
    d_branch = (d_mid * vectors[4]).astype(jnp.bfloat16)
    g_out = jnp.dot(attn_low.T, d_branch, preferred_element_type=jnp.float32)
    d_attn_low = jnp.dot(d_branch, w_out.T, preferred_element_type=jnp.float32).astype(jnp.bfloat16)
    d_attn = jnp.where(
        keep_rows[:, :, None, None],
        d_attn_low.reshape(seq_count, frame_span, head_count, head_size),
        jnp.zeros((), jnp.bfloat16),
    )
    seq_index = 0
    query_parts = []
    key_parts = []
    value_parts = []
    for number, head_start in enumerate(range(0, head_count, group_size)):
        head_end = head_start + group_size
        d_query, d_keys, d_values = attend_back(
            query_low[seq_index, :, head_start:head_end],
            key_wide[seq_index, :, head_start:head_end],
            value_wide[seq_index, :, head_start:head_end],
            window_mask[seq_index],
            total_list[seq_index][number],
            d_attn[seq_index, :, head_start:head_end],
        )
        query_parts.append(d_query)
        key_parts.append(d_keys)
        value_parts.append(d_values)
    query_grads = [jnp.concatenate(query_parts, axis=1)]
    key_grads = [jnp.concatenate(key_parts, axis=1)]
    value_grads = [jnp.concatenate(value_parts, axis=1)]
    d_query_all = jnp.stack(query_grads)
    d_pair = jnp.concatenate([jnp.stack(key_grads), jnp.stack(value_grads)], axis=2).reshape(
        seq_count, key_count, 2 * model_width
    )
    rim_rows = jnp.concatenate(
        [d_pair[:, :window_reach], d_pair[:, window_reach + frame_span :]], axis=1
    )
    taken_rows = padded(rim_rows.astype(jnp.bfloat16), (("seq", 1),), window_reach).astype(
        rim_rows.dtype
    )
    own_rows = d_pair[:, window_reach : window_reach + frame_span]
    own_rows = own_rows + jnp.pad(
        taken_rows[:, :window_reach], ((0, 0), (0, frame_span - window_reach), (0, 0))
    )
    own_rows = own_rows + jnp.pad(
        taken_rows[:, 3 * window_reach :], ((0, 0), (frame_span - window_reach, 0), (0, 0))
    )
    own_rows = own_rows.reshape(seq_count, frame_span, 2, head_count, head_size)
    d_qkv = jnp.stack(
        [
            rotate(d_query_all, pos_rows, -1.0),
            rotate(own_rows[:, :, 0], pos_rows, -1.0),
            own_rows[:, :, 1],
        ],
        axis=2,
    )
    d_qkv = d_qkv.reshape(row_count, 3 * model_width).astype(jnp.bfloat16)
    g_qkv = jnp.dot(a_low.T, d_qkv, preferred_element_type=jnp.float32)
    d_one = jnp.dot(d_qkv, w_qkv.T, preferred_element_type=jnp.float32)
    d_norm_one, g_gain_one, g_bias_one = norm_backward(d_one, normed_one, scale_one, vectors[0])
    frames_grad = (
        (d_mid + d_norm_one).astype(jnp.bfloat16).reshape(seq_count, frame_span, model_width)
    )
    small_grads = jnp.stack(
        [g_gain_one, g_bias_one, g_gain_two, g_bias_two, g_scale_attn, g_scale_mlp]
    )
    whole_grad = jnp.concatenate(
        [
            g_qkv.reshape(-1),
            g_out.reshape(-1),
            g_gate_up.reshape(-1),
            g_down.reshape(-1),
            small_grads.reshape(-1),
        ]
    )
    params_grad = lax.psum_scatter(whole_grad, ("dp", "seq"), scatter_dimension=0, tiled=True)
    new_params, new_first, new_second = adam_update(
        params, params_grad, first_moment, second_moment
    )
    return (output, frames_grad, params_grad, new_params, new_first, new_second)


EVERY = ("z", "x", "c", "y")
GROUP = ("z", "x")
RING = ((0, 0), (1, 0), (2, 0), (3, 0), (3, 1), (2, 1), (1, 1), (0, 1))
PLACES = tuple(2 * z + x for z, x in RING)
AHEAD = tuple((PLACES[i], PLACES[(i + 1) % 8]) for i in range(8))
BACK = tuple((b, a) for a, b in AHEAD)
SWAP = ((0, 1), (1, 0))
LINES = 4096
TAIL = 64
PITCH = 72
SLAB = 16
ROWS = 128 + SLAB
OWN = 256
SCALE = HEAD_DIM ** (-0.5)
SCALAR = pl.BlockSpec(memory_space=pltpu.SMEM)
WHOLE = pl.BlockSpec(memory_space=pltpu.VMEM)
HBM = pl.BlockSpec(memory_space=pltpu.HBM)
ANY = pl.BlockSpec(memory_space=pl.ANY)


def vmem(mebibytes):
    return pltpu.CompilerParams(vmem_limit_bytes=mebibytes << 20)


def ring_place(me, step):
    z, x = lax.div(me, 8), lax.rem(lax.div(me, 4), 2)
    at = lax.rem(jnp.where(x == 0, z, 7 - z) + step, 8)
    return jnp.where(at < 4, 2 * at, 15 - 2 * at)


def kind_of(shard):
    if shard < 6:
        return 0
    return 2 if 8 <= shard < 24 else 1


def piece_lines(kind, dest, pitch=64):
    place, member = divmod(dest, 4)
    if kind == 0:
        return [(512 * place + member, 8), (512 * place + 4 + member, 8)]
    if kind == 1:
        return [(1024 * member + place, 8), (1024 * member + 512 + place, 8)]
    return [(dest, pitch), (32 + dest, pitch)]


def tail_lines(kind, dest):
    place, member = divmod(dest, 4)
    if kind == 0:
        return [(0, 6, member, 8), (8, 6, 4 + member, 8)] if place == 0 else []
    if kind == 1:
        return [(0, 6, place, 8)] if member == 0 else []
    return [(0, 1, dest, 1)] + ([(8, 1, 32 + dest, 1)] if dest < 16 else [])


def is_kind(shard, kind):
    if kind == 0:
        return shard < 6
    gate_up = (shard >= 8) & (shard < 24)
    if kind == 2:
        return gate_up
    return (shard >= 6) & jnp.logical_not(gate_up) & (shard < 32)


def spread_kernel(me_ref, flat_ref, out_ref, lines_ref, tail_ref):
    me = me_ref[0]
    odd = lax.rem(me, 2) == 1
    start = 48 - (3 * me + 1) // 2
    lane = lax.broadcasted_iota(jnp.int32, (64, 128), 1)

    def shifted(step):
        here = flat_ref[pl.ds(start + step * 64, 64), :]
        after = flat_ref[pl.ds(start + step * 64 + 1, 64), :]
        mixed = jnp.where(lane < 64, pltpu.roll(here, 64, 1), pltpu.roll(after, 64, 1))
        return jnp.where(odd, mixed, here)

    def fill(pitch):
        def body(step, carry):
            lines_ref[pl.ds(pl.multiple_of(step * pitch, 8), 64), :] = shifted(step)
            return carry

        lax.fori_loop(0, LINES // 64, body, 0, unroll=4)

    tail_ref[:TAIL, :] = shifted(LINES // 64)
    for kind in range(3):

        @pl.when(is_kind(me, kind))
        def _(kind=kind):
            pitch = PITCH if kind == 2 else 64
            fill(pitch)
            for dest in range(32):
                for half, (first, stride) in enumerate(piece_lines(kind, dest, pitch)):
                    rows = lines_ref[pl.ds(first, 64, stride), :]
                    out_ref[dest, 64 * half : 64 * half + 64, :] = rows.astype(jnp.bfloat16)

    def slab_of(parts):
        slab = [jnp.zeros((8, 128), jnp.float32)] * 2
        row = lax.broadcasted_iota(jnp.int32, (8, 128), 0)
        for at, count, first, stride in parts:
            if count == 1:
                value = jnp.broadcast_to(tail_ref[first : first + 1, :], (8, 128))
            else:
                value = tail_ref[pl.ds(first, 8, stride), :]
            slab[at // 8] = jnp.where(row < count, value, 0.0)
        return jnp.concatenate(slab, axis=0).astype(jnp.bfloat16)

    for kind in range(3):

        @pl.when(is_kind(me + 1, kind))
        def _(kind=kind):
            for dest in range(32):
                out_ref[dest, 128:ROWS, :] = slab_of(tail_lines(kind, dest))

    @pl.when(me == 31)
    def _():
        for dest in range(32):
            out_ref[dest, 128:ROWS, :] = slab_of([(0, 6, 6 * (dest // 4), 1)])


def spread(params, me):
    flat = jnp.pad(params, (48 * 128, 4224 * 128 - 48 * 128 - params.shape[0])).reshape(4224, 128)
    return pl.pallas_call(
        spread_kernel,
        out_shape=jax.ShapeDtypeStruct((32, ROWS, 128), jnp.bfloat16),
        in_specs=[
            pl.BlockSpec(memory_space=pltpu.SMEM),
            pl.BlockSpec(memory_space=pltpu.VMEM),
        ],
        out_specs=pl.BlockSpec(memory_space=pltpu.VMEM),
        scratch_shapes=[
            pltpu.VMEM((LINES // 64 * PITCH + PITCH, 128), jnp.float32),
            pltpu.VMEM((TAIL + 16, 128), jnp.float32),
        ],
        compiler_params=vmem(12),
        name="spread",
    )(me, flat)


def collect_kernel(me_ref, piece_ref, out_ref, lines_ref, rows_ref):
    me = me_ref[0]
    odd = lax.rem(me, 2) == 1
    lines_ref[LINES:, :] = jnp.zeros((TAIL, 128), jnp.float32)
    for kind in range(3):

        @pl.when(is_kind(me, kind))
        def _(kind=kind):
            if kind == 2:
                for dest in range(32):
                    rows_ref[136 * dest : 136 * dest + 128, :] = piece_ref[dest, :128, :].astype(jnp.float32)
                for row in range(128):
                    first = 64 * (row % 64) + 32 * (row // 64)
                    lines_ref[first : first + 32, :] = rows_ref[pl.ds(row, 32, 136), :]
                return
            for dest in range(32):
                for half, (first, stride) in enumerate(piece_lines(kind, dest)):
                    rows = piece_ref[dest, 64 * half : 64 * half + 64, :].astype(jnp.float32)
                    lines_ref[pl.ds(first, 64, stride), :] = rows

    for kind in range(3):

        @pl.when(is_kind(me + 1, kind))
        def _(kind=kind):
            for dest in range(32):
                slab = piece_ref[dest, 128:ROWS, :].astype(jnp.float32)
                for at, count, first, stride in tail_lines(kind, dest):
                    for k in range(count):
                        line = LINES + first + k * stride
                        lines_ref[line : line + 1, :] = slab[at + k : at + k + 1, :]

    @pl.when(me == 31)
    def _():
        for place in range(8):
            total = piece_ref[4 * place, 128:ROWS, :].astype(jnp.float32)
            for member in range(1, 4):
                total = total + piece_ref[4 * place + member, 128:ROWS, :].astype(jnp.float32)
            for k in range(6):
                line = LINES + 6 * place + k
                lines_ref[line : line + 1, :] = total[k : k + 1, :]

    start = (3 * me) // 2
    lane = lax.broadcasted_iota(jnp.int32, (24, 128), 1)

    def shift(step, carry):
        here = lines_ref[pl.ds(start + step * 24, 24), :]
        after = lines_ref[pl.ds(start + step * 24 + 1, 24), :]
        mixed = jnp.where(lane < 64, pltpu.roll(here, 64, 1), pltpu.roll(after, 64, 1))
        out_ref[pl.ds(pl.multiple_of(step * 24, 8), 24), :] = jnp.where(odd, mixed, here)
        return carry

    lax.fori_loop(0, 4104 // 24, shift, 0, unroll=9)


def collect(pieces, me, count):
    lines = pl.pallas_call(
        collect_kernel,
        out_shape=jax.ShapeDtypeStruct((4104, 128), jnp.float32),
        in_specs=[
            pl.BlockSpec(memory_space=pltpu.SMEM),
            pl.BlockSpec(memory_space=pltpu.VMEM),
        ],
        out_specs=pl.BlockSpec(memory_space=pltpu.VMEM),
        scratch_shapes=[
            pltpu.VMEM((LINES + TAIL, 128), jnp.float32),
            pltpu.VMEM((33 * 136, 128), jnp.float32),
        ],
        compiler_params=vmem(12),
        name="collect",
    )(me, pieces)
    return lines.reshape(-1)[:count]


def swap_halves(rows):
    lane = lax.broadcasted_iota(jnp.int32, rows.shape, 1)
    return jnp.where(
        lax.rem(lane, 64) < 32, pltpu.roll(rows, 96, 1), pltpu.roll(rows, 32, 1)
    )


def turn(rows, cosine, signed_sine):
    parts = []
    for at in range(0, rows.shape[1], 128):
        part = rows[:, at : at + 128]
        parts.append(part * cosine + swap_halves(part) * signed_sine)
    return jnp.concatenate(parts, axis=1)


def clip_of(length_ref, frame):
    first = length_ref[0, 0]
    return (frame >= first).astype(jnp.int32) + (frame >= first + length_ref[0, 1]).astype(jnp.int32)


def mask_of(length_ref, block):
    row = lax.broadcasted_iota(jnp.int32, (256, 384), 0) + 256 * block
    key = lax.broadcasted_iota(jnp.int32, (256, 384), 1) + 128 * block
    own = clip_of(length_ref, lax.broadcasted_iota(jnp.int32, (256, 1), 0) + 256 * block)
    others = clip_of(length_ref, lax.broadcasted_iota(jnp.int32, (1, 384), 1) + 128 * block)
    return (jnp.abs(row - key) < WINDOW) & (own == others), own != 1


def nt(left, right):
    return lax.dot_general(left, right, (((1,), (1,)), ((), ())), preferred_element_type=jnp.float32)


def tn(left, right):
    return lax.dot_general(left, right, (((0,), (0,)), ((), ())), preferred_element_type=jnp.float32)


def nn(left, right):
    return jnp.dot(left, right, preferred_element_type=jnp.float32)


def cost(flops, moved):
    return pl.CostEstimate(flops=flops, bytes_accessed=moved, transcendentals=0)


def fix_kernel(piece_ref, first_ref, second_ref, third_ref):
    for source in range(32):
        out, at = (first_ref, source) if source < 8 else (second_ref, source - 8) if source < 24 else (third_ref, source - 24)
        out[128 * at : 128 * at + 128, :] = piece_ref[source, :128, :]
        if source:
            slab = piece_ref[source - 1, 128:ROWS, :].astype(jnp.float32)
            for half in range(2):
                rows = piece_ref[source, 64 * half : 64 * half + 16, :].astype(jnp.float32)
                extra = jnp.concatenate([slab[8 * half : 8 * half + 8], jnp.zeros((8, 128), jnp.float32)])
                out[128 * at + 64 * half : 128 * at + 64 * half + 16, :] = (rows + extra).astype(jnp.bfloat16)
    first_ref[1024:, :] = piece_ref[31, 128:ROWS, :]


def fix(pieces):
    return pl.pallas_call(
        fix_kernel,
        out_shape=tuple(jax.ShapeDtypeStruct((n, 128), jnp.bfloat16) for n in (1024 + SLAB, 2048, 1024)),
        in_specs=[WHOLE],
        out_specs=(WHOLE,) * 3,
        compiler_params=vmem(12),
        cost_estimate=cost(0, 1 << 22),
        name="fix",
    )(pieces)


def in_order(refs, seq, half, second):
    mine, other = refs[2 * seq], refs[2 * seq + 1]
    return jnp.where(lax.rem(second, 2) == half, mine[...], other[...])


def ring_parts(me_ref, refs):
    me = me_ref[0]
    parts = [(ring_place(me, 0), refs[0], None)]
    for step in range(1, 4):
        parts += [(ring_place(me, 8 - step), refs[2 * step - 1], None), (ring_place(me, step), refs[2 * step], None)]
    half = refs[7].shape[0]
    last = ring_place(me, 4)
    return parts + [(last, refs[7], (0, half)), (last, refs[8], (half, half + refs[8].shape[0]))]


def copy_all(pairs, done):
    copies = [pltpu.make_async_copy(source, target, done.at[k]) for k, (source, target) in enumerate(pairs)]
    for copy in copies:
        copy.start()
    for copy in copies:
        copy.wait()


def join_first_kernel(me_ref, *refs):
    blocks, (qkv_ref, out_ref, vec_ref, lines_ref, _) = refs[:9], refs[9:]
    for place, block, rows in ring_parts(me_ref, blocks):
        lo, hi = rows or (0, 1024 + SLAB)
        for at, end, ref in ((0, 768, qkv_ref), (768, 1024, out_ref), (1024, 1024 + SLAB, lines_ref)):
            first, last = max(at, lo), min(end, hi)
            if first < last:
                ref[place, first - at : last - at, :] = block[first - lo : last - lo, :]
    slabs = [lines_ref[place].astype(jnp.float32) for place in range(8)]
    for v in range(6):
        for k in range(8):
            line = 8 * v + k
            vec_ref[v : v + 1, 128 * k : 128 * k + 128] = slabs[line // 6][line % 6 : line % 6 + 1]


def join_gate_up_kernel(which, me_ref, *refs):
    blocks, (out_ref, done) = refs[:9], refs[-2:]
    pairs = []
    for place, block, rows in ring_parts(me_ref, blocks)[which]:
        lo, hi = rows or (0, 16)
        for half in range(2):
            at = pl.multiple_of(256 * half + 128 * lax.rem(place, 2), 128)
            pairs.append((block.at[:, half], out_ref.at[lax.div(place, 2), lo:hi, :, pl.ds(at, 128)]))
    copy_all(pairs, done)


def join_down_kernel(which, me_ref, *refs):
    blocks, (out_ref, done) = refs[:9], refs[-2:]
    pairs = []
    for place, block, rows in ring_parts(me_ref, blocks)[which]:
        lo, hi = rows or (0, 1024)
        pairs.append((block, out_ref.at[lo:hi, pl.ds(pl.multiple_of(128 * place, 128), 128)]))
    copy_all(pairs, done)


def join_out_kernel(*refs):
    w_ref = refs[4]
    for k in range(4):
        for place in range(8):
            w_ref[256 * k : 256 * k + 256, 128 * place : 128 * place + 128] = refs[k][place]


def join_out(parts):
    return pl.pallas_call(
        join_out_kernel,
        out_shape=jax.ShapeDtypeStruct((D, D), jnp.bfloat16),
        in_specs=[WHOLE] * 4,
        out_specs=WHOLE,
        compiler_params=vmem(12),
        cost_estimate=cost(0, 4 << 20),
        name="join_out",
    )(*parts)


def join(kernel, me, blocks, out_shape, name, scratch=(), space=WHOLE):
    if space is HBM:
        blocks = [pltpu.with_memory_space_constraint(block, pltpu.HBM) for block in blocks]
    return pl.pallas_call(
        kernel,
        out_shape=out_shape,
        in_specs=[SCALAR] + [space] * 9,
        out_specs=jax.tree.map(lambda _: WHOLE, out_shape),
        scratch_shapes=list(scratch) + [pltpu.SemaphoreType.DMA((32,))],
        compiler_params=vmem(12),
        cost_estimate=cost(0, 4 << 20),
        name=name,
    )(me, *blocks)


def join_rest_kernel(kernel, me_ref, last_ref, end_ref, _, out_ref, done):
    kernel(slice(7, 9), me_ref, *([last_ref] * 8 + [end_ref]), out_ref, done)


def join_twice(kernel, me, blocks, out_shape, name):
    early = [pltpu.with_memory_space_constraint(block, pltpu.HBM) for block in blocks[:7]]
    whole = pl.pallas_call(
        lambda me_ref, *refs: kernel(slice(0, 7), me_ref, *refs[:7], refs[6], refs[6], *refs[7:]),
        out_shape=out_shape,
        in_specs=[SCALAR] + [HBM] * 7,
        out_specs=WHOLE,
        scratch_shapes=[pltpu.SemaphoreType.DMA((32,))],
        compiler_params=vmem(12),
        cost_estimate=cost(0, 4 << 20),
        name=name,
    )(me, *early)
    last = after(tuple(blocks[7:]), whole)
    return pl.pallas_call(
        functools.partial(join_rest_kernel, kernel),
        out_shape=out_shape,
        in_specs=[SCALAR, ANY, ANY, WHOLE],
        out_specs=WHOLE,
        input_output_aliases={3: 0},
        scratch_shapes=[pltpu.SemaphoreType.DMA((32,))],
        compiler_params=vmem(12),
        cost_estimate=cost(0, 4 << 20),
        name=name + "_rest",
    )(me, *last, whole)


def prep_kernel(y_ref, own_ref, pair_ref, far_ref, last_ref, x_ref, mean_ref, inv_ref):
    for block in range(4):
        rows = slice(256 * block, 256 * block + 256)
        x_low = in_order((own_ref, pair_ref, far_ref, last_ref), block // 2, block % 2, y_ref[0])
        x_ref[rows, :] = x_low
        x_rows = x_low.astype(jnp.float32)
        mean = jnp.mean(x_rows, axis=1, keepdims=True)
        centered = x_rows - mean
        mean_ref[rows, :] = mean
        inv_ref[rows, :] = lax.rsqrt(jnp.mean(centered * centered, axis=1, keepdims=True) + eps_norm)


def prep(second, rows):
    return pl.pallas_call(
        prep_kernel,
        out_shape=(
            jax.ShapeDtypeStruct((1024, D), jnp.bfloat16),
            jax.ShapeDtypeStruct((1024, 1), jnp.float32),
            jax.ShapeDtypeStruct((1024, 1), jnp.float32),
        ),
        in_specs=[SCALAR] + [WHOLE] * 4,
        out_specs=(WHOLE,) * 3,
        compiler_params=vmem(12),
        cost_estimate=cost(1 << 24, 5 << 20),
        name="prep",
    )(second, *rows)


def front_kernel(
    x_ref, mean_ref, inv_ref, ring_ref, vec_ref, order_ref, cos_ref, sin_ref, length_ref, far_length_ref,
    a_out, w_out, low_out, attn_ref, lse_out,
    a_ref, w_ref, low_ref, lse_ref, done,
):
    copies = [
        pltpu.make_async_copy(ref, out, done.at[k])
        for k, (ref, out) in enumerate(((w_ref, w_out), (a_ref, a_out), (low_ref, low_out), (lse_ref, lse_out)))
    ]
    gain, bias = vec_ref[0:1, :], vec_ref[1:2, :]
    for block in range(8):
        parts = []
        for chunk in range(6 * block, 6 * block + 6):
            at = 128 * (chunk // 8)
            parts.append(
                jnp.concatenate(
                    [ring_ref[chunk % 8, at : at + 64, :], ring_ref[chunk % 8, at + 64 : at + 128, :]], axis=1
                )
            )
        rows = nn(order_ref[...], jnp.concatenate(parts, axis=0)).astype(jnp.bfloat16)
        for third in range(3):
            w_ref[128 * block : 128 * block + 128, OWN * third : OWN * third + OWN] = rows[
                128 * third : 128 * third + 128
            ]
    copies[0].start()
    for block in range(4):
        rows = slice(256 * block, 256 * block + 256)
        seq, at = block // 2, 256 * (block % 2)
        normed = (x_ref[rows, :].astype(jnp.float32) - mean_ref[rows, :]) * inv_ref[rows, :]
        a_low = (normed * gain + bias).astype(jnp.bfloat16)
        a_ref[rows, :] = a_low
        qkv = nn(a_low, w_ref[...])
        cosine, sine = cos_ref[seq, at : at + 256, :], sin_ref[seq, at : at + 256, :]
        low_ref[rows, : 2 * OWN] = turn(qkv[:, : 2 * OWN], cosine, sine).astype(jnp.bfloat16)
        low_ref[rows, 2 * OWN :] = qkv[:, 2 * OWN :].astype(jnp.bfloat16)
    copies[1].start()
    copies[2].start()
    for seq in range(2):
        for block in range(2):
            at = 512 * seq + 256 * block
            rows = slice(at, at + 256)
            keys = slice(512 * seq + 128 * block, 512 * seq + 128 * block + 384)
            mask, keep = mask_of((length_ref, far_length_ref)[seq], block)
            heads, sums = [], []
            for head in range(4):
                lane = 64 * head
                query = low_ref[rows, lane : lane + 64]
                key = low_ref[keys, OWN + lane : OWN + lane + 64]
                value = low_ref[keys, 2 * OWN + lane : 2 * OWN + lane + 64]
                masked = jnp.where(mask, nt(query, key) * SCALE, neg_large)
                top = jnp.max(masked, axis=1, keepdims=True)
                weight = jnp.exp(masked - top)
                total = jnp.sum(weight, axis=1, keepdims=True)
                probs = (weight * (1.0 / total)).astype(jnp.bfloat16)
                heads.append(jnp.where(keep, nn(probs, value), 0.0))
                sums.append(top + jnp.log(total))
            attn_ref[rows, :] = jnp.concatenate(heads, axis=1).astype(jnp.bfloat16)
            lse_ref[rows, :] = jnp.concatenate(sums, axis=1)
    copies[3].start()
    for copy in copies:
        copy.wait()


def front(x_all, mean, inv, ring, vectors, order, cosine, sine, lengths):
    return pl.pallas_call(
        front_kernel,
        out_shape=(
            pltpu.HBM((1024, D), jnp.bfloat16),
            pltpu.HBM((D, 3 * OWN), jnp.bfloat16),
            pltpu.HBM((1024, 3 * OWN), jnp.bfloat16),
            jax.ShapeDtypeStruct((1024, OWN), jnp.bfloat16),
            pltpu.HBM((1024, 4), jnp.float32),
        ),
        in_specs=[WHOLE] * 8 + [SCALAR] * 2,
        out_specs=(HBM, HBM, HBM, WHOLE, HBM),
        scratch_shapes=[
            pltpu.VMEM((1024, D), jnp.bfloat16),
            pltpu.VMEM((D, 3 * OWN), jnp.bfloat16),
            pltpu.VMEM((1024, 3 * OWN), jnp.bfloat16),
            pltpu.VMEM((1024, 4), jnp.float32),
            pltpu.SemaphoreType.DMA((4,)),
        ],
        compiler_params=vmem(14),
        cost_estimate=cost(12 << 30, 8 << 20),
        name="front",
    )(x_all, mean, inv, ring, vectors, order, cosine, sine, *lengths)


def mix_kernel(x_ref, own_ref, pair_ref, far_ref, last_ref, w_ref, vec_ref, c_ref, branch_ref):
    for block in range(4):
        rows = slice(256 * block, 256 * block + 256)
        other = (block + 2) % 4
        far = slice(256 * other, 256 * other + 256)
        attn = jnp.concatenate([own_ref[rows, :], pair_ref[rows, :], far_ref[far, :], last_ref[far, :]], axis=1)
        branch = nn(attn, w_ref[...])
        normed, _ = normed_of(x_ref[rows, :].astype(jnp.float32) + vec_ref[4:5, :] * branch)
        c_ref[rows, :] = (normed * vec_ref[2:3, :] + vec_ref[3:4, :]).astype(jnp.bfloat16)
        if block < 2:
            branch_ref[rows, :] = branch


def mix(x_all, attn, w_out, vectors):
    return pl.pallas_call(
        mix_kernel,
        out_shape=(
            pltpu.VMEM((1024, D), jnp.bfloat16),
            jax.ShapeDtypeStruct((512, D), jnp.float32),
        ),
        in_specs=[WHOLE] * 7,
        out_specs=(WHOLE, WHOLE),
        compiler_params=vmem(12),
        cost_estimate=cost(3 << 30, 10 << 20),
        name="mix",
    )(x_all, *attn, w_out, vectors)


def gate_kernel(c_ref, w_ref, gate_up_ref, hidden_ref):
    for block in range(4):
        rows = slice(256 * block, 256 * block + 256)
        for chunk in range(4):
            both = nn(c_ref[rows, :], w_ref[chunk])
            gate_up_ref[chunk, rows, :] = both
            gate, up = both[:, :256], both[:, 256:]
            hidden_ref[rows, 256 * chunk : 256 * chunk + 256] = (gate * jax.nn.sigmoid(gate) * up).astype(
                jnp.bfloat16
            )


def gate_step(c_low, w_gate_up):
    return pl.pallas_call(
        gate_kernel,
        out_shape=(
            jax.ShapeDtypeStruct((4, 1024, 512), jnp.float32),
            jax.ShapeDtypeStruct((1024, 1024), jnp.bfloat16),
        ),
        in_specs=[WHOLE] * 2,
        out_specs=(WHOLE, WHOLE),
        compiler_params=vmem(12),
        cost_estimate=cost(5 << 30, 16 << 20),
        name="gate",
    )(c_low, w_gate_up)


def down_grad_kernel(me_ref, hidden_ref, own_ref, pair_ref, far_ref, last_ref, vec_ref, g_ref, d_mlp_ref):
    for block in range(4):
        rows = in_order((own_ref, pair_ref, far_ref, last_ref), block // 2, block % 2, me_ref[0])
        d_mlp_ref[256 * block : 256 * block + 256, :] = (rows.astype(jnp.float32) * vec_ref[5:6, :]).astype(
            jnp.bfloat16
        )
    for source in range(0, 8, 2):
        g_down = tn(hidden_ref[:, 128 * source : 128 * source + 256], d_mlp_ref[...]).astype(jnp.bfloat16)
        for pair in range(2):
            for place in range(8):
                at = 128 * (source + pair)
                g_ref[place, at : at + 128, :] = g_down[128 * pair : 128 * pair + 128, 128 * place : 128 * place + 128]


def down_grad(me, hidden, cot, vectors):
    return pl.pallas_call(
        down_grad_kernel,
        out_shape=(
            jax.ShapeDtypeStruct((8, 1024, 128), jnp.bfloat16),
            jax.ShapeDtypeStruct((1024, D), jnp.bfloat16),
        ),
        in_specs=[SCALAR] + [WHOLE] * 6,
        out_specs=(WHOLE, WHOLE),
        compiler_params=vmem(12),
        cost_estimate=cost(3 << 30, 8 << 20),
        name="down_grad",
    )(me, hidden, *cot, vectors)


def put_rows(me, whole_ref, refs, done=None):
    y = lax.rem(me, 2)
    copies = []
    for k, (ref, half) in enumerate(zip(refs, (1 - y, y, 1 - y, y))):
        rows = pl.ds(pl.multiple_of(512 * (k // 2) + 256 * half, 256), 256)
        if done is not None and k < 2:
            copies.append(pltpu.make_async_copy(whole_ref.at[rows, :], ref, done.at[k]))
            copies[-1].start()
        else:
            ref[...] = whole_ref[rows, :].astype(ref.dtype)
    for copy in copies:
        copy.wait()


PARTS = tuple(jax.ShapeDtypeStruct((256, D), t) for t in (jnp.float32, jnp.float32, jnp.bfloat16, jnp.bfloat16))


def hidden_back_kernel(gate_up_ref, d_mlp_ref, w_ref, d_both_ref):
    for block in range(4):
        rows = slice(256 * block, 256 * block + 256)
        for chunk in range(4):
            d_hidden = nt(d_mlp_ref[rows, :], w_ref[256 * chunk : 256 * chunk + 256, :])
            gate, up = gate_up_ref[chunk, rows, :256], gate_up_ref[chunk, rows, 256:]
            sig = jax.nn.sigmoid(gate)
            d_both_ref[chunk, rows, :256] = (d_hidden * up * sig * (1.0 + gate * (1.0 - sig))).astype(jnp.bfloat16)
            d_both_ref[chunk, rows, 256:] = (d_hidden * gate * sig).astype(jnp.bfloat16)


def hidden_back(gate_up, d_mlp, w_down):
    return pl.pallas_call(
        hidden_back_kernel,
        out_shape=jax.ShapeDtypeStruct((4, 1024, 512), jnp.bfloat16),
        in_specs=[WHOLE] * 3,
        out_specs=WHOLE,
        compiler_params=vmem(12),
        cost_estimate=cost(4 << 30, 18 << 20),
        name="hidden_back",
    )(gate_up, d_mlp, w_down)


def norm_back_kernel(y_ref, d_both_ref, w_ref, near_sent_ref, near_ref, far_sent_ref, far_ref, d_c_ref):
    for block in range(4):
        rows = slice(256 * block, 256 * block + 256)
        d_c = nt(d_both_ref[0, rows, :], w_ref[0])
        for chunk in range(1, 4):
            d_c += nt(d_both_ref[chunk, rows, :], w_ref[chunk])
        d_c_ref[rows, :] = d_c
    put_rows(y_ref[0], d_c_ref, (near_sent_ref, near_ref, far_sent_ref, far_ref))


def norm_back(second, d_both, w_gate_up):
    return pl.pallas_call(
        norm_back_kernel,
        out_shape=PARTS,
        in_specs=[SCALAR, WHOLE, WHOLE],
        scratch_shapes=[pltpu.VMEM((1024, D), jnp.float32)],
        out_specs=(WHOLE,) * 4,
        compiler_params=vmem(12),
        cost_estimate=cost(5 << 30, 12 << 20),
        name="norm_back",
    )(second, d_both, w_gate_up)


def gate_grad_kernel(c_ref, d_both_ref, g_ref):
    for chunk in range(4):
        for block in range(4):
            grad = tn(c_ref[:, 256 * block : 256 * block + 256], d_both_ref[chunk]).astype(jnp.bfloat16)
            for part in range(4):
                source = 4 * block + part
                for pair in range(2):
                    for half in range(2):
                        at = 256 * half + 128 * pair
                        first = 128 * source + 64 * half
                        g_ref[2 * chunk + pair, first : first + 64, :] = grad[64 * part : 64 * part + 64, at : at + 128]


def gate_grad(c_low, d_both):
    return pl.pallas_call(
        gate_grad_kernel,
        out_shape=jax.ShapeDtypeStruct((8, 2048, 128), jnp.bfloat16),
        in_specs=[WHOLE] * 2,
        out_specs=WHOLE,
        compiler_params=vmem(12),
        cost_estimate=cost(5 << 30, 10 << 20),
        name="gate_grad",
    )(c_low, d_both)


def out_kernel(
    y_ref, hidden_ref, w_ref, own_ref, pair_ref, last_ref, end_ref,
    near_sent_ref, near_ref, far_sent_ref, far_ref, g_scale_ref,
    branch_ref, done,
):
    total = jnp.zeros((1, D), jnp.float32)
    for block in range(4):
        rows = slice(256 * block, 256 * block + 256)
        branch = nn(hidden_ref[rows, :], w_ref[...])
        branch_ref[rows, :] = branch
        cot = in_order((own_ref, pair_ref, last_ref, end_ref), block // 2, block % 2, y_ref[0])
        total += jnp.sum(cot.astype(jnp.float32) * branch, axis=0, keepdims=True)
    g_scale_ref[...] = total
    put_rows(y_ref[0], branch_ref, (near_sent_ref, near_ref, far_sent_ref, far_ref), done)


def out_step(second, hidden, down, cot):
    return pl.pallas_call(
        out_kernel,
        out_shape=(pltpu.HBM((256, D), jnp.float32),) * 2 + PARTS[2:] + (jax.ShapeDtypeStruct((1, D), jnp.float32),),
        in_specs=[SCALAR] + [WHOLE] * 6,
        scratch_shapes=[pltpu.VMEM((1024, D), jnp.float32), pltpu.SemaphoreType.DMA((2,))],
        out_specs=(HBM, HBM, WHOLE, WHOLE, WHOLE),
        compiler_params=vmem(12),
        cost_estimate=cost(3 << 30, 10 << 20),
        name="out",
    )(second, hidden, down, *cot)


def attend_back_kernel(
    y_ref, own_ref, pair_ref, far_ref, last_ref, ring_ref, attn_ref, low_ref, lse_ref, cos_ref, sin_ref,
    length_ref, far_length_ref,
    d_qkv_ref, g_ref,
    d_branch_ref, w_out_ref, key_ref, value_ref,
):
    for place in range(8):
        w_out_ref[:, 128 * place : 128 * place + 128] = ring_ref[place]
    for block in range(4):
        d_branch_ref[256 * block : 256 * block + 256, :] = in_order(
            (own_ref, pair_ref, far_ref, last_ref), block // 2, block % 2, y_ref[0]
        )
    g_out = tn(attn_ref[...], d_branch_ref[...]).astype(jnp.bfloat16)
    for place in range(8):
        g_ref[place] = g_out[:, 128 * place : 128 * place + 128]
    for seq in range(2):
        key_ref[...] = jnp.zeros_like(key_ref)
        value_ref[...] = jnp.zeros_like(value_ref)
        cosine, sine = cos_ref[seq], -sin_ref[seq]
        for block in range(2):
            at = 512 * seq + 256 * block
            rows = slice(at, at + 256)
            span = slice(128 * block, 128 * block + 384)
            keys = slice(512 * seq + 128 * block, 512 * seq + 128 * block + 384)
            mask, keep = mask_of((length_ref, far_length_ref)[seq], block)
            d_attn_all = nt(d_branch_ref[rows, :], w_out_ref[...]).astype(jnp.bfloat16)
            d_attn_all = jnp.where(keep, d_attn_all, jnp.zeros_like(d_attn_all))
            d_queries, d_keys, d_values = [], [], []
            for head in range(4):
                lane = 64 * head
                query = low_ref[rows, lane : lane + 64]
                key = low_ref[keys, OWN + lane : OWN + lane + 64]
                value = low_ref[keys, 2 * OWN + lane : 2 * OWN + lane + 64]
                d_attn = d_attn_all[:, lane : lane + 64]
                masked = jnp.where(mask, nt(query, key) * SCALE, neg_large)
                probs = jnp.exp(masked - lse_ref[rows, head : head + 1])
                d_values.append(tn(probs.astype(jnp.bfloat16), d_attn))
                d_probs = nt(d_attn, value)
                inner = jnp.sum(probs * d_probs, axis=1, keepdims=True)
                d_scores = (probs * (d_probs - inner)).astype(jnp.bfloat16)
                d_queries.append(nn(d_scores, key) * SCALE)
                d_keys.append(tn(d_scores, query) * SCALE)
            part = slice(256 * block, 256 * block + 256)
            d_query = turn(jnp.concatenate(d_queries, axis=1), cosine[part], sine[part])
            d_qkv_ref[rows, :OWN] = d_query.astype(jnp.bfloat16)
            key_ref[span, :] += jnp.concatenate(d_keys, axis=1)
            value_ref[span, :] += jnp.concatenate(d_values, axis=1)
        whole = slice(512 * seq, 512 * seq + 512)
        d_qkv_ref[whole, OWN : 2 * OWN] = turn(key_ref[...], cosine, sine).astype(jnp.bfloat16)
        d_qkv_ref[whole, 2 * OWN :] = value_ref[...].astype(jnp.bfloat16)


def attention_back(me, d_branch, ring, attn, low, lse, cosine, sine, lengths):
    return pl.pallas_call(
        attend_back_kernel,
        out_shape=(
            jax.ShapeDtypeStruct((1024, 3 * OWN), jnp.bfloat16),
            jax.ShapeDtypeStruct((8, OWN, 128), jnp.bfloat16),
        ),
        in_specs=[SCALAR] + [WHOLE] * 10 + [SCALAR] * 2,
        out_specs=(WHOLE, WHOLE),
        scratch_shapes=[
            pltpu.VMEM((1024, D), jnp.bfloat16),
            pltpu.VMEM((OWN, D), jnp.bfloat16),
            pltpu.VMEM((512, OWN), jnp.float32),
            pltpu.VMEM((512, OWN), jnp.float32),
        ],
        compiler_params=vmem(12),
        cost_estimate=cost(12 << 30, 10 << 20),
        name="attend_back",
    )(me, *d_branch, ring, attn, low, lse, cosine, sine, *lengths)


def grad_kernel(
    y_ref, a_ref, w_ref, order_ref, d_qkv_ref, g_out_ref, x_ref, mean_ref, inv_ref, small_ref,
    g_ref, near_sent_ref, near_ref, far_sent_ref, far_ref,
    d_a_ref,
):
    g_gain, g_bias = jnp.zeros((1, D), jnp.float32), jnp.zeros((1, D), jnp.float32)
    for block in range(4):
        rows = slice(256 * block, 256 * block + 256)
        d_a = nt(d_qkv_ref[rows, :], w_ref[...])
        normed = (x_ref[rows, :].astype(jnp.float32) - mean_ref[rows, :]) * inv_ref[rows, :]
        g_gain += jnp.sum(d_a * normed, axis=0, keepdims=True)
        g_bias += jnp.sum(d_a, axis=0, keepdims=True)
        d_a_ref[rows, :] = d_a
    put_rows(y_ref[0], d_a_ref, (near_sent_ref, near_ref, far_sent_ref, far_ref))
    for block in range(8):
        grad = tn(a_ref[:, 128 * block : 128 * block + 128], d_qkv_ref[...]).astype(jnp.bfloat16)
        grad = jnp.concatenate([grad[:, OWN * third : OWN * third + OWN] for third in range(3)], axis=0)
        grad = tn(order_ref[...], grad).astype(jnp.bfloat16)
        for part in range(6):
            chunk = 6 * block + part
            at = 128 * (chunk // 8)
            g_ref[chunk % 8, at : at + 64, :] = grad[64 * part : 64 * part + 64, :128]
            g_ref[chunk % 8, at + 64 : at + 128, :] = grad[64 * part : 64 * part + 64, 128:]
    vectors = [g_gain, g_bias] + [small_ref[k : k + 1, :] for k in range(4)]
    lines = [v[:, 128 * k : 128 * k + 128] for v in vectors for k in range(8)]
    for place in range(8):
        g_ref[place, 768:1024, :] = g_out_ref[place]
        rows = lines[6 * place : 6 * place + 6] + [jnp.zeros((SLAB - 6, 128), jnp.float32)]
        g_ref[place, 1024:, :] = jnp.concatenate(rows, axis=0).astype(jnp.bfloat16)


def grad_step(second, a_low, w_qkv, order, d_qkv, g_out, x_all, mean, inv, small):
    return pl.pallas_call(
        grad_kernel,
        out_shape=(jax.ShapeDtypeStruct((8, 1024 + SLAB, 128), jnp.bfloat16),) + PARTS,
        in_specs=[SCALAR] + [WHOLE] * 9,
        scratch_shapes=[pltpu.VMEM((1024, D), jnp.float32)],
        out_specs=(WHOLE,) * 5,
        compiler_params=vmem(12),
        cost_estimate=cost(8 << 30, 12 << 20),
        name="grad",
    )(second, a_low, w_qkv, order, d_qkv, g_out, x_all, mean, inv, small)


def after(values, *others):
    if isinstance(values, tuple):
        return lax.optimization_barrier(values + others)[: len(values)]
    return lax.optimization_barrier((values,) + others)[0]


def both_ways(ahead, back):
    return lax.optimization_barrier((lax.ppermute(ahead, GROUP, AHEAD), lax.ppermute(back, GROUP, BACK)))


class Gather:
    def __init__(self, block):
        self.blocks = [block]
        self.next = (block, block)
        self.half = (block.shape[0] // 2 + 15) // 16 * 16
        self.count = 0

    def step(self, *waits, hold=()):
        self.count += 1
        ahead, back = after(self.next, *waits) if waits else self.next
        if self.count == 4:
            ahead, back = ahead[: self.half], back[self.half :]
        self.next = after(both_ways(ahead, back), *hold)
        self.blocks += self.next
        return self.next


class Scatter:
    def __init__(self, blocks, me):
        self.blocks, self.me = blocks, me
        self.rows = blocks.shape[1]
        self.half = (self.rows // 2 + 15) // 16 * 16
        self.count = 0
        self.next = (self.get(4, 0, self.half), self.get(4, self.half))

    def get(self, step, lo=0, hi=None):
        hi = self.rows if hi is None else hi
        at = (ring_place(self.me, step % 8), 0 * self.me + lo, 0 * self.me)
        return lax.dynamic_slice(self.blocks, at, (1, hi - lo, 128))[0]

    def step(self, *waits, hold=()):
        self.count += 1
        ahead, back = came = after(both_ways(*(after(self.next, *waits) if waits else self.next)), *hold)

        def add(moved, own):
            return (moved.astype(jnp.float32) + own.astype(jnp.float32)).astype(jnp.bfloat16)

        if self.count == 1:
            half = self.half
            ahead = jnp.concatenate([add(ahead, self.get(3, 0, half)), self.get(3, half)])
            back = jnp.concatenate([self.get(5, 0, half), add(back, self.get(5, half))])
        elif self.count < 4:
            ahead, back = add(ahead, self.get(4 - self.count)), add(back, self.get(4 + self.count))
        else:
            total = self.get(0).astype(jnp.float32) + ahead.astype(jnp.float32) + back.astype(jnp.float32)
            self.total = total.astype(jnp.bfloat16)
        self.next = (ahead, back)
        return came


def to_pair(rows, *waits):
    rows = after(rows, *waits) if waits else rows
    return rows, lax.ppermute(rows, "y", SWAP)


def to_group(pair, *waits):
    pair = after(tuple(pair), *waits) if waits else pair
    return tuple(pair) + tuple(lax.ppermute(rows, "c", SWAP) for rows in pair)


def half_sum(near_sent, near, far_sent, far):
    sent = near_sent + lax.ppermute(far_sent, "c", SWAP).astype(jnp.float32)
    kept = near + lax.ppermute(far, "c", SWAP).astype(jnp.float32)
    return lax.optimization_barrier((sent.astype(jnp.bfloat16), kept))


def full_sum(sent, kept):
    return kept + lax.ppermute(sent, "y", SWAP).astype(jnp.float32)


def normed_of(rows):
    centered = rows - jnp.mean(rows, axis=-1, keepdims=True)
    inv_scale = lax.rsqrt(jnp.mean(centered * centered, axis=-1, keepdims=True) + eps_norm)
    return centered * inv_scale, inv_scale


def norm_rows_back(out_grad, normed, inv_scale, gain):
    inner = out_grad * gain
    return inv_scale * (
        inner
        - jnp.mean(inner, axis=-1, keepdims=True)
        - normed * jnp.mean(inner * normed, axis=-1, keepdims=True)
    )


def fast_body(frames, cotangent, clip_lengths, params, first_moment, second_moment):
    z, x, c, y = (lax.axis_index(axis) for axis in EVERY)
    device = (((z * 2 + x) * 2 + c) * 2 + y).astype(jnp.int32)
    me = device[None]
    lengths = (clip_lengths, lax.ppermute(clip_lengths, "c", SWAP))
    order = np.zeros((384, 384), np.float32)
    for row in range(384):
        order[(row % 3) * 128 + row // 3, row] = 1.0
    order = jnp.asarray(order, jnp.bfloat16)

    pieces = spread(params, me)
    pieces = lax.all_to_all(pieces, EVERY, split_axis=0, concat_axis=0, tiled=True)
    first_piece, second_piece, third_piece = fix(pieces)
    first, second, third = Gather(first_piece), Gather(second_piece), Gather(third_piece)
    frames_pair = to_pair(frames[0], first_piece)
    came = first.step()
    cot_pair = to_pair(cotangent[0], frames_pair[1])
    lengths = after(lengths, first_piece)
    both = jnp.concatenate(lengths)
    frame = jnp.arange(512, dtype=jnp.int32)
    starts, ends = both[:, :1], both[:, :1] + both[:, 1:]
    position = jnp.where((frame >= starts) & (frame < ends), frame - starts, frame).astype(jnp.float32)
    inverse = jnp.exp(
        jnp.asarray(np.arange(128) % 32, jnp.float32) * (-2.0 * math.log(rope_base) / HEAD_DIM)
    )
    angle = position[:, :, None] * inverse
    cosine = jnp.cos(angle)
    sine = jnp.sin(angle) * jnp.asarray(np.where(np.arange(128) % 64 < 32, -1.0, 1.0), jnp.float32)
    came_second = first.step(cosine, sine)
    frames_parts = to_group(after(frames_pair, *came))
    first.step(frames_pair[1])
    x_all, mean_one, inv_one = prep(me, frames_parts)
    first.step(x_all)
    second.step(*came_second)
    ring_qkv, w_own, vectors = join(
        join_first_kernel,
        me,
        first.blocks,
        (
            jax.ShapeDtypeStruct((8, 768, 128), jnp.bfloat16),
            jax.ShapeDtypeStruct((8, OWN, 128), jnp.bfloat16),
            jax.ShapeDtypeStruct((6, D), jnp.float32),
        ),
        "join_first",
        [pltpu.VMEM((8, SLAB, 128), jnp.bfloat16)],
    )

    w_pair = to_pair(w_own)
    x_all, ring_qkv = after((x_all, ring_qkv), *second.next, cot_pair[1])
    came = second.step(ring_qkv)
    a_low, w_qkv, low, attn_own, lse = front(x_all, mean_one, inv_one, ring_qkv, vectors, order, cosine, sine, lengths)
    attn_pair = to_pair(attn_own, *came, w_pair[1])
    w_out = join_out(to_group(w_pair, attn_own))
    came = second.step(attn_own)
    attn_parts = to_group(attn_pair, w_out)
    attn_parts = attn_parts[:2] + after(attn_parts[2:], *came)
    c_low, branch_seq = mix(x_all, attn_parts, w_out, vectors)
    third.step(*attn_parts[2:])
    came = second.step(*attn_parts[2:])
    second.blocks[7:] = after(came, c_low)
    came = third.next
    blocks = [block.reshape(-1, 2, 64, 128) for block in second.blocks]
    shape = jax.ShapeDtypeStruct((4, 16, 64, 512), jnp.bfloat16)
    w_gate_up = join(functools.partial(join_gate_up_kernel, slice(0, 9)), me, blocks, shape, "join_gate_up", space=HBM)
    w_gate_up = w_gate_up.reshape(4, 1024, 512)
    cot_parts = to_group(cot_pair, c_low)
    gate_up, hidden = gate_step(after(c_low, *came), w_gate_up)
    came = third.step(c_low)
    g_down, d_mlp = down_grad(me, after(hidden, *came), cot_parts, vectors)
    third.step(hidden)
    third.step(g_down)
    shape = jax.ShapeDtypeStruct((1024, D), jnp.bfloat16)
    third.blocks[0] = after(third.blocks[0], g_down)
    w_down = join_twice(join_down_kernel, me, third.blocks, shape, "join_down")

    down = Scatter(g_down, device)
    d_both = hidden_back(gate_up, d_mlp, w_down)
    came = down.step(*third.next)
    d_both = after(d_both, *came)
    d_c_parts = norm_back(me, d_both, w_gate_up)
    came = down.step(d_both)
    d_c_sent, d_c_kept = half_sum(*after(tuple(d_c_parts), *came))
    g_gate_up = gate_grad(c_low, after(d_both, d_c_sent, d_c_kept))
    came = down.step(d_c_sent, hold=(g_gate_up,))
    gate_grads = Scatter(g_gate_up, device)

    x_own = frames[0].astype(jnp.float32)
    cot_own = cotangent[0].astype(jnp.float32)
    branch_own = jnp.where(y == 0, branch_seq[:256], branch_seq[256:])
    mid_own = x_own + vectors[4] * branch_own
    normed_two, scale_two = normed_of(mid_own)
    d_c_own = full_sum(d_c_sent, d_c_kept)
    d_mid = cot_own + norm_rows_back(d_c_own, normed_two, scale_two, vectors[2])
    d_branch_own = (d_mid * vectors[4]).astype(jnp.bfloat16)
    d_branch_pair = to_pair(d_branch_own)
    down.step(hold=(d_branch_own,))
    came = gate_grads.step(hold=(d_branch_own,))
    hidden = after(hidden, d_branch_own, *came)
    *out_parts, g_scale_mlp = out_step(me, hidden, w_down, cot_parts)
    came = gate_grads.step(d_branch_own, hold=(g_scale_mlp,))
    d_branch = to_group(d_branch_pair, *came, g_scale_mlp)
    out_sent, out_kept = half_sum(*out_parts)
    g_gain_two = jnp.sum(d_c_own * normed_two, axis=0)
    g_bias_two = jnp.sum(d_c_own, axis=0)
    g_scale_attn = jnp.sum(d_mid * branch_own, axis=0)
    small = jnp.concatenate([jnp.stack([g_gain_two, g_bias_two, g_scale_attn]), g_scale_mlp], axis=0)

    d_branch = after(d_branch, small)
    d_qkv, g_out = attention_back(me, d_branch, w_own, attn_own, low, lse, cosine, sine, lengths)
    came = gate_grads.step(*d_branch, hold=(d_qkv,))
    out_sent = after(out_sent, *d_branch)
    output = (mid_own + vectors[5] * full_sum(out_sent, out_kept)).astype(jnp.bfloat16)
    d_qkv = after(d_qkv, *came)
    g_first, *d_a_parts = grad_step(me, a_low, w_qkv, order, d_qkv, g_out, x_all, mean_one, inv_one, small)
    came = gate_grads.step(d_qkv, hold=(g_first,))
    first_grads = Scatter(after(g_first, *came), device)
    first_grads.step(output)
    d_a_sent, d_a_kept = half_sum(*d_a_parts)
    first_grads.step(d_a_sent)
    first_grads.step()
    normed_one, scale_one = normed_of(x_own)
    d_one = norm_rows_back(full_sum(d_a_sent, d_a_kept), normed_one, scale_one, vectors[0])
    frames_grad = (d_mid + d_one).astype(jnp.bfloat16)
    first_grads.step(frames_grad)
    g_first, g_gate_up, g_down = first_grads.total, gate_grads.total, down.total

    main = jnp.concatenate([g_first[:1024], g_gate_up, g_down]).reshape(32, 128, 128)
    slab = jnp.concatenate([main[1:, :8], main[1:, 64:72]], axis=1)
    slab = jnp.concatenate([slab, g_first[None, 1024:]])
    pieces = jnp.concatenate([main, slab], axis=1)
    pieces = lax.all_to_all(pieces, EVERY, split_axis=0, concat_axis=0, tiled=True)
    params_grad = collect(pieces, me, params.shape[0])
    new_params, new_first, new_second = adam_update(params, params_grad, first_moment, second_moment)
    return (output[None], frames_grad[None], params_grad, new_params, new_first, new_second)


def solution(mesh):
    def run(frames, cotangent, clip_lengths, params, first_moment, second_moment):
        fits = (
            mesh.shape["dp"] == 16
            and mesh.shape["seq"] == 2
            and frames.shape == (16, 512, D)
            and clip_lengths.shape == (16, 2)
        )
        if fits:
            over = Mesh(mesh.devices.reshape(4, 2, 2, 2), EVERY)
            rows, clips, flat = P(("z", "x", "c"), "y", None), P(("z", "x", "c"), None), P(EVERY)
        else:
            over = mesh
            rows, clips, flat = P("dp", "seq", None), P("dp", None), P(("dp", "seq"))
        step = jax.shard_map(
            fast_body if fits else body,
            mesh=over,
            in_specs=(rows, rows, clips, flat, flat, flat),
            out_specs=(rows, rows, flat, flat, flat, flat),
            check_vma=False,
        )
        return step(frames, cotangent, clip_lengths, params, first_moment, second_moment)

    return run
```
